32 devices in a mesh: seq: 8 (over z, y), rep: 4 (over x, core).
Axes of the slice: x: 2, y: 2, z: 4, core: 2. Of those that a mesh axis runs over, the one named last changes fastest.
Arguments:
- tokens: bfloat16 [1024, 2048], P('seq'), may hold values from -6 to 6
- norm_gain: float32 [2048], replicated, may hold values from 0.25 to 1.75
- refusal_dir: float32 [2048], replicated, may hold values from -6 to 6
- expert_ids: int32 [1024, 8], P('seq'), may hold values from 0 to 127, as said below
- gate_probs: float32 [1024, 8], P('seq'), may hold values from 0.05 to 0.5
- w_gate: bfloat16 [128, 768, 2048], P('seq', 'rep'), may hold values from -0.125 to 0.125
- w_up: bfloat16 [128, 768, 2048], P('seq', 'rep'), may hold values from -0.125 to 0.125
- w_down: bfloat16 [128, 768, 2048], P('seq', 'rep'), may hold values from -0.21875 to 0.21875
Outputs:
- ablated: bfloat16 [1024, 2048], P('seq', 'rep')
The draws below stay inside these ranges and needn't reach their ends.
Inputs may be any that keep to these rules, and one draw needn't show every extreme that they name: `expert_ids`: each row names 8 different experts. Among the 128 rows of one device no expert is named more than 12 times, and some expert is named exactly 12 times in the rows of every device.
All inputs are finite; a program needn't handle non-finite values.
Results may differ from the reference program's by a relative error of at most 0.0095.
Values may be sent and summed in bfloat16 or wider, within the bound.
No kernel may reach another device: no remote copies, remote signals or barrier semaphores. Data moves between devices by JAX's collectives and lax.ppermute only.
A program may use at most 128 MiB of HBM per device.

```python
import math
import jax
import jax.numpy as jnp
from jax import lax

D = 2048
HID = 768
EXPERTS = 128
TOP = 8
TOK_DEV = 128
TOKENS = 1024
CAP = 12
N_SEQ = 8
N_REP = 4


def draw_expert_ids(key, part):
    blocks = TOKENS // TOK_DEV
    slot_count = TOK_DEV * TOP
    mean_load = slot_count // EXPERTS
    quarter_count = EXPERTS // 4
    low_count = EXPERTS - 2 * quarter_count
    ranking = jax.random.permutation(jax.random.fold_in(key, 7), EXPERTS).astype(jnp.int32)

    def one_block(block_key):
        key_a = jax.random.fold_in(block_key, 1)
        key_b = jax.random.fold_in(block_key, 2)
        key_c = jax.random.fold_in(block_key, 3)
        key_d = jax.random.fold_in(block_key, 4)
        others = jax.random.permutation(key_a, ranking[quarter_count:])
        signs = jax.random.randint(key_b, (low_count // 2,), 0, 2).astype(jnp.int32)
        offsets = jnp.stack([signs, -signs], axis=1).reshape(low_count)
        order_ids = jnp.concatenate([ranking[:quarter_count], others])
        loads = jnp.concatenate([jnp.full((quarter_count,), 3 * mean_load // 2, jnp.int32), jnp.full((quarter_count,), mean_load, jnp.int32), 3 * mean_load // 4 + offsets])
        shuffle = jax.random.permutation(key_c, EXPERTS).astype(jnp.int32)
        order_ids = order_ids[shuffle]
        loads = loads[shuffle]
        ends = jnp.cumsum(loads).astype(jnp.int32)
        slot_iota = jnp.arange(slot_count, dtype=jnp.int32)
        run_of = jnp.searchsorted(ends, slot_iota, side='right').astype(jnp.int32)
        expert_of = order_ids[run_of]
        token_perm = jax.random.permutation(key_d, TOK_DEV).astype(jnp.int32)
        chosen = jnp.zeros((TOK_DEV, TOP), jnp.int32)
        return chosen.at[token_perm[slot_iota % TOK_DEV], slot_iota // TOK_DEV].set(expert_of)
    block_keys = jax.random.split(jax.random.fold_in(key, 11), blocks)
    return jax.vmap(one_block)(block_keys).reshape(TOKENS, TOP)


def steps_of(stream_key, dims, shards, smallest, top_value):
    loudness = 1.0
    for axis_at, shards_of in shards:
        steps = jax.random.uniform(jax.random.fold_in(jax.random.fold_in(stream_key, 6), axis_at), (shards_of,), jnp.float32, smallest / len(shards), top_value / len(shards))
        loudness = loudness * jnp.repeat(jnp.exp(steps), dims[axis_at] // shards_of).reshape((-1,) + (1,) * (len(dims) - 1 - axis_at))
    return loudness


def centred(own_key, dims, scale, most, cuts=(), kind=jnp.bfloat16):
    array = jax.random.normal(own_key, dims, jnp.float32) * scale
    if len(cuts) > 0:
        array = steps_of(own_key, dims, cuts, -0.22, 0.18) * array
    return jnp.clip(array, min=-most, max=most).astype(kind)


def setup_inputs(seed: int = 0) -> dict:
    keys = jax.random.split(jax.random.key(seed), 9)
    tokens = centred(keys[0], (TOKENS, D), 1.0, 6.0, ((0, 8),))
    norm_gain = jnp.clip(1.0 + 0.15 * jax.random.normal(keys[1], (D,), jnp.float32), 0.25, 1.75)
    refusal_dir = centred(keys[2], (D,), 1.0, 6.0, (), jnp.float32)
    expert_ids = draw_expert_ids(jax.random.fold_in(keys[8], 71), 0)
    gate_probs = jnp.clip(jnp.exp(math.log(0.5) - 2.3025851 * jax.random.uniform(keys[4], (TOKENS, TOP), jnp.float32) ** steps_of(keys[4], (TOKENS, TOP), ((0, 8),), -0.2, 0.2)), 0.05, 0.5)
    w_gate = centred(keys[5], (EXPERTS, HID, D), D ** -0.5, 0.125, ((0, 8), (1, 4)))
    w_up = centred(keys[6], (EXPERTS, HID, D), D ** -0.5, 0.125, ((0, 8), (1, 4)))
    w_down = centred(keys[7], (EXPERTS, HID, D), HID ** -0.5, 0.21875, ((0, 8), (1, 4)))
    return {"tokens": tokens, "norm_gain": norm_gain, "refusal_dir": refusal_dir, "expert_ids": expert_ids, "gate_probs": gate_probs, "w_gate": w_gate, "w_up": w_up, "w_down": w_down}


def reference(tokens, norm_gain, refusal_dir, expert_ids, gate_probs, w_gate, w_up, w_down):
    tokens_f32 = tokens.astype(jnp.float32)
    inv_rms = lax.rsqrt(lax.optimization_barrier(jnp.mean(tokens_f32 * tokens_f32, axis=1, keepdims=True)) + 1e-06)
    normed = (tokens_f32 * inv_rms * norm_gain).astype(jnp.bfloat16)
    slot_count = TOKENS * TOP
    flat_ids = expert_ids.reshape(slot_count)
    flat_probs = gate_probs.reshape(slot_count)
    rows_most = N_SEQ * CAP
    quarter_width = HID // N_REP

    def per_expert(mixed, expert):
        picked = jnp.nonzero(flat_ids == expert, size=rows_most, fill_value=slot_count)[0].astype(jnp.int32)
        filled = picked < slot_count
        where_at = jnp.where(filled, picked, 0).astype(jnp.int32)
        token_at = where_at // TOP
        weight_at = jnp.where(filled, flat_probs[where_at], jnp.float32(0.0))
        row_block = normed[token_at]
        gate_val = jnp.einsum('rd,fd->rf', row_block, w_gate[expert], preferred_element_type=jnp.float32)
        up_val = jnp.einsum('rd,fd->rf', row_block, w_up[expert], preferred_element_type=jnp.float32)
        hidden = (jax.nn.silu(gate_val) * up_val).astype(jnp.bfloat16)
        hidden_q = hidden.reshape(rows_most, N_REP, quarter_width).astype(jnp.float32)
        down_q = w_down[expert].reshape(N_REP, quarter_width, D).astype(jnp.float32)
        pieces = jnp.einsum('rqh,qhd->rqd', hidden_q, down_q).astype(jnp.bfloat16).astype(jnp.float32)
        expert_out = lax.optimization_barrier(jnp.sum(pieces, axis=1)) * weight_at[:, None]
        return (mixed.at[token_at].add(expert_out), None)
    mixed, _ = lax.scan(per_expert, jnp.zeros((TOKENS, D), jnp.float32), jnp.arange(EXPERTS, dtype=jnp.int32))
    residual = tokens_f32 + mixed
    unit_dir = refusal_dir / jnp.sqrt(jnp.sum(refusal_dir * refusal_dir) + 1e-06)
    along_dir = lax.optimization_barrier(jnp.sum(residual * unit_dir, axis=1))
    return (residual - along_dir[:, None] * unit_dir).astype(jnp.bfloat16)
```

```python
import functools

import jax
import jax.numpy as jnp
from jax import lax
from jax.experimental import pallas as pl
from jax.experimental.pallas import tpu as pltpu
from jax.sharding import PartitionSpec as P

CAP = 12
SLOTS = 16


def contract(lhs, rhs, lhs_dim, rhs_dim):
    return lax.dot_general(
        lhs, rhs, (((lhs_dim,), (rhs_dim,)), ((), ())), preferred_element_type=jnp.float32
    )


def moe_kernel(
    ids_ref, probs_ref, unit_ref, toks_ref, w_gate_hbm, w_up_hbm, w_down_hbm, out_ref,
    w_gate, w_up, w_down, rows, onehots, row_probs, mixed, sems,
):
    n_seq, top_k, tok_rows = ids_ref.shape
    exp_dev = w_gate.shape[0]
    n_rep = toks_ref.shape[0] // n_seq
    part = toks_ref.shape[2]
    slots_src = exp_dev * SLOTS
    copies = []
    for e in range(exp_dev):
        triple = [
            pltpu.make_async_copy(src.at[e], dst.at[e], sems.at[i, e])
            for i, (src, dst) in enumerate(
                ((w_gate_hbm, w_gate), (w_up_hbm, w_up), (w_down_hbm, w_down))
            )
        ]
        for copy in triple:
            copy.start()
        copies.append(triple)

    exp_iota = lax.broadcasted_iota(jnp.int32, (exp_dev, tok_rows), 0)
    earlier = (
        lax.broadcasted_iota(jnp.int32, (tok_rows, tok_rows), 0)
        < lax.broadcasted_iota(jnp.int32, (tok_rows, tok_rows), 1)
    ).astype(jnp.float32).astype(jnp.bfloat16)
    slot_iota = lax.broadcasted_iota(jnp.int32, (exp_dev, SLOTS, tok_rows), 1).astype(jnp.float32)

    def gather_source(s, carry):
        ids = ids_ref[s]
        probs = probs_ref[s]
        hit = jnp.zeros((exp_dev, tok_rows), jnp.float32)
        prob = jnp.zeros((exp_dev, tok_rows), jnp.float32)
        for k in range(top_k):
            same = ids[k : k + 1, :] == exp_iota
            hit = jnp.where(same, 1.0, hit)
            prob = jnp.where(same, probs[k : k + 1, :], prob)
        rank = contract(hit.astype(jnp.bfloat16), earlier, 1, 0)
        slot = jnp.where(hit > 0.0, rank, -1.0)
        onehot = jnp.where(slot[:, None, :] == slot_iota, 1.0, 0.0)
        row_probs[s] = jnp.sum(onehot * prob[:, None, :], axis=2, keepdims=True)
        onehot = onehot.reshape(slots_src, tok_rows).astype(jnp.bfloat16)
        onehots[s] = onehot
        for r in range(n_rep):
            got = contract(onehot, toks_ref[s * n_rep + r], 1, 0)
            rows[s, :, :, r * part : (r + 1) * part] = got.astype(jnp.bfloat16).reshape(
                exp_dev, SLOTS, part
            )
        return carry

    lax.fori_loop(0, n_seq, gather_source, 0)

    for e in range(exp_dev):
        for copy in copies[e]:
            copy.wait()
        taken = rows[:, e].reshape(n_seq * SLOTS, n_rep * part)
        gate_val = contract(taken, w_gate[e], 1, 1)
        up_val = contract(taken, w_up[e], 1, 1)
        hidden = (gate_val / (1.0 + jnp.exp(-gate_val)) * up_val).astype(jnp.bfloat16)
        weight = row_probs[:, e].reshape(n_seq * SLOTS, 1)
        for r in range(n_rep):
            cols = slice(r * part, (r + 1) * part)
            piece = contract(hidden, w_down[e, :, cols], 1, 0) * weight
            rows[:, e, :, cols] = piece.astype(jnp.bfloat16).reshape(n_seq, SLOTS, part)

    def combine_source(s, carry):
        along = jnp.zeros((tok_rows, 1), jnp.float32)
        for r in range(n_rep):
            cols = slice(r * part, (r + 1) * part)
            got = contract(onehots[s], rows[s, :, :, cols].reshape(slots_src, part), 0, 0)
            mixed[:, cols] = got
            along += jnp.sum(got * unit_ref[:, cols], axis=1, keepdims=True)
        for r in range(n_rep):
            cols = slice(r * part, (r + 1) * part)
            out_ref[s * n_rep + r] = (mixed[:, cols] - along * unit_ref[:, cols]).astype(
                jnp.bfloat16
            )
        return carry

    lax.fori_loop(0, n_seq, combine_source, 0)


def moe_partial(ids, probs, unit_dir, toks, w_gate, w_up, w_down):
    n_seq, top_k, tok_rows = ids.shape
    exp_dev, hid_dev, model_width = w_gate.shape
    vmem = pl.BlockSpec(memory_space=pltpu.VMEM)
    hbm = pl.BlockSpec(memory_space=pl.ANY)
    return pl.pallas_call(
        moe_kernel,
        out_shape=jax.ShapeDtypeStruct(toks.shape, jnp.bfloat16),
        in_specs=[vmem, vmem, vmem, vmem, hbm, hbm, hbm],
        out_specs=vmem,
        scratch_shapes=[
            pltpu.VMEM(w_gate.shape, jnp.bfloat16),
            pltpu.VMEM(w_up.shape, jnp.bfloat16),
            pltpu.VMEM(w_down.shape, jnp.bfloat16),
            pltpu.VMEM((n_seq, exp_dev, SLOTS, model_width), jnp.bfloat16),
            pltpu.VMEM((n_seq, exp_dev * SLOTS, tok_rows), jnp.bfloat16),
            pltpu.VMEM((n_seq, exp_dev, SLOTS, 1), jnp.float32),
            pltpu.VMEM((tok_rows, model_width), jnp.float32),
            pltpu.SemaphoreType.DMA((3, exp_dev)),
        ],
        compiler_params=pltpu.CompilerParams(vmem_limit_bytes=62 * 1024 * 1024),
        cost_estimate=pl.CostEstimate(
            flops=6 * n_seq * SLOTS * exp_dev * hid_dev * model_width,
            bytes_accessed=6 * exp_dev * hid_dev * model_width + 4 * toks.size,
            transcendentals=0,
        ),
    )(ids, probs, unit_dir, toks, w_gate, w_up, w_down)


def gathered(tokens, norm_gain, refusal_dir, expert_ids, gate_probs, w_gate, w_up, w_down):
    tok_rows, model_width = tokens.shape
    n_rep = lax.axis_size("rep")
    exp_dev = w_gate.shape[0]
    part = model_width // n_rep
    rep_offset = lax.axis_index("rep") * part

    meta = jnp.concatenate([expert_ids.T.astype(jnp.float32), gate_probs.T], axis=0)
    meta = lax.all_gather(meta, "seq")
    top_k = expert_ids.shape[1]
    ids = meta[:, :top_k].astype(jnp.int32) - lax.axis_index("seq") * exp_dev
    probs = meta[:, top_k:]

    tokens_f32 = tokens.astype(jnp.float32)
    inv_rms = lax.rsqrt(jnp.mean(tokens_f32 * tokens_f32, axis=1, keepdims=True) + 1e-06)
    own_tokens = lax.dynamic_slice_in_dim(tokens, rep_offset, part, 1).astype(jnp.float32)
    own_gain = lax.dynamic_slice_in_dim(norm_gain, rep_offset, part, 0)
    normed = (own_tokens * inv_rms * own_gain).astype(jnp.bfloat16)
    toks = lax.all_gather(normed, ("seq", "rep"))

    unit_dir = refusal_dir / jnp.sqrt(jnp.sum(refusal_dir * refusal_dir) + 1e-06)
    partial = moe_partial(ids, probs, unit_dir[None, :], toks, w_gate, w_up, w_down)
    summed = lax.psum_scatter(partial, ("seq", "rep"), scatter_dimension=0, tiled=True)[0]

    along_dir = jnp.sum(tokens_f32 * unit_dir, axis=1, keepdims=True)
    unit_slice = lax.dynamic_slice_in_dim(unit_dir, rep_offset, part, 0)
    ablated = own_tokens - along_dir * unit_slice + summed.astype(jnp.float32)
    return ablated.astype(jnp.bfloat16)


def exchanged(tokens, norm_gain, refusal_dir, expert_ids, gate_probs, w_gate, w_up, w_down):
    tok_rows, model_width = tokens.shape
    top_k = expert_ids.shape[1]
    n_seq = lax.axis_size("seq")
    n_rep = lax.axis_size("rep")
    exp_dev = w_gate.shape[0]
    experts = exp_dev * n_seq
    slot_count = tok_rows * top_k
    part_width = model_width // n_rep
    tokens_f32 = tokens.astype(jnp.float32)
    inv_rms = lax.rsqrt(jnp.mean(tokens_f32 * tokens_f32, axis=1, keepdims=True) + 1e-06)
    normed = (tokens_f32 * inv_rms * norm_gain).astype(jnp.bfloat16)
    flat_ids = expert_ids.reshape(slot_count)
    onehot = (flat_ids[:, None] == jnp.arange(experts, dtype=jnp.int32)[None, :]).astype(jnp.int32)
    slot_rank = jnp.sum(jnp.cumsum(onehot, axis=0) * onehot, axis=1) - 1
    target = flat_ids * CAP + slot_rank
    repeated = jnp.broadcast_to(normed[:, None, :], (tok_rows, top_k, model_width)).reshape(
        slot_count, model_width
    )
    sendbuf = jnp.zeros((experts * CAP, model_width), jnp.bfloat16).at[target].set(repeated)
    sendbuf = sendbuf.reshape(n_seq, exp_dev, CAP, model_width)
    arrived = lax.all_to_all(sendbuf, "seq", split_axis=0, concat_axis=0, tiled=True)
    gate_val = jnp.einsum("secd,efd->secf", arrived, w_gate, preferred_element_type=jnp.float32)
    up_val = jnp.einsum("secd,efd->secf", arrived, w_up, preferred_element_type=jnp.float32)
    hidden = (jax.nn.silu(gate_val) * up_val).astype(jnp.bfloat16)
    pieces = jnp.einsum(
        "secf,efd->secd", hidden, w_down, preferred_element_type=jnp.float32
    ).astype(jnp.bfloat16)
    probs_flat = gate_probs.reshape(slot_count)[:, None]
    returned = lax.all_to_all(pieces, "seq", split_axis=0, concat_axis=0, tiled=True)
    returned = returned.reshape(experts * CAP, model_width)
    weighted = returned[target].astype(jnp.float32) * probs_flat
    moe_part = jnp.sum(weighted.reshape(tok_rows, top_k, model_width), axis=1)
    summed = lax.psum_scatter(
        moe_part.astype(jnp.bfloat16), "rep", scatter_dimension=1, tiled=True
    ).astype(jnp.float32)
    unit_dir = refusal_dir / jnp.sqrt(jnp.sum(refusal_dir * refusal_dir) + 1e-06)
    rep_offset = lax.axis_index("rep") * part_width
    unit_slice = lax.dynamic_slice_in_dim(unit_dir, rep_offset, part_width, 0)
    own_tokens = lax.dynamic_slice_in_dim(tokens_f32, rep_offset, part_width, 1)
    residual = own_tokens + summed
    along_dir = lax.psum(jnp.sum(residual * unit_slice, axis=1), "rep")
    return (residual - along_dir[:, None] * unit_slice).astype(jnp.bfloat16)


def local(tokens, norm_gain, refusal_dir, expert_ids, gate_probs, w_gate, w_up, w_down):
    plan = gathered if w_gate.shape[0] * CAP >= tokens.shape[0] else exchanged
    return plan(tokens, norm_gain, refusal_dir, expert_ids, gate_probs, w_gate, w_up, w_down)


def solution(mesh):
    placed = (
        P("seq", None),
        P(),
        P(),
        P("seq", None),
        P("seq", None),
        P("seq", "rep", None),
        P("seq", "rep", None),
        P("seq", "rep", None),
    )
    return jax.shard_map(
        local, mesh=mesh, in_specs=placed, out_specs=P("seq", "rep"), check_vma=False
    )
```

```python
import functools

import jax
import jax.numpy as jnp
from jax import lax
from jax.experimental import pallas as pl
from jax.experimental.pallas import tpu as pltpu
from jax.sharding import PartitionSpec as P

CAP = 12
SLOTS = 16


def contract(lhs, rhs, lhs_dim, rhs_dim):
    return lax.dot_general(
        lhs, rhs, (((lhs_dim,), (rhs_dim,)), ((), ())), preferred_element_type=jnp.float32
    )


def group_offset(rep, color, dx, dc, width):
    return pl.multiple_of((rep ^ (2 * dx + dc)) * 2 * width + color * width, width)


def token_pieces(n_z, width):
    others = range(1, n_z)
    pieces = [[(2 * d, [(0, 0), (1, 0)])] for d in others]
    pieces.append([(1, [(0, 0), (1, 0), (1, 1)])])
    pieces.append(
        [(2 * d, [(1, 1)]) for d in others] + [(2 * d, [(0, 1)]) for d in others] + [(1, [(0, 1)])]
    )
    pieces.append([(2 * d + 1, [(0, 0)]) for d in others])
    pieces.append([(2 * d + 1, [(0, 1)]) for d in others])
    pieces.append([(2 * d + 1, [(1, 0), (1, 1)]) for d in others])
    return pieces


def sum_pieces(n_z):
    blocks = range(2 * n_z)
    return [
        (list(blocks), [(0, 1)]),
        ([2 * d + 1 for d in range(n_z)], [(1, 0), (1, 1)]),
        (list(blocks), [(0, 0)]),
        ([2 * d for d in range(n_z)], [(1, 0), (1, 1)]),
    ]


def moe_kernel(n_pieces, *refs):
    ids_ref, probs_ref, unit_ref, own_hbm = refs[:4]
    pieces_hbm = refs[4 : 4 + n_pieces]
    w_gate_hbm, w_up_hbm, w_down_hbm = refs[4 + n_pieces : 7 + n_pieces]
    out_refs = refs[7 + n_pieces : 15 + n_pieces]
    own = refs[15 + n_pieces]
    pieces = refs[16 + n_pieces : 16 + 2 * n_pieces]
    (w_gate, w_up, w_down, rows, onehots, row_probs, mixed, tok_sems, sems) = refs[
        16 + 2 * n_pieces :
    ]
    n_seq, top_k, tok_rows = ids_ref.shape
    n_z = n_seq // 2
    exp_dev = w_gate.shape[0]
    model_width = own.shape[1]
    width = model_width // 8
    slots_src = exp_dev * SLOTS
    rep = lax.axis_index("rep")
    tok_copies = [
        pltpu.make_async_copy(src, dst, tok_sems.at[i])
        for i, (src, dst) in enumerate(zip((own_hbm, *pieces_hbm), (own, *pieces)))
    ]
    for copy in tok_copies:
        copy.start()
    copies = []
    for e in range(exp_dev):
        triple = [
            pltpu.make_async_copy(src.at[e], dst.at[e], sems.at[i, e])
            for i, (src, dst) in enumerate(
                ((w_gate_hbm, w_gate), (w_up_hbm, w_up), (w_down_hbm, w_down))
            )
        ]
        for copy in triple:
            copy.start()
        copies.append(triple)

    exp_iota = lax.broadcasted_iota(jnp.int32, (exp_dev, tok_rows), 0)
    earlier = (
        lax.broadcasted_iota(jnp.int32, (tok_rows, tok_rows), 0)
        < lax.broadcasted_iota(jnp.int32, (tok_rows, tok_rows), 1)
    ).astype(jnp.float32).astype(jnp.bfloat16)
    slot_iota = lax.broadcasted_iota(jnp.int32, (exp_dev, SLOTS, tok_rows), 1).astype(jnp.float32)

    def place_block(j, carry):
        ids = ids_ref[j]
        probs = probs_ref[j]
        hit = jnp.zeros((exp_dev, tok_rows), jnp.float32)
        prob = jnp.zeros((exp_dev, tok_rows), jnp.float32)
        for k in range(top_k):
            same = ids[k : k + 1, :] == exp_iota
            hit = jnp.where(same, 1.0, hit)
            prob = jnp.where(same, probs[k : k + 1, :], prob)
        rank = contract(hit.astype(jnp.bfloat16), earlier, 1, 0)
        slot = jnp.where(hit > 0.0, rank, -1.0)
        onehot = jnp.where(slot[:, None, :] == slot_iota, 1.0, 0.0)
        row_probs[j] = jnp.sum(onehot * prob[:, None, :], axis=2, keepdims=True)
        onehots[j] = onehot.reshape(slots_src, tok_rows).astype(jnp.bfloat16)
        return carry

    lax.fori_loop(0, n_seq, place_block, 0)

    def pick(j, toks, columns):
        got = contract(onehots[j], toks, 1, 0).astype(jnp.bfloat16)
        rows[j, :, :, columns] = got.reshape(exp_dev, SLOTS, toks.shape[1])

    tok_copies[0].wait()
    for q in range(4):
        cols = slice(2 * q * width, 2 * (q + 1) * width)
        pick(0, own[:, cols], cols)
    kinds = token_pieces(n_z, width)
    for i, piece in enumerate(pieces):
        tok_copies[1 + i].wait()
        dc = i // len(kinds)
        for at, (j, runs) in enumerate(kinds[i % len(kinds)]):
            for n, (color, dx) in enumerate(runs):
                cols = slice(n * width, (n + 1) * width)
                toks = piece[:, cols] if len(piece.shape) == 2 else piece[at, :, cols]
                pick(j, toks, pl.ds(group_offset(rep, color, dx, dc, width), width))

    for e in range(exp_dev):
        for copy in copies[e]:
            copy.wait()
        taken = rows[:, e].reshape(n_seq * SLOTS, model_width)
        gate_val = contract(taken, w_gate[e], 1, 1)
        up_val = contract(taken, w_up[e], 1, 1)
        hidden = (gate_val / (1.0 + jnp.exp(-gate_val)) * up_val).astype(jnp.bfloat16)
        weight = row_probs[:, e].reshape(n_seq * SLOTS, 1)
        for q in range(4):
            cols = slice(2 * q * width, 2 * (q + 1) * width)
            piece = contract(hidden, w_down[e, :, cols], 1, 0) * weight
            rows[:, e, :, cols] = piece.astype(jnp.bfloat16).reshape(n_seq, SLOTS, 2 * width)

    places = {}
    for i, (blocks, runs) in enumerate(sum_pieces(n_z)):
        for at, j in enumerate(blocks):
            places.setdefault(j, []).append((i, at, runs))
    for j in range(n_seq):
        along = jnp.zeros((tok_rows, 1), jnp.float32)
        for q in range(4):
            cols = slice(2 * q * width, 2 * (q + 1) * width)
            got = contract(onehots[j], rows[j, :, :, cols].reshape(slots_src, 2 * width), 0, 0)
            mixed[:, cols] = got
            along += jnp.sum(got * unit_ref[:, cols], axis=1, keepdims=True)
        for dc in range(2):
            for i, at, runs in places[j]:
                for n, (color, dx) in enumerate(runs):
                    cols = pl.ds(group_offset(rep, color, dx, dc, width), width)
                    value = mixed[:, cols] - along * unit_ref[:, cols]
                    out_refs[4 * dc + i][at, :, n * width : (n + 1) * width] = value.astype(
                        jnp.bfloat16
                    )


def moe_partial(ids, probs, unit_dir, own, pieces, w_gate, w_up, w_down):
    n_seq, top_k, tok_rows = ids.shape
    exp_dev, hid_dev, model_width = w_gate.shape
    width = model_width // 8
    vmem = pl.BlockSpec(memory_space=pltpu.VMEM)
    hbm = pl.BlockSpec(memory_space=pl.ANY)
    n_pieces = len(pieces)
    outs = [
        jax.ShapeDtypeStruct((len(blocks), tok_rows, len(runs) * width), jnp.bfloat16)
        for _ in range(2)
        for blocks, runs in sum_pieces(n_seq // 2)
    ]
    return pl.pallas_call(
        functools.partial(moe_kernel, n_pieces),
        out_shape=outs,
        in_specs=[vmem] * 3 + [hbm] * (n_pieces + 4),
        out_specs=[vmem] * len(outs),
        scratch_shapes=[
            pltpu.VMEM(own.shape, jnp.bfloat16),
            *[pltpu.VMEM(piece.shape, jnp.bfloat16) for piece in pieces],
            pltpu.VMEM(w_gate.shape, jnp.bfloat16),
            pltpu.VMEM(w_up.shape, jnp.bfloat16),
            pltpu.VMEM(w_down.shape, jnp.bfloat16),
            pltpu.VMEM((n_seq, exp_dev, SLOTS, model_width), jnp.bfloat16),
            pltpu.VMEM((n_seq, exp_dev * SLOTS, tok_rows), jnp.bfloat16),
            pltpu.VMEM((n_seq, exp_dev, SLOTS, 1), jnp.float32),
            pltpu.VMEM((tok_rows, model_width), jnp.float32),
            pltpu.SemaphoreType.DMA((1 + n_pieces,)),
            pltpu.SemaphoreType.DMA((3, exp_dev)),
        ],
        compiler_params=pltpu.CompilerParams(vmem_limit_bytes=62 * 1024 * 1024),
        cost_estimate=pl.CostEstimate(
            flops=6 * n_seq * SLOTS * exp_dev * hid_dev * model_width,
            bytes_accessed=6 * exp_dev * hid_dev * model_width + 4 * n_seq * own.size,
            transcendentals=0,
        ),
    )(ids, probs, unit_dir, own, *pieces, w_gate, w_up, w_down)


def swap(value, axis, distance):
    size = lax.axis_size(axis)
    return lax.ppermute(value, axis, [(i, i ^ distance) for i in range(size)])


def added(*terms):
    return sum(term.astype(jnp.float32) for term in terms).astype(jnp.bfloat16)


def gathered(tokens, norm_gain, refusal_dir, expert_ids, gate_probs, w_gate, w_up, w_down):
    tok_rows, model_width = tokens.shape
    top_k = expert_ids.shape[1]
    n_seq = lax.axis_size("seq")
    n_z = n_seq // 2
    others = range(1, n_z)
    exp_dev = w_gate.shape[0]
    width = model_width // 8
    part = 2 * width
    rep = lax.axis_index("rep")

    meta = jnp.concatenate([expert_ids.T.astype(jnp.float32), gate_probs.T], axis=0)
    meta = [meta] + [swap(meta, "seq", 2 * d) for d in others]
    meta_y = swap(jnp.stack(meta), "seq", 1)
    meta = jnp.stack([m for d in range(n_z) for m in (meta[d], meta_y[d])])
    ids = meta[:, :top_k].astype(jnp.int32) - lax.axis_index("seq") * exp_dev
    probs = meta[:, top_k:]

    tokens_f32 = tokens.astype(jnp.float32)
    inv_rms = lax.rsqrt(jnp.mean(tokens_f32 * tokens_f32, axis=1, keepdims=True) + 1e-06)
    normed = (tokens_f32 * inv_rms * norm_gain).astype(jnp.bfloat16)

    def group(color, dx, count):
        return lax.dynamic_slice_in_dim(
            normed, group_offset(rep, color, dx, 0, width), count * width, 1
        )

    both = group(0, 0, 2)
    from_z = [swap(both, "seq", 2 * d) for d in others]
    from_y = swap(jnp.concatenate([both, group(1, 1, 1)], axis=1), "seq", 1)
    first = [piece[:, :width] for piece in from_z]
    second = [piece[:, width:] for piece in from_z]
    x_two = swap(jnp.stack(second + first + [from_y[:, :width]]), "rep", 2)
    y_two = swap(jnp.stack(first), "seq", 1)
    x_three = swap(y_two, "rep", 2)
    y_three = swap(
        jnp.concatenate([jnp.stack(second), x_two[: n_z - 1]], axis=2), "seq", 1
    )
    pieces = [*from_z, from_y, x_two, y_two, x_three, y_three]
    pieces = pieces + [swap(piece, "rep", 1) for piece in pieces]

    unit_dir = refusal_dir / jnp.sqrt(jnp.sum(refusal_dir * refusal_dir) + 1e-06)
    sums = moe_partial(ids, probs, unit_dir[None, :], normed, pieces, w_gate, w_up, w_down)
    kept, sent = sums[:4], sums[4:]
    first_far, second_far, first_near, second_near = [
        added(mine, swap(theirs, "rep", 1)) for mine, theirs in zip(kept, sent)
    ]
    first_sum = added(first_near, swap(first_far, "rep", 2))
    second_sum = added(second_near, swap(second_far, "seq", 1))
    by_y = first_sum.reshape(n_z, 2, tok_rows, width)
    first_sum = added(by_y[:, 0], swap(by_y[:, 1], "seq", 1))
    second_sum = added(second_sum[:, :, :width], swap(second_sum[:, :, width:], "rep", 2))
    blocks = jnp.concatenate([first_sum, second_sum], axis=2)
    arrived = [swap(blocks[d], "seq", 2 * d) for d in others]
    summed = sum(term.astype(jnp.float32) for term in [blocks[0], *arrived])

    along_dir = jnp.sum(tokens_f32 * unit_dir, axis=1, keepdims=True)
    unit_slice = lax.dynamic_slice_in_dim(unit_dir, rep * part, part, 0)
    own_tokens = lax.dynamic_slice_in_dim(tokens, rep * part, part, 1).astype(jnp.float32)
    return (own_tokens - along_dir * unit_slice + summed).astype(jnp.bfloat16)


def exchanged(tokens, norm_gain, refusal_dir, expert_ids, gate_probs, w_gate, w_up, w_down):
    tok_rows, model_width = tokens.shape
    top_k = expert_ids.shape[1]
    n_seq = lax.axis_size("seq")
    n_rep = lax.axis_size("rep")
    exp_dev = w_gate.shape[0]
    experts = exp_dev * n_seq
    slot_count = tok_rows * top_k
    part_width = model_width // n_rep
    tokens_f32 = tokens.astype(jnp.float32)
    inv_rms = lax.rsqrt(jnp.mean(tokens_f32 * tokens_f32, axis=1, keepdims=True) + 1e-06)
    normed = (tokens_f32 * inv_rms * norm_gain).astype(jnp.bfloat16)
    flat_ids = expert_ids.reshape(slot_count)
    onehot = (flat_ids[:, None] == jnp.arange(experts, dtype=jnp.int32)[None, :]).astype(jnp.int32)
    slot_rank = jnp.sum(jnp.cumsum(onehot, axis=0) * onehot, axis=1) - 1
    target = flat_ids * CAP + slot_rank
    repeated = jnp.broadcast_to(normed[:, None, :], (tok_rows, top_k, model_width)).reshape(
        slot_count, model_width
    )
    sendbuf = jnp.zeros((experts * CAP, model_width), jnp.bfloat16).at[target].set(repeated)
    sendbuf = sendbuf.reshape(n_seq, exp_dev, CAP, model_width)
    arrived = lax.all_to_all(sendbuf, "seq", split_axis=0, concat_axis=0, tiled=True)
    gate_val = jnp.einsum("secd,efd->secf", arrived, w_gate, preferred_element_type=jnp.float32)
    up_val = jnp.einsum("secd,efd->secf", arrived, w_up, preferred_element_type=jnp.float32)
    hidden = (jax.nn.silu(gate_val) * up_val).astype(jnp.bfloat16)
    pieces = jnp.einsum(
        "secf,efd->secd", hidden, w_down, preferred_element_type=jnp.float32
    ).astype(jnp.bfloat16)
    probs_flat = gate_probs.reshape(slot_count)[:, None]
    returned = lax.all_to_all(pieces, "seq", split_axis=0, concat_axis=0, tiled=True)
    returned = returned.reshape(experts * CAP, model_width)
    weighted = returned[target].astype(jnp.float32) * probs_flat
    moe_part = jnp.sum(weighted.reshape(tok_rows, top_k, model_width), axis=1)
    summed = lax.psum_scatter(
        moe_part.astype(jnp.bfloat16), "rep", scatter_dimension=1, tiled=True
    ).astype(jnp.float32)
    unit_dir = refusal_dir / jnp.sqrt(jnp.sum(refusal_dir * refusal_dir) + 1e-06)
    rep_offset = lax.axis_index("rep") * part_width
    unit_slice = lax.dynamic_slice_in_dim(unit_dir, rep_offset, part_width, 0)
    own_tokens = lax.dynamic_slice_in_dim(tokens_f32, rep_offset, part_width, 1)
    residual = own_tokens + summed
    along_dir = lax.psum(jnp.sum(residual * unit_slice, axis=1), "rep")
    return (residual - along_dir[:, None] * unit_slice).astype(jnp.bfloat16)


def local(tokens, norm_gain, refusal_dir, expert_ids, gate_probs, w_gate, w_up, w_down):
    plan = gathered if w_gate.shape[0] * CAP >= tokens.shape[0] else exchanged
    return plan(tokens, norm_gain, refusal_dir, expert_ids, gate_probs, w_gate, w_up, w_down)


def solution(mesh):
    placed = (
        P("seq", None),
        P(),
        P(),
        P("seq", None),
        P("seq", None),
        P("seq", "rep", None),
        P("seq", "rep", None),
        P("seq", "rep", None),
    )
    return jax.shard_map(
        local, mesh=mesh, in_specs=placed, out_specs=P("seq", "rep"), check_vma=False
    )
```

```python
import functools

import jax
import jax.numpy as jnp
from jax import lax
from jax.experimental import pallas as pl
from jax.experimental.pallas import tpu as pltpu
from jax.sharding import PartitionSpec as P

CAP = 12
SLOTS = 16


def contract(lhs, rhs, lhs_dim, rhs_dim):
    return lax.dot_general(
        lhs, rhs, (((lhs_dim,), (rhs_dim,)), ((), ())), preferred_element_type=jnp.float32
    )


def group_offset(rep, color, dx, dc, width):
    return pl.multiple_of((rep ^ (2 * dx + dc)) * 2 * width + color * width, width)


def token_pieces(n_z, width):
    others = range(1, n_z)
    pieces = [[(2 * d, [(0, 0), (1, 0)])] for d in others]
    pieces.append([(1, [(0, 0), (1, 0), (1, 1)])])
    pieces.append(
        [(2 * d, [(1, 1)]) for d in others] + [(2 * d, [(0, 1)]) for d in others] + [(1, [(0, 1)])]
    )
    pieces.append([(2 * d + 1, [(0, 0)]) for d in others])
    pieces.append([(2 * d + 1, [(0, 1)]) for d in others])
    pieces.append([(2 * d + 1, [(1, 0), (1, 1)]) for d in others])
    return pieces


def norm_kernel(
    tokens_ref, gain_ref, refusal_ref, normed_ref, to_z_ref, to_y_ref, unit_ref, base_ref
):
    width = tokens_ref.shape[1] // 8
    rep = lax.axis_index("rep")
    toks = tokens_ref[...].astype(jnp.float32)
    refusal = refusal_ref[...]
    unit = refusal / jnp.sqrt(jnp.sum(refusal * refusal, axis=1, keepdims=True) + 1e-06)
    unit_ref[...] = unit
    inv_rms = lax.rsqrt(jnp.mean(toks * toks, axis=1, keepdims=True) + 1e-06)
    normed_ref[...] = (toks * inv_rms * gain_ref[...]).astype(jnp.bfloat16)
    own = pl.ds(group_offset(rep, 0, 0, 0, width), 2 * width)
    to_z_ref[...] = normed_ref[:, own]
    to_y_ref[:, : 2 * width] = normed_ref[:, own]
    to_y_ref[:, 2 * width :] = normed_ref[:, pl.ds(group_offset(rep, 1, 1, 0, width), width)]
    along = jnp.sum(toks * unit, axis=1, keepdims=True)
    base_ref[...] = tokens_ref[:, own].astype(jnp.float32) - along * unit_ref[:, own]


def norm_and_base(tokens, norm_gain, refusal_dir):
    tok_rows, model_width = tokens.shape
    width = model_width // 8
    vmem = pl.BlockSpec(memory_space=pltpu.VMEM)
    return pl.pallas_call(
        norm_kernel,
        out_shape=[
            jax.ShapeDtypeStruct((tok_rows, model_width), jnp.bfloat16),
            jax.ShapeDtypeStruct((tok_rows, 2 * width), jnp.bfloat16),
            jax.ShapeDtypeStruct((tok_rows, 3 * width), jnp.bfloat16),
            jax.ShapeDtypeStruct((1, model_width), jnp.float32),
            jax.ShapeDtypeStruct((tok_rows, 2 * width), jnp.float32),
        ],
        in_specs=[vmem] * 3,
        out_specs=[vmem] * 5,
    )(tokens, norm_gain[None, :], refusal_dir[None, :])


def route_kernel(exp_dev, meta_ref, onehots_ref, row_probs_ref):
    n_seq, twice_k, tok_rows = meta_ref.shape
    top_k = twice_k // 2
    first = (lax.axis_index("seq") * exp_dev).astype(jnp.float32)
    exp_iota = lax.broadcasted_iota(jnp.int32, (exp_dev, tok_rows), 0).astype(jnp.float32) + first
    earlier = (
        lax.broadcasted_iota(jnp.int32, (tok_rows, tok_rows), 0)
        < lax.broadcasted_iota(jnp.int32, (tok_rows, tok_rows), 1)
    ).astype(jnp.float32).astype(jnp.bfloat16)
    slot_iota = lax.broadcasted_iota(jnp.int32, (exp_dev, SLOTS, tok_rows), 1).astype(jnp.float32)

    def place_block(j, carry):
        meta = meta_ref[j]
        hit = jnp.zeros((exp_dev, tok_rows), jnp.float32)
        prob = jnp.zeros((exp_dev, tok_rows), jnp.float32)
        for k in range(top_k):
            same = meta[k : k + 1, :] == exp_iota
            hit = jnp.where(same, 1.0, hit)
            prob = jnp.where(same, meta[top_k + k : top_k + k + 1, :], prob)
        rank = contract(hit.astype(jnp.bfloat16), earlier, 1, 0)
        slot = jnp.where(hit > 0.0, rank, -1.0)
        onehot = jnp.where(slot[:, None, :] == slot_iota, 1.0, 0.0)
        row_probs_ref[j] = jnp.sum(onehot * prob[:, None, :], axis=2, keepdims=True)
        onehots_ref[j] = onehot.reshape(exp_dev * SLOTS, tok_rows).astype(jnp.bfloat16)
        return carry

    lax.fori_loop(0, n_seq, place_block, 0)


def route(meta, exp_dev):
    n_seq, _, tok_rows = meta.shape
    vmem = pl.BlockSpec(memory_space=pltpu.VMEM)
    return pl.pallas_call(
        functools.partial(route_kernel, exp_dev),
        out_shape=[
            jax.ShapeDtypeStruct((n_seq, exp_dev * SLOTS, tok_rows), jnp.bfloat16),
            jax.ShapeDtypeStruct((n_seq, exp_dev, SLOTS, 1), jnp.float32),
        ],
        in_specs=[vmem],
        out_specs=[vmem] * 2,
    )(meta)


def moe_kernel(n_pieces, *refs):
    onehots, row_probs, unit_ref, own_hbm = refs[:4]
    pieces_hbm = refs[4 : 4 + n_pieces]
    w_hbm = refs[4 + n_pieces : 7 + n_pieces]
    out_refs = refs[7 + n_pieces : 15 + n_pieces]
    (w_gate, w_up, w_down, toks, rows, mixed, tok_sems, sems) = refs[15 + n_pieces :]
    n_seq, tok_rows, model_width = toks.shape
    n_z = n_seq // 2
    exp_dev = w_gate.shape[0]
    width = model_width // 8
    slots_src = exp_dev * SLOTS
    rep = lax.axis_index("rep")

    pltpu.make_async_copy(own_hbm, toks.at[0], tok_sems.at[0]).start()
    kinds = token_pieces(n_z, width)
    for i, piece in enumerate(pieces_hbm):
        dc = i // len(kinds)
        for at, (j, runs) in enumerate(kinds[i % len(kinds)]):
            block = piece if len(piece.shape) == 2 else piece.at[at]
            for n, (color, dx) in enumerate(runs):
                cols = pl.ds(group_offset(rep, color, dx, dc, width), width)
                pltpu.make_async_copy(
                    block.at[:, pl.ds(n * width, width)], toks.at[j, :, cols], tok_sems.at[j]
                ).start()

    def weight_copies(e):
        return [
            pltpu.make_async_copy(src.at[e], dst.at[e], sems.at[i, e])
            for i, (src, dst) in enumerate(zip(w_hbm, (w_gate, w_up, w_down)))
        ]

    def fetch(e, carry):
        for copy in weight_copies(e):
            copy.start()
        return carry

    lax.fori_loop(0, exp_dev, fetch, 0)
    quarters = [slice(2 * q * width, 2 * (q + 1) * width) for q in range(4)]

    def pick(j, carry):
        pltpu.make_async_copy(toks.at[j], toks.at[j], tok_sems.at[j]).wait()
        onehot = onehots[j]
        for cols in quarters:
            got = contract(onehot, toks[j, :, cols], 1, 0).astype(jnp.bfloat16)
            rows[j, :, :, cols] = got.reshape(exp_dev, SLOTS, 2 * width)
        return carry

    lax.fori_loop(0, n_seq, pick, 0)

    def expert(e, carry):
        for copy in weight_copies(e):
            copy.wait()
        taken = rows[:, e].reshape(n_seq * SLOTS, model_width)
        gate_val = contract(taken, w_gate[e], 1, 1)
        up_val = contract(taken, w_up[e], 1, 1)
        hidden = (gate_val / (1.0 + jnp.exp(-gate_val)) * up_val).astype(jnp.bfloat16)
        weight = row_probs[:, e].reshape(n_seq * SLOTS, 1)
        for cols in quarters:
            piece = contract(hidden, w_down[e, :, cols], 1, 0) * weight
            rows[:, e, :, cols] = piece.astype(jnp.bfloat16).reshape(n_seq, SLOTS, 2 * width)
        return carry

    lax.fori_loop(0, exp_dev, expert, 0)

    def combine(dz, carry):
        for dy in range(2):
            j = 2 * dz + dy
            onehot = onehots[j]
            along = jnp.zeros((tok_rows, 1), jnp.float32)
            for cols in quarters:
                got = contract(onehot, rows[j, :, :, cols].reshape(slots_src, 2 * width), 0, 0)
                mixed[:, cols] = got
                along += jnp.sum(got * unit_ref[:, cols], axis=1, keepdims=True)
            for dc in range(2):
                first_far, second_far, first_near, second_near = out_refs[4 * dc : 4 * dc + 4]
                second = second_far if dy else second_near
                for dst, at, start, color, dx in (
                    (first_far, j, 0, 0, 1),
                    (first_near, j, 0, 0, 0),
                    (second, dz, 0, 1, 0),
                    (second, dz, width, 1, 1),
                ):
                    cols = pl.ds(group_offset(rep, color, dx, dc, width), width)
                    value = mixed[:, cols] - along * unit_ref[:, cols]
                    dst[at, :, start : start + width] = value.astype(jnp.bfloat16)
        return carry

    lax.fori_loop(0, n_z, combine, 0)


def moe_partial(onehots, row_probs, unit_dir, own, pieces, w_gate, w_up, w_down):
    n_seq, _, tok_rows = onehots.shape
    exp_dev, hid_dev, model_width = w_gate.shape
    width = model_width // 8
    vmem = pl.BlockSpec(memory_space=pltpu.VMEM)
    hbm = pl.BlockSpec(memory_space=pl.ANY)
    n_pieces = len(pieces)
    outs = [
        jax.ShapeDtypeStruct((blocks, tok_rows, runs * width), jnp.bfloat16)
        for _ in range(2)
        for blocks, runs in ((n_seq, 1), (n_seq // 2, 2), (n_seq, 1), (n_seq // 2, 2))
    ]
    return pl.pallas_call(
        functools.partial(moe_kernel, n_pieces),
        out_shape=outs,
        in_specs=[vmem] * 3 + [hbm] * (n_pieces + 4),
        out_specs=[vmem] * len(outs),
        scratch_shapes=[
            pltpu.VMEM(w_gate.shape, jnp.bfloat16),
            pltpu.VMEM(w_up.shape, jnp.bfloat16),
            pltpu.VMEM(w_down.shape, jnp.bfloat16),
            pltpu.VMEM((n_seq, tok_rows, model_width), jnp.bfloat16),
            pltpu.VMEM((n_seq, exp_dev, SLOTS, model_width), jnp.bfloat16),
            pltpu.VMEM((tok_rows, model_width), jnp.float32),
            pltpu.SemaphoreType.DMA((n_seq,)),
            pltpu.SemaphoreType.DMA((3, exp_dev)),
        ],
        compiler_params=pltpu.CompilerParams(vmem_limit_bytes=62 * 1024 * 1024),
        cost_estimate=pl.CostEstimate(
            flops=6 * n_seq * SLOTS * exp_dev * hid_dev * model_width,
            bytes_accessed=6 * exp_dev * hid_dev * model_width + 4 * n_seq * own.size,
            transcendentals=0,
        ),
    )(onehots, row_probs, unit_dir, own, *pieces, w_gate, w_up, w_down)


def swap(value, axis, distance):
    size = lax.axis_size(axis)
    return lax.ppermute(value, axis, [(i, i ^ distance) for i in range(size)])


def added(*terms):
    return sum(term.astype(jnp.float32) for term in terms).astype(jnp.bfloat16)


def gathered(tokens, norm_gain, refusal_dir, expert_ids, gate_probs, w_gate, w_up, w_down):
    tok_rows, model_width = tokens.shape
    top_k = expert_ids.shape[1]
    n_seq = lax.axis_size("seq")
    n_z = n_seq // 2
    others = range(1, n_z)
    exp_dev = w_gate.shape[0]
    width = model_width // 8

    meta = jnp.concatenate([expert_ids.T.astype(jnp.float32), gate_probs.T], axis=0)
    meta = [meta] + [swap(meta, "seq", 2 * d) for d in others]
    meta_y = swap(jnp.stack(meta), "seq", 1)
    meta = jnp.stack([m for d in range(n_z) for m in (meta[d], meta_y[d])])
    onehots, row_probs = route(meta, exp_dev)

    normed, to_z, to_y, unit_dir, base = norm_and_base(tokens, norm_gain, refusal_dir)
    from_z = [swap(to_z, "seq", 2 * d) for d in others]
    from_y = swap(to_y, "seq", 1)
    first = [piece[:, :width] for piece in from_z]
    second = [piece[:, width:] for piece in from_z]
    x_two = swap(jnp.stack(second + first + [from_y[:, :width]]), "rep", 2)
    y_two = swap(jnp.stack(first), "seq", 1)
    x_three = swap(y_two, "rep", 2)
    y_three = swap(
        jnp.concatenate([jnp.stack(second), x_two[: n_z - 1]], axis=2), "seq", 1
    )
    pieces = [*from_z, from_y, x_two, y_two, x_three, y_three]
    pieces = pieces + [swap(piece, "rep", 1) for piece in pieces]

    sums = moe_partial(onehots, row_probs, unit_dir, normed, pieces, w_gate, w_up, w_down)
    kept, sent = sums[:4], sums[4:]
    first_far, second_far, first_near, second_near = [
        added(mine, swap(theirs, "rep", 1)) for mine, theirs in zip(kept, sent)
    ]
    first_sum = added(first_near, swap(first_far, "rep", 2))
    second_sum = added(second_near, swap(second_far, "seq", 1))
    by_y = first_sum.reshape(n_z, 2, tok_rows, width)
    first_sum = added(by_y[:, 0], swap(by_y[:, 1], "seq", 1))
    second_sum = added(second_sum[:, :, :width], swap(second_sum[:, :, width:], "rep", 2))
    blocks = jnp.concatenate([first_sum, second_sum], axis=2)
    arrived = [swap(blocks[d], "seq", 2 * d) for d in others]
    summed = sum(term.astype(jnp.float32) for term in [blocks[0], *arrived])

    return (base + summed).astype(jnp.bfloat16)


def exchanged(tokens, norm_gain, refusal_dir, expert_ids, gate_probs, w_gate, w_up, w_down):
    tok_rows, model_width = tokens.shape
    top_k = expert_ids.shape[1]
    n_seq = lax.axis_size("seq")
    n_rep = lax.axis_size("rep")
    exp_dev = w_gate.shape[0]
    experts = exp_dev * n_seq
    slot_count = tok_rows * top_k
    part_width = model_width // n_rep
    tokens_f32 = tokens.astype(jnp.float32)
    inv_rms = lax.rsqrt(jnp.mean(tokens_f32 * tokens_f32, axis=1, keepdims=True) + 1e-06)
    normed = (tokens_f32 * inv_rms * norm_gain).astype(jnp.bfloat16)
    flat_ids = expert_ids.reshape(slot_count)
    onehot = (flat_ids[:, None] == jnp.arange(experts, dtype=jnp.int32)[None, :]).astype(jnp.int32)
    slot_rank = jnp.sum(jnp.cumsum(onehot, axis=0) * onehot, axis=1) - 1
    target = flat_ids * CAP + slot_rank
    repeated = jnp.broadcast_to(normed[:, None, :], (tok_rows, top_k, model_width)).reshape(
        slot_count, model_width
    )
    sendbuf = jnp.zeros((experts * CAP, model_width), jnp.bfloat16).at[target].set(repeated)
    sendbuf = sendbuf.reshape(n_seq, exp_dev, CAP, model_width)
    arrived = lax.all_to_all(sendbuf, "seq", split_axis=0, concat_axis=0, tiled=True)
    gate_val = jnp.einsum("secd,efd->secf", arrived, w_gate, preferred_element_type=jnp.float32)
    up_val = jnp.einsum("secd,efd->secf", arrived, w_up, preferred_element_type=jnp.float32)
    hidden = (jax.nn.silu(gate_val) * up_val).astype(jnp.bfloat16)
    pieces = jnp.einsum(
        "secf,efd->secd", hidden, w_down, preferred_element_type=jnp.float32
    ).astype(jnp.bfloat16)
    probs_flat = gate_probs.reshape(slot_count)[:, None]
    returned = lax.all_to_all(pieces, "seq", split_axis=0, concat_axis=0, tiled=True)
    returned = returned.reshape(experts * CAP, model_width)
    weighted = returned[target].astype(jnp.float32) * probs_flat
    moe_part = jnp.sum(weighted.reshape(tok_rows, top_k, model_width), axis=1)
    summed = lax.psum_scatter(
        moe_part.astype(jnp.bfloat16), "rep", scatter_dimension=1, tiled=True
    ).astype(jnp.float32)
    unit_dir = refusal_dir / jnp.sqrt(jnp.sum(refusal_dir * refusal_dir) + 1e-06)
    rep_offset = lax.axis_index("rep") * part_width
    unit_slice = lax.dynamic_slice_in_dim(unit_dir, rep_offset, part_width, 0)
    own_tokens = lax.dynamic_slice_in_dim(tokens_f32, rep_offset, part_width, 1)
    residual = own_tokens + summed
    along_dir = lax.psum(jnp.sum(residual * unit_slice, axis=1), "rep")
    return (residual - along_dir[:, None] * unit_slice).astype(jnp.bfloat16)


def local(tokens, norm_gain, refusal_dir, expert_ids, gate_probs, w_gate, w_up, w_down):
    plan = gathered if w_gate.shape[0] * CAP >= tokens.shape[0] else exchanged
    return plan(tokens, norm_gain, refusal_dir, expert_ids, gate_probs, w_gate, w_up, w_down)


def solution(mesh):
    placed = (
        P("seq", None),
        P(),
        P(),
        P("seq", None),
        P("seq", None),
        P("seq", "rep", None),
        P("seq", "rep", None),
        P("seq", "rep", None),
    )
    return jax.shard_map(
        local, mesh=mesh, in_specs=placed, out_specs=P("seq", "rep"), check_vma=False
    )
```

```python
import functools

import jax
import jax.numpy as jnp
from jax import lax
from jax.experimental import pallas as pl
from jax.experimental.pallas import tpu as pltpu
from jax.sharding import PartitionSpec as P

CAP = 12
SLOTS = 16
RING = 6


def contract(lhs, rhs, lhs_dim, rhs_dim):
    return lax.dot_general(
        lhs, rhs, (((lhs_dim,), (rhs_dim,)), ((), ())), preferred_element_type=jnp.float32
    )


def group_offset(rep, color, dx, dc, width):
    return pl.multiple_of((rep ^ (2 * dx + dc)) * 2 * width + color * width, width)


def token_pieces(n_z, width):
    others = range(1, n_z)
    pieces = [[(2 * d, [(0, 0), (1, 0)])] for d in others]
    pieces.append([(1, [(0, 0), (1, 0), (1, 1)])])
    pieces.append([(2 * d, [(1, 1)]) for d in others])
    pieces.append([(2 * d, [(0, 1)]) for d in others] + [(1, [(0, 1)])])
    pieces.append([(2 * d + 1, [(0, 0)]) for d in others])
    pieces.append([(2 * d + 1, [(0, 1)]) for d in others])
    pieces.append([(2 * d + 1, [(1, 0), (1, 1)]) for d in others])
    return pieces


def norm_kernel(
    tokens_ref, gain_ref, refusal_ref, ids_ref, probs_ref,
    normed_ref, to_z_ref, to_y_ref, unit_ref, base_ref, meta_ref,
):
    width = tokens_ref.shape[1] // 8
    top_k = ids_ref.shape[0]
    rep = lax.axis_index("rep")
    meta_ref[:top_k] = ids_ref[...].astype(jnp.float32)
    meta_ref[top_k:] = probs_ref[...]
    toks = tokens_ref[...].astype(jnp.float32)
    refusal = refusal_ref[...]
    unit = refusal / jnp.sqrt(jnp.sum(refusal * refusal, axis=1, keepdims=True) + 1e-06)
    unit_ref[...] = unit
    inv_rms = lax.rsqrt(jnp.mean(toks * toks, axis=1, keepdims=True) + 1e-06)
    normed_ref[...] = (toks * inv_rms * gain_ref[...]).astype(jnp.bfloat16)
    own = pl.ds(group_offset(rep, 0, 0, 0, width), 2 * width)
    to_z_ref[...] = normed_ref[:, own]
    to_y_ref[:, : 2 * width] = normed_ref[:, own]
    to_y_ref[:, 2 * width :] = normed_ref[:, pl.ds(group_offset(rep, 1, 1, 0, width), width)]
    along = jnp.sum(toks * unit, axis=1, keepdims=True)
    base_ref[...] = tokens_ref[:, own].astype(jnp.float32) - along * unit_ref[:, own]


def norm_and_base(tokens, norm_gain, refusal_dir, expert_ids, gate_probs):
    tok_rows, model_width = tokens.shape
    width = model_width // 8
    vmem = pl.BlockSpec(memory_space=pltpu.VMEM)
    return pl.pallas_call(
        norm_kernel,
        out_shape=[
            jax.ShapeDtypeStruct((tok_rows, model_width), jnp.bfloat16),
            jax.ShapeDtypeStruct((tok_rows, 2 * width), jnp.bfloat16),
            jax.ShapeDtypeStruct((tok_rows, 3 * width), jnp.bfloat16),
            jax.ShapeDtypeStruct((1, model_width), jnp.float32),
            jax.ShapeDtypeStruct((tok_rows, 2 * width), jnp.float32),
            jax.ShapeDtypeStruct((2 * expert_ids.shape[1], tok_rows), jnp.float32),
        ],
        in_specs=[vmem] * 5,
        out_specs=[vmem] * 6,
    )(tokens, norm_gain[None, :], refusal_dir[None, :], expert_ids.T, gate_probs.T)


def route_kernel(exp_dev, n_z, *refs):
    near_refs, far_ref, picks_ref, weights_ref, meta_ref = (
        refs[:n_z], refs[n_z], refs[n_z + 1], refs[n_z + 2], refs[n_z + 3]
    )
    n_seq, twice_k, tok_rows = meta_ref.shape
    top_k = twice_k // 2
    for d in range(n_z):
        meta_ref[2 * d] = near_refs[d][...]
        meta_ref[2 * d + 1] = far_ref[d]
    first = (lax.axis_index("seq") * exp_dev).astype(jnp.float32)
    exp_iota = lax.broadcasted_iota(jnp.int32, (exp_dev, tok_rows), 0).astype(jnp.float32) + first
    earlier = (
        lax.broadcasted_iota(jnp.int32, (tok_rows, tok_rows), 0)
        < lax.broadcasted_iota(jnp.int32, (tok_rows, tok_rows), 1)
    ).astype(jnp.float32).astype(jnp.bfloat16)
    slot_iota = lax.broadcasted_iota(jnp.int32, (exp_dev, SLOTS, tok_rows), 1).astype(jnp.float32)

    def place_block(j, carry):
        meta = meta_ref[j]
        hit = jnp.zeros((exp_dev, tok_rows), jnp.float32)
        prob = jnp.zeros((exp_dev, tok_rows), jnp.float32)
        for k in range(top_k):
            same = meta[k : k + 1, :] == exp_iota
            hit = jnp.where(same, 1.0, hit)
            prob = jnp.where(same, meta[top_k + k : top_k + k + 1, :], prob)
        rank = contract(hit.astype(jnp.bfloat16), earlier, 1, 0)
        slot = jnp.where(hit > 0.0, rank, -1.0)
        here = slot[:, None, :] == slot_iota
        onehot = jnp.where(here, 1.0, 0.0).reshape(exp_dev * SLOTS, tok_rows)
        weight = jnp.where(here, prob[:, None, :], 0.0).reshape(exp_dev * SLOTS, tok_rows)
        picks_ref[j] = onehot.astype(jnp.bfloat16)
        weights_ref[j] = weight.T.astype(jnp.bfloat16)
        return carry

    lax.fori_loop(0, n_seq, place_block, 0)


def route(near, far, exp_dev):
    n_z, twice_k, tok_rows = far.shape
    n_seq = 2 * n_z
    vmem = pl.BlockSpec(memory_space=pltpu.VMEM)
    return pl.pallas_call(
        functools.partial(route_kernel, exp_dev, n_z),
        out_shape=[
            jax.ShapeDtypeStruct((n_seq, exp_dev * SLOTS, tok_rows), jnp.bfloat16),
            jax.ShapeDtypeStruct((n_seq, tok_rows, exp_dev * SLOTS), jnp.bfloat16),
        ],
        in_specs=[vmem] * (n_z + 1),
        out_specs=[vmem] * 2,
        scratch_shapes=[pltpu.VMEM((n_seq, twice_k, tok_rows), jnp.float32)],
        cost_estimate=pl.CostEstimate(
            flops=4_000_000_000, bytes_accessed=8 * n_seq * exp_dev * SLOTS * tok_rows,
            transcendentals=0,
        ),
    )(*near, far)


def moe_kernel(n_pieces, *refs):
    picks, weights, unit_ref, own_hbm = refs[:4]
    pieces_hbm = refs[4 : 4 + n_pieces]
    w_gate_hbm, w_up_hbm, w_down_hbm = refs[4 + n_pieces : 7 + n_pieces]
    out_refs = refs[7 + n_pieces : 15 + n_pieces]
    (w_in, w_down, toks, rows, mixed, tok_sems, sems) = refs[15 + n_pieces :]
    n_seq, tok_rows, model_width = toks.shape
    n_z = n_seq // 2
    exp_dev, hid_dev, _ = w_gate_hbm.shape
    width = model_width // 8
    slots_src = exp_dev * SLOTS
    rep = lax.axis_index("rep")

    pltpu.make_async_copy(own_hbm, toks.at[0], tok_sems.at[0]).start()
    kinds = token_pieces(n_z, width)
    for i, piece in enumerate(pieces_hbm):
        dc = i // len(kinds)
        for at, (j, runs) in enumerate(kinds[i % len(kinds)]):
            block = piece if len(piece.shape) == 2 else piece.at[at]
            for n, (color, dx) in enumerate(runs):
                cols = pl.ds(group_offset(rep, color, dx, dc, width), width)
                pltpu.make_async_copy(
                    block.at[:, pl.ds(n * width, width)], toks.at[j, :, cols], tok_sems.at[j]
                ).start()

    def weight_copies(e):
        at = lax.rem(e, RING)
        gate_at, up_at = pl.ds(0, hid_dev), pl.ds(hid_dev, hid_dev)
        return [
            pltpu.make_async_copy(w_gate_hbm.at[e], w_in.at[at, gate_at], sems.at[0, at]),
            pltpu.make_async_copy(w_up_hbm.at[e], w_in.at[at, up_at], sems.at[1, at]),
            pltpu.make_async_copy(w_down_hbm.at[e], w_down.at[at], sems.at[2, at]),
        ]

    def fetch(e, carry):
        for copy in weight_copies(e):
            copy.start()
        return carry

    lax.fori_loop(0, min(RING, exp_dev), fetch, 0)
    quarters = [slice(2 * q * width, 2 * (q + 1) * width) for q in range(4)]

    def pick(j, carry):
        pltpu.make_async_copy(toks.at[j], toks.at[j], tok_sems.at[j]).wait()
        onehot = picks[j]
        for cols in quarters:
            got = contract(onehot, toks[j, :, cols], 1, 0).astype(jnp.bfloat16)
            rows[j, :, :, cols] = got.reshape(exp_dev, SLOTS, 2 * width)
        return carry

    lax.fori_loop(0, n_seq, pick, 0)

    def expert(e, carry):
        at = lax.rem(e, RING)
        for copy in weight_copies(e):
            copy.wait()
        taken = rows[:, e].reshape(n_seq * SLOTS, model_width)
        both = contract(w_in[at], taken, 1, 1)
        gate_val, up_val = both[:hid_dev], both[hid_dev:]
        hidden = gate_val / (1.0 + jnp.exp(-gate_val)) * up_val
        hidden = hidden.T.astype(jnp.bfloat16)
        for cols in quarters:
            piece = contract(hidden, w_down[at, :, cols], 1, 0).astype(jnp.bfloat16)
            rows[:, e, :, cols] = piece.reshape(n_seq, SLOTS, 2 * width)

        @pl.when(e + RING < exp_dev)
        def _():
            fetch(e + RING, 0)

        return carry

    lax.fori_loop(0, exp_dev, expert, 0)

    def combine(dz, carry):
        for dy in range(2):
            j = 2 * dz + dy
            weight = weights[j]
            along = jnp.zeros((tok_rows, 1), jnp.float32)
            for cols in quarters:
                got = contract(weight, rows[j, :, :, cols].reshape(slots_src, 2 * width), 1, 0)
                mixed[:, cols] = got
                along += jnp.sum(got * unit_ref[:, cols], axis=1, keepdims=True)
            for dc in range(2):
                first_far, second_far, first_near, second_near = out_refs[4 * dc : 4 * dc + 4]
                second = second_far if dy else second_near
                for dst, at, start, color, dx in (
                    (first_far, j, 0, 0, 1),
                    (first_near, j, 0, 0, 0),
                    (second, dz, 0, 1, 0),
                    (second, dz, width, 1, 1),
                ):
                    cols = pl.ds(group_offset(rep, color, dx, dc, width), width)
                    value = mixed[:, cols] - along * unit_ref[:, cols]
                    dst[at, :, start : start + width] = value.astype(jnp.bfloat16)
        return carry

    lax.fori_loop(0, n_z, combine, 0)


def moe_partial(picks, weights, unit_dir, own, pieces, w_gate, w_up, w_down):
    n_seq, _, tok_rows = picks.shape
    exp_dev, hid_dev, model_width = w_gate.shape
    width = model_width // 8
    vmem = pl.BlockSpec(memory_space=pltpu.VMEM)
    hbm = pl.BlockSpec(memory_space=pl.ANY)
    n_pieces = len(pieces)
    outs = [
        jax.ShapeDtypeStruct((blocks, tok_rows, runs * width), jnp.bfloat16)
        for _ in range(2)
        for blocks, runs in ((n_seq, 1), (n_seq // 2, 2), (n_seq, 1), (n_seq // 2, 2))
    ]
    return pl.pallas_call(
        functools.partial(moe_kernel, n_pieces),
        out_shape=outs,
        in_specs=[vmem] * 3 + [hbm] * (n_pieces + 4),
        out_specs=[vmem] * len(outs),
        scratch_shapes=[
            pltpu.VMEM((RING, 2 * hid_dev, model_width), jnp.bfloat16),
            pltpu.VMEM((RING, hid_dev, model_width), jnp.bfloat16),
            pltpu.VMEM((n_seq, tok_rows, model_width), jnp.bfloat16),
            pltpu.VMEM((n_seq, exp_dev, SLOTS, model_width), jnp.bfloat16),
            pltpu.VMEM((tok_rows, model_width), jnp.float32),
            pltpu.SemaphoreType.DMA((n_seq,)),
            pltpu.SemaphoreType.DMA((3, RING)),
        ],
        compiler_params=pltpu.CompilerParams(vmem_limit_bytes=42 * 1024 * 1024),
        cost_estimate=pl.CostEstimate(
            flops=6 * n_seq * SLOTS * exp_dev * hid_dev * model_width,
            bytes_accessed=6 * exp_dev * hid_dev * model_width + 4 * n_seq * own.size,
            transcendentals=0,
        ),
    )(picks, weights, unit_dir, own, *pieces, w_gate, w_up, w_down)


def swap(value, axis, distance):
    size = lax.axis_size(axis)
    return lax.ppermute(value, axis, [(i, i ^ distance) for i in range(size)])


def added(*terms):
    return sum(term.astype(jnp.float32) for term in terms).astype(jnp.bfloat16)


def gathered(tokens, norm_gain, refusal_dir, expert_ids, gate_probs, w_gate, w_up, w_down):
    tok_rows, model_width = tokens.shape
    n_z = lax.axis_size("seq") // 2
    others = range(1, n_z)
    exp_dev = w_gate.shape[0]
    width = model_width // 8

    normed, to_z, to_y, unit_dir, base, meta = norm_and_base(
        tokens, norm_gain, refusal_dir, expert_ids, gate_probs
    )
    from_z = [swap(to_z, "seq", 2 * d) for d in others]
    from_y = swap(to_y, "seq", 1)
    near = [meta] + [swap(meta, "seq", 2 * d) for d in others]
    picks, weights = route(near, swap(jnp.stack(near), "seq", 1), exp_dev)

    first = jnp.stack([piece[:, :width] for piece in from_z])
    second = jnp.stack([piece[:, width:] for piece in from_z])
    second, picks, weights = lax.optimization_barrier((second, picks, weights))
    x_two = swap(second, "rep", 2)
    y_two = swap(first, "seq", 1)
    x_one = swap(jnp.concatenate([first, from_y[None, :, :width]]), "rep", 2)
    sibling = [swap(piece, "rep", 1) for piece in (*from_z, from_y)]
    to_y, y_two, *sibling = lax.optimization_barrier(
        (jnp.concatenate([second, x_two], axis=2), y_two, *sibling)
    )
    y_three = swap(to_y, "seq", 1)
    x_three = swap(y_two, "rep", 2)
    last = [x_two, x_one, y_two, x_three, y_three]
    pieces = [*from_z, from_y, *last, *sibling, *[swap(piece, "rep", 1) for piece in last]]

    sums = moe_partial(picks, weights, unit_dir, normed, pieces, w_gate, w_up, w_down)
    kept, sent = sums[:4], sums[4:]
    first_far, second_far, first_near, second_near = [
        added(mine, swap(theirs, "rep", 1)) for mine, theirs in zip(kept, sent)
    ]
    first_sum = added(first_near, swap(first_far, "rep", 2))
    second_sum = added(second_near, swap(second_far, "seq", 1))
    by_y = first_sum.reshape(n_z, 2, tok_rows, width)
    first_sum = added(by_y[:, 0], swap(by_y[:, 1], "seq", 1))
    second_sum = added(second_sum[:, :, :width], swap(second_sum[:, :, width:], "rep", 2))
    blocks = jnp.concatenate([first_sum, second_sum], axis=2)
    arrived = [swap(blocks[d], "seq", 2 * d) for d in others]
    summed = sum(term.astype(jnp.float32) for term in [blocks[0], *arrived])

    return (base + summed).astype(jnp.bfloat16)


def exchanged(tokens, norm_gain, refusal_dir, expert_ids, gate_probs, w_gate, w_up, w_down):
    tok_rows, model_width = tokens.shape
    top_k = expert_ids.shape[1]
    n_seq = lax.axis_size("seq")
    n_rep = lax.axis_size("rep")
    exp_dev = w_gate.shape[0]
    experts = exp_dev * n_seq
    slot_count = tok_rows * top_k
    part_width = model_width // n_rep
    tokens_f32 = tokens.astype(jnp.float32)
    inv_rms = lax.rsqrt(jnp.mean(tokens_f32 * tokens_f32, axis=1, keepdims=True) + 1e-06)
    normed = (tokens_f32 * inv_rms * norm_gain).astype(jnp.bfloat16)
    flat_ids = expert_ids.reshape(slot_count)
    onehot = (flat_ids[:, None] == jnp.arange(experts, dtype=jnp.int32)[None, :]).astype(jnp.int32)
    slot_rank = jnp.sum(jnp.cumsum(onehot, axis=0) * onehot, axis=1) - 1
    target = flat_ids * CAP + slot_rank
    repeated = jnp.broadcast_to(normed[:, None, :], (tok_rows, top_k, model_width)).reshape(
        slot_count, model_width
    )
    sendbuf = jnp.zeros((experts * CAP, model_width), jnp.bfloat16).at[target].set(repeated)
    sendbuf = sendbuf.reshape(n_seq, exp_dev, CAP, model_width)
    arrived = lax.all_to_all(sendbuf, "seq", split_axis=0, concat_axis=0, tiled=True)
    gate_val = jnp.einsum("secd,efd->secf", arrived, w_gate, preferred_element_type=jnp.float32)
    up_val = jnp.einsum("secd,efd->secf", arrived, w_up, preferred_element_type=jnp.float32)
    hidden = (jax.nn.silu(gate_val) * up_val).astype(jnp.bfloat16)
    pieces = jnp.einsum(
        "secf,efd->secd", hidden, w_down, preferred_element_type=jnp.float32
    ).astype(jnp.bfloat16)
    probs_flat = gate_probs.reshape(slot_count)[:, None]
    returned = lax.all_to_all(pieces, "seq", split_axis=0, concat_axis=0, tiled=True)
    returned = returned.reshape(experts * CAP, model_width)
    weighted = returned[target].astype(jnp.float32) * probs_flat
    moe_part = jnp.sum(weighted.reshape(tok_rows, top_k, model_width), axis=1)
    summed = lax.psum_scatter(
        moe_part.astype(jnp.bfloat16), "rep", scatter_dimension=1, tiled=True
    ).astype(jnp.float32)
    unit_dir = refusal_dir / jnp.sqrt(jnp.sum(refusal_dir * refusal_dir) + 1e-06)
    rep_offset = lax.axis_index("rep") * part_width
    unit_slice = lax.dynamic_slice_in_dim(unit_dir, rep_offset, part_width, 0)
    own_tokens = lax.dynamic_slice_in_dim(tokens_f32, rep_offset, part_width, 1)
    residual = own_tokens + summed
    along_dir = lax.psum(jnp.sum(residual * unit_slice, axis=1), "rep")
    return (residual - along_dir[:, None] * unit_slice).astype(jnp.bfloat16)


def local(tokens, norm_gain, refusal_dir, expert_ids, gate_probs, w_gate, w_up, w_down):
    plan = gathered if w_gate.shape[0] * CAP >= tokens.shape[0] else exchanged
    return plan(tokens, norm_gain, refusal_dir, expert_ids, gate_probs, w_gate, w_up, w_down)


def solution(mesh):
    placed = (
        P("seq", None),
        P(),
        P(),
        P("seq", None),
        P("seq", None),
        P("seq", "rep", None),
        P("seq", "rep", None),
        P("seq", "rep", None),
    )
    return jax.shard_map(
        local, mesh=mesh, in_specs=placed, out_specs=P("seq", "rep"), check_vma=False
    )
```

```python
import functools

import jax
import jax.numpy as jnp
from jax import lax
from jax.experimental import pallas as pl
from jax.experimental.pallas import tpu as pltpu
from jax.sharding import PartitionSpec as P

CAP = 12
SLOTS = 16
RING = 8


def contract(lhs, rhs, lhs_dim, rhs_dim):
    return lax.dot_general(
        lhs, rhs, (((lhs_dim,), (rhs_dim,)), ((), ())), preferred_element_type=jnp.float32
    )


def group_offset(rep, color, dx, dc, width):
    return pl.multiple_of((rep ^ (2 * dx + dc)) * 2 * width + color * width, width)


def token_pieces(n_z, width):
    others = range(1, n_z)
    pieces = [[(2 * d, [(0, 0), (1, 0)])] for d in others]
    pieces.append([(1, [(0, 0), (1, 0), (1, 1)])])
    pieces.append([(2 * d, [(1, 1)]) for d in others])
    pieces.append([(2 * d, [(0, 1)]) for d in others] + [(1, [(0, 1)])])
    pieces.append([(2 * d + 1, [(0, 0)]) for d in others])
    pieces.append([(2 * d + 1, [(0, 1)]) for d in others])
    pieces.append([(2 * d + 1, [(1, 0), (1, 1)]) for d in others])
    return pieces


def norm_kernel(
    tokens_ref, gain_ref, refusal_ref, ids_ref, probs_ref,
    normed_ref, to_z_ref, to_y_ref, unit_ref, base_ref, meta_ref,
):
    width = tokens_ref.shape[1] // 8
    top_k = ids_ref.shape[0]
    rep = lax.axis_index("rep")
    meta_ref[:top_k] = ids_ref[...].astype(jnp.float32)
    meta_ref[top_k:] = probs_ref[...]
    toks = tokens_ref[...].astype(jnp.float32)
    refusal = refusal_ref[...]
    unit = refusal / jnp.sqrt(jnp.sum(refusal * refusal, axis=1, keepdims=True) + 1e-06)
    unit_ref[...] = unit
    inv_rms = lax.rsqrt(jnp.mean(toks * toks, axis=1, keepdims=True) + 1e-06)
    normed_ref[...] = (toks * inv_rms * gain_ref[...]).astype(jnp.bfloat16)
    own = pl.ds(group_offset(rep, 0, 0, 0, width), 2 * width)
    to_z_ref[...] = normed_ref[:, own]
    to_y_ref[:, : 2 * width] = normed_ref[:, own]
    to_y_ref[:, 2 * width :] = normed_ref[:, pl.ds(group_offset(rep, 1, 1, 0, width), width)]
    along = jnp.sum(toks * unit, axis=1, keepdims=True)
    base_ref[...] = tokens_ref[:, own].astype(jnp.float32) - along * unit_ref[:, own]


def norm_and_base(tokens, norm_gain, refusal_dir, expert_ids, gate_probs):
    tok_rows, model_width = tokens.shape
    width = model_width // 8
    vmem = pl.BlockSpec(memory_space=pltpu.VMEM)
    return pl.pallas_call(
        norm_kernel,
        out_shape=[
            jax.ShapeDtypeStruct((tok_rows, model_width), jnp.bfloat16),
            jax.ShapeDtypeStruct((tok_rows, 2 * width), jnp.bfloat16),
            jax.ShapeDtypeStruct((tok_rows, 3 * width), jnp.bfloat16),
            jax.ShapeDtypeStruct((1, model_width), jnp.float32),
            jax.ShapeDtypeStruct((tok_rows, 2 * width), jnp.float32),
            jax.ShapeDtypeStruct((2 * expert_ids.shape[1], tok_rows), jnp.float32),
        ],
        in_specs=[vmem] * 5,
        out_specs=[vmem] * 6,
    )(tokens, norm_gain[None, :], refusal_dir[None, :], expert_ids.T, gate_probs.T)


def route_kernel(exp_dev, n_z, *refs):
    near_refs, far_ref, picks_ref, weights_ref, meta_ref = (
        refs[:n_z], refs[n_z], refs[n_z + 1], refs[n_z + 2], refs[n_z + 3]
    )
    n_seq, twice_k, tok_rows = meta_ref.shape
    top_k = twice_k // 2
    for d in range(n_z):
        meta_ref[2 * d] = near_refs[d][...]
        meta_ref[2 * d + 1] = far_ref[d]
    first = (lax.axis_index("seq") * exp_dev).astype(jnp.float32)
    exp_iota = lax.broadcasted_iota(jnp.int32, (exp_dev, tok_rows), 0).astype(jnp.float32) + first
    earlier = (
        lax.broadcasted_iota(jnp.int32, (tok_rows, tok_rows), 0)
        < lax.broadcasted_iota(jnp.int32, (tok_rows, tok_rows), 1)
    ).astype(jnp.float32).astype(jnp.bfloat16)
    slot_iota = lax.broadcasted_iota(jnp.int32, (exp_dev, SLOTS, tok_rows), 1).astype(jnp.float32)

    def place_block(j, carry):
        meta = meta_ref[j]
        hit = jnp.zeros((exp_dev, tok_rows), jnp.float32)
        prob = jnp.zeros((exp_dev, tok_rows), jnp.float32)
        for k in range(top_k):
            same = meta[k : k + 1, :] == exp_iota
            hit = jnp.where(same, 1.0, hit)
            prob = jnp.where(same, meta[top_k + k : top_k + k + 1, :], prob)
        rank = contract(hit.astype(jnp.bfloat16), earlier, 1, 0)
        slot = jnp.where(hit > 0.0, rank, -1.0)
        here = slot[:, None, :] == slot_iota
        onehot = jnp.where(here, 1.0, 0.0).reshape(exp_dev * SLOTS, tok_rows)
        weight = jnp.where(here, prob[:, None, :], 0.0).reshape(exp_dev * SLOTS, tok_rows)
        picks_ref[j] = onehot.astype(jnp.bfloat16)
        weights_ref[j] = weight.T.astype(jnp.bfloat16)
        return carry

    lax.fori_loop(0, n_seq, place_block, 0)


def route(near, far, exp_dev):
    n_z, twice_k, tok_rows = far.shape
    n_seq = 2 * n_z
    vmem = pl.BlockSpec(memory_space=pltpu.VMEM)
    return pl.pallas_call(
        functools.partial(route_kernel, exp_dev, n_z),
        out_shape=[
            jax.ShapeDtypeStruct((n_seq, exp_dev * SLOTS, tok_rows), jnp.bfloat16),
            jax.ShapeDtypeStruct((n_seq, tok_rows, exp_dev * SLOTS), jnp.bfloat16),
        ],
        in_specs=[vmem] * (n_z + 1),
        out_specs=[vmem] * 2,
        scratch_shapes=[pltpu.VMEM((n_seq, twice_k, tok_rows), jnp.float32)],
        cost_estimate=pl.CostEstimate(
            flops=4_000_000_000, bytes_accessed=8 * n_seq * exp_dev * SLOTS * tok_rows,
            transcendentals=0,
        ),
    )(*near, far)


def moe_kernel(n_pieces, *refs):
    picks, weights, unit_ref, own_hbm = refs[:4]
    pieces_hbm = refs[4 : 4 + n_pieces]
    w_gate, w_up_hbm, w_down_hbm = refs[4 + n_pieces : 7 + n_pieces]
    out_refs = refs[7 + n_pieces : 15 + n_pieces]
    (w_up, w_down, toks, rows, mixed, tok_sems, sems) = refs[15 + n_pieces :]
    n_seq, tok_rows, model_width = toks.shape
    n_z = n_seq // 2
    exp_dev = w_gate.shape[0]
    width = model_width // 8
    slots_src = exp_dev * SLOTS
    rep = lax.axis_index("rep")

    pltpu.make_async_copy(own_hbm, toks.at[0], tok_sems.at[0]).start()
    kinds = token_pieces(n_z, width)
    for i, piece in enumerate(pieces_hbm):
        dc = i // len(kinds)
        for at, (j, runs) in enumerate(kinds[i % len(kinds)]):
            block = piece if len(piece.shape) == 2 else piece.at[at]
            for n, (color, dx) in enumerate(runs):
                cols = pl.ds(group_offset(rep, color, dx, dc, width), width)
                pltpu.make_async_copy(
                    block.at[:, pl.ds(n * width, width)], toks.at[j, :, cols], tok_sems.at[j]
                ).start()

    def fetches(e):
        at = lax.rem(e, RING)
        return [
            pltpu.make_async_copy(src.at[e], dst.at[at], sems.at[i, at])
            for i, (src, dst) in enumerate(((w_up_hbm, w_up), (w_down_hbm, w_down)))
        ]

    for e in range(min(RING, exp_dev)):
        for copy in fetches(e):
            copy.start()
    quarters = [slice(2 * q * width, 2 * (q + 1) * width) for q in range(4)]

    def pick(j, carry):
        pltpu.make_async_copy(toks.at[j], toks.at[j], tok_sems.at[j]).wait()
        onehot = picks[j]
        for cols in quarters:
            got = contract(onehot, toks[j, :, cols], 1, 0).astype(jnp.bfloat16)
            rows[j, :, :, cols] = got.reshape(exp_dev, SLOTS, 2 * width)
        return carry

    lax.fori_loop(0, n_seq, pick, 0)

    def expert(e, carry):
        taken = rows[:, e].reshape(n_seq * SLOTS, model_width)
        gate_val = contract(w_gate[e], taken, 1, 1)
        for copy in fetches(e):
            copy.wait()
        at = lax.rem(e, RING)
        up_val = contract(w_up[at], taken, 1, 1)
        hidden = gate_val / (1.0 + jnp.exp(-gate_val)) * up_val
        hidden = hidden.T.astype(jnp.bfloat16)
        for cols in quarters:
            piece = contract(hidden, w_down[at, :, cols], 1, 0).astype(jnp.bfloat16)
            rows[:, e, :, cols] = piece.reshape(n_seq, SLOTS, 2 * width)

        @pl.when(e + RING < exp_dev)
        def _():
            for copy in fetches(e + RING):
                copy.start()

        return carry

    lax.fori_loop(0, exp_dev, expert, 0)

    def combine(dz, carry):
        for dy in range(2):
            j = 2 * dz + dy
            weight = weights[j]
            along = jnp.zeros((tok_rows, 1), jnp.float32)
            for cols in quarters:
                got = contract(weight, rows[j, :, :, cols].reshape(slots_src, 2 * width), 1, 0)
                mixed[:, cols] = got
                along += jnp.sum(got * unit_ref[:, cols], axis=1, keepdims=True)
            for dc in range(2):
                first_far, second_far, first_near, second_near = out_refs[4 * dc : 4 * dc + 4]
                second = second_far if dy else second_near
                for dst, at, start, color, dx in (
                    (first_far, j, 0, 0, 1),
                    (first_near, j, 0, 0, 0),
                    (second, dz, 0, 1, 0),
                    (second, dz, width, 1, 1),
                ):
                    cols = pl.ds(group_offset(rep, color, dx, dc, width), width)
                    value = mixed[:, cols] - along * unit_ref[:, cols]
                    dst[at, :, start : start + width] = value.astype(jnp.bfloat16)
        return carry

    lax.fori_loop(0, n_z, combine, 0)


def moe_partial(picks, weights, unit_dir, own, pieces, w_gate, w_up, w_down):
    n_seq, _, tok_rows = picks.shape
    exp_dev, hid_dev, model_width = w_gate.shape
    width = model_width // 8
    vmem = pl.BlockSpec(memory_space=pltpu.VMEM)
    hbm = pl.BlockSpec(memory_space=pl.ANY)
    n_pieces = len(pieces)
    w_gate = pltpu.with_memory_space_constraint(w_gate, pltpu.VMEM)
    pieces = [pltpu.with_memory_space_constraint(piece, pltpu.VMEM) for piece in pieces]
    outs = [
        jax.ShapeDtypeStruct((blocks, tok_rows, runs * width), jnp.bfloat16)
        for _ in range(2)
        for blocks, runs in ((n_seq, 1), (n_seq // 2, 2), (n_seq, 1), (n_seq // 2, 2))
    ]
    return pl.pallas_call(
        functools.partial(moe_kernel, n_pieces),
        out_shape=outs,
        in_specs=[vmem] * 3 + [hbm] * (n_pieces + 1) + [vmem, hbm, hbm],
        out_specs=[vmem] * len(outs),
        scratch_shapes=[
            pltpu.VMEM((RING, hid_dev, model_width), jnp.bfloat16),
            pltpu.VMEM((RING, hid_dev, model_width), jnp.bfloat16),
            pltpu.VMEM((n_seq, tok_rows, model_width), jnp.bfloat16),
            pltpu.VMEM((n_seq, exp_dev, SLOTS, model_width), jnp.bfloat16),
            pltpu.VMEM((tok_rows, model_width), jnp.float32),
            pltpu.SemaphoreType.DMA((n_seq,)),
            pltpu.SemaphoreType.DMA((2, RING)),
        ],
        compiler_params=pltpu.CompilerParams(vmem_limit_bytes=32 * 1024 * 1024),
        cost_estimate=pl.CostEstimate(
            flops=6 * n_seq * SLOTS * exp_dev * hid_dev * model_width,
            bytes_accessed=6 * exp_dev * hid_dev * model_width + 4 * n_seq * own.size,
            transcendentals=0,
        ),
    )(picks, weights, unit_dir, own, *pieces, w_gate, w_up, w_down)


def swap(value, axis, distance):
    size = lax.axis_size(axis)
    return lax.ppermute(value, axis, [(i, i ^ distance) for i in range(size)])


def added(*terms):
    return sum(term.astype(jnp.float32) for term in terms).astype(jnp.bfloat16)


def gathered(tokens, norm_gain, refusal_dir, expert_ids, gate_probs, w_gate, w_up, w_down):
    tok_rows, model_width = tokens.shape
    n_z = lax.axis_size("seq") // 2
    others = range(1, n_z)
    exp_dev = w_gate.shape[0]
    width = model_width // 8

    normed, to_z, to_y, unit_dir, base, meta = norm_and_base(
        tokens, norm_gain, refusal_dir, expert_ids, gate_probs
    )
    from_z = [swap(to_z, "seq", 2 * d) for d in others]
    from_y = swap(to_y, "seq", 1)
    near = [meta] + [swap(meta, "seq", 2 * d) for d in others]
    picks, weights = route(near, swap(jnp.stack(near), "seq", 1), exp_dev)

    first = jnp.stack([piece[:, :width] for piece in from_z])
    second = jnp.stack([piece[:, width:] for piece in from_z])
    second, picks, weights = lax.optimization_barrier((second, picks, weights))
    x_two = swap(second, "rep", 2)
    y_two = swap(first, "seq", 1)
    x_one = swap(jnp.concatenate([first, from_y[None, :, :width]]), "rep", 2)
    sibling = [swap(piece, "rep", 1) for piece in (*from_z, from_y)]
    to_y, y_two, *sibling = lax.optimization_barrier(
        (jnp.concatenate([second, x_two], axis=2), y_two, *sibling)
    )
    y_three = swap(to_y, "seq", 1)
    x_three = swap(y_two, "rep", 2)
    last = [x_two, x_one, y_two, x_three, y_three]
    pieces = [*from_z, from_y, *last, *sibling, *[swap(piece, "rep", 1) for piece in last]]

    sums = moe_partial(picks, weights, unit_dir, normed, pieces, w_gate, w_up, w_down)
    kept, sent = sums[:4], sums[4:]
    first_far, second_far, first_near, second_near = [
        added(mine, swap(theirs, "rep", 1)) for mine, theirs in zip(kept, sent)
    ]
    first_sum = added(first_near, swap(first_far, "rep", 2))
    second_sum = added(second_near, swap(second_far, "seq", 1))
    by_y = first_sum.reshape(n_z, 2, tok_rows, width)
    first_sum = added(by_y[:, 0], swap(by_y[:, 1], "seq", 1))
    second_sum = added(second_sum[:, :, :width], swap(second_sum[:, :, width:], "rep", 2))
    blocks = jnp.concatenate([first_sum, second_sum], axis=2)
    arrived = [swap(blocks[d], "seq", 2 * d) for d in others]
    summed = sum(term.astype(jnp.float32) for term in [blocks[0], *arrived])

    return (base + summed).astype(jnp.bfloat16)


def exchanged(tokens, norm_gain, refusal_dir, expert_ids, gate_probs, w_gate, w_up, w_down):
    tok_rows, model_width = tokens.shape
    top_k = expert_ids.shape[1]
    n_seq = lax.axis_size("seq")
    n_rep = lax.axis_size("rep")
    exp_dev = w_gate.shape[0]
    experts = exp_dev * n_seq
    slot_count = tok_rows * top_k
    part_width = model_width // n_rep
    tokens_f32 = tokens.astype(jnp.float32)
    inv_rms = lax.rsqrt(jnp.mean(tokens_f32 * tokens_f32, axis=1, keepdims=True) + 1e-06)
    normed = (tokens_f32 * inv_rms * norm_gain).astype(jnp.bfloat16)
    flat_ids = expert_ids.reshape(slot_count)
    onehot = (flat_ids[:, None] == jnp.arange(experts, dtype=jnp.int32)[None, :]).astype(jnp.int32)
    slot_rank = jnp.sum(jnp.cumsum(onehot, axis=0) * onehot, axis=1) - 1
    target = flat_ids * CAP + slot_rank
    repeated = jnp.broadcast_to(normed[:, None, :], (tok_rows, top_k, model_width)).reshape(
        slot_count, model_width
    )
    sendbuf = jnp.zeros((experts * CAP, model_width), jnp.bfloat16).at[target].set(repeated)
    sendbuf = sendbuf.reshape(n_seq, exp_dev, CAP, model_width)
    arrived = lax.all_to_all(sendbuf, "seq", split_axis=0, concat_axis=0, tiled=True)
    gate_val = jnp.einsum("secd,efd->secf", arrived, w_gate, preferred_element_type=jnp.float32)
    up_val = jnp.einsum("secd,efd->secf", arrived, w_up, preferred_element_type=jnp.float32)
    hidden = (jax.nn.silu(gate_val) * up_val).astype(jnp.bfloat16)
    pieces = jnp.einsum(
        "secf,efd->secd", hidden, w_down, preferred_element_type=jnp.float32
    ).astype(jnp.bfloat16)
    probs_flat = gate_probs.reshape(slot_count)[:, None]
    returned = lax.all_to_all(pieces, "seq", split_axis=0, concat_axis=0, tiled=True)
    returned = returned.reshape(experts * CAP, model_width)
    weighted = returned[target].astype(jnp.float32) * probs_flat
    moe_part = jnp.sum(weighted.reshape(tok_rows, top_k, model_width), axis=1)
    summed = lax.psum_scatter(
        moe_part.astype(jnp.bfloat16), "rep", scatter_dimension=1, tiled=True
    ).astype(jnp.float32)
    unit_dir = refusal_dir / jnp.sqrt(jnp.sum(refusal_dir * refusal_dir) + 1e-06)
    rep_offset = lax.axis_index("rep") * part_width
    unit_slice = lax.dynamic_slice_in_dim(unit_dir, rep_offset, part_width, 0)
    own_tokens = lax.dynamic_slice_in_dim(tokens_f32, rep_offset, part_width, 1)
    residual = own_tokens + summed
    along_dir = lax.psum(jnp.sum(residual * unit_slice, axis=1), "rep")
    return (residual - along_dir[:, None] * unit_slice).astype(jnp.bfloat16)


def local(tokens, norm_gain, refusal_dir, expert_ids, gate_probs, w_gate, w_up, w_down):
    plan = gathered if w_gate.shape[0] * CAP >= tokens.shape[0] else exchanged
    return plan(tokens, norm_gain, refusal_dir, expert_ids, gate_probs, w_gate, w_up, w_down)


def solution(mesh):
    placed = (
        P("seq", None),
        P(),
        P(),
        P("seq", None),
        P("seq", None),
        P("seq", "rep", None),
        P("seq", "rep", None),
        P("seq", "rep", None),
    )
    return jax.shard_map(
        local, mesh=mesh, in_specs=placed, out_specs=P("seq", "rep"), check_vma=False
    )
```

```python
import functools

import jax
import jax.numpy as jnp
from jax import lax
from jax.experimental import pallas as pl
from jax.experimental.pallas import tpu as pltpu
from jax.sharding import PartitionSpec as P

CAP = 12
SLOTS = 16
RING = 6


def contract(lhs, rhs, lhs_dim, rhs_dim):
    return lax.dot_general(
        lhs, rhs, (((lhs_dim,), (rhs_dim,)), ((), ())), preferred_element_type=jnp.float32
    )


def group_offset(rep, color, dx, dc, width):
    return pl.multiple_of((rep ^ (2 * dx + dc)) * 2 * width + color * width, width)


def token_pieces(n_z, width):
    others = range(1, n_z)
    pieces = [[(2 * d, [(0, 0), (1, 0)])] for d in others]
    pieces.append([(1, [(0, 0), (1, 0), (1, 1)])])
    pieces.append([(2 * d, [(1, 1)]) for d in others])
    pieces.append([(2 * d, [(0, 1)]) for d in others] + [(1, [(0, 1)])])
    pieces.append([(2 * d + 1, [(0, 0)]) for d in others])
    pieces.append([(2 * d + 1, [(0, 1)]) for d in others])
    pieces.append([(2 * d + 1, [(1, 0), (1, 1)]) for d in others])
    return pieces


def norm_kernel(
    tokens_ref, gain_ref, refusal_ref, ids_ref, probs_ref,
    normed_ref, to_z_ref, to_y_ref, unit_ref, base_ref, meta_ref,
):
    tok_rows, model_width = tokens_ref.shape
    width = model_width // 8
    rep = lax.axis_index("rep")
    toks = tokens_ref[...].astype(jnp.float32)
    refusal = refusal_ref[...]
    unit = refusal / jnp.sqrt(jnp.sum(refusal * refusal, axis=1, keepdims=True) + 1e-06)
    unit_ref[...] = unit
    inv_rms = lax.rsqrt(jnp.mean(toks * toks, axis=1, keepdims=True) + 1e-06)
    normed_ref[...] = (toks * inv_rms * gain_ref[...]).astype(jnp.bfloat16)
    own = pl.ds(group_offset(rep, 0, 0, 0, width), 2 * width)
    other = pl.ds(group_offset(rep, 1, 1, 0, width), width)
    meta = jnp.concatenate([ids_ref[...].astype(jnp.float32), probs_ref[...]], axis=0)
    meta = meta.astype(jnp.bfloat16)
    meta_ref[...] = meta
    for ref in (to_z_ref, to_y_ref):
        ref[:tok_rows, : 2 * width] = normed_ref[:, own]
        ref[tok_rows:] = jnp.zeros((meta.shape[0], ref.shape[1]), jnp.bfloat16)
        ref[tok_rows:, :tok_rows] = meta
    to_y_ref[:tok_rows, 2 * width :] = normed_ref[:, other]
    along = jnp.sum(toks * unit, axis=1, keepdims=True)
    base_ref[...] = tokens_ref[:, own].astype(jnp.float32) - along * unit_ref[:, own]


def norm_and_base(tokens, norm_gain, refusal_dir, expert_ids, gate_probs):
    tok_rows, model_width = tokens.shape
    width = model_width // 8
    meta_rows = 2 * expert_ids.shape[1]
    vmem = pl.BlockSpec(memory_space=pltpu.VMEM)
    return pl.pallas_call(
        norm_kernel,
        out_shape=[
            jax.ShapeDtypeStruct((tok_rows, model_width), jnp.bfloat16),
            jax.ShapeDtypeStruct((tok_rows + meta_rows, 2 * width), jnp.bfloat16),
            jax.ShapeDtypeStruct((tok_rows + meta_rows, 3 * width), jnp.bfloat16),
            jax.ShapeDtypeStruct((1, model_width), jnp.float32),
            jax.ShapeDtypeStruct((tok_rows, 2 * width), jnp.float32),
            jax.ShapeDtypeStruct((meta_rows, tok_rows), jnp.bfloat16),
        ],
        in_specs=[vmem] * 5,
        out_specs=[vmem] * 6,
    )(tokens, norm_gain[None, :], refusal_dir[None, :], expert_ids.T, gate_probs.T)


def route_kernel(exp_dev, meta_ref, picks_ref, weights_ref):
    n_seq, twice_k, tok_rows = meta_ref.shape
    top_k = twice_k // 2
    first = (lax.axis_index("seq") * exp_dev).astype(jnp.float32)
    exp_iota = lax.broadcasted_iota(jnp.int32, (exp_dev, tok_rows), 0).astype(jnp.float32) + first
    earlier = (
        lax.broadcasted_iota(jnp.int32, (tok_rows, tok_rows), 0)
        < lax.broadcasted_iota(jnp.int32, (tok_rows, tok_rows), 1)
    ).astype(jnp.float32).astype(jnp.bfloat16)
    slot_iota = lax.broadcasted_iota(jnp.int32, (exp_dev, SLOTS, tok_rows), 1).astype(jnp.float32)

    def place_block(j, carry):
        meta = meta_ref[j].astype(jnp.float32)
        hit = jnp.zeros((exp_dev, tok_rows), jnp.float32)
        prob = jnp.zeros((exp_dev, tok_rows), jnp.float32)
        for k in range(top_k):
            same = meta[k : k + 1, :] == exp_iota
            hit = jnp.where(same, 1.0, hit)
            prob = jnp.where(same, meta[top_k + k : top_k + k + 1, :], prob)
        rank = contract(hit.astype(jnp.bfloat16), earlier, 1, 0)
        slot = jnp.where(hit > 0.0, rank, -1.0)
        here = slot[:, None, :] == slot_iota
        onehot = jnp.where(here, 1.0, 0.0).reshape(exp_dev * SLOTS, tok_rows)
        weight = jnp.where(here, prob[:, None, :], 0.0).reshape(exp_dev * SLOTS, tok_rows)
        picks_ref[j] = onehot.astype(jnp.bfloat16)
        weights_ref[j] = weight.T.astype(jnp.bfloat16)
        return carry

    lax.fori_loop(0, n_seq, place_block, 0)


def route(meta, exp_dev):
    n_seq, _, tok_rows = meta.shape
    vmem = pl.BlockSpec(memory_space=pltpu.VMEM)
    return pl.pallas_call(
        functools.partial(route_kernel, exp_dev),
        out_shape=[
            jax.ShapeDtypeStruct((n_seq, exp_dev * SLOTS, tok_rows), jnp.bfloat16),
            jax.ShapeDtypeStruct((n_seq, tok_rows, exp_dev * SLOTS), jnp.bfloat16),
        ],
        in_specs=[vmem],
        out_specs=[vmem] * 2,
        cost_estimate=pl.CostEstimate(
            flops=4_000_000_000, bytes_accessed=8 * n_seq * exp_dev * SLOTS * tok_rows,
            transcendentals=0,
        ),
    )(meta)


def moe_kernel(n_pieces, *refs):
    picks_hbm, weights_hbm, unit_ref, own_hbm = refs[:4]
    pieces_in = refs[4 : 4 + n_pieces]
    w_gate_hbm, w_up_hbm, w_down_hbm = refs[4 + n_pieces : 7 + n_pieces]
    out_refs = refs[7 + n_pieces : 15 + n_pieces]
    (picks, weights, w_in, w_down, toks, rows, hidden, mixed, table_sems, tok_sems, in_sems,
     down_sems) = refs[15 + n_pieces :]
    n_seq, tok_rows, model_width = toks.shape
    n_z = n_seq // 2
    exp_dev, hid_dev, _ = w_gate_hbm.shape
    width = model_width // 8
    slots_src = exp_dev * SLOTS
    rep = lax.axis_index("rep")
    tables = [
        pltpu.make_async_copy(picks_hbm, picks, table_sems.at[0]),
        pltpu.make_async_copy(weights_hbm, weights, table_sems.at[1]),
    ]
    tables[0].start()

    pltpu.make_async_copy(own_hbm, toks.at[0], tok_sems.at[0]).start()
    kinds = token_pieces(n_z, width)
    for i, piece in enumerate(pieces_in):
        dc = i // len(kinds)
        for at, (j, runs) in enumerate(kinds[i % len(kinds)]):
            block = piece if len(piece.shape) == 2 else piece.at[at]
            for n, (color, dx) in enumerate(runs):
                cols = pl.ds(group_offset(rep, color, dx, dc, width), width)
                pltpu.make_async_copy(
                    block.at[pl.ds(0, tok_rows), pl.ds(n * width, width)],
                    toks.at[j, :, cols],
                    tok_sems.at[j],
                ).start()

    def in_copies(e):
        at = lax.rem(e, RING)
        return [
            pltpu.make_async_copy(
                src.at[e], w_in.at[at, pl.ds(i * hid_dev, hid_dev)], in_sems.at[i, at]
            )
            for i, src in enumerate((w_gate_hbm, w_up_hbm))
        ]

    def down_copy(e):
        return pltpu.make_async_copy(w_down_hbm.at[e], w_down.at[e], down_sems.at[e])

    for e in range(min(RING, exp_dev)):
        for copy in in_copies(e):
            copy.start()
    tables[1].start()
    quarters = [slice(2 * q * width, 2 * (q + 1) * width) for q in range(4)]
    tables[0].wait()

    def pick(pair, carry):
        for j in (2 * pair, 2 * pair + 1):
            pltpu.make_async_copy(toks.at[j], toks.at[j], tok_sems.at[j]).wait()
        for j in (2 * pair, 2 * pair + 1):
            onehot = picks[j]
            for cols in quarters:
                got = contract(onehot, toks[j, :, cols], 1, 0).astype(jnp.bfloat16)
                rows[j, :, :, cols] = got.reshape(exp_dev, SLOTS, 2 * width)
        return carry

    lax.fori_loop(0, n_z, pick, 0)

    def widen(pair, carry):
        experts = (2 * pair, 2 * pair + 1)
        for e in experts:
            for copy in in_copies(e):
                copy.wait()
        both = [
            contract(
                w_in[lax.rem(e, RING)], rows[:, e].reshape(n_seq * SLOTS, model_width), 1, 1
            )
            for e in experts
        ]
        for e, value in zip(experts, both):
            gate_val, up_val = value[:hid_dev], value[hid_dev:]
            act = gate_val / (1.0 + jnp.exp(-gate_val)) * up_val
            hidden[e] = act.T.astype(jnp.bfloat16)
        for e in experts:
            down_copy(e).start()

            @pl.when(e + RING < exp_dev)
            def _():
                for copy in in_copies(e + RING):
                    copy.start()

        return carry

    lax.fori_loop(0, exp_dev // 2, widen, 0)

    def narrow(pair, carry):
        experts = (2 * pair, 2 * pair + 1)
        for e in experts:
            down_copy(e).wait()
        for e in experts:
            for cols in quarters:
                piece = contract(hidden[e], w_down[e, :, cols], 1, 0).astype(jnp.bfloat16)
                rows[:, e, :, cols] = piece.reshape(n_seq, SLOTS, 2 * width)
        return carry

    lax.fori_loop(0, exp_dev // 2, narrow, 0)
    tables[1].wait()

    def combine(dz, carry):
        along = [jnp.zeros((tok_rows, 1), jnp.float32)] * 2
        for dy in range(2):
            j = 2 * dz + dy
            weight = weights[j]
            for cols in quarters:
                got = contract(weight, rows[j, :, :, cols].reshape(slots_src, 2 * width), 1, 0)
                mixed[dy, :, cols] = got
                along[dy] += jnp.sum(got * unit_ref[:, cols], axis=1, keepdims=True)
        for dy in range(2):
            for dc in range(2):
                first_far, second_far, first_near, second_near = out_refs[4 * dc : 4 * dc + 4]
                second = second_far if dy else second_near
                for dst, at, start, color, dx in (
                    (first_far, 2 * dz + dy, 0, 0, 1),
                    (first_near, 2 * dz + dy, 0, 0, 0),
                    (second, dz, 0, 1, 0),
                    (second, dz, width, 1, 1),
                ):
                    cols = pl.ds(group_offset(rep, color, dx, dc, width), width)
                    value = mixed[dy, :, cols] - along[dy] * unit_ref[:, cols]
                    dst[at, :, start : start + width] = value.astype(jnp.bfloat16)
        return carry

    lax.fori_loop(0, n_z, combine, 0)


def moe_partial(picks, weights, unit_dir, own, pieces, w_gate, w_up, w_down):
    n_seq, _, tok_rows = picks.shape
    exp_dev, hid_dev, model_width = w_gate.shape
    width = model_width // 8
    vmem = pl.BlockSpec(memory_space=pltpu.VMEM)
    hbm = pl.BlockSpec(memory_space=pltpu.HBM)
    whole = pl.BlockSpec(memory_space=pl.ANY)
    n_pieces = len(pieces)
    pieces = [pltpu.with_memory_space_constraint(piece, pltpu.VMEM) for piece in pieces]
    outs = [
        jax.ShapeDtypeStruct((blocks, tok_rows, runs * width), jnp.bfloat16)
        for _ in range(2)
        for blocks, runs in ((n_seq, 1), (n_seq // 2, 2), (n_seq, 1), (n_seq // 2, 2))
    ]
    return pl.pallas_call(
        functools.partial(moe_kernel, n_pieces),
        out_shape=outs,
        in_specs=[hbm, hbm, vmem, hbm] + [whole] * n_pieces + [hbm] * 3,
        out_specs=[vmem] * len(outs),
        scratch_shapes=[
            pltpu.VMEM(picks.shape, jnp.bfloat16),
            pltpu.VMEM(weights.shape, jnp.bfloat16),
            pltpu.VMEM((RING, 2 * hid_dev, model_width), jnp.bfloat16),
            pltpu.VMEM(w_down.shape, jnp.bfloat16),
            pltpu.VMEM((n_seq, tok_rows, model_width), jnp.bfloat16),
            pltpu.VMEM((n_seq, exp_dev, SLOTS, model_width), jnp.bfloat16),
            pltpu.VMEM((exp_dev, n_seq * SLOTS, hid_dev), jnp.bfloat16),
            pltpu.VMEM((2, tok_rows, model_width), jnp.float32),
            pltpu.SemaphoreType.DMA((2,)),
            pltpu.SemaphoreType.DMA((n_seq,)),
            pltpu.SemaphoreType.DMA((2, RING)),
            pltpu.SemaphoreType.DMA((exp_dev,)),
        ],
        compiler_params=pltpu.CompilerParams(vmem_limit_bytes=42 * 1024 * 1024),
        cost_estimate=pl.CostEstimate(
            flops=6 * n_seq * SLOTS * exp_dev * hid_dev * model_width,
            bytes_accessed=6 * exp_dev * hid_dev * model_width + 4 * n_seq * own.size,
            transcendentals=0,
        ),
    )(picks, weights, unit_dir, own, *pieces, w_gate, w_up, w_down)


def swap(value, axis, distance):
    size = lax.axis_size(axis)
    return lax.ppermute(value, axis, [(i, i ^ distance) for i in range(size)])


def added(*terms):
    return sum(term.astype(jnp.float32) for term in terms).astype(jnp.bfloat16)


def gathered(tokens, norm_gain, refusal_dir, expert_ids, gate_probs, w_gate, w_up, w_down):
    tok_rows, model_width = tokens.shape
    n_z = lax.axis_size("seq") // 2
    others = range(1, n_z)
    exp_dev = w_gate.shape[0]
    width = model_width // 8

    normed, to_z, to_y, unit_dir, base, meta = norm_and_base(
        tokens, norm_gain, refusal_dir, expert_ids, gate_probs
    )
    from_z = [swap(to_z, "seq", 2 * d) for d in others]
    from_y = swap(to_y, "seq", 1)
    first = jnp.stack([piece[:, :width] for piece in from_z])
    second = jnp.stack([piece[:tok_rows, width:] for piece in from_z])
    x_two = swap(second, "rep", 2)
    y_two = swap(first, "seq", 1)
    x_one = swap(
        jnp.concatenate([first[:, :tok_rows], from_y[None, :tok_rows, :width]]), "rep", 2
    )
    sibling = [swap(piece, "rep", 1) for piece in (*from_z, from_y)]
    to_y, y_two, *sibling = lax.optimization_barrier(
        (jnp.concatenate([second, x_two], axis=2), y_two, *sibling)
    )
    y_three = swap(to_y, "seq", 1)
    below = [meta, from_y[tok_rows:, :tok_rows]]
    for d in range(n_z - 1):
        below += [from_z[d][tok_rows:, :tok_rows], y_two[d, tok_rows:, :tok_rows]]
    picks, weights = route(jnp.stack(below), exp_dev)
    to_x, picks, weights = lax.optimization_barrier((y_two[:, :tok_rows], picks, weights))
    x_three = swap(to_x, "rep", 2)
    last = [x_two, x_one, y_two, x_three, y_three]
    pieces = [*from_z, from_y, *last, *sibling, *[swap(piece, "rep", 1) for piece in last]]

    sums = moe_partial(picks, weights, unit_dir, normed, pieces, w_gate, w_up, w_down)
    kept, sent = sums[:4], sums[4:]
    first_far, second_far, first_near, second_near = [
        added(mine, swap(theirs, "rep", 1)) for mine, theirs in zip(kept, sent)
    ]
    first_sum = added(first_near, swap(first_far, "rep", 2))
    second_sum = added(second_near, swap(second_far, "seq", 1))
    by_y = first_sum.reshape(n_z, 2, tok_rows, width)
    first_sum = added(by_y[:, 0], swap(by_y[:, 1], "seq", 1))
    second_sum = added(second_sum[:, :, :width], swap(second_sum[:, :, width:], "rep", 2))
    blocks = jnp.concatenate([first_sum, second_sum], axis=2)
    arrived = [swap(blocks[d], "seq", 2 * d) for d in others]
    summed = sum(term.astype(jnp.float32) for term in [blocks[0], *arrived])

    return (base + summed).astype(jnp.bfloat16)


def exchanged(tokens, norm_gain, refusal_dir, expert_ids, gate_probs, w_gate, w_up, w_down):
    tok_rows, model_width = tokens.shape
    top_k = expert_ids.shape[1]
    n_seq = lax.axis_size("seq")
    n_rep = lax.axis_size("rep")
    exp_dev = w_gate.shape[0]
    experts = exp_dev * n_seq
    slot_count = tok_rows * top_k
    part_width = model_width // n_rep
    tokens_f32 = tokens.astype(jnp.float32)
    inv_rms = lax.rsqrt(jnp.mean(tokens_f32 * tokens_f32, axis=1, keepdims=True) + 1e-06)
    normed = (tokens_f32 * inv_rms * norm_gain).astype(jnp.bfloat16)
    flat_ids = expert_ids.reshape(slot_count)
    onehot = (flat_ids[:, None] == jnp.arange(experts, dtype=jnp.int32)[None, :]).astype(jnp.int32)
    slot_rank = jnp.sum(jnp.cumsum(onehot, axis=0) * onehot, axis=1) - 1
    target = flat_ids * CAP + slot_rank
    repeated = jnp.broadcast_to(normed[:, None, :], (tok_rows, top_k, model_width)).reshape(
        slot_count, model_width
    )
    sendbuf = jnp.zeros((experts * CAP, model_width), jnp.bfloat16).at[target].set(repeated)
    sendbuf = sendbuf.reshape(n_seq, exp_dev, CAP, model_width)
    arrived = lax.all_to_all(sendbuf, "seq", split_axis=0, concat_axis=0, tiled=True)
    gate_val = jnp.einsum("secd,efd->secf", arrived, w_gate, preferred_element_type=jnp.float32)
    up_val = jnp.einsum("secd,efd->secf", arrived, w_up, preferred_element_type=jnp.float32)
    hidden = (jax.nn.silu(gate_val) * up_val).astype(jnp.bfloat16)
    pieces = jnp.einsum(
        "secf,efd->secd", hidden, w_down, preferred_element_type=jnp.float32
    ).astype(jnp.bfloat16)
    probs_flat = gate_probs.reshape(slot_count)[:, None]
    returned = lax.all_to_all(pieces, "seq", split_axis=0, concat_axis=0, tiled=True)
    returned = returned.reshape(experts * CAP, model_width)
    weighted = returned[target].astype(jnp.float32) * probs_flat
    moe_part = jnp.sum(weighted.reshape(tok_rows, top_k, model_width), axis=1)
    summed = lax.psum_scatter(
        moe_part.astype(jnp.bfloat16), "rep", scatter_dimension=1, tiled=True
    ).astype(jnp.float32)
    unit_dir = refusal_dir / jnp.sqrt(jnp.sum(refusal_dir * refusal_dir) + 1e-06)
    rep_offset = lax.axis_index("rep") * part_width
    unit_slice = lax.dynamic_slice_in_dim(unit_dir, rep_offset, part_width, 0)
    own_tokens = lax.dynamic_slice_in_dim(tokens_f32, rep_offset, part_width, 1)
    residual = own_tokens + summed
    along_dir = lax.psum(jnp.sum(residual * unit_slice, axis=1), "rep")
    return (residual - along_dir[:, None] * unit_slice).astype(jnp.bfloat16)


def local(tokens, norm_gain, refusal_dir, expert_ids, gate_probs, w_gate, w_up, w_down):
    plan = gathered if w_gate.shape[0] * CAP >= tokens.shape[0] else exchanged
    return plan(tokens, norm_gain, refusal_dir, expert_ids, gate_probs, w_gate, w_up, w_down)


def solution(mesh):
    placed = (
        P("seq", None),
        P(),
        P(),
        P("seq", None),
        P("seq", None),
        P("seq", "rep", None),
        P("seq", "rep", None),
        P("seq", "rep", None),
    )
    return jax.shard_map(
        local, mesh=mesh, in_specs=placed, out_specs=P("seq", "rep"), check_vma=False
    )
```

```python
import functools

import jax
import jax.numpy as jnp
from jax import lax
from jax.experimental import pallas as pl
from jax.experimental.pallas import tpu as pltpu
from jax.sharding import PartitionSpec as P

CAP = 12
SLOTS = 16
RING = 6


def contract(lhs, rhs, lhs_dim, rhs_dim):
    return lax.dot_general(
        lhs, rhs, (((lhs_dim,), (rhs_dim,)), ((), ())), preferred_element_type=jnp.float32
    )


def group_offset(rep, color, dx, dc, width):
    return pl.multiple_of((rep ^ (2 * dx + dc)) * 2 * width + color * width, width)


def token_pieces(n_z):
    near = [2 * d for d in range(1, n_z)]
    far = [2 * d + 1 for d in range(1, n_z)]
    return [
        [(j, [(1, 0)]) for j in near],
        [(j, [(0, 0)]) for j in near],
        [(1, [(0, 0), (1, 0), (0, 1), (1, 1)])],
        [(j, [(1, 1)]) for j in near],
        [(j, [(1, 0)]) for j in far],
        [(j, [(0, 1)]) for j in near],
        [(j, [(0, 0)]) for j in far],
        [(j, [(1, 1)]) for j in far],
        [(j, [(0, 1)]) for j in far],
    ]


def norm_kernel(
    tokens_ref, gain_ref, refusal_ref, ids_ref, probs_ref,
    normed_ref, second_ref, first_ref, to_y_ref, unit_ref, base_ref, meta_ref,
):
    tok_rows, model_width = tokens_ref.shape
    width = model_width // 8
    rep = lax.axis_index("rep")
    toks = tokens_ref[...].astype(jnp.float32)
    refusal = refusal_ref[...]
    unit = refusal / jnp.sqrt(jnp.sum(refusal * refusal, axis=1, keepdims=True) + 1e-06)
    unit_ref[...] = unit
    inv_rms = lax.rsqrt(jnp.mean(toks * toks, axis=1, keepdims=True) + 1e-06)
    normed_ref[...] = (toks * inv_rms * gain_ref[...]).astype(jnp.bfloat16)
    own = pl.ds(group_offset(rep, 0, 0, 0, width), 2 * width)
    other = pl.ds(group_offset(rep, 0, 1, 0, width), 2 * width)
    first_ref[...] = normed_ref[:, pl.ds(group_offset(rep, 0, 0, 0, width), width)]
    second_ref[:tok_rows] = normed_ref[:, pl.ds(group_offset(rep, 1, 0, 0, width), width)]
    to_y_ref[:tok_rows, : 2 * width] = normed_ref[:, own]
    to_y_ref[:tok_rows, 2 * width :] = normed_ref[:, other]
    meta = jnp.concatenate([ids_ref[...].astype(jnp.float32), probs_ref[...]], axis=0)
    meta = meta.astype(jnp.bfloat16)
    meta_ref[...] = meta
    for ref in (second_ref, to_y_ref):
        ref[tok_rows:] = jnp.zeros((meta.shape[0], ref.shape[1]), jnp.bfloat16)
        ref[tok_rows:, :tok_rows] = meta
    along = jnp.sum(toks * unit, axis=1, keepdims=True)
    base_ref[...] = tokens_ref[:, own].astype(jnp.float32) - along * unit_ref[:, own]


def norm_and_base(tokens, norm_gain, refusal_dir, expert_ids, gate_probs):
    tok_rows, model_width = tokens.shape
    width = model_width // 8
    meta_rows = 2 * expert_ids.shape[1]
    vmem = pl.BlockSpec(memory_space=pltpu.VMEM)
    return pl.pallas_call(
        norm_kernel,
        out_shape=[
            jax.ShapeDtypeStruct((tok_rows, model_width), jnp.bfloat16),
            jax.ShapeDtypeStruct((tok_rows + meta_rows, width), jnp.bfloat16),
            jax.ShapeDtypeStruct((tok_rows, width), jnp.bfloat16),
            jax.ShapeDtypeStruct((tok_rows + meta_rows, 4 * width), jnp.bfloat16),
            jax.ShapeDtypeStruct((1, model_width), jnp.float32),
            jax.ShapeDtypeStruct((tok_rows, 2 * width), jnp.float32),
            jax.ShapeDtypeStruct((meta_rows, tok_rows), jnp.bfloat16),
        ],
        in_specs=[vmem] * 5,
        out_specs=[vmem] * 7,
    )(tokens, norm_gain[None, :], refusal_dir[None, :], expert_ids.T, gate_probs.T)


def route_kernel(exp_dev, meta_ref, picks_ref, weights_ref):
    n_seq, twice_k, tok_rows = meta_ref.shape
    top_k = twice_k // 2
    first = (lax.axis_index("seq") * exp_dev).astype(jnp.float32)
    exp_iota = lax.broadcasted_iota(jnp.int32, (exp_dev, tok_rows), 0).astype(jnp.float32) + first
    earlier = (
        lax.broadcasted_iota(jnp.int32, (tok_rows, tok_rows), 0)
        < lax.broadcasted_iota(jnp.int32, (tok_rows, tok_rows), 1)
    ).astype(jnp.float32).astype(jnp.bfloat16)
    slot_iota = lax.broadcasted_iota(jnp.int32, (exp_dev, SLOTS, tok_rows), 1).astype(jnp.float32)

    def place_block(j, carry):
        meta = meta_ref[j].astype(jnp.float32)
        hit = jnp.zeros((exp_dev, tok_rows), jnp.float32)
        prob = jnp.zeros((exp_dev, tok_rows), jnp.float32)
        for k in range(top_k):
            same = meta[k : k + 1, :] == exp_iota
            hit = jnp.where(same, 1.0, hit)
            prob = jnp.where(same, meta[top_k + k : top_k + k + 1, :], prob)
        rank = contract(hit.astype(jnp.bfloat16), earlier, 1, 0)
        slot = jnp.where(hit > 0.0, rank, -1.0)
        here = slot[:, None, :] == slot_iota
        onehot = jnp.where(here, 1.0, 0.0).reshape(exp_dev * SLOTS, tok_rows)
        weight = jnp.where(here, prob[:, None, :], 0.0).reshape(exp_dev * SLOTS, tok_rows)
        picks_ref[j] = onehot.astype(jnp.bfloat16)
        weights_ref[j] = weight.T.astype(jnp.bfloat16)
        return carry

    lax.fori_loop(0, n_seq, place_block, 0)


def route(meta, exp_dev):
    n_seq, _, tok_rows = meta.shape
    vmem = pl.BlockSpec(memory_space=pltpu.VMEM)
    return pl.pallas_call(
        functools.partial(route_kernel, exp_dev),
        out_shape=[
            jax.ShapeDtypeStruct((n_seq, exp_dev * SLOTS, tok_rows), jnp.bfloat16),
            jax.ShapeDtypeStruct((n_seq, tok_rows, exp_dev * SLOTS), jnp.bfloat16),
        ],
        in_specs=[vmem],
        out_specs=[vmem] * 2,
        cost_estimate=pl.CostEstimate(
            flops=4_000_000_000, bytes_accessed=8 * n_seq * exp_dev * SLOTS * tok_rows,
            transcendentals=0,
        ),
    )(meta)


def moe_kernel(n_pieces, *refs):
    picks_hbm, weights_hbm, unit_ref, own_hbm = refs[:4]
    pieces_in = refs[4 : 4 + n_pieces]
    w_gate_hbm, w_up_hbm, w_down_hbm = refs[4 + n_pieces : 7 + n_pieces]
    out_refs = refs[7 + n_pieces : 11 + n_pieces]
    (picks, weights, w_in, w_down, toks, rows, hidden, mixed, table_sems, tok_sems, in_sems,
     down_sems) = refs[11 + n_pieces :]
    n_seq, tok_rows, model_width = toks.shape
    n_z = n_seq // 2
    exp_dev, hid_dev, _ = w_gate_hbm.shape
    width = model_width // 8
    slots_src = exp_dev * SLOTS
    rep = lax.axis_index("rep")
    tables = [
        pltpu.make_async_copy(picks_hbm, picks, table_sems.at[0]),
        pltpu.make_async_copy(weights_hbm, weights, table_sems.at[1]),
    ]
    tables[0].start()

    pltpu.make_async_copy(own_hbm, toks.at[0], tok_sems.at[0]).start()
    kinds = token_pieces(n_z)
    for i, piece in enumerate(pieces_in):
        dc = i // len(kinds)
        for at, (j, runs) in enumerate(kinds[i % len(kinds)]):
            block = piece if len(piece.shape) == 2 else piece.at[at]
            for n, (color, dx) in enumerate(runs):
                cols = pl.ds(group_offset(rep, color, dx, dc, width), width)
                pltpu.make_async_copy(
                    block.at[pl.ds(0, tok_rows), pl.ds(n * width, width)],
                    toks.at[j, :, cols],
                    tok_sems.at[j],
                ).start()

    def in_copies(e):
        at = lax.rem(e, RING)
        return [
            pltpu.make_async_copy(
                src.at[e], w_in.at[at, pl.ds(i * hid_dev, hid_dev)], in_sems.at[i, at]
            )
            for i, src in enumerate((w_gate_hbm, w_up_hbm))
        ]

    def down_copy(e):
        return pltpu.make_async_copy(w_down_hbm.at[e], w_down.at[e], down_sems.at[e])

    for e in range(min(RING, exp_dev)):
        for copy in in_copies(e):
            copy.start()
    tables[1].start()
    quarters = [slice(2 * q * width, 2 * (q + 1) * width) for q in range(4)]
    tables[0].wait()

    def pick(pair, carry):
        for j in (2 * pair, 2 * pair + 1):
            pltpu.make_async_copy(toks.at[j], toks.at[j], tok_sems.at[j]).wait()
        for j in (2 * pair, 2 * pair + 1):
            onehot = picks[j]
            for cols in quarters:
                got = contract(onehot, toks[j, :, cols], 1, 0).astype(jnp.bfloat16)
                rows[j, :, :, cols] = got.reshape(exp_dev, SLOTS, 2 * width)
        return carry

    lax.fori_loop(0, n_z, pick, 0)

    def widen(pair, carry):
        experts = (2 * pair, 2 * pair + 1)
        for e in experts:
            for copy in in_copies(e):
                copy.wait()
        both = [
            contract(
                w_in[lax.rem(e, RING)], rows[:, e].reshape(n_seq * SLOTS, model_width), 1, 1
            )
            for e in experts
        ]
        for e, value in zip(experts, both):
            gate_val, up_val = value[:hid_dev], value[hid_dev:]
            act = gate_val / (1.0 + jnp.exp(-gate_val)) * up_val
            hidden[e] = act.T.astype(jnp.bfloat16)
        for e in experts:
            down_copy(e).start()

            @pl.when(e + RING < exp_dev)
            def _():
                for copy in in_copies(e + RING):
                    copy.start()

        return carry

    lax.fori_loop(0, exp_dev // 2, widen, 0)

    def narrow(pair, carry):
        experts = (2 * pair, 2 * pair + 1)
        for e in experts:
            down_copy(e).wait()
        for e in experts:
            for cols in quarters:
                piece = contract(hidden[e], w_down[e, :, cols], 1, 0).astype(jnp.bfloat16)
                rows[:, e, :, cols] = piece.reshape(n_seq, SLOTS, 2 * width)
        return carry

    lax.fori_loop(0, exp_dev // 2, narrow, 0)
    tables[1].wait()

    def combine(dz, carry):
        along = [jnp.zeros((tok_rows, 1), jnp.float32)] * 2
        for dy in range(2):
            j = 2 * dz + dy
            weight = weights[j]
            for cols in quarters:
                got = contract(weight, rows[j, :, :, cols].reshape(slots_src, 2 * width), 1, 0)
                mixed[dy, :, cols] = got
                along[dy] += jnp.sum(got * unit_ref[:, cols], axis=1, keepdims=True)
        half = tok_rows // 2
        for dy in range(2):
            for dc in range(2):
                for n, (color, dx) in enumerate(((0, 1), (0, 0), (1, 0), (1, 1))):
                    cols = pl.ds(group_offset(rep, color, dx, dc, width), width)
                    value = mixed[dy, :, cols] - along[dy] * unit_ref[:, cols]
                    value = value.astype(jnp.bfloat16)
                    at = slice(n * width, (n + 1) * width)
                    out_refs[2 * dc][dy, dz, :, at] = value[:half]
                    out_refs[2 * dc + 1][dy, dz, :, at] = value[half:]
        return carry

    lax.fori_loop(0, n_z, combine, 0)


def moe_partial(picks, weights, unit_dir, own, pieces, w_gate, w_up, w_down):
    n_seq, _, tok_rows = picks.shape
    exp_dev, hid_dev, model_width = w_gate.shape
    width = model_width // 8
    vmem = pl.BlockSpec(memory_space=pltpu.VMEM)
    hbm = pl.BlockSpec(memory_space=pltpu.HBM)
    whole = pl.BlockSpec(memory_space=pl.ANY)
    n_pieces = len(pieces)
    pieces = [pltpu.with_memory_space_constraint(piece, pltpu.VMEM) for piece in pieces]
    picks, weights, own = [
        pltpu.with_memory_space_constraint(value, pltpu.HBM) for value in (picks, weights, own)
    ]
    outs = [
        jax.ShapeDtypeStruct((2, n_seq // 2, tok_rows // 2, 4 * width), jnp.bfloat16)
        for _ in range(4)
    ]
    return pl.pallas_call(
        functools.partial(moe_kernel, n_pieces),
        out_shape=outs,
        in_specs=[hbm, hbm, vmem, hbm] + [whole] * n_pieces + [hbm] * 3,
        out_specs=[vmem] * len(outs),
        scratch_shapes=[
            pltpu.VMEM(picks.shape, jnp.bfloat16),
            pltpu.VMEM(weights.shape, jnp.bfloat16),
            pltpu.VMEM((RING, 2 * hid_dev, model_width), jnp.bfloat16),
            pltpu.VMEM(w_down.shape, jnp.bfloat16),
            pltpu.VMEM((n_seq, tok_rows, model_width), jnp.bfloat16),
            pltpu.VMEM((n_seq, exp_dev, SLOTS, model_width), jnp.bfloat16),
            pltpu.VMEM((exp_dev, n_seq * SLOTS, hid_dev), jnp.bfloat16),
            pltpu.VMEM((2, tok_rows, model_width), jnp.float32),
            pltpu.SemaphoreType.DMA((2,)),
            pltpu.SemaphoreType.DMA((n_seq,)),
            pltpu.SemaphoreType.DMA((2, RING)),
            pltpu.SemaphoreType.DMA((exp_dev,)),
        ],
        compiler_params=pltpu.CompilerParams(vmem_limit_bytes=42 * 1024 * 1024),
        cost_estimate=pl.CostEstimate(
            flops=6 * n_seq * SLOTS * exp_dev * hid_dev * model_width,
            bytes_accessed=6 * exp_dev * hid_dev * model_width + 4 * n_seq * own.size,
            transcendentals=0,
        ),
    )(picks, weights, unit_dir, own, *pieces, w_gate, w_up, w_down)


def swap(value, axis, distance):
    size = lax.axis_size(axis)
    return lax.ppermute(value, axis, [(i, i ^ distance) for i in range(size)])


def added(*terms):
    return sum(term.astype(jnp.float32) for term in terms).astype(jnp.bfloat16)


def gathered(tokens, norm_gain, refusal_dir, expert_ids, gate_probs, w_gate, w_up, w_down):
    tok_rows, model_width = tokens.shape
    n_z = lax.axis_size("seq") // 2
    others = range(1, n_z)
    exp_dev = w_gate.shape[0]
    width = model_width // 8

    normed, second, first, to_y, unit_dir, base, meta = norm_and_base(
        tokens, norm_gain, refusal_dir, expert_ids, gate_probs
    )
    second = [swap(second, "seq", 2 * d) for d in others]
    from_y = swap(to_y, "seq", 1)
    first, second, from_y = lax.optimization_barrier((first, jnp.stack(second), from_y))
    first = jnp.stack([swap(first, "seq", 2 * d) for d in others])
    x_two = swap(second[:, :tok_rows], "rep", 2)
    y_one = swap(second, "seq", 1)
    y_two = swap(first, "seq", 1)
    x_one = swap(first, "rep", 2)
    to_y, to_core, to_core_y = lax.optimization_barrier((x_two, second, from_y))
    y_three = swap(to_y, "seq", 1)
    early = [swap(piece, "rep", 1) for piece in (to_core, first, to_core_y)]
    below = [meta, from_y[tok_rows:, :tok_rows]]
    for d in range(n_z - 1):
        below += [second[d, tok_rows:, :tok_rows], y_one[d, tok_rows:, :tok_rows]]
    picks, weights = route(jnp.stack(below), exp_dev)
    to_x, picks, weights = lax.optimization_barrier((y_two, picks, weights))
    x_three = swap(to_x, "rep", 2)
    last = [x_two, y_one, x_one, y_two, y_three, x_three]
    pieces = [second, first, from_y, *last, *early, *[swap(piece, "rep", 1) for piece in last]]

    kept_0, kept_1, sent_0, sent_1 = moe_partial(
        picks, weights, unit_dir, normed, pieces, w_gate, w_up, w_down
    )
    summed = jnp.concatenate(
        [summed_up(kept_0, sent_0, width), summed_up(kept_1, sent_1, width)], axis=0
    )
    return (base + summed).astype(jnp.bfloat16)


def summed_up(kept, sent, width):
    n_z = kept.shape[1]
    arrived = swap(sent, "rep", 1)
    x_far = swap(added(kept[..., :width], arrived[..., :width]), "rep", 2)
    y_far = swap(added(kept[1, ..., 2 * width :], arrived[1, ..., 2 * width :]), "seq", 1)
    mid = slice(width, 2 * width)
    first_far = swap(added(kept[1, ..., mid], arrived[1, ..., mid], x_far[1]), "seq", 1)
    end = slice(3 * width, 4 * width)
    second_far = swap(
        added(kept[0, ..., end], arrived[0, ..., end], y_far[..., width:]), "rep", 2
    )
    first = added(kept[0, ..., mid], arrived[0, ..., mid], x_far[0], first_far)
    near = slice(2 * width, 3 * width)
    second = added(kept[0, ..., near], arrived[0, ..., near], y_far[..., :width], second_far)
    blocks = jnp.concatenate([first, second], axis=2)
    terms = [blocks[0]] + [swap(blocks[d], "seq", 2 * d) for d in range(1, n_z)]
    return sum(term.astype(jnp.float32) for term in terms)


def exchanged(tokens, norm_gain, refusal_dir, expert_ids, gate_probs, w_gate, w_up, w_down):
    tok_rows, model_width = tokens.shape
    top_k = expert_ids.shape[1]
    n_seq = lax.axis_size("seq")
    n_rep = lax.axis_size("rep")
    exp_dev = w_gate.shape[0]
    experts = exp_dev * n_seq
    slot_count = tok_rows * top_k
    part_width = model_width // n_rep
    tokens_f32 = tokens.astype(jnp.float32)
    inv_rms = lax.rsqrt(jnp.mean(tokens_f32 * tokens_f32, axis=1, keepdims=True) + 1e-06)
    normed = (tokens_f32 * inv_rms * norm_gain).astype(jnp.bfloat16)
    flat_ids = expert_ids.reshape(slot_count)
    onehot = (flat_ids[:, None] == jnp.arange(experts, dtype=jnp.int32)[None, :]).astype(jnp.int32)
    slot_rank = jnp.sum(jnp.cumsum(onehot, axis=0) * onehot, axis=1) - 1
    target = flat_ids * CAP + slot_rank
    repeated = jnp.broadcast_to(normed[:, None, :], (tok_rows, top_k, model_width)).reshape(
        slot_count, model_width
    )
    sendbuf = jnp.zeros((experts * CAP, model_width), jnp.bfloat16).at[target].set(repeated)
    sendbuf = sendbuf.reshape(n_seq, exp_dev, CAP, model_width)
    arrived = lax.all_to_all(sendbuf, "seq", split_axis=0, concat_axis=0, tiled=True)
    gate_val = jnp.einsum("secd,efd->secf", arrived, w_gate, preferred_element_type=jnp.float32)
    up_val = jnp.einsum("secd,efd->secf", arrived, w_up, preferred_element_type=jnp.float32)
    hidden = (jax.nn.silu(gate_val) * up_val).astype(jnp.bfloat16)
    pieces = jnp.einsum(
        "secf,efd->secd", hidden, w_down, preferred_element_type=jnp.float32
    ).astype(jnp.bfloat16)
    probs_flat = gate_probs.reshape(slot_count)[:, None]
    returned = lax.all_to_all(pieces, "seq", split_axis=0, concat_axis=0, tiled=True)
    returned = returned.reshape(experts * CAP, model_width)
    weighted = returned[target].astype(jnp.float32) * probs_flat
    moe_part = jnp.sum(weighted.reshape(tok_rows, top_k, model_width), axis=1)
    summed = lax.psum_scatter(
        moe_part.astype(jnp.bfloat16), "rep", scatter_dimension=1, tiled=True
    ).astype(jnp.float32)
    unit_dir = refusal_dir / jnp.sqrt(jnp.sum(refusal_dir * refusal_dir) + 1e-06)
    rep_offset = lax.axis_index("rep") * part_width
    unit_slice = lax.dynamic_slice_in_dim(unit_dir, rep_offset, part_width, 0)
    own_tokens = lax.dynamic_slice_in_dim(tokens_f32, rep_offset, part_width, 1)
    residual = own_tokens + summed
    along_dir = lax.psum(jnp.sum(residual * unit_slice, axis=1), "rep")
    return (residual - along_dir[:, None] * unit_slice).astype(jnp.bfloat16)


def local(tokens, norm_gain, refusal_dir, expert_ids, gate_probs, w_gate, w_up, w_down):
    plan = gathered if w_gate.shape[0] * CAP >= tokens.shape[0] else exchanged
    return plan(tokens, norm_gain, refusal_dir, expert_ids, gate_probs, w_gate, w_up, w_down)


def solution(mesh):
    placed = (
        P("seq", None),
        P(),
        P(),
        P("seq", None),
        P("seq", None),
        P("seq", "rep", None),
        P("seq", "rep", None),
        P("seq", "rep", None),
    )
    return jax.shard_map(
        local, mesh=mesh, in_specs=placed, out_specs=P("seq", "rep"), check_vma=False
    )
```

```python
import functools

import jax
import jax.numpy as jnp
from jax import lax
from jax.experimental import pallas as pl
from jax.experimental.pallas import tpu as pltpu
from jax.sharding import PartitionSpec as P

CAP = 12
SLOTS = 16
RING = 6


def contract(lhs, rhs, lhs_dim, rhs_dim):
    return lax.dot_general(
        lhs, rhs, (((lhs_dim,), (rhs_dim,)), ((), ())), preferred_element_type=jnp.float32
    )


def group_offset(rep, color, dx, dc, width):
    return pl.multiple_of((rep ^ (2 * dx + dc)) * 2 * width + color * width, width)


def token_pieces(n_z):
    near = [2 * d for d in range(1, n_z)]
    far = [2 * d + 1 for d in range(1, n_z)]
    return [
        [(j, [(1, 0)]) for j in near],
        [(j, [(0, 0)]) for j in near],
        [(1, [(0, 0), (1, 0), (0, 1), (1, 1)])],
        [(j, [(1, 1)]) for j in near],
        [(j, [(1, 0)]) for j in far],
        [(j, [(0, 1)]) for j in near],
        [(j, [(0, 0)]) for j in far],
        [(j, [(1, 1)]) for j in far],
        [(j, [(0, 1)]) for j in far],
    ]


def norm_kernel(
    tokens_ref, gain_ref, refusal_ref, ids_ref, probs_ref,
    normed_ref, second_ref, first_ref, to_y_ref, unit_ref, base_ref, meta_ref,
):
    tok_rows, model_width = tokens_ref.shape
    width = model_width // 8
    rep = lax.axis_index("rep")
    toks = tokens_ref[...].astype(jnp.float32)
    refusal = refusal_ref[...]
    unit = refusal / jnp.sqrt(jnp.sum(refusal * refusal, axis=1, keepdims=True) + 1e-06)
    unit_ref[...] = unit
    inv_rms = lax.rsqrt(jnp.mean(toks * toks, axis=1, keepdims=True) + 1e-06)
    normed_ref[...] = (toks * inv_rms * gain_ref[...]).astype(jnp.bfloat16)
    own = pl.ds(group_offset(rep, 0, 0, 0, width), 2 * width)
    other = pl.ds(group_offset(rep, 0, 1, 0, width), 2 * width)
    first_ref[...] = normed_ref[:, pl.ds(group_offset(rep, 0, 0, 0, width), width)]
    second_ref[:tok_rows] = normed_ref[:, pl.ds(group_offset(rep, 1, 0, 0, width), width)]
    to_y_ref[:tok_rows, : 2 * width] = normed_ref[:, own]
    to_y_ref[:tok_rows, 2 * width :] = normed_ref[:, other]
    meta = jnp.concatenate([ids_ref[...].astype(jnp.float32), probs_ref[...]], axis=0)
    meta = meta.astype(jnp.bfloat16)
    meta_ref[...] = meta
    for ref in (second_ref, to_y_ref):
        ref[tok_rows:] = jnp.zeros((meta.shape[0], ref.shape[1]), jnp.bfloat16)
        ref[tok_rows:, :tok_rows] = meta
    along = jnp.sum(toks * unit, axis=1, keepdims=True)
    base_ref[...] = tokens_ref[:, own].astype(jnp.float32) - along * unit_ref[:, own]


def norm_and_base(tokens, norm_gain, refusal_dir, expert_ids, gate_probs):
    tok_rows, model_width = tokens.shape
    width = model_width // 8
    meta_rows = 2 * expert_ids.shape[1]
    vmem = pl.BlockSpec(memory_space=pltpu.VMEM)
    return pl.pallas_call(
        norm_kernel,
        out_shape=[
            jax.ShapeDtypeStruct((tok_rows, model_width), jnp.bfloat16),
            jax.ShapeDtypeStruct((tok_rows + meta_rows, width), jnp.bfloat16),
            jax.ShapeDtypeStruct((tok_rows, width), jnp.bfloat16),
            jax.ShapeDtypeStruct((tok_rows + meta_rows, 4 * width), jnp.bfloat16),
            jax.ShapeDtypeStruct((1, model_width), jnp.float32),
            jax.ShapeDtypeStruct((tok_rows, 2 * width), jnp.float32),
            jax.ShapeDtypeStruct((meta_rows, tok_rows), jnp.bfloat16),
        ],
        in_specs=[vmem] * 5,
        out_specs=[vmem] * 7,
    )(tokens, norm_gain[None, :], refusal_dir[None, :], expert_ids.T, gate_probs.T)


def route_kernel(exp_dev, meta_ref, picks_ref, weights_ref):
    n_seq, twice_k, tok_rows = meta_ref.shape
    top_k = twice_k // 2
    first = (lax.axis_index("seq") * exp_dev).astype(jnp.float32)
    exp_iota = lax.broadcasted_iota(jnp.int32, (exp_dev, tok_rows), 0).astype(jnp.float32) + first
    earlier = (
        lax.broadcasted_iota(jnp.int32, (tok_rows, tok_rows), 0)
        < lax.broadcasted_iota(jnp.int32, (tok_rows, tok_rows), 1)
    ).astype(jnp.float32).astype(jnp.bfloat16)
    slot_iota = lax.broadcasted_iota(jnp.int32, (exp_dev, SLOTS, tok_rows), 1).astype(jnp.float32)

    def place_block(j, carry):
        meta = meta_ref[j].astype(jnp.float32)
        hit = jnp.zeros((exp_dev, tok_rows), jnp.float32)
        prob = jnp.zeros((exp_dev, tok_rows), jnp.float32)
        for k in range(top_k):
            same = meta[k : k + 1, :] == exp_iota
            hit = jnp.where(same, 1.0, hit)
            prob = jnp.where(same, meta[top_k + k : top_k + k + 1, :], prob)
        rank = contract(hit.astype(jnp.bfloat16), earlier, 1, 0)
        slot = jnp.where(hit > 0.0, rank, -1.0)
        here = slot[:, None, :] == slot_iota
        onehot = jnp.where(here, 1.0, 0.0).reshape(exp_dev * SLOTS, tok_rows)
        weight = jnp.where(here, prob[:, None, :], 0.0).reshape(exp_dev * SLOTS, tok_rows)
        picks_ref[j] = onehot.astype(jnp.bfloat16)
        weights_ref[j] = weight.T.astype(jnp.bfloat16)
        return carry

    lax.fori_loop(0, n_seq, place_block, 0)


def route(meta, exp_dev):
    n_seq, _, tok_rows = meta.shape
    vmem = pl.BlockSpec(memory_space=pltpu.VMEM)
    return pl.pallas_call(
        functools.partial(route_kernel, exp_dev),
        out_shape=[
            jax.ShapeDtypeStruct((n_seq, exp_dev * SLOTS, tok_rows), jnp.bfloat16),
            jax.ShapeDtypeStruct((n_seq, tok_rows, exp_dev * SLOTS), jnp.bfloat16),
        ],
        in_specs=[vmem],
        out_specs=[vmem] * 2,
        cost_estimate=pl.CostEstimate(
            flops=4_000_000_000, bytes_accessed=8 * n_seq * exp_dev * SLOTS * tok_rows,
            transcendentals=0,
        ),
    )(meta)


def most_rows(tok_rows):
    return tok_rows // 64 * 48


def moe_kernel(n_pieces, *refs):
    picks_hbm, weights_hbm, unit_ref, own_hbm = refs[:4]
    pieces_in = refs[4 : 4 + n_pieces]
    w_gate_hbm, w_up_hbm, w_down_hbm = refs[4 + n_pieces : 7 + n_pieces]
    out_refs = refs[7 + n_pieces : 13 + n_pieces]
    (picks, weights, w_in, w_down, toks, rows, hidden, mixed, table_sems, tok_sems, in_sems,
     down_sems) = refs[13 + n_pieces :]
    n_seq, tok_rows, model_width = toks.shape
    n_z = n_seq // 2
    exp_dev, hid_dev, _ = w_gate_hbm.shape
    width = model_width // 8
    slots_src = exp_dev * SLOTS
    rep = lax.axis_index("rep")
    split = most_rows(tok_rows)
    tables = [
        pltpu.make_async_copy(picks_hbm, picks, table_sems.at[0]),
        pltpu.make_async_copy(weights_hbm, weights, table_sems.at[1]),
    ]
    tables[0].start()

    pltpu.make_async_copy(own_hbm, toks.at[0], tok_sems.at[0]).start()
    kinds = token_pieces(n_z)
    for i, piece in enumerate(pieces_in):
        dc = i // len(kinds)
        for at, (j, runs) in enumerate(kinds[i % len(kinds)]):
            block = piece if len(piece.shape) == 2 else piece.at[at]
            for n, (color, dx) in enumerate(runs):
                cols = pl.ds(group_offset(rep, color, dx, dc, width), width)
                pltpu.make_async_copy(
                    block.at[pl.ds(0, tok_rows), pl.ds(n * width, width)],
                    toks.at[j, :, cols],
                    tok_sems.at[j],
                ).start()

    def in_copies(e):
        at = lax.rem(e, RING)
        return [
            pltpu.make_async_copy(
                src.at[e], w_in.at[at, pl.ds(i * hid_dev, hid_dev)], in_sems.at[i, at]
            )
            for i, src in enumerate((w_gate_hbm, w_up_hbm))
        ]

    def down_copy(e):
        return pltpu.make_async_copy(w_down_hbm.at[e], w_down.at[e], down_sems.at[e])

    for e in range(min(RING, exp_dev)):
        for copy in in_copies(e):
            copy.start()
    tables[1].start()
    quarters = [slice(2 * q * width, 2 * (q + 1) * width) for q in range(4)]
    tables[0].wait()

    def pick(pair, carry):
        for j in (2 * pair, 2 * pair + 1):
            pltpu.make_async_copy(toks.at[j], toks.at[j], tok_sems.at[j]).wait()
        for j in (2 * pair, 2 * pair + 1):
            onehot = picks[j]
            for cols in quarters:
                got = contract(onehot, toks[j, :, cols], 1, 0).astype(jnp.bfloat16)
                rows[j, :, :, cols] = got.reshape(exp_dev, SLOTS, 2 * width)
        return carry

    lax.fori_loop(0, n_z, pick, 0)

    def widen(pair, carry):
        experts = (2 * pair, 2 * pair + 1)
        for e in experts:
            for copy in in_copies(e):
                copy.wait()
        both = [
            contract(
                w_in[lax.rem(e, RING)], rows[:, e].reshape(n_seq * SLOTS, model_width), 1, 1
            )
            for e in experts
        ]
        for e, value in zip(experts, both):
            gate_val, up_val = value[:hid_dev], value[hid_dev:]
            act = gate_val / (1.0 + jnp.exp(-gate_val)) * up_val
            hidden[e] = act.T.astype(jnp.bfloat16)
        for e in experts:
            down_copy(e).start()

            @pl.when(e + RING < exp_dev)
            def _():
                for copy in in_copies(e + RING):
                    copy.start()

        return carry

    lax.fori_loop(0, exp_dev // 2, widen, 0)

    def narrow(pair, carry):
        experts = (2 * pair, 2 * pair + 1)
        for e in experts:
            down_copy(e).wait()
        for e in experts:
            for cols in quarters:
                piece = contract(hidden[e], w_down[e, :, cols], 1, 0).astype(jnp.bfloat16)
                rows[:, e, :, cols] = piece.reshape(n_seq, SLOTS, 2 * width)
        return carry

    lax.fori_loop(0, exp_dev // 2, narrow, 0)
    tables[1].wait()

    def combine(dz, carry):
        along = [jnp.zeros((tok_rows, 1), jnp.float32)] * 2
        for dy in range(2):
            j = 2 * dz + dy
            weight = weights[j]
            for cols in quarters:
                got = contract(weight, rows[j, :, :, cols].reshape(slots_src, 2 * width), 1, 0)
                mixed[dy, :, cols] = got
                along[dy] += jnp.sum(got * unit_ref[:, cols], axis=1, keepdims=True)
        for dy in range(2):
            for dc in range(2):
                far, near, rest = out_refs[3 * dc : 3 * dc + 3]
                for n, (color, dx) in enumerate(((0, 1), (0, 0), (1, 0), (1, 1))):
                    cols = pl.ds(group_offset(rep, color, dx, dc, width), width)
                    value = mixed[dy, :, cols] - along[dy] * unit_ref[:, cols]
                    value = value.astype(jnp.bfloat16)
                    rest[dz, dy, :, n * width : (n + 1) * width] = value[split:]
                    leaves, kind = (dy, 2 + dx) if color else (dx, dy)
                    (far if leaves else near)[kind, dz] = value[:split]
        return carry

    lax.fori_loop(0, n_z, combine, 0)


def moe_partial(picks, weights, unit_dir, own, pieces, w_gate, w_up, w_down):
    n_seq, _, tok_rows = picks.shape
    exp_dev, hid_dev, model_width = w_gate.shape
    width = model_width // 8
    vmem = pl.BlockSpec(memory_space=pltpu.VMEM)
    hbm = pl.BlockSpec(memory_space=pltpu.HBM)
    whole = pl.BlockSpec(memory_space=pl.ANY)
    n_pieces = len(pieces)
    pieces = [pltpu.with_memory_space_constraint(piece, pltpu.VMEM) for piece in pieces]
    picks, weights, own = [
        pltpu.with_memory_space_constraint(value, pltpu.HBM) for value in (picks, weights, own)
    ]
    n_z, split = n_seq // 2, most_rows(tok_rows)
    most = (4, n_z, split, width)
    rest = (n_z, 2, tok_rows - split, 4 * width)
    outs = [
        jax.ShapeDtypeStruct(shape, jnp.bfloat16) for _ in range(2) for shape in (most, most, rest)
    ]
    return pl.pallas_call(
        functools.partial(moe_kernel, n_pieces),
        out_shape=outs,
        in_specs=[hbm, hbm, vmem, hbm] + [whole] * n_pieces + [hbm] * 3,
        out_specs=[vmem] * len(outs),
        scratch_shapes=[
            pltpu.VMEM(picks.shape, jnp.bfloat16),
            pltpu.VMEM(weights.shape, jnp.bfloat16),
            pltpu.VMEM((RING, 2 * hid_dev, model_width), jnp.bfloat16),
            pltpu.VMEM(w_down.shape, jnp.bfloat16),
            pltpu.VMEM((n_seq, tok_rows, model_width), jnp.bfloat16),
            pltpu.VMEM((n_seq, exp_dev, SLOTS, model_width), jnp.bfloat16),
            pltpu.VMEM((exp_dev, n_seq * SLOTS, hid_dev), jnp.bfloat16),
            pltpu.VMEM((2, tok_rows, model_width), jnp.float32),
            pltpu.SemaphoreType.DMA((2,)),
            pltpu.SemaphoreType.DMA((n_seq,)),
            pltpu.SemaphoreType.DMA((2, RING)),
            pltpu.SemaphoreType.DMA((exp_dev,)),
        ],
        compiler_params=pltpu.CompilerParams(vmem_limit_bytes=42 * 1024 * 1024),
        cost_estimate=pl.CostEstimate(
            flops=6 * n_seq * SLOTS * exp_dev * hid_dev * model_width,
            bytes_accessed=6 * exp_dev * hid_dev * model_width + 4 * n_seq * own.size,
            transcendentals=0,
        ),
    )(picks, weights, unit_dir, own, *pieces, w_gate, w_up, w_down)


def swap(value, axis, distance):
    size = lax.axis_size(axis)
    return lax.ppermute(value, axis, [(i, i ^ distance) for i in range(size)])


def added(*terms):
    return sum(term.astype(jnp.float32) for term in terms).astype(jnp.bfloat16)


def gathered(tokens, norm_gain, refusal_dir, expert_ids, gate_probs, w_gate, w_up, w_down):
    tok_rows, model_width = tokens.shape
    n_z = lax.axis_size("seq") // 2
    others = range(1, n_z)
    exp_dev = w_gate.shape[0]
    width = model_width // 8

    normed, second, first, to_y, unit_dir, base, meta = norm_and_base(
        tokens, norm_gain, refusal_dir, expert_ids, gate_probs
    )
    second = [swap(second, "seq", 2 * d) for d in others]
    from_y = swap(to_y, "seq", 1)
    first, second, from_y = lax.optimization_barrier((first, jnp.stack(second), from_y))
    first = jnp.stack([swap(first, "seq", 2 * d) for d in others])
    x_two = swap(second[:, :tok_rows], "rep", 2)
    y_one = swap(second, "seq", 1)
    y_two = swap(first, "seq", 1)
    x_one = swap(first, "rep", 2)
    to_y, to_core, to_core_y = lax.optimization_barrier((x_two, second, from_y))
    y_three = swap(to_y, "seq", 1)
    early = [swap(piece, "rep", 1) for piece in (to_core, first, to_core_y)]
    below = [meta, from_y[tok_rows:, :tok_rows]]
    for d in range(n_z - 1):
        below += [second[d, tok_rows:, :tok_rows], y_one[d, tok_rows:, :tok_rows]]
    picks, weights = route(jnp.stack(below), exp_dev)
    to_x, picks, weights = lax.optimization_barrier((y_two, picks, weights))
    x_three = swap(to_x, "rep", 2)
    last = [x_two, y_one, x_one, y_two, y_three, x_three]
    pieces = [second, first, from_y, *last, *early, *[swap(piece, "rep", 1) for piece in last]]

    sums = moe_partial(picks, weights, unit_dir, normed, pieces, w_gate, w_up, w_down)
    return (base + summed_up(sums[:3], sums[3:], width)).astype(jnp.bfloat16)


def summed_up(kept, sent, width):
    n_z = kept[0].shape[1]
    others = range(1, n_z)
    far, near, rest = zip(kept, [swap(piece, "rep", 1) for piece in sent])

    to_x, to_y, rest_kept = lax.optimization_barrier(
        (added(*[term[:2] for term in far]), added(*[term[2:] for term in far]), rest[0])
    )
    by_x, by_y = swap(to_x, "rep", 2), swap(to_y, "seq", 1)
    rest = added(rest_kept, rest[1])
    by_z = [swap(rest[d], "seq", 2 * d) for d in others]
    to_y, to_x, by_z[-1] = lax.optimization_barrier(
        (
            added(*[term[1] for term in near], by_x[1]),
            added(*[term[3] for term in near], by_y[1]),
            by_z[-1],
        )
    )
    first_far, second_far = swap(to_y, "seq", 1), swap(to_x, "rep", 2)
    first = added(*[term[0] for term in near], by_x[0], first_far)
    second = added(*[term[2] for term in near], by_y[0], second_far)
    blocks = jnp.concatenate([first, second], axis=2)
    most = [blocks[0]] + [swap(blocks[d], "seq", 2 * d) for d in others]
    most[-1], rest = lax.optimization_barrier((most[-1], rest[0]))
    rest = added(rest, *by_z)
    rest = added(rest[0], swap(rest[1], "seq", 1))
    far = jnp.concatenate([rest[:, :width], rest[:, 3 * width :]], axis=1)
    rest = [rest[:, width : 3 * width], swap(far, "rep", 2)]
    return jnp.concatenate(
        [sum(term.astype(jnp.float32) for term in terms) for terms in (most, rest)], axis=0
    )


def exchanged(tokens, norm_gain, refusal_dir, expert_ids, gate_probs, w_gate, w_up, w_down):
    tok_rows, model_width = tokens.shape
    top_k = expert_ids.shape[1]
    n_seq = lax.axis_size("seq")
    n_rep = lax.axis_size("rep")
    exp_dev = w_gate.shape[0]
    experts = exp_dev * n_seq
    slot_count = tok_rows * top_k
    part_width = model_width // n_rep
    tokens_f32 = tokens.astype(jnp.float32)
    inv_rms = lax.rsqrt(jnp.mean(tokens_f32 * tokens_f32, axis=1, keepdims=True) + 1e-06)
    normed = (tokens_f32 * inv_rms * norm_gain).astype(jnp.bfloat16)
    flat_ids = expert_ids.reshape(slot_count)
    onehot = (flat_ids[:, None] == jnp.arange(experts, dtype=jnp.int32)[None, :]).astype(jnp.int32)
    slot_rank = jnp.sum(jnp.cumsum(onehot, axis=0) * onehot, axis=1) - 1
    target = flat_ids * CAP + slot_rank
    repeated = jnp.broadcast_to(normed[:, None, :], (tok_rows, top_k, model_width)).reshape(
        slot_count, model_width
    )
    sendbuf = jnp.zeros((experts * CAP, model_width), jnp.bfloat16).at[target].set(repeated)
    sendbuf = sendbuf.reshape(n_seq, exp_dev, CAP, model_width)
    arrived = lax.all_to_all(sendbuf, "seq", split_axis=0, concat_axis=0, tiled=True)
    gate_val = jnp.einsum("secd,efd->secf", arrived, w_gate, preferred_element_type=jnp.float32)
    up_val = jnp.einsum("secd,efd->secf", arrived, w_up, preferred_element_type=jnp.float32)
    hidden = (jax.nn.silu(gate_val) * up_val).astype(jnp.bfloat16)
    pieces = jnp.einsum(
        "secf,efd->secd", hidden, w_down, preferred_element_type=jnp.float32
    ).astype(jnp.bfloat16)
    probs_flat = gate_probs.reshape(slot_count)[:, None]
    returned = lax.all_to_all(pieces, "seq", split_axis=0, concat_axis=0, tiled=True)
    returned = returned.reshape(experts * CAP, model_width)
    weighted = returned[target].astype(jnp.float32) * probs_flat
    moe_part = jnp.sum(weighted.reshape(tok_rows, top_k, model_width), axis=1)
    summed = lax.psum_scatter(
        moe_part.astype(jnp.bfloat16), "rep", scatter_dimension=1, tiled=True
    ).astype(jnp.float32)
    unit_dir = refusal_dir / jnp.sqrt(jnp.sum(refusal_dir * refusal_dir) + 1e-06)
    rep_offset = lax.axis_index("rep") * part_width
    unit_slice = lax.dynamic_slice_in_dim(unit_dir, rep_offset, part_width, 0)
    own_tokens = lax.dynamic_slice_in_dim(tokens_f32, rep_offset, part_width, 1)
    residual = own_tokens + summed
    along_dir = lax.psum(jnp.sum(residual * unit_slice, axis=1), "rep")
    return (residual - along_dir[:, None] * unit_slice).astype(jnp.bfloat16)


def local(tokens, norm_gain, refusal_dir, expert_ids, gate_probs, w_gate, w_up, w_down):
    plan = gathered if w_gate.shape[0] * CAP >= tokens.shape[0] else exchanged
    return plan(tokens, norm_gain, refusal_dir, expert_ids, gate_probs, w_gate, w_up, w_down)


def solution(mesh):
    placed = (
        P("seq", None),
        P(),
        P(),
        P("seq", None),
        P("seq", None),
        P("seq", "rep", None),
        P("seq", "rep", None),
        P("seq", "rep", None),
    )
    return jax.shard_map(
        local, mesh=mesh, in_specs=placed, out_specs=P("seq", "rep"), check_vma=False
    )
```

```python
import functools

import jax
import jax.numpy as jnp
from jax import lax
from jax.experimental import pallas as pl
from jax.experimental.pallas import tpu as pltpu
from jax.sharding import PartitionSpec as P

CAP = 12
SLOTS = 16
RING = 6


def contract(lhs, rhs, lhs_dim, rhs_dim):
    return lax.dot_general(
        lhs, rhs, (((lhs_dim,), (rhs_dim,)), ((), ())), preferred_element_type=jnp.float32
    )


def group_offset(rep, color, dx, dc, width):
    return pl.multiple_of((rep ^ (2 * dx + dc)) * 2 * width + color * width, width)


def token_pieces(n_z):
    near = [2 * d for d in range(1, n_z)]
    far = [2 * d + 1 for d in range(1, n_z)]
    return [
        [(j, [(1, 0)]) for j in near],
        [(j, [(0, 0)]) for j in near],
        [(1, [(0, 0), (1, 0), (1, 1)])],
        [(j, [(1, 1)]) for j in near],
        [(j, [(1, 0)]) for j in far],
        [(j, [(0, 1)]) for j in (*near, 1)],
        [(j, [(0, 0)]) for j in far],
        [(j, [(1, 1)]) for j in far],
        [(j, [(0, 1)]) for j in far],
    ]


def norm_kernel(
    tokens_ref, gain_ref, refusal_ref, ids_ref, probs_ref,
    normed_ref, second_ref, first_ref, to_y_ref, unit_ref, base_ref, meta_ref,
):
    tok_rows, model_width = tokens_ref.shape
    width = model_width // 8
    rep = lax.axis_index("rep")
    toks = tokens_ref[...].astype(jnp.float32)
    refusal = refusal_ref[...]
    unit = refusal / jnp.sqrt(jnp.sum(refusal * refusal, axis=1, keepdims=True) + 1e-06)
    unit_ref[...] = unit
    inv_rms = lax.rsqrt(jnp.mean(toks * toks, axis=1, keepdims=True) + 1e-06)
    normed_ref[...] = (toks * inv_rms * gain_ref[...]).astype(jnp.bfloat16)
    own = pl.ds(group_offset(rep, 0, 0, 0, width), 2 * width)
    other = pl.ds(group_offset(rep, 1, 1, 0, width), width)
    first_ref[...] = normed_ref[:, pl.ds(group_offset(rep, 0, 0, 0, width), width)]
    second_ref[:tok_rows] = normed_ref[:, pl.ds(group_offset(rep, 1, 0, 0, width), width)]
    to_y_ref[:tok_rows, : 2 * width] = normed_ref[:, own]
    to_y_ref[:tok_rows, 2 * width :] = normed_ref[:, other]
    meta = jnp.concatenate([ids_ref[...].astype(jnp.float32), probs_ref[...]], axis=0)
    meta = meta.astype(jnp.bfloat16)
    meta_ref[...] = meta
    for ref in (second_ref, to_y_ref):
        ref[tok_rows:] = jnp.zeros((meta.shape[0], ref.shape[1]), jnp.bfloat16)
        ref[tok_rows:, :tok_rows] = meta
    along = jnp.sum(toks * unit, axis=1, keepdims=True)
    base_ref[...] = tokens_ref[:, own].astype(jnp.float32) - along * unit_ref[:, own]


def norm_and_base(tokens, norm_gain, refusal_dir, expert_ids, gate_probs):
    tok_rows, model_width = tokens.shape
    width = model_width // 8
    meta_rows = 2 * expert_ids.shape[1]
    vmem = pl.BlockSpec(memory_space=pltpu.VMEM)
    return pl.pallas_call(
        norm_kernel,
        out_shape=[
            jax.ShapeDtypeStruct((tok_rows, model_width), jnp.bfloat16),
            jax.ShapeDtypeStruct((tok_rows + meta_rows, width), jnp.bfloat16),
            jax.ShapeDtypeStruct((tok_rows, width), jnp.bfloat16),
            jax.ShapeDtypeStruct((tok_rows + meta_rows, 3 * width), jnp.bfloat16),
            jax.ShapeDtypeStruct((1, model_width), jnp.float32),
            jax.ShapeDtypeStruct((tok_rows, 2 * width), jnp.float32),
            jax.ShapeDtypeStruct((meta_rows, tok_rows), jnp.bfloat16),
        ],
        in_specs=[vmem] * 5,
        out_specs=[vmem] * 7,
    )(tokens, norm_gain[None, :], refusal_dir[None, :], expert_ids.T, gate_probs.T)


def route_kernel(exp_dev, meta_ref, picks_ref, weights_ref):
    n_seq, twice_k, tok_rows = meta_ref.shape
    top_k = twice_k // 2
    first = (lax.axis_index("seq") * exp_dev).astype(jnp.float32)
    exp_iota = lax.broadcasted_iota(jnp.int32, (exp_dev, tok_rows), 0).astype(jnp.float32) + first
    earlier = (
        lax.broadcasted_iota(jnp.int32, (tok_rows, tok_rows), 0)
        < lax.broadcasted_iota(jnp.int32, (tok_rows, tok_rows), 1)
    ).astype(jnp.float32).astype(jnp.bfloat16)
    slot_iota = lax.broadcasted_iota(jnp.int32, (exp_dev, SLOTS, tok_rows), 1).astype(jnp.float32)

    def place_pair(pair, carry):
        blocks = (2 * pair, 2 * pair + 1)
        hits, probs = [], []
        for j in blocks:
            meta = meta_ref[j].astype(jnp.float32)
            hit = jnp.zeros((exp_dev, tok_rows), jnp.float32)
            prob = jnp.zeros((exp_dev, tok_rows), jnp.float32)
            for k in range(top_k):
                same = meta[k : k + 1, :] == exp_iota
                hit = jnp.where(same, 1.0, hit)
                prob = jnp.where(same, meta[top_k + k : top_k + k + 1, :], prob)
            hits.append(hit)
            probs.append(prob)
        ranks = contract(jnp.concatenate(hits, axis=0).astype(jnp.bfloat16), earlier, 1, 0)
        for n, j in enumerate(blocks):
            rank = ranks[n * exp_dev : (n + 1) * exp_dev]
            slot = jnp.where(hits[n] > 0.0, rank, -1.0)
            here = slot[:, None, :] == slot_iota
            onehot = jnp.where(here, 1.0, 0.0).reshape(exp_dev * SLOTS, tok_rows)
            weight = jnp.where(here, probs[n][:, None, :], 0.0)
            weight = weight.reshape(exp_dev * SLOTS, tok_rows)
            picks_ref[j] = onehot.astype(jnp.bfloat16)
            weights_ref[j] = weight.T.astype(jnp.bfloat16)
        return carry

    lax.fori_loop(0, n_seq // 2, place_pair, 0)


def route(meta, exp_dev):
    n_seq, _, tok_rows = meta.shape
    vmem = pl.BlockSpec(memory_space=pltpu.VMEM)
    return pl.pallas_call(
        functools.partial(route_kernel, exp_dev),
        out_shape=[
            jax.ShapeDtypeStruct((n_seq, exp_dev * SLOTS, tok_rows), jnp.bfloat16),
            jax.ShapeDtypeStruct((n_seq, tok_rows, exp_dev * SLOTS), jnp.bfloat16),
        ],
        in_specs=[vmem],
        out_specs=[vmem] * 2,
        cost_estimate=pl.CostEstimate(
            flops=4_000_000_000, bytes_accessed=8 * n_seq * exp_dev * SLOTS * tok_rows,
            transcendentals=0,
        ),
    )(meta)


def most_rows(tok_rows):
    return tok_rows // 128 * 112


def moe_kernel(n_pieces, *refs):
    picks_hbm, weights_hbm, unit_ref, own_hbm = refs[:4]
    pieces_in = refs[4 : 4 + n_pieces]
    w_gate_hbm, w_up_hbm, w_down_hbm = refs[4 + n_pieces : 7 + n_pieces]
    out_refs = refs[7 + n_pieces : 13 + n_pieces]
    (picks, weights, w_in, w_down, toks, rows, hidden, mixed, table_sems, tok_sems, in_sems,
     down_sems) = refs[13 + n_pieces :]
    n_seq, tok_rows, model_width = toks.shape
    n_z = n_seq // 2
    exp_dev, hid_dev, _ = w_gate_hbm.shape
    width = model_width // 8
    slots_src = exp_dev * SLOTS
    rep = lax.axis_index("rep")
    split = most_rows(tok_rows)
    tables = [
        pltpu.make_async_copy(picks_hbm, picks, table_sems.at[0]),
        pltpu.make_async_copy(weights_hbm, weights, table_sems.at[1]),
    ]
    tables[0].start()

    pltpu.make_async_copy(own_hbm, toks.at[0], tok_sems.at[0]).start()
    kinds = token_pieces(n_z)
    for i, piece in enumerate(pieces_in):
        dc = i // len(kinds)
        for at, (j, runs) in enumerate(kinds[i % len(kinds)]):
            block = piece if len(piece.shape) == 2 else piece.at[at]
            for n, (color, dx) in enumerate(runs):
                cols = pl.ds(group_offset(rep, color, dx, dc, width), width)
                pltpu.make_async_copy(
                    block.at[pl.ds(0, tok_rows), pl.ds(n * width, width)],
                    toks.at[j, :, cols],
                    tok_sems.at[j],
                ).start()

    def in_copies(e):
        at = lax.rem(e, RING)
        return [
            pltpu.make_async_copy(
                src.at[e], w_in.at[at, pl.ds(i * hid_dev, hid_dev)], in_sems.at[i, at]
            )
            for i, src in enumerate((w_gate_hbm, w_up_hbm))
        ]

    def down_copy(e):
        return pltpu.make_async_copy(w_down_hbm.at[e], w_down.at[e], down_sems.at[e])

    for e in range(min(RING, exp_dev)):
        for copy in in_copies(e):
            copy.start()
    tables[1].start()
    quarters = [slice(2 * q * width, 2 * (q + 1) * width) for q in range(4)]
    tables[0].wait()

    def pick(pair, carry):
        for j in (2 * pair, 2 * pair + 1):
            pltpu.make_async_copy(toks.at[j], toks.at[j], tok_sems.at[j]).wait()
        for j in (2 * pair, 2 * pair + 1):
            onehot = picks[j]
            for cols in quarters:
                got = contract(onehot, toks[j, :, cols], 1, 0).astype(jnp.bfloat16)
                rows[j, :, :, cols] = got.reshape(exp_dev, SLOTS, 2 * width)
        return carry

    lax.fori_loop(0, n_z, pick, 0)

    def widen(pair, carry):
        experts = (2 * pair, 2 * pair + 1)
        for e in experts:
            for copy in in_copies(e):
                copy.wait()
        both = [
            contract(
                w_in[lax.rem(e, RING)], rows[:, e].reshape(n_seq * SLOTS, model_width), 1, 1
            )
            for e in experts
        ]
        for e, value in zip(experts, both):
            gate_val, up_val = value[:hid_dev], value[hid_dev:]
            act = gate_val / (1.0 + jnp.exp(-gate_val)) * up_val
            hidden[e] = act.T.astype(jnp.bfloat16)
        for e in experts:
            down_copy(e).start()

            @pl.when(e + RING < exp_dev)
            def _():
                for copy in in_copies(e + RING):
                    copy.start()

        return carry

    lax.fori_loop(0, exp_dev // 2, widen, 0)

    def narrow(pair, carry):
        experts = (2 * pair, 2 * pair + 1)
        for e in experts:
            down_copy(e).wait()
        for e in experts:
            for cols in quarters:
                piece = contract(hidden[e], w_down[e, :, cols], 1, 0).astype(jnp.bfloat16)
                rows[:, e, :, cols] = piece.reshape(n_seq, SLOTS, 2 * width)
        return carry

    lax.fori_loop(0, exp_dev // 2, narrow, 0)
    tables[1].wait()

    def combine(dz, carry):
        along = [jnp.zeros((tok_rows, 1), jnp.float32)] * 2
        for dy in range(2):
            j = 2 * dz + dy
            weight = weights[j]
            for cols in quarters:
                got = contract(weight, rows[j, :, :, cols].reshape(slots_src, 2 * width), 1, 0)
                mixed[dy, :, cols] = got
                along[dy] += jnp.sum(got * unit_ref[:, cols], axis=1, keepdims=True)
        for dy in range(2):
            for dc in range(2):
                far, near, rest = out_refs[3 * dc : 3 * dc + 3]
                for n, (color, dx) in enumerate(((0, 1), (0, 0), (1, 0), (1, 1))):
                    cols = pl.ds(group_offset(rep, color, dx, dc, width), width)
                    value = mixed[dy, :, cols] - along[dy] * unit_ref[:, cols]
                    value = value.astype(jnp.bfloat16)
                    rest[dz, dy, :, n * width : (n + 1) * width] = value[split:]
                    leaves, kind = (dy, 2 + dx) if color else (dx, dy)
                    (far if leaves else near)[kind, dz] = value[:split]
        return carry

    lax.fori_loop(0, n_z, combine, 0)


def moe_partial(picks, weights, unit_dir, own, pieces, w_gate, w_up, w_down):
    n_seq, _, tok_rows = picks.shape
    exp_dev, hid_dev, model_width = w_gate.shape
    width = model_width // 8
    vmem = pl.BlockSpec(memory_space=pltpu.VMEM)
    hbm = pl.BlockSpec(memory_space=pltpu.HBM)
    whole = pl.BlockSpec(memory_space=pl.ANY)
    n_pieces = len(pieces)
    pieces = [pltpu.with_memory_space_constraint(piece, pltpu.VMEM) for piece in pieces]
    picks, weights, own = [
        pltpu.with_memory_space_constraint(value, pltpu.HBM) for value in (picks, weights, own)
    ]
    n_z, split = n_seq // 2, most_rows(tok_rows)
    most = (4, n_z, split, width)
    rest = (n_z, 2, tok_rows - split, 4 * width)
    outs = [
        jax.ShapeDtypeStruct(shape, jnp.bfloat16) for _ in range(2) for shape in (most, most, rest)
    ]
    return pl.pallas_call(
        functools.partial(moe_kernel, n_pieces),
        out_shape=outs,
        in_specs=[hbm, hbm, vmem, hbm] + [whole] * n_pieces + [hbm] * 3,
        out_specs=[vmem] * len(outs),
        scratch_shapes=[
            pltpu.VMEM(picks.shape, jnp.bfloat16),
            pltpu.VMEM(weights.shape, jnp.bfloat16),
            pltpu.VMEM((RING, 2 * hid_dev, model_width), jnp.bfloat16),
            pltpu.VMEM(w_down.shape, jnp.bfloat16),
            pltpu.VMEM((n_seq, tok_rows, model_width), jnp.bfloat16),
            pltpu.VMEM((n_seq, exp_dev, SLOTS, model_width), jnp.bfloat16),
            pltpu.VMEM((exp_dev, n_seq * SLOTS, hid_dev), jnp.bfloat16),
            pltpu.VMEM((2, tok_rows, model_width), jnp.float32),
            pltpu.SemaphoreType.DMA((2,)),
            pltpu.SemaphoreType.DMA((n_seq,)),
            pltpu.SemaphoreType.DMA((2, RING)),
            pltpu.SemaphoreType.DMA((exp_dev,)),
        ],
        compiler_params=pltpu.CompilerParams(vmem_limit_bytes=42 * 1024 * 1024),
        cost_estimate=pl.CostEstimate(
            flops=6 * n_seq * SLOTS * exp_dev * hid_dev * model_width,
            bytes_accessed=6 * exp_dev * hid_dev * model_width + 4 * n_seq * own.size,
            transcendentals=0,
        ),
    )(picks, weights, unit_dir, own, *pieces, w_gate, w_up, w_down)


def swap(value, axis, distance):
    size = lax.axis_size(axis)
    return lax.ppermute(value, axis, [(i, i ^ distance) for i in range(size)])


def added(*terms):
    return sum(term.astype(jnp.float32) for term in terms).astype(jnp.bfloat16)


def gathered(tokens, norm_gain, refusal_dir, expert_ids, gate_probs, w_gate, w_up, w_down):
    tok_rows, model_width = tokens.shape
    n_z = lax.axis_size("seq") // 2
    others = range(1, n_z)
    exp_dev = w_gate.shape[0]
    width = model_width // 8

    normed, second, first, to_y, unit_dir, base, meta = norm_and_base(
        tokens, norm_gain, refusal_dir, expert_ids, gate_probs
    )
    second = [swap(second, "seq", 2 * d) for d in others]
    from_y = swap(to_y, "seq", 1)
    first, second, from_y = lax.optimization_barrier((first, jnp.stack(second), from_y))
    first = jnp.stack([swap(first, "seq", 2 * d) for d in others])
    x_two = swap(second[:, :tok_rows], "rep", 2)
    y_one = swap(second, "seq", 1)
    y_two = swap(first, "seq", 1)
    x_one = swap(jnp.concatenate([first, from_y[None, :tok_rows, :width]]), "rep", 2)
    to_y, to_core, to_core_y = lax.optimization_barrier((x_two, second, from_y))
    y_three = swap(to_y, "seq", 1)
    early = [swap(piece, "rep", 1) for piece in (to_core, first, to_core_y)]
    below = [meta, from_y[tok_rows:, :tok_rows]]
    for d in range(n_z - 1):
        below += [second[d, tok_rows:, :tok_rows], y_one[d, tok_rows:, :tok_rows]]
    picks, weights = route(jnp.stack(below), exp_dev)
    to_x, picks, weights = lax.optimization_barrier((y_two, picks, weights))
    x_three = swap(to_x, "rep", 2)
    last = [x_two, y_one, x_one, y_two, y_three, x_three]
    pieces = [second, first, from_y, *last, *early, *[swap(piece, "rep", 1) for piece in last]]

    sums = moe_partial(picks, weights, unit_dir, normed, pieces, w_gate, w_up, w_down)
    return (base + summed_up(sums[:3], sums[3:], width)).astype(jnp.bfloat16)


def summed_up(kept, sent, width):
    n_z = kept[0].shape[1]
    others = range(1, n_z)
    far, near, rest = zip(kept, [swap(piece, "rep", 1) for piece in sent])

    to_x, to_y, rest_kept = lax.optimization_barrier(
        (added(*[term[:2] for term in far]), added(*[term[2:] for term in far]), rest[0])
    )
    by_x, by_y = swap(to_x, "rep", 2), swap(to_y, "seq", 1)
    rest = added(rest_kept, rest[1])
    by_z = [swap(rest[d], "seq", 2 * d) for d in others]
    to_y, to_x, *by_z = lax.optimization_barrier(
        (
            added(*[term[1] for term in near], by_x[1]),
            added(*[term[3] for term in near], by_y[1]),
            *by_z,
        )
    )
    first_far, second_far = swap(to_y, "seq", 1), swap(to_x, "rep", 2)
    first = added(*[term[0] for term in near], by_x[0], first_far)
    second = added(*[term[2] for term in near], by_y[0], second_far)
    blocks = jnp.concatenate([first, second], axis=2)
    most = [blocks[0]] + [swap(blocks[d], "seq", 2 * d) for d in others]
    rest = added(rest[0], *by_z)
    rest = added(rest[0], swap(rest[1], "seq", 1))
    far = jnp.concatenate([rest[:, :width], rest[:, 3 * width :]], axis=1)
    rest = [rest[:, width : 3 * width], swap(far, "rep", 2)]
    return jnp.concatenate(
        [sum(term.astype(jnp.float32) for term in terms) for terms in (most, rest)], axis=0
    )


def exchanged(tokens, norm_gain, refusal_dir, expert_ids, gate_probs, w_gate, w_up, w_down):
    tok_rows, model_width = tokens.shape
    top_k = expert_ids.shape[1]
    n_seq = lax.axis_size("seq")
    n_rep = lax.axis_size("rep")
    exp_dev = w_gate.shape[0]
    experts = exp_dev * n_seq
    slot_count = tok_rows * top_k
    part_width = model_width // n_rep
    tokens_f32 = tokens.astype(jnp.float32)
    inv_rms = lax.rsqrt(jnp.mean(tokens_f32 * tokens_f32, axis=1, keepdims=True) + 1e-06)
    normed = (tokens_f32 * inv_rms * norm_gain).astype(jnp.bfloat16)
    flat_ids = expert_ids.reshape(slot_count)
    onehot = (flat_ids[:, None] == jnp.arange(experts, dtype=jnp.int32)[None, :]).astype(jnp.int32)
    slot_rank = jnp.sum(jnp.cumsum(onehot, axis=0) * onehot, axis=1) - 1
    target = flat_ids * CAP + slot_rank
    repeated = jnp.broadcast_to(normed[:, None, :], (tok_rows, top_k, model_width)).reshape(
        slot_count, model_width
    )
    sendbuf = jnp.zeros((experts * CAP, model_width), jnp.bfloat16).at[target].set(repeated)
    sendbuf = sendbuf.reshape(n_seq, exp_dev, CAP, model_width)
    arrived = lax.all_to_all(sendbuf, "seq", split_axis=0, concat_axis=0, tiled=True)
    gate_val = jnp.einsum("secd,efd->secf", arrived, w_gate, preferred_element_type=jnp.float32)
    up_val = jnp.einsum("secd,efd->secf", arrived, w_up, preferred_element_type=jnp.float32)
    hidden = (jax.nn.silu(gate_val) * up_val).astype(jnp.bfloat16)
    pieces = jnp.einsum(
        "secf,efd->secd", hidden, w_down, preferred_element_type=jnp.float32
    ).astype(jnp.bfloat16)
    probs_flat = gate_probs.reshape(slot_count)[:, None]
    returned = lax.all_to_all(pieces, "seq", split_axis=0, concat_axis=0, tiled=True)
    returned = returned.reshape(experts * CAP, model_width)
    weighted = returned[target].astype(jnp.float32) * probs_flat
    moe_part = jnp.sum(weighted.reshape(tok_rows, top_k, model_width), axis=1)
    summed = lax.psum_scatter(
        moe_part.astype(jnp.bfloat16), "rep", scatter_dimension=1, tiled=True
    ).astype(jnp.float32)
    unit_dir = refusal_dir / jnp.sqrt(jnp.sum(refusal_dir * refusal_dir) + 1e-06)
    rep_offset = lax.axis_index("rep") * part_width
    unit_slice = lax.dynamic_slice_in_dim(unit_dir, rep_offset, part_width, 0)
    own_tokens = lax.dynamic_slice_in_dim(tokens_f32, rep_offset, part_width, 1)
    residual = own_tokens + summed
    along_dir = lax.psum(jnp.sum(residual * unit_slice, axis=1), "rep")
    return (residual - along_dir[:, None] * unit_slice).astype(jnp.bfloat16)


def local(tokens, norm_gain, refusal_dir, expert_ids, gate_probs, w_gate, w_up, w_down):
    plan = gathered if w_gate.shape[0] * CAP >= tokens.shape[0] else exchanged
    return plan(tokens, norm_gain, refusal_dir, expert_ids, gate_probs, w_gate, w_up, w_down)


def solution(mesh):
    placed = (
        P("seq", None),
        P(),
        P(),
        P("seq", None),
        P("seq", None),
        P("seq", "rep", None),
        P("seq", "rep", None),
        P("seq", "rep", None),
    )
    return jax.shard_map(
        local, mesh=mesh, in_specs=placed, out_specs=P("seq", "rep"), check_vma=False
    )
```

```python
import functools

import jax
import jax.numpy as jnp
from jax import lax
from jax.experimental import pallas as pl
from jax.experimental.pallas import tpu as pltpu
from jax.sharding import PartitionSpec as P

CAP = 12
SLOTS = 16
RING = 8


def contract(lhs, rhs, lhs_dim, rhs_dim):
    return lax.dot_general(
        lhs, rhs, (((lhs_dim,), (rhs_dim,)), ((), ())), preferred_element_type=jnp.float32
    )


def group_offset(rep, color, dx, dc, width):
    return pl.multiple_of((rep ^ (2 * dx + dc)) * 2 * width + color * width, width)


def token_pieces(n_z):
    near = [2 * d for d in range(1, n_z)]
    far = [2 * d + 1 for d in range(1, n_z)]
    return [
        [(j, [(1, 0)]) for j in near],
        [(j, [(0, 0)]) for j in near],
        [(1, [(0, 0), (1, 0), (1, 1)])],
        [(j, [(1, 1)]) for j in near],
        [(j, [(1, 0)]) for j in far],
        [(j, [(0, 1)]) for j in (*near, 1)],
        [(j, [(0, 0)]) for j in far],
        [(j, [(1, 1)]) for j in far],
        [(j, [(0, 1)]) for j in far],
    ]


def norm_kernel(
    tokens_ref, gain_ref, refusal_ref, ids_ref, probs_ref,
    normed_ref, second_ref, first_ref, to_y_ref, unit_ref, base_ref, meta_ref,
):
    tok_rows, model_width = tokens_ref.shape
    width = model_width // 8
    rep = lax.axis_index("rep")
    toks = tokens_ref[...].astype(jnp.float32)
    refusal = refusal_ref[...]
    unit = refusal / jnp.sqrt(jnp.sum(refusal * refusal, axis=1, keepdims=True) + 1e-06)
    unit_ref[...] = unit
    inv_rms = lax.rsqrt(jnp.mean(toks * toks, axis=1, keepdims=True) + 1e-06)
    normed_ref[...] = (toks * inv_rms * gain_ref[...]).astype(jnp.bfloat16)
    own = pl.ds(group_offset(rep, 0, 0, 0, width), 2 * width)
    other = pl.ds(group_offset(rep, 1, 1, 0, width), width)
    first_ref[...] = normed_ref[:, pl.ds(group_offset(rep, 0, 0, 0, width), width)]
    second_ref[:tok_rows] = normed_ref[:, pl.ds(group_offset(rep, 1, 0, 0, width), width)]
    to_y_ref[:tok_rows, : 2 * width] = normed_ref[:, own]
    to_y_ref[:tok_rows, 2 * width :] = normed_ref[:, other]
    meta = jnp.concatenate([ids_ref[...].astype(jnp.float32), probs_ref[...]], axis=0)
    meta = meta.astype(jnp.bfloat16)
    meta_ref[...] = meta
    for ref in (second_ref, to_y_ref):
        ref[tok_rows:] = jnp.zeros((meta.shape[0], ref.shape[1]), jnp.bfloat16)
        ref[tok_rows:, :tok_rows] = meta
    along = jnp.sum(toks * unit, axis=1, keepdims=True)
    base_ref[...] = tokens_ref[:, own].astype(jnp.float32) - along * unit_ref[:, own]


def norm_and_base(tokens, norm_gain, refusal_dir, expert_ids, gate_probs):
    tok_rows, model_width = tokens.shape
    width = model_width // 8
    meta_rows = 2 * expert_ids.shape[1]
    vmem = pl.BlockSpec(memory_space=pltpu.VMEM)
    return pl.pallas_call(
        norm_kernel,
        out_shape=[
            jax.ShapeDtypeStruct((tok_rows, model_width), jnp.bfloat16),
            jax.ShapeDtypeStruct((tok_rows + meta_rows, width), jnp.bfloat16),
            jax.ShapeDtypeStruct((tok_rows, width), jnp.bfloat16),
            jax.ShapeDtypeStruct((tok_rows + meta_rows, 3 * width), jnp.bfloat16),
            jax.ShapeDtypeStruct((1, model_width), jnp.float32),
            jax.ShapeDtypeStruct((tok_rows, 2 * width), jnp.float32),
            jax.ShapeDtypeStruct((meta_rows, tok_rows), jnp.bfloat16),
        ],
        in_specs=[vmem] * 5,
        out_specs=[vmem] * 7,
    )(tokens, norm_gain[None, :], refusal_dir[None, :], expert_ids.T, gate_probs.T)


def route_kernel(exp_dev, meta_ref, picks_ref, weights_ref):
    n_seq, twice_k, tok_rows = meta_ref.shape
    top_k = twice_k // 2
    first = (lax.axis_index("seq") * exp_dev).astype(jnp.float32)
    exp_iota = lax.broadcasted_iota(jnp.int32, (exp_dev, tok_rows), 0).astype(jnp.float32) + first
    earlier = (
        lax.broadcasted_iota(jnp.int32, (tok_rows, tok_rows), 0)
        < lax.broadcasted_iota(jnp.int32, (tok_rows, tok_rows), 1)
    ).astype(jnp.float32).astype(jnp.bfloat16)
    slot_iota = lax.broadcasted_iota(jnp.int32, (exp_dev, SLOTS, tok_rows), 1).astype(jnp.float32)

    def place_pair(pair, carry):
        blocks = (2 * pair, 2 * pair + 1)
        hits, probs = [], []
        for j in blocks:
            meta = meta_ref[j].astype(jnp.float32)
            hit = jnp.zeros((exp_dev, tok_rows), jnp.float32)
            prob = jnp.zeros((exp_dev, tok_rows), jnp.float32)
            for k in range(top_k):
                same = meta[k : k + 1, :] == exp_iota
                hit = jnp.where(same, 1.0, hit)
                prob = jnp.where(same, meta[top_k + k : top_k + k + 1, :], prob)
            hits.append(hit)
            probs.append(prob)
        ranks = contract(jnp.concatenate(hits, axis=0).astype(jnp.bfloat16), earlier, 1, 0)
        for n, j in enumerate(blocks):
            rank = ranks[n * exp_dev : (n + 1) * exp_dev]
            slot = jnp.where(hits[n] > 0.0, rank, -1.0)
            here = slot[:, None, :] == slot_iota
            onehot = jnp.where(here, 1.0, 0.0).reshape(exp_dev * SLOTS, tok_rows)
            weight = jnp.where(here, probs[n][:, None, :], 0.0)
            weight = weight.reshape(exp_dev * SLOTS, tok_rows)
            picks_ref[j] = onehot.astype(jnp.bfloat16)
            weights_ref[j] = weight.T.astype(jnp.bfloat16)
        return carry

    lax.fori_loop(0, n_seq // 2, place_pair, 0)


def route(meta, exp_dev):
    n_seq, _, tok_rows = meta.shape
    vmem = pl.BlockSpec(memory_space=pltpu.VMEM)
    return pl.pallas_call(
        functools.partial(route_kernel, exp_dev),
        out_shape=[
            jax.ShapeDtypeStruct((n_seq, exp_dev * SLOTS, tok_rows), jnp.bfloat16),
            jax.ShapeDtypeStruct((n_seq, tok_rows, exp_dev * SLOTS), jnp.bfloat16),
        ],
        in_specs=[vmem],
        out_specs=[vmem] * 2,
        cost_estimate=pl.CostEstimate(
            flops=4_000_000_000, bytes_accessed=8 * n_seq * exp_dev * SLOTS * tok_rows,
            transcendentals=0,
        ),
    )(meta)


def most_rows(tok_rows):
    return tok_rows // 128 * 112


def moe_kernel(n_pieces, *refs):
    picks_hbm, weights_hbm, unit_ref, own_hbm = refs[:4]
    pieces_in = refs[4 : 4 + n_pieces]
    w_gate_hbm, w_up_hbm, w_down_hbm = refs[4 + n_pieces : 7 + n_pieces]
    out_refs = refs[7 + n_pieces : 13 + n_pieces]
    (picks, weights, w_in, w_down, toks, rows, hidden, mixed, table_sems, tok_sems, in_sems,
     down_sems) = refs[13 + n_pieces :]
    n_seq, tok_rows, model_width = toks.shape
    n_z = n_seq // 2
    exp_dev, hid_dev, _ = w_gate_hbm.shape
    width = model_width // 8
    slots_src = exp_dev * SLOTS
    rep = lax.axis_index("rep")
    split = most_rows(tok_rows)
    def in_copies(e):
        at = lax.rem(e, RING)
        return [
            pltpu.make_async_copy(
                src.at[e], w_in.at[at, pl.ds(i * hid_dev, hid_dev)], in_sems.at[i, at]
            )
            for i, src in enumerate((w_gate_hbm, w_up_hbm))
        ]

    def down_copy(e):
        return pltpu.make_async_copy(w_down_hbm.at[e], w_down.at[e], down_sems.at[e])

    def start_down(e, carry):
        down_copy(e).start()
        return carry

    for e in range(min(RING, exp_dev)):
        for copy in in_copies(e):
            copy.start()
    tables = [
        pltpu.make_async_copy(picks_hbm, picks, table_sems.at[0]),
        pltpu.make_async_copy(weights_hbm, weights, table_sems.at[1]),
    ]
    tables[0].start()

    pltpu.make_async_copy(own_hbm, toks.at[0], tok_sems.at[0]).start()
    kinds = token_pieces(n_z)
    for i, piece in enumerate(pieces_in):
        dc = i // len(kinds)
        for at, (j, runs) in enumerate(kinds[i % len(kinds)]):
            block = piece if len(piece.shape) == 2 else piece.at[at]
            for n, (color, dx) in enumerate(runs):
                cols = pl.ds(group_offset(rep, color, dx, dc, width), width)
                pltpu.make_async_copy(
                    block.at[pl.ds(0, tok_rows), pl.ds(n * width, width)],
                    toks.at[j, :, cols],
                    tok_sems.at[j],
                ).start()

    tables[1].start()
    quarters = [slice(2 * q * width, 2 * (q + 1) * width) for q in range(4)]
    tables[0].wait()

    def pick(pair, carry):
        for j in (2 * pair, 2 * pair + 1):
            pltpu.make_async_copy(toks.at[j], toks.at[j], tok_sems.at[j]).wait()
        for j in (2 * pair, 2 * pair + 1):
            onehot = picks[j]
            for cols in quarters:
                got = contract(onehot, toks[j, :, cols], 1, 0).astype(jnp.bfloat16)
                rows[j, :, :, cols] = got.reshape(exp_dev, SLOTS, 2 * width)
        return carry

    lax.fori_loop(0, n_z, pick, 0)

    def widen(pair, carry):
        experts = (2 * pair, 2 * pair + 1)
        for e in experts:
            for copy in in_copies(e):
                copy.wait()
        both = [
            contract(
                w_in[lax.rem(e, RING)], rows[:, e].reshape(n_seq * SLOTS, model_width), 1, 1
            )
            for e in experts
        ]
        for e, value in zip(experts, both):
            gate_val, up_val = value[:hid_dev], value[hid_dev:]
            act = gate_val / (1.0 + jnp.exp(-gate_val)) * up_val
            hidden[e] = act.T.astype(jnp.bfloat16)
        for e in experts:

            @pl.when(e + RING < exp_dev)
            def _():
                for copy in in_copies(e + RING):
                    copy.start()

        @pl.when(pair == max((exp_dev - RING) // 2 - 1, 0))
        def _():
            lax.fori_loop(0, exp_dev, start_down, 0)

        return carry

    lax.fori_loop(0, exp_dev // 2, widen, 0)

    def narrow(pair, carry):
        experts = (2 * pair, 2 * pair + 1)
        for e in experts:
            down_copy(e).wait()
        for e in experts:
            for cols in quarters:
                piece = contract(hidden[e], w_down[e, :, cols], 1, 0).astype(jnp.bfloat16)
                rows[:, e, :, cols] = piece.reshape(n_seq, SLOTS, 2 * width)
        return carry

    lax.fori_loop(0, exp_dev // 2, narrow, 0)
    tables[1].wait()

    def combine(dz, carry):
        along = [jnp.zeros((tok_rows, 1), jnp.float32)] * 2
        for dy in range(2):
            j = 2 * dz + dy
            weight = weights[j]
            for cols in quarters:
                got = contract(weight, rows[j, :, :, cols].reshape(slots_src, 2 * width), 1, 0)
                mixed[dy, :, cols] = got
                along[dy] += jnp.sum(got * unit_ref[:, cols], axis=1, keepdims=True)
        for dy in range(2):
            for dc in range(2):
                far, near, rest = out_refs[3 * dc : 3 * dc + 3]
                for n, (color, dx) in enumerate(((0, 1), (0, 0), (1, 0), (1, 1))):
                    cols = pl.ds(group_offset(rep, color, dx, dc, width), width)
                    value = mixed[dy, :, cols] - along[dy] * unit_ref[:, cols]
                    value = value.astype(jnp.bfloat16)
                    rest[dz, dy, :, n * width : (n + 1) * width] = value[split:]
                    leaves, kind = (dy, 2 + dx) if color else (dx, dy)
                    (far if leaves else near)[kind, dz] = value[:split]
        return carry

    lax.fori_loop(0, n_z, combine, 0)


def moe_partial(picks, weights, unit_dir, own, pieces, w_gate, w_up, w_down):
    n_seq, _, tok_rows = picks.shape
    exp_dev, hid_dev, model_width = w_gate.shape
    width = model_width // 8
    vmem = pl.BlockSpec(memory_space=pltpu.VMEM)
    hbm = pl.BlockSpec(memory_space=pltpu.HBM)
    whole = pl.BlockSpec(memory_space=pl.ANY)
    n_pieces = len(pieces)
    pieces = [pltpu.with_memory_space_constraint(piece, pltpu.VMEM) for piece in pieces]
    picks, weights, own = [
        pltpu.with_memory_space_constraint(value, pltpu.HBM) for value in (picks, weights, own)
    ]
    n_z, split = n_seq // 2, most_rows(tok_rows)
    most = (4, n_z, split, width)
    rest = (n_z, 2, tok_rows - split, 4 * width)
    outs = [
        jax.ShapeDtypeStruct(shape, jnp.bfloat16) for _ in range(2) for shape in (most, most, rest)
    ]
    return pl.pallas_call(
        functools.partial(moe_kernel, n_pieces),
        out_shape=outs,
        in_specs=[hbm, hbm, vmem, hbm] + [whole] * n_pieces + [hbm] * 3,
        out_specs=[vmem] * len(outs),
        scratch_shapes=[
            pltpu.VMEM(picks.shape, jnp.bfloat16),
            pltpu.VMEM(weights.shape, jnp.bfloat16),
            pltpu.VMEM((RING, 2 * hid_dev, model_width), jnp.bfloat16),
            pltpu.VMEM(w_down.shape, jnp.bfloat16),
            pltpu.VMEM((n_seq, tok_rows, model_width), jnp.bfloat16),
            pltpu.VMEM((n_seq, exp_dev, SLOTS, model_width), jnp.bfloat16),
            pltpu.VMEM((exp_dev, n_seq * SLOTS, hid_dev), jnp.bfloat16),
            pltpu.VMEM((2, tok_rows, model_width), jnp.float32),
            pltpu.SemaphoreType.DMA((2,)),
            pltpu.SemaphoreType.DMA((n_seq,)),
            pltpu.SemaphoreType.DMA((2, RING)),
            pltpu.SemaphoreType.DMA((exp_dev,)),
        ],
        compiler_params=pltpu.CompilerParams(vmem_limit_bytes=46 * 1024 * 1024),
        cost_estimate=pl.CostEstimate(
            flops=6 * n_seq * SLOTS * exp_dev * hid_dev * model_width,
            bytes_accessed=6 * exp_dev * hid_dev * model_width + 4 * n_seq * own.size,
            transcendentals=0,
        ),
    )(picks, weights, unit_dir, own, *pieces, w_gate, w_up, w_down)


def swap(value, axis, distance):
    size = lax.axis_size(axis)
    return lax.ppermute(value, axis, [(i, i ^ distance) for i in range(size)])


def added(*terms):
    return sum(term.astype(jnp.float32) for term in terms).astype(jnp.bfloat16)


def gathered(tokens, norm_gain, refusal_dir, expert_ids, gate_probs, w_gate, w_up, w_down):
    tok_rows, model_width = tokens.shape
    n_z = lax.axis_size("seq") // 2
    others = range(1, n_z)
    exp_dev = w_gate.shape[0]
    width = model_width // 8

    normed, second, first, to_y, unit_dir, base, meta = norm_and_base(
        tokens, norm_gain, refusal_dir, expert_ids, gate_probs
    )
    second = [swap(second, "seq", 2 * d) for d in others]
    from_y = swap(to_y, "seq", 1)
    first, second, from_y = lax.optimization_barrier((first, jnp.stack(second), from_y))
    first = jnp.stack([swap(first, "seq", 2 * d) for d in others])
    x_two = swap(second[:, :tok_rows], "rep", 2)
    y_one = swap(second, "seq", 1)
    y_two = swap(first, "seq", 1)
    x_one = swap(jnp.concatenate([first, from_y[None, :tok_rows, :width]]), "rep", 2)
    to_y, to_core = lax.optimization_barrier((x_two, second))
    y_three = swap(to_y, "seq", 1)
    below = [meta, from_y[tok_rows:, :tok_rows]]
    for d in range(n_z - 1):
        below += [second[d, tok_rows:, :tok_rows], y_one[d, tok_rows:, :tok_rows]]
    picks, weights = route(jnp.stack(below), exp_dev)
    to_core_y, picks, weights = lax.optimization_barrier((from_y, picks, weights))
    early = [swap(piece, "rep", 1) for piece in (to_core, first, to_core_y)]
    x_three = swap(y_two, "rep", 2)
    last = [x_two, y_one, x_one, y_two, y_three, x_three]
    pieces = [second, first, from_y, *last, *early, *[swap(piece, "rep", 1) for piece in last]]

    sums = moe_partial(picks, weights, unit_dir, normed, pieces, w_gate, w_up, w_down)
    return (base + summed_up(sums[:3], sums[3:], width)).astype(jnp.bfloat16)


def summed_up(kept, sent, width):
    n_z = kept[0].shape[1]
    others = range(1, n_z)
    far, near, rest = zip(kept, [swap(piece, "rep", 1) for piece in sent])

    to_x, to_y, rest_kept = lax.optimization_barrier(
        (added(*[term[:2] for term in far]), added(*[term[2:] for term in far]), rest[0])
    )
    by_x, by_y = swap(to_x, "rep", 2), swap(to_y, "seq", 1)
    rest = added(rest_kept, rest[1])
    by_z = [swap(rest[d], "seq", 2 * d) for d in others]
    to_y, to_x, *by_z = lax.optimization_barrier(
        (
            added(*[term[1] for term in near], by_x[1]),
            added(*[term[3] for term in near], by_y[1]),
            *by_z,
        )
    )
    first_far, second_far = swap(to_y, "seq", 1), swap(to_x, "rep", 2)
    first = added(*[term[0] for term in near], by_x[0], first_far)
    second = added(*[term[2] for term in near], by_y[0], second_far)
    blocks = jnp.concatenate([first, second], axis=2)
    most = [swap(blocks[d], "seq", 2 * d) for d in reversed(others)] + [blocks[0]]
    rest = added(rest[0], *by_z)
    rest = added(rest[0], swap(rest[1], "seq", 1))
    far = jnp.concatenate([rest[:, :width], rest[:, 3 * width :]], axis=1)
    rest = [rest[:, width : 3 * width], swap(far, "rep", 2)]
    return jnp.concatenate(
        [sum(term.astype(jnp.float32) for term in terms) for terms in (most, rest)], axis=0
    )


def exchanged(tokens, norm_gain, refusal_dir, expert_ids, gate_probs, w_gate, w_up, w_down):
    tok_rows, model_width = tokens.shape
    top_k = expert_ids.shape[1]
    n_seq = lax.axis_size("seq")
    n_rep = lax.axis_size("rep")
    exp_dev = w_gate.shape[0]
    experts = exp_dev * n_seq
    slot_count = tok_rows * top_k
    part_width = model_width // n_rep
    tokens_f32 = tokens.astype(jnp.float32)
    inv_rms = lax.rsqrt(jnp.mean(tokens_f32 * tokens_f32, axis=1, keepdims=True) + 1e-06)
    normed = (tokens_f32 * inv_rms * norm_gain).astype(jnp.bfloat16)
    flat_ids = expert_ids.reshape(slot_count)
    onehot = (flat_ids[:, None] == jnp.arange(experts, dtype=jnp.int32)[None, :]).astype(jnp.int32)
    slot_rank = jnp.sum(jnp.cumsum(onehot, axis=0) * onehot, axis=1) - 1
    target = flat_ids * CAP + slot_rank
    repeated = jnp.broadcast_to(normed[:, None, :], (tok_rows, top_k, model_width)).reshape(
        slot_count, model_width
    )
    sendbuf = jnp.zeros((experts * CAP, model_width), jnp.bfloat16).at[target].set(repeated)
    sendbuf = sendbuf.reshape(n_seq, exp_dev, CAP, model_width)
    arrived = lax.all_to_all(sendbuf, "seq", split_axis=0, concat_axis=0, tiled=True)
    gate_val = jnp.einsum("secd,efd->secf", arrived, w_gate, preferred_element_type=jnp.float32)
    up_val = jnp.einsum("secd,efd->secf", arrived, w_up, preferred_element_type=jnp.float32)
    hidden = (jax.nn.silu(gate_val) * up_val).astype(jnp.bfloat16)
    pieces = jnp.einsum(
        "secf,efd->secd", hidden, w_down, preferred_element_type=jnp.float32
    ).astype(jnp.bfloat16)
    probs_flat = gate_probs.reshape(slot_count)[:, None]
    returned = lax.all_to_all(pieces, "seq", split_axis=0, concat_axis=0, tiled=True)
    returned = returned.reshape(experts * CAP, model_width)
    weighted = returned[target].astype(jnp.float32) * probs_flat
    moe_part = jnp.sum(weighted.reshape(tok_rows, top_k, model_width), axis=1)
    summed = lax.psum_scatter(
        moe_part.astype(jnp.bfloat16), "rep", scatter_dimension=1, tiled=True
    ).astype(jnp.float32)
    unit_dir = refusal_dir / jnp.sqrt(jnp.sum(refusal_dir * refusal_dir) + 1e-06)
    rep_offset = lax.axis_index("rep") * part_width
    unit_slice = lax.dynamic_slice_in_dim(unit_dir, rep_offset, part_width, 0)
    own_tokens = lax.dynamic_slice_in_dim(tokens_f32, rep_offset, part_width, 1)
    residual = own_tokens + summed
    along_dir = lax.psum(jnp.sum(residual * unit_slice, axis=1), "rep")
    return (residual - along_dir[:, None] * unit_slice).astype(jnp.bfloat16)


def local(tokens, norm_gain, refusal_dir, expert_ids, gate_probs, w_gate, w_up, w_down):
    plan = gathered if w_gate.shape[0] * CAP >= tokens.shape[0] else exchanged
    return plan(tokens, norm_gain, refusal_dir, expert_ids, gate_probs, w_gate, w_up, w_down)


def solution(mesh):
    placed = (
        P("seq", None),
        P(),
        P(),
        P("seq", None),
        P("seq", None),
        P("seq", "rep", None),
        P("seq", "rep", None),
        P("seq", "rep", None),
    )
    return jax.shard_map(
        local, mesh=mesh, in_specs=placed, out_specs=P("seq", "rep"), check_vma=False
    )
```

```python
import functools

import jax
import jax.numpy as jnp
from jax import lax
from jax.experimental import pallas as pl
from jax.experimental.pallas import tpu as pltpu
from jax.sharding import PartitionSpec as P

CAP = 12
SLOTS = 16
RING = 6


def contract(lhs, rhs, lhs_dim, rhs_dim):
    return lax.dot_general(
        lhs, rhs, (((lhs_dim,), (rhs_dim,)), ((), ())), preferred_element_type=jnp.float32
    )


def group_offset(rep, color, dx, dc, width):
    return pl.multiple_of((rep ^ (2 * dx + dc)) * 2 * width + color * width, width)


def token_pieces(n_z):
    near = [2 * d for d in range(1, n_z)]
    far = [2 * d + 1 for d in range(1, n_z)]
    return [
        [(j, [(1, 0)]) for j in near],
        [(j, [(0, 0)]) for j in near],
        [(1, [(0, 0), (1, 0), (1, 1)])],
        [(j, [(1, 1)]) for j in near],
        [(j, [(1, 0)]) for j in far],
        [(j, [(0, 1)]) for j in (*near, 1)],
        [(j, [(0, 0)]) for j in far],
        [(j, [(1, 1)]) for j in far],
        [(j, [(0, 1)]) for j in far],
    ]


def norm_kernel(
    tokens_ref, gain_ref, refusal_ref, ids_ref, probs_ref,
    normed_ref, second_ref, first_ref, to_y_ref, rest_ref, unit_ref, base_ref, meta_ref,
):
    tok_rows, model_width = tokens_ref.shape
    width = model_width // 8
    rep = lax.axis_index("rep")
    toks = tokens_ref[...].astype(jnp.float32)
    refusal = refusal_ref[...]
    unit = refusal / jnp.sqrt(jnp.sum(refusal * refusal, axis=1, keepdims=True) + 1e-06)
    unit_ref[...] = unit
    inv_rms = lax.rsqrt(jnp.mean(toks * toks, axis=1, keepdims=True) + 1e-06)
    normed_ref[...] = (toks * inv_rms * gain_ref[...]).astype(jnp.bfloat16)
    own = pl.ds(group_offset(rep, 0, 0, 0, width), 2 * width)
    other = pl.ds(group_offset(rep, 0, 1, 0, width), 2 * width)
    split = most_rows(tok_rows)
    first_ref[...] = normed_ref[:split, pl.ds(group_offset(rep, 0, 0, 0, width), width)]
    second_ref[:split] = normed_ref[:split, pl.ds(group_offset(rep, 1, 0, 0, width), width)]
    to_y_ref[:split, : 2 * width] = normed_ref[:split, own]
    to_y_ref[:split, 2 * width :] = normed_ref[
        :split, pl.ds(group_offset(rep, 1, 1, 0, width), width)
    ]
    rest_ref[:, : 2 * width] = normed_ref[split:, own]
    rest_ref[:, 2 * width :] = normed_ref[split:, other]
    meta = jnp.concatenate([ids_ref[...].astype(jnp.float32), probs_ref[...]], axis=0)
    meta = meta.astype(jnp.bfloat16)
    meta_ref[...] = meta
    for ref in (second_ref, to_y_ref):
        ref[split:] = jnp.zeros((meta.shape[0], ref.shape[1]), jnp.bfloat16)
        ref[split:, :tok_rows] = meta
    along = jnp.sum(toks * unit, axis=1, keepdims=True)
    base_ref[...] = tokens_ref[:, own].astype(jnp.float32) - along * unit_ref[:, own]


def norm_and_base(tokens, norm_gain, refusal_dir, expert_ids, gate_probs):
    tok_rows, model_width = tokens.shape
    width = model_width // 8
    meta_rows = 2 * expert_ids.shape[1]
    split = most_rows(tok_rows)
    vmem = pl.BlockSpec(memory_space=pltpu.VMEM)
    return pl.pallas_call(
        norm_kernel,
        out_shape=[
            jax.ShapeDtypeStruct((tok_rows, model_width), jnp.bfloat16),
            jax.ShapeDtypeStruct((split + meta_rows, width), jnp.bfloat16),
            jax.ShapeDtypeStruct((split, width), jnp.bfloat16),
            jax.ShapeDtypeStruct((split + meta_rows, 3 * width), jnp.bfloat16),
            jax.ShapeDtypeStruct((tok_rows - split, 4 * width), jnp.bfloat16),
            jax.ShapeDtypeStruct((1, model_width), jnp.float32),
            jax.ShapeDtypeStruct((tok_rows, 2 * width), jnp.float32),
            jax.ShapeDtypeStruct((meta_rows, tok_rows), jnp.bfloat16),
        ],
        in_specs=[vmem] * 5,
        out_specs=[vmem] * 8,
    )(tokens, norm_gain[None, :], refusal_dir[None, :], expert_ids.T, gate_probs.T)


def route_kernel(exp_dev, meta_ref, picks_ref, weights_ref):
    n_seq, twice_k, tok_rows = meta_ref.shape
    top_k = twice_k // 2
    first = (lax.axis_index("seq") * exp_dev).astype(jnp.float32)
    exp_iota = lax.broadcasted_iota(jnp.int32, (exp_dev, tok_rows), 0).astype(jnp.float32) + first
    earlier = (
        lax.broadcasted_iota(jnp.int32, (tok_rows, tok_rows), 0)
        < lax.broadcasted_iota(jnp.int32, (tok_rows, tok_rows), 1)
    ).astype(jnp.float32).astype(jnp.bfloat16)
    slot_iota = lax.broadcasted_iota(jnp.int32, (exp_dev, SLOTS, tok_rows), 1).astype(jnp.float32)

    def place_pair(pair, carry):
        blocks = (2 * pair, 2 * pair + 1)
        hits, probs = [], []
        for j in blocks:
            meta = meta_ref[j].astype(jnp.float32)
            hit = jnp.zeros((exp_dev, tok_rows), jnp.float32)
            prob = jnp.zeros((exp_dev, tok_rows), jnp.float32)
            for k in range(top_k):
                same = meta[k : k + 1, :] == exp_iota
                hit = jnp.where(same, 1.0, hit)
                prob = jnp.where(same, meta[top_k + k : top_k + k + 1, :], prob)
            hits.append(hit)
            probs.append(prob)
        ranks = contract(jnp.concatenate(hits, axis=0).astype(jnp.bfloat16), earlier, 1, 0)
        for n, j in enumerate(blocks):
            rank = ranks[n * exp_dev : (n + 1) * exp_dev]
            slot = jnp.where(hits[n] > 0.0, rank, -1.0)
            here = slot[:, None, :] == slot_iota
            onehot = jnp.where(here, 1.0, 0.0).reshape(exp_dev * SLOTS, tok_rows)
            weight = jnp.where(here, probs[n][:, None, :], 0.0)
            weight = weight.reshape(exp_dev * SLOTS, tok_rows)
            picks_ref[j] = onehot.astype(jnp.bfloat16)
            weights_ref[j] = weight.T.astype(jnp.bfloat16)
        return carry

    lax.fori_loop(0, n_seq // 2, place_pair, 0)


def route(meta, exp_dev):
    n_seq, _, tok_rows = meta.shape
    vmem = pl.BlockSpec(memory_space=pltpu.VMEM)
    return pl.pallas_call(
        functools.partial(route_kernel, exp_dev),
        out_shape=[
            jax.ShapeDtypeStruct((n_seq, exp_dev * SLOTS, tok_rows), jnp.bfloat16),
            jax.ShapeDtypeStruct((n_seq, tok_rows, exp_dev * SLOTS), jnp.bfloat16),
        ],
        in_specs=[vmem],
        out_specs=[vmem] * 2,
        cost_estimate=pl.CostEstimate(
            flops=4_000_000_000, bytes_accessed=8 * n_seq * exp_dev * SLOTS * tok_rows,
            transcendentals=0,
        ),
    )(meta)


def most_rows(tok_rows):
    return tok_rows // 4 * 3


def moe_kernel(n_pieces, *refs):
    picks_hbm, weights_hbm, unit_ref, own_hbm = refs[:4]
    pieces_in = refs[4 : 4 + n_pieces]
    rest_in = refs[4 + n_pieces : 6 + n_pieces]
    w_gate_hbm, w_up_hbm, w_down_hbm = refs[6 + n_pieces : 9 + n_pieces]
    out_refs = refs[9 + n_pieces : 15 + n_pieces]
    (picks, weights, w_in, w_down, toks, rows, hidden, mixed, table_sems, tok_sems, in_sems,
     down_sems) = refs[15 + n_pieces :]
    n_seq, tok_rows, model_width = toks.shape
    n_z = n_seq // 2
    exp_dev, hid_dev, _ = w_gate_hbm.shape
    width = model_width // 8
    slots_src = exp_dev * SLOTS
    rep, z = lax.axis_index("rep"), lax.axis_index("seq") // 2
    split = most_rows(tok_rows)
    def in_copies(e):
        at = lax.rem(e, RING)
        return [
            pltpu.make_async_copy(
                src.at[e], w_in.at[at, pl.ds(i * hid_dev, hid_dev)], in_sems.at[i, at]
            )
            for i, src in enumerate((w_gate_hbm, w_up_hbm))
        ]

    def down_copy(e):
        return pltpu.make_async_copy(w_down_hbm.at[e], w_down.at[e], down_sems.at[e])

    for e in range(min(RING, exp_dev)):
        for copy in in_copies(e):
            copy.start()
    tables = [
        pltpu.make_async_copy(picks_hbm, picks, table_sems.at[0]),
        pltpu.make_async_copy(weights_hbm, weights, table_sems.at[1]),
    ]
    tables[0].start()

    pltpu.make_async_copy(own_hbm, toks.at[0], tok_sems.at[0]).start()
    kinds = token_pieces(n_z)
    for i, piece in enumerate(pieces_in):
        dc = i // len(kinds)
        for at, (j, runs) in enumerate(kinds[i % len(kinds)]):
            block = piece if len(piece.shape) == 2 else piece.at[at]
            for n, (color, dx) in enumerate(runs):
                cols = pl.ds(group_offset(rep, color, dx, dc, width), width)
                pltpu.make_async_copy(
                    block.at[pl.ds(0, split), pl.ds(n * width, width)],
                    toks.at[j, pl.ds(0, split), cols],
                    tok_sems.at[j],
                ).start()
    for at in range(n_z):
        for dy in range(2):
            j = 2 * (at ^ z) + dy

            @pl.when(j > 0)
            def _():
                for dc in range(2):
                    for dx in range(2):
                        cols = pl.ds(group_offset(rep, 0, dx, dc, width), 2 * width)
                        pltpu.make_async_copy(
                            rest_in[dc].at[at, dy, :, pl.ds(2 * dx * width, 2 * width)],
                            toks.at[j, pl.ds(split, tok_rows - split), cols],
                            tok_sems.at[j],
                        ).start()

    tables[1].start()
    quarters = [slice(2 * q * width, 2 * (q + 1) * width) for q in range(4)]
    tables[0].wait()

    def pick(pair, carry):
        for j in (2 * pair, 2 * pair + 1):
            pltpu.make_async_copy(toks.at[j], toks.at[j], tok_sems.at[j]).wait()
        for j in (2 * pair, 2 * pair + 1):
            onehot = picks[j]
            for cols in quarters:
                got = contract(onehot, toks[j, :, cols], 1, 0).astype(jnp.bfloat16)
                rows[j, :, :, cols] = got.reshape(exp_dev, SLOTS, 2 * width)
        return carry

    lax.fori_loop(0, n_z, pick, 0)

    def widen(pair, carry):
        experts = (2 * pair, 2 * pair + 1)
        for e in experts:
            for copy in in_copies(e):
                copy.wait()
        both = [
            contract(
                w_in[lax.rem(e, RING)], rows[:, e].reshape(n_seq * SLOTS, model_width), 1, 1
            )
            for e in experts
        ]
        for e, value in zip(experts, both):
            gate_val, up_val = value[:hid_dev], value[hid_dev:]
            act = gate_val / (1.0 + jnp.exp(-gate_val)) * up_val
            hidden[e] = act.T.astype(jnp.bfloat16)
        for e in experts:
            down_copy(e).start()

            @pl.when(e + RING < exp_dev)
            def _():
                for copy in in_copies(e + RING):
                    copy.start()

        return carry

    lax.fori_loop(0, exp_dev // 2, widen, 0)

    def narrow(pair, carry):
        experts = (2 * pair, 2 * pair + 1)
        for e in experts:
            down_copy(e).wait()
        for e in experts:
            for cols in quarters:
                piece = contract(hidden[e], w_down[e, :, cols], 1, 0).astype(jnp.bfloat16)
                rows[:, e, :, cols] = piece.reshape(n_seq, SLOTS, 2 * width)
        return carry

    lax.fori_loop(0, exp_dev // 2, narrow, 0)
    tables[1].wait()

    def combine(dz, carry):
        along = [jnp.zeros((tok_rows, 1), jnp.float32)] * 2
        for dy in range(2):
            j = 2 * dz + dy
            weight = weights[j]
            for cols in quarters:
                got = contract(weight, rows[j, :, :, cols].reshape(slots_src, 2 * width), 1, 0)
                mixed[dy, :, cols] = got
                along[dy] += jnp.sum(got * unit_ref[:, cols], axis=1, keepdims=True)
        for dy in range(2):
            for dc in range(2):
                far, near, rest = out_refs[3 * dc : 3 * dc + 3]
                for n, (color, dx) in enumerate(((0, 1), (0, 0), (1, 0), (1, 1))):
                    cols = pl.ds(group_offset(rep, color, dx, dc, width), width)
                    value = mixed[dy, :, cols] - along[dy] * unit_ref[:, cols]
                    value = value.astype(jnp.bfloat16)
                    rest[dz ^ z, dy, :, n * width : (n + 1) * width] = value[split:]
                    leaves, kind = (dy, 2 + dx) if color else (dx, dy)
                    (far if leaves else near)[kind, dz] = value[:split]
        return carry

    lax.fori_loop(0, n_z, combine, 0)


def moe_partial(picks, weights, unit_dir, own, pieces, rest, w_gate, w_up, w_down):
    n_seq, _, tok_rows = picks.shape
    exp_dev, hid_dev, model_width = w_gate.shape
    width = model_width // 8
    vmem = pl.BlockSpec(memory_space=pltpu.VMEM)
    hbm = pl.BlockSpec(memory_space=pltpu.HBM)
    whole = pl.BlockSpec(memory_space=pl.ANY)
    n_pieces = len(pieces)
    pieces = [pltpu.with_memory_space_constraint(piece, pltpu.VMEM) for piece in pieces]
    picks, weights, own = [
        pltpu.with_memory_space_constraint(value, pltpu.HBM) for value in (picks, weights, own)
    ]
    n_z, split = n_seq // 2, most_rows(tok_rows)
    most = (4, n_z, split, width)
    shapes = [most, most, (n_z, 2, tok_rows - split, 4 * width)]
    outs = [
        jax.ShapeDtypeStruct(shape, jnp.bfloat16) for _ in range(2) for shape in shapes
    ]
    return pl.pallas_call(
        functools.partial(moe_kernel, n_pieces),
        out_shape=outs,
        in_specs=[hbm, hbm, vmem, hbm] + [whole] * (n_pieces + 2) + [hbm] * 3,
        out_specs=[vmem] * len(outs),
        scratch_shapes=[
            pltpu.VMEM(picks.shape, jnp.bfloat16),
            pltpu.VMEM(weights.shape, jnp.bfloat16),
            pltpu.VMEM((RING, 2 * hid_dev, model_width), jnp.bfloat16),
            pltpu.VMEM(w_down.shape, jnp.bfloat16),
            pltpu.VMEM((n_seq, tok_rows, model_width), jnp.bfloat16),
            pltpu.VMEM((n_seq, exp_dev, SLOTS, model_width), jnp.bfloat16),
            pltpu.VMEM((exp_dev, n_seq * SLOTS, hid_dev), jnp.bfloat16),
            pltpu.VMEM((2, tok_rows, model_width), jnp.float32),
            pltpu.SemaphoreType.DMA((2,)),
            pltpu.SemaphoreType.DMA((n_seq,)),
            pltpu.SemaphoreType.DMA((2, RING)),
            pltpu.SemaphoreType.DMA((exp_dev,)),
        ],
        compiler_params=pltpu.CompilerParams(vmem_limit_bytes=42 * 1024 * 1024),
        cost_estimate=pl.CostEstimate(
            flops=6 * n_seq * SLOTS * exp_dev * hid_dev * model_width,
            bytes_accessed=6 * exp_dev * hid_dev * model_width + 4 * n_seq * own.size,
            transcendentals=0,
        ),
    )(picks, weights, unit_dir, own, *pieces, *rest, w_gate, w_up, w_down)


def swap(value, axis, distance):
    size = lax.axis_size(axis)
    return lax.ppermute(value, axis, [(i, i ^ distance) for i in range(size)])


def added(*terms):
    return sum(term.astype(jnp.float32) for term in terms).astype(jnp.bfloat16)


def gathered(tokens, norm_gain, refusal_dir, expert_ids, gate_probs, w_gate, w_up, w_down):
    tok_rows, model_width = tokens.shape
    n_z = lax.axis_size("seq") // 2
    others = range(1, n_z)
    exp_dev = w_gate.shape[0]
    width = model_width // 8

    normed, second, first, to_y, rest, unit_dir, base, meta = norm_and_base(
        tokens, norm_gain, refusal_dir, expert_ids, gate_probs
    )
    split = most_rows(tok_rows)
    groups = z_groups(n_z)
    second = [swap(second, "seq", 2 * d) for d in others]
    from_y = swap(to_y, "seq", 1)
    rest = lax.all_gather(jnp.stack([rest, swap(rest, "seq", 1)]), "seq", axis_index_groups=groups)
    first, second, from_y = lax.optimization_barrier((first, jnp.stack(second), from_y))
    first = jnp.stack([swap(first, "seq", 2 * d) for d in others])
    x_two = swap(second[:, :split], "rep", 2)
    y_one = swap(second, "seq", 1)
    y_two = swap(first, "seq", 1)
    x_one = swap(jnp.concatenate([first, from_y[None, :split, :width]]), "rep", 2)
    to_y, to_core = lax.optimization_barrier((x_two, second))
    y_three = swap(to_y, "seq", 1)
    below = [meta, from_y[split:, :tok_rows]]
    for d in range(n_z - 1):
        below += [second[d, split:, :tok_rows], y_one[d, split:, :tok_rows]]
    picks, weights = route(jnp.stack(below), exp_dev)
    to_core_y, picks, weights = lax.optimization_barrier((from_y, picks, weights))
    early = [swap(piece, "rep", 1) for piece in (to_core, first, to_core_y)]
    x_three = swap(y_two, "rep", 2)
    last = [x_two, y_one, x_one, y_two, y_three, x_three]
    pieces = [second, first, from_y, *last, *early, *[swap(piece, "rep", 1) for piece in last]]

    rest = [rest, swap(rest, "rep", 1)]
    sums = moe_partial(picks, weights, unit_dir, normed, pieces, rest, w_gate, w_up, w_down)
    return (base + summed_up(sums[:3], sums[3:], width)).astype(jnp.bfloat16)


def z_groups(n_z):
    return [[2 * z + y for z in range(n_z)] for y in range(2)]


def summed_up(kept, sent, width):
    n_z = kept[0].shape[1]
    others = range(1, n_z)
    far, near, rest = zip(kept, [swap(piece, "rep", 1) for piece in sent])

    by_x = swap(added(*[term[:2] for term in far]), "rep", 2)
    by_y = swap(added(*[term[2:] for term in far]), "seq", 1)
    rest = lax.psum_scatter(added(*rest), "seq", axis_index_groups=z_groups(n_z))
    first_far = swap(added(*[term[1] for term in near], by_x[1]), "seq", 1)
    second_far = swap(added(*[term[3] for term in near], by_y[1]), "rep", 2)
    first_far, second_far, rest = lax.optimization_barrier((first_far, second_far, rest))
    first = added(*[term[0] for term in near], by_x[0], first_far)
    second = added(*[term[2] for term in near], by_y[0], second_far)
    blocks = jnp.concatenate([first, second], axis=2)
    most = [swap(blocks[d], "seq", 2 * d) for d in reversed(others)] + [blocks[0]]
    rest = added(rest[0], swap(rest[1], "seq", 1))
    most[0], rest = lax.optimization_barrier((most[0], rest))
    far = jnp.concatenate([rest[:, :width], rest[:, 3 * width :]], axis=1)
    rest = [rest[:, width : 3 * width], swap(far, "rep", 2)]
    return jnp.concatenate(
        [sum(term.astype(jnp.float32) for term in terms) for terms in (most, rest)], axis=0
    )


def exchanged(tokens, norm_gain, refusal_dir, expert_ids, gate_probs, w_gate, w_up, w_down):
    tok_rows, model_width = tokens.shape
    top_k = expert_ids.shape[1]
    n_seq = lax.axis_size("seq")
    n_rep = lax.axis_size("rep")
    exp_dev = w_gate.shape[0]
    experts = exp_dev * n_seq
    slot_count = tok_rows * top_k
    part_width = model_width // n_rep
    tokens_f32 = tokens.astype(jnp.float32)
    inv_rms = lax.rsqrt(jnp.mean(tokens_f32 * tokens_f32, axis=1, keepdims=True) + 1e-06)
    normed = (tokens_f32 * inv_rms * norm_gain).astype(jnp.bfloat16)
    flat_ids = expert_ids.reshape(slot_count)
    onehot = (flat_ids[:, None] == jnp.arange(experts, dtype=jnp.int32)[None, :]).astype(jnp.int32)
    slot_rank = jnp.sum(jnp.cumsum(onehot, axis=0) * onehot, axis=1) - 1
    target = flat_ids * CAP + slot_rank
    repeated = jnp.broadcast_to(normed[:, None, :], (tok_rows, top_k, model_width)).reshape(
        slot_count, model_width
    )
    sendbuf = jnp.zeros((experts * CAP, model_width), jnp.bfloat16).at[target].set(repeated)
    sendbuf = sendbuf.reshape(n_seq, exp_dev, CAP, model_width)
    arrived = lax.all_to_all(sendbuf, "seq", split_axis=0, concat_axis=0, tiled=True)
    gate_val = jnp.einsum("secd,efd->secf", arrived, w_gate, preferred_element_type=jnp.float32)
    up_val = jnp.einsum("secd,efd->secf", arrived, w_up, preferred_element_type=jnp.float32)
    hidden = (jax.nn.silu(gate_val) * up_val).astype(jnp.bfloat16)
    pieces = jnp.einsum(
        "secf,efd->secd", hidden, w_down, preferred_element_type=jnp.float32
    ).astype(jnp.bfloat16)
    probs_flat = gate_probs.reshape(slot_count)[:, None]
    returned = lax.all_to_all(pieces, "seq", split_axis=0, concat_axis=0, tiled=True)
    returned = returned.reshape(experts * CAP, model_width)
    weighted = returned[target].astype(jnp.float32) * probs_flat
    moe_part = jnp.sum(weighted.reshape(tok_rows, top_k, model_width), axis=1)
    summed = lax.psum_scatter(
        moe_part.astype(jnp.bfloat16), "rep", scatter_dimension=1, tiled=True
    ).astype(jnp.float32)
    unit_dir = refusal_dir / jnp.sqrt(jnp.sum(refusal_dir * refusal_dir) + 1e-06)
    rep_offset = lax.axis_index("rep") * part_width
    unit_slice = lax.dynamic_slice_in_dim(unit_dir, rep_offset, part_width, 0)
    own_tokens = lax.dynamic_slice_in_dim(tokens_f32, rep_offset, part_width, 1)
    residual = own_tokens + summed
    along_dir = lax.psum(jnp.sum(residual * unit_slice, axis=1), "rep")
    return (residual - along_dir[:, None] * unit_slice).astype(jnp.bfloat16)


def local(tokens, norm_gain, refusal_dir, expert_ids, gate_probs, w_gate, w_up, w_down):
    plan = gathered if w_gate.shape[0] * CAP >= tokens.shape[0] else exchanged
    return plan(tokens, norm_gain, refusal_dir, expert_ids, gate_probs, w_gate, w_up, w_down)


def solution(mesh):
    placed = (
        P("seq", None),
        P(),
        P(),
        P("seq", None),
        P("seq", None),
        P("seq", "rep", None),
        P("seq", "rep", None),
        P("seq", "rep", None),
    )
    return jax.shard_map(
        local, mesh=mesh, in_specs=placed, out_specs=P("seq", "rep"), check_vma=False
    )
```

```python
import functools

import jax
import jax.numpy as jnp
from jax import lax
from jax.experimental import pallas as pl
from jax.experimental.pallas import tpu as pltpu
from jax.sharding import PartitionSpec as P

CAP = 12
SLOTS = 16
RING = 6


def contract(lhs, rhs, lhs_dim, rhs_dim):
    return lax.dot_general(
        lhs, rhs, (((lhs_dim,), (rhs_dim,)), ((), ())), preferred_element_type=jnp.float32
    )


def group_offset(rep, color, dx, dc, width):
    return pl.multiple_of((rep ^ (2 * dx + dc)) * 2 * width + color * width, width)


def token_pieces(n_z):
    near, far = (0, 1, n_z - 1, 0), (0, 1, n_z - 1, 1)
    return [
        ([near], [(1, 0)]),
        ([near], [(0, 0)]),
        ([(0, 0, 1, 1)], [(0, 0), (1, 0), (1, 1)]),
        ([near], [(1, 1)]),
        ([far], [(1, 0)]),
        ([(0, 0, 1, 1), (1, 1, n_z - 1, 0)], [(0, 1)]),
        ([far], [(0, 0)]),
        ([far], [(1, 1)]),
        ([far], [(0, 1)]),
    ]


def norm_kernel(
    tokens_ref, gain_ref, refusal_ref, ids_ref, probs_ref,
    normed_ref, second_ref, first_ref, to_y_ref, unit_ref, base_ref, meta_ref,
):
    tok_rows, model_width = tokens_ref.shape
    width = model_width // 8
    rep = lax.axis_index("rep")
    toks = tokens_ref[...].astype(jnp.float32)
    refusal = refusal_ref[...]
    unit = refusal / jnp.sqrt(jnp.sum(refusal * refusal, axis=1, keepdims=True) + 1e-06)
    unit_ref[...] = unit
    inv_rms = lax.rsqrt(jnp.mean(toks * toks, axis=1, keepdims=True) + 1e-06)
    normed_ref[...] = (toks * inv_rms * gain_ref[...]).astype(jnp.bfloat16)
    own = pl.ds(group_offset(rep, 0, 0, 0, width), 2 * width)
    other = pl.ds(group_offset(rep, 1, 1, 0, width), width)
    first_ref[...] = normed_ref[:, pl.ds(group_offset(rep, 0, 0, 0, width), width)]
    second_ref[:tok_rows] = normed_ref[:, pl.ds(group_offset(rep, 1, 0, 0, width), width)]
    to_y_ref[:tok_rows, : 2 * width] = normed_ref[:, own]
    to_y_ref[:tok_rows, 2 * width :] = normed_ref[:, other]
    meta = jnp.concatenate([ids_ref[...].astype(jnp.float32), probs_ref[...]], axis=0)
    meta = meta.astype(jnp.bfloat16)
    meta_ref[...] = meta
    for ref in (second_ref, to_y_ref):
        ref[tok_rows:] = jnp.zeros((meta.shape[0], ref.shape[1]), jnp.bfloat16)
        ref[tok_rows:, :tok_rows] = meta
    along = jnp.sum(toks * unit, axis=1, keepdims=True)
    base_ref[...] = tokens_ref[:, own].astype(jnp.float32) - along * unit_ref[:, own]


def norm_and_base(tokens, norm_gain, refusal_dir, expert_ids, gate_probs):
    tok_rows, model_width = tokens.shape
    width = model_width // 8
    meta_rows = 2 * expert_ids.shape[1]
    vmem = pl.BlockSpec(memory_space=pltpu.VMEM)
    return pl.pallas_call(
        norm_kernel,
        out_shape=[
            jax.ShapeDtypeStruct((tok_rows, model_width), jnp.bfloat16),
            jax.ShapeDtypeStruct((tok_rows + meta_rows, width), jnp.bfloat16),
            jax.ShapeDtypeStruct((tok_rows, width), jnp.bfloat16),
            jax.ShapeDtypeStruct((tok_rows + meta_rows, 3 * width), jnp.bfloat16),
            jax.ShapeDtypeStruct((1, model_width), jnp.float32),
            jax.ShapeDtypeStruct((tok_rows, 2 * width), jnp.float32),
            jax.ShapeDtypeStruct((meta_rows, tok_rows), jnp.bfloat16),
        ],
        in_specs=[vmem] * 5,
        out_specs=[vmem] * 7,
    )(tokens, norm_gain[None, :], refusal_dir[None, :], expert_ids.T, gate_probs.T)


def route_kernel(exp_dev, meta_ref, picks_ref, weights_ref):
    n_seq, twice_k, tok_rows = meta_ref.shape
    top_k = twice_k // 2
    first = (lax.axis_index("seq") * exp_dev).astype(jnp.float32)
    exp_iota = lax.broadcasted_iota(jnp.int32, (exp_dev, tok_rows), 0).astype(jnp.float32) + first
    earlier = (
        lax.broadcasted_iota(jnp.int32, (tok_rows, tok_rows), 0)
        < lax.broadcasted_iota(jnp.int32, (tok_rows, tok_rows), 1)
    ).astype(jnp.float32).astype(jnp.bfloat16)
    slot_iota = lax.broadcasted_iota(jnp.int32, (exp_dev, SLOTS, tok_rows), 1).astype(jnp.float32)

    def place_pair(pair, carry):
        blocks = (2 * pair, 2 * pair + 1)
        hits, probs = [], []
        for j in blocks:
            meta = meta_ref[j].astype(jnp.float32)
            hit = jnp.zeros((exp_dev, tok_rows), jnp.float32)
            prob = jnp.zeros((exp_dev, tok_rows), jnp.float32)
            for k in range(top_k):
                same = meta[k : k + 1, :] == exp_iota
                hit = jnp.where(same, 1.0, hit)
                prob = jnp.where(same, meta[top_k + k : top_k + k + 1, :], prob)
            hits.append(hit)
            probs.append(prob)
        ranks = contract(jnp.concatenate(hits, axis=0).astype(jnp.bfloat16), earlier, 1, 0)
        for n, j in enumerate(blocks):
            rank = ranks[n * exp_dev : (n + 1) * exp_dev]
            slot = jnp.where(hits[n] > 0.0, rank, -1.0)
            here = slot[:, None, :] == slot_iota
            onehot = jnp.where(here, 1.0, 0.0).reshape(exp_dev * SLOTS, tok_rows)
            weight = jnp.where(here, probs[n][:, None, :], 0.0)
            weight = weight.reshape(exp_dev * SLOTS, tok_rows)
            picks_ref[j] = onehot.astype(jnp.bfloat16)
            weights_ref[j] = weight.T.astype(jnp.bfloat16)
        return carry

    lax.fori_loop(0, n_seq // 2, place_pair, 0)


def route(meta, exp_dev):
    n_seq, _, tok_rows = meta.shape
    vmem = pl.BlockSpec(memory_space=pltpu.VMEM)
    return pl.pallas_call(
        functools.partial(route_kernel, exp_dev),
        out_shape=[
            jax.ShapeDtypeStruct((n_seq, exp_dev * SLOTS, tok_rows), jnp.bfloat16),
            jax.ShapeDtypeStruct((n_seq, tok_rows, exp_dev * SLOTS), jnp.bfloat16),
        ],
        in_specs=[vmem],
        out_specs=[vmem] * 2,
        cost_estimate=pl.CostEstimate(
            flops=4_000_000_000, bytes_accessed=8 * n_seq * exp_dev * SLOTS * tok_rows,
            transcendentals=0,
        ),
    )(meta)


def most_rows(tok_rows):
    return tok_rows // 128 * 112


def moe_kernel(n_pieces, *refs):
    picks_hbm, weights_hbm, unit_ref, own_hbm = refs[:4]
    pieces_in = refs[4 : 4 + n_pieces]
    w_gate_hbm, w_up_hbm, w_down_hbm = refs[4 + n_pieces : 7 + n_pieces]
    out_refs = refs[7 + n_pieces : 13 + n_pieces]
    (picks, weights, w_in, w_down, toks, rows, hidden, mixed, table_sems, tok_sems, in_sems,
     down_sems) = refs[13 + n_pieces :]
    n_z, _, tok_rows, model_width = toks.shape
    n_seq = 2 * n_z
    exp_dev, hid_dev, _ = w_gate_hbm.shape
    width = model_width // 8
    slots_src = exp_dev * SLOTS
    rep = lax.axis_index("rep")
    split = most_rows(tok_rows)
    def in_copies(e):
        at = lax.rem(e, RING)
        return [
            pltpu.make_async_copy(
                src.at[e], w_in.at[at, pl.ds(i * hid_dev, hid_dev)], in_sems.at[i, at]
            )
            for i, src in enumerate((w_gate_hbm, w_up_hbm))
        ]

    def down_copy(e):
        return pltpu.make_async_copy(w_down_hbm.at[e], w_down.at[e], down_sems.at[e])

    tables = [
        pltpu.make_async_copy(picks_hbm, picks, table_sems.at[0]),
        pltpu.make_async_copy(weights_hbm, weights, table_sems.at[1]),
    ]
    tables[0].start()

    kinds = token_pieces(n_z)
    tok_copies = [pltpu.make_async_copy(own_hbm, toks.at[0, 0], tok_sems.at[0])]
    for i, piece in enumerate(pieces_in):
        blocks, runs = kinds[i % len(kinds)]
        for n, (color, dx) in enumerate(runs):
            cols = pl.ds(group_offset(rep, color, dx, i // len(kinds), width), width)
            for at, dz, count, dy in blocks:
                tok_copies.append(
                    pltpu.make_async_copy(
                        piece.at[pl.ds(at, count), pl.ds(0, tok_rows), pl.ds(n * width, width)],
                        toks.at[pl.ds(dz, count), dy, :, cols],
                        tok_sems.at[len(tok_copies)],
                    )
                )
    for copy in tok_copies:
        copy.start()

    for e in range(min(RING, exp_dev)):
        for copy in in_copies(e):
            copy.start()
    tables[1].start()
    quarters = [slice(2 * q * width, 2 * (q + 1) * width) for q in range(4)]
    tables[0].wait()

    tok_copies[0].wait()

    def pick(j, carry):
        @pl.when(j == 1)
        def _():
            for copy in tok_copies[1:]:
                copy.wait()

        onehot = picks[j]
        for cols in quarters:
            got = contract(onehot, toks[j // 2, j % 2, :, cols], 1, 0).astype(jnp.bfloat16)
            rows[j, :, :, cols] = got.reshape(exp_dev, SLOTS, 2 * width)
        return carry

    lax.fori_loop(0, n_seq, pick, 0)

    def widen(pair, carry):
        experts = (2 * pair, 2 * pair + 1)
        for e in experts:
            for copy in in_copies(e):
                copy.wait()
        both = [
            contract(
                w_in[lax.rem(e, RING)], rows[:, e].reshape(n_seq * SLOTS, model_width), 1, 1
            )
            for e in experts
        ]
        for e, value in zip(experts, both):
            gate_val, up_val = value[:hid_dev], value[hid_dev:]
            act = gate_val / (1.0 + jnp.exp(-gate_val)) * up_val
            hidden[e] = act.T.astype(jnp.bfloat16)
        for e in experts:
            down_copy(e).start()

            @pl.when(e + RING < exp_dev)
            def _():
                for copy in in_copies(e + RING):
                    copy.start()

        return carry

    lax.fori_loop(0, exp_dev // 2, widen, 0)

    def narrow(pair, carry):
        experts = (2 * pair, 2 * pair + 1)
        for e in experts:
            down_copy(e).wait()
        for e in experts:
            for cols in quarters:
                piece = contract(hidden[e], w_down[e, :, cols], 1, 0).astype(jnp.bfloat16)
                rows[:, e, :, cols] = piece.reshape(n_seq, SLOTS, 2 * width)
        return carry

    lax.fori_loop(0, exp_dev // 2, narrow, 0)
    tables[1].wait()

    def combine(dz, carry):
        along = [jnp.zeros((tok_rows, 1), jnp.float32)] * 2
        for dy in range(2):
            j = 2 * dz + dy
            weight = weights[j]
            for cols in quarters:
                got = contract(weight, rows[j, :, :, cols].reshape(slots_src, 2 * width), 1, 0)
                mixed[dy, :, cols] = got
                along[dy] += jnp.sum(got * unit_ref[:, cols], axis=1, keepdims=True)
        for dy in range(2):
            for dc in range(2):
                far, near, rest = out_refs[3 * dc : 3 * dc + 3]
                for n, (color, dx) in enumerate(((0, 1), (0, 0), (1, 0), (1, 1))):
                    cols = pl.ds(group_offset(rep, color, dx, dc, width), width)
                    value = mixed[dy, :, cols] - along[dy] * unit_ref[:, cols]
                    value = value.astype(jnp.bfloat16)
                    rest[dz, dy, :, n * width : (n + 1) * width] = value[split:]
                    leaves, kind = (dy, 2 + dx) if color else (dx, dy)
                    (far if leaves else near)[kind, dz] = value[:split]
        return carry

    lax.fori_loop(0, n_z, combine, 0)


def moe_partial(picks, weights, unit_dir, own, pieces, w_gate, w_up, w_down):
    n_seq, _, tok_rows = picks.shape
    exp_dev, hid_dev, model_width = w_gate.shape
    width = model_width // 8
    vmem = pl.BlockSpec(memory_space=pltpu.VMEM)
    hbm = pl.BlockSpec(memory_space=pltpu.HBM)
    whole = pl.BlockSpec(memory_space=pl.ANY)
    n_pieces = len(pieces)
    pieces = [pltpu.with_memory_space_constraint(piece, pltpu.VMEM) for piece in pieces]
    picks, weights, own = [
        pltpu.with_memory_space_constraint(value, pltpu.HBM) for value in (picks, weights, own)
    ]
    n_z, split = n_seq // 2, most_rows(tok_rows)
    most = (4, n_z, split, width)
    rest = (n_z, 2, tok_rows - split, 4 * width)
    outs = [
        jax.ShapeDtypeStruct(shape, jnp.bfloat16) for _ in range(2) for shape in (most, most, rest)
    ]
    return pl.pallas_call(
        functools.partial(moe_kernel, n_pieces),
        out_shape=outs,
        in_specs=[hbm, hbm, vmem, hbm] + [whole] * n_pieces + [hbm] * 3,
        out_specs=[vmem] * len(outs),
        scratch_shapes=[
            pltpu.VMEM(picks.shape, jnp.bfloat16),
            pltpu.VMEM(weights.shape, jnp.bfloat16),
            pltpu.VMEM((RING, 2 * hid_dev, model_width), jnp.bfloat16),
            pltpu.VMEM(w_down.shape, jnp.bfloat16),
            pltpu.VMEM((n_z, 2, tok_rows, model_width), jnp.bfloat16),
            pltpu.VMEM((n_seq, exp_dev, SLOTS, model_width), jnp.bfloat16),
            pltpu.VMEM((exp_dev, n_seq * SLOTS, hid_dev), jnp.bfloat16),
            pltpu.VMEM((2, tok_rows, model_width), jnp.float32),
            pltpu.SemaphoreType.DMA((2,)),
            pltpu.SemaphoreType.DMA((len(pieces) + 7,)),
            pltpu.SemaphoreType.DMA((2, RING)),
            pltpu.SemaphoreType.DMA((exp_dev,)),
        ],
        compiler_params=pltpu.CompilerParams(vmem_limit_bytes=42 * 1024 * 1024),
        cost_estimate=pl.CostEstimate(
            flops=6 * n_seq * SLOTS * exp_dev * hid_dev * model_width,
            bytes_accessed=6 * exp_dev * hid_dev * model_width + 4 * n_seq * own.size,
            transcendentals=0,
        ),
    )(picks, weights, unit_dir, own, *pieces, w_gate, w_up, w_down)


def swap(value, axis, distance):
    size = lax.axis_size(axis)
    return lax.ppermute(value, axis, [(i, i ^ distance) for i in range(size)])


def added(*terms):
    return sum(term.astype(jnp.float32) for term in terms).astype(jnp.bfloat16)


def gathered(tokens, norm_gain, refusal_dir, expert_ids, gate_probs, w_gate, w_up, w_down):
    tok_rows, model_width = tokens.shape
    n_z = lax.axis_size("seq") // 2
    others = range(1, n_z)
    exp_dev = w_gate.shape[0]
    width = model_width // 8

    normed, second, first, to_y, unit_dir, base, meta = norm_and_base(
        tokens, norm_gain, refusal_dir, expert_ids, gate_probs
    )
    second = [swap(second, "seq", 2 * d) for d in others]
    from_y = swap(to_y[None], "seq", 1)
    first, second, from_y = lax.optimization_barrier((first, jnp.stack(second), from_y))
    first = jnp.stack([swap(first, "seq", 2 * d) for d in others])
    x_two = swap(second[:, :tok_rows], "rep", 2)
    y_one = swap(second, "seq", 1)
    y_two = swap(first, "seq", 1)
    x_one = swap(jnp.concatenate([from_y[:, :tok_rows, :width], first]), "rep", 2)
    to_y, to_core = lax.optimization_barrier((x_two, second))
    y_three = swap(to_y, "seq", 1)
    below = [meta, from_y[0, tok_rows:, :tok_rows]]
    for d in range(n_z - 1):
        below += [second[d, tok_rows:, :tok_rows], y_one[d, tok_rows:, :tok_rows]]
    picks, weights = route(jnp.stack(below), exp_dev)
    to_core_y, picks, weights = lax.optimization_barrier((from_y, picks, weights))
    early = [swap(piece, "rep", 1) for piece in (to_core, first, to_core_y)]
    x_three = swap(y_two, "rep", 2)
    last = [x_two, y_one, x_one, y_two, y_three, x_three]
    pieces = [second, first, from_y, *last, *early, *[swap(piece, "rep", 1) for piece in last]]

    sums = moe_partial(picks, weights, unit_dir, normed, pieces, w_gate, w_up, w_down)
    return (base + summed_up(sums[:3], sums[3:], width)).astype(jnp.bfloat16)


def summed_up(kept, sent, width):
    n_z = kept[0].shape[1]
    others = range(1, n_z)
    far, near, rest = zip(kept, [swap(piece, "rep", 1) for piece in sent])

    to_x, to_y, rest_kept = lax.optimization_barrier(
        (added(*[term[:2] for term in far]), added(*[term[2:] for term in far]), rest[0])
    )
    by_x, by_y = swap(to_x, "rep", 2), swap(to_y, "seq", 1)
    rest = added(rest_kept, rest[1])
    by_z = [swap(rest[d], "seq", 2 * d) for d in others]
    to_y, to_x, *by_z = lax.optimization_barrier(
        (
            added(*[term[1] for term in near], by_x[1]),
            added(*[term[3] for term in near], by_y[1]),
            *by_z,
        )
    )
    first_far, second_far = swap(to_y, "seq", 1), swap(to_x, "rep", 2)
    first = added(*[term[0] for term in near], by_x[0], first_far)
    second = added(*[term[2] for term in near], by_y[0], second_far)
    blocks = jnp.concatenate([first, second], axis=2)
    most = [swap(blocks[d], "seq", 2 * d) for d in reversed(others)] + [blocks[0]]
    rest = added(rest[0], *by_z)
    rest = added(rest[0], swap(rest[1], "seq", 1))
    far = jnp.concatenate([rest[:, :width], rest[:, 3 * width :]], axis=1)
    rest = [rest[:, width : 3 * width], swap(far, "rep", 2)]
    return jnp.concatenate(
        [sum(term.astype(jnp.float32) for term in terms) for terms in (most, rest)], axis=0
    )


def exchanged(tokens, norm_gain, refusal_dir, expert_ids, gate_probs, w_gate, w_up, w_down):
    tok_rows, model_width = tokens.shape
    top_k = expert_ids.shape[1]
    n_seq = lax.axis_size("seq")
    n_rep = lax.axis_size("rep")
    exp_dev = w_gate.shape[0]
    experts = exp_dev * n_seq
    slot_count = tok_rows * top_k
    part_width = model_width // n_rep
    tokens_f32 = tokens.astype(jnp.float32)
    inv_rms = lax.rsqrt(jnp.mean(tokens_f32 * tokens_f32, axis=1, keepdims=True) + 1e-06)
    normed = (tokens_f32 * inv_rms * norm_gain).astype(jnp.bfloat16)
    flat_ids = expert_ids.reshape(slot_count)
    onehot = (flat_ids[:, None] == jnp.arange(experts, dtype=jnp.int32)[None, :]).astype(jnp.int32)
    slot_rank = jnp.sum(jnp.cumsum(onehot, axis=0) * onehot, axis=1) - 1
    target = flat_ids * CAP + slot_rank
    repeated = jnp.broadcast_to(normed[:, None, :], (tok_rows, top_k, model_width)).reshape(
        slot_count, model_width
    )
    sendbuf = jnp.zeros((experts * CAP, model_width), jnp.bfloat16).at[target].set(repeated)
    sendbuf = sendbuf.reshape(n_seq, exp_dev, CAP, model_width)
    arrived = lax.all_to_all(sendbuf, "seq", split_axis=0, concat_axis=0, tiled=True)
    gate_val = jnp.einsum("secd,efd->secf", arrived, w_gate, preferred_element_type=jnp.float32)
    up_val = jnp.einsum("secd,efd->secf", arrived, w_up, preferred_element_type=jnp.float32)
    hidden = (jax.nn.silu(gate_val) * up_val).astype(jnp.bfloat16)
    pieces = jnp.einsum(
        "secf,efd->secd", hidden, w_down, preferred_element_type=jnp.float32
    ).astype(jnp.bfloat16)
    probs_flat = gate_probs.reshape(slot_count)[:, None]
    returned = lax.all_to_all(pieces, "seq", split_axis=0, concat_axis=0, tiled=True)
    returned = returned.reshape(experts * CAP, model_width)
    weighted = returned[target].astype(jnp.float32) * probs_flat
    moe_part = jnp.sum(weighted.reshape(tok_rows, top_k, model_width), axis=1)
    summed = lax.psum_scatter(
        moe_part.astype(jnp.bfloat16), "rep", scatter_dimension=1, tiled=True
    ).astype(jnp.float32)
    unit_dir = refusal_dir / jnp.sqrt(jnp.sum(refusal_dir * refusal_dir) + 1e-06)
    rep_offset = lax.axis_index("rep") * part_width
    unit_slice = lax.dynamic_slice_in_dim(unit_dir, rep_offset, part_width, 0)
    own_tokens = lax.dynamic_slice_in_dim(tokens_f32, rep_offset, part_width, 1)
    residual = own_tokens + summed
    along_dir = lax.psum(jnp.sum(residual * unit_slice, axis=1), "rep")
    return (residual - along_dir[:, None] * unit_slice).astype(jnp.bfloat16)


def local(tokens, norm_gain, refusal_dir, expert_ids, gate_probs, w_gate, w_up, w_down):
    plan = gathered if w_gate.shape[0] * CAP >= tokens.shape[0] else exchanged
    return plan(tokens, norm_gain, refusal_dir, expert_ids, gate_probs, w_gate, w_up, w_down)


def solution(mesh):
    placed = (
        P("seq", None),
        P(),
        P(),
        P("seq", None),
        P("seq", None),
        P("seq", "rep", None),
        P("seq", "rep", None),
        P("seq", "rep", None),
    )
    return jax.shard_map(
        local, mesh=mesh, in_specs=placed, out_specs=P("seq", "rep"), check_vma=False
    )
```

```python
import functools

import jax
import jax.numpy as jnp
from jax import lax
from jax.experimental import pallas as pl
from jax.experimental.pallas import tpu as pltpu
from jax.sharding import PartitionSpec as P

CAP = 12
SLOTS = 16
RING = 6


def contract(lhs, rhs, lhs_dim, rhs_dim):
    return lax.dot_general(
        lhs, rhs, (((lhs_dim,), (rhs_dim,)), ((), ())), preferred_element_type=jnp.float32
    )


def group_offset(rep, color, dx, dc, width):
    return pl.multiple_of((rep ^ (2 * dx + dc)) * 2 * width + color * width, width)


def token_pieces(n_z):
    near, far = (0, 1, n_z - 1, 0), (0, 1, n_z - 1, 1)
    return [
        ([near], [(1, 0)]),
        ([near], [(0, 0)]),
        ([(0, 0, 1, 1)], [(0, 0), (1, 0), (1, 1)]),
        ([near], [(1, 1)]),
        ([far], [(1, 0)]),
        ([(0, 0, 1, 1), (1, 1, n_z - 1, 0)], [(0, 1)]),
        ([far], [(0, 0)]),
        ([far], [(1, 1)]),
        ([far], [(0, 1)]),
    ]


def norm_kernel(
    tokens_ref, gain_ref, refusal_ref, ids_ref, probs_ref,
    normed_ref, second_ref, first_ref, to_y_ref, unit_ref, base_ref, meta_ref,
):
    tok_rows, model_width = tokens_ref.shape
    width = model_width // 8
    rep = lax.axis_index("rep")
    toks = tokens_ref[...].astype(jnp.float32)
    refusal = refusal_ref[...]
    unit = refusal / jnp.sqrt(jnp.sum(refusal * refusal, axis=1, keepdims=True) + 1e-06)
    unit_ref[...] = unit
    inv_rms = lax.rsqrt(jnp.mean(toks * toks, axis=1, keepdims=True) + 1e-06)
    normed_ref[...] = (toks * inv_rms * gain_ref[...]).astype(jnp.bfloat16)
    own = pl.ds(group_offset(rep, 0, 0, 0, width), 2 * width)
    other = pl.ds(group_offset(rep, 1, 1, 0, width), width)
    first_ref[...] = normed_ref[:, pl.ds(group_offset(rep, 0, 0, 0, width), width)]
    second_ref[:tok_rows] = normed_ref[:, pl.ds(group_offset(rep, 1, 0, 0, width), width)]
    to_y_ref[:tok_rows, : 2 * width] = normed_ref[:, own]
    to_y_ref[:tok_rows, 2 * width :] = normed_ref[:, other]
    meta = jnp.concatenate([ids_ref[...].astype(jnp.float32), probs_ref[...]], axis=0)
    meta = meta.astype(jnp.bfloat16)
    meta_ref[...] = meta
    for ref in (second_ref, to_y_ref):
        ref[tok_rows:] = jnp.zeros((meta.shape[0], ref.shape[1]), jnp.bfloat16)
        ref[tok_rows:, :tok_rows] = meta
    along = jnp.sum(toks * unit, axis=1, keepdims=True)
    base_ref[...] = tokens_ref[:, own].astype(jnp.float32) - along * unit_ref[:, own]


def norm_and_base(tokens, norm_gain, refusal_dir, expert_ids, gate_probs):
    tok_rows, model_width = tokens.shape
    width = model_width // 8
    meta_rows = 2 * expert_ids.shape[1]
    vmem = pl.BlockSpec(memory_space=pltpu.VMEM)
    return pl.pallas_call(
        norm_kernel,
        out_shape=[
            jax.ShapeDtypeStruct((tok_rows, model_width), jnp.bfloat16),
            jax.ShapeDtypeStruct((tok_rows + meta_rows, width), jnp.bfloat16),
            jax.ShapeDtypeStruct((tok_rows, width), jnp.bfloat16),
            jax.ShapeDtypeStruct((tok_rows + meta_rows, 3 * width), jnp.bfloat16),
            jax.ShapeDtypeStruct((1, model_width), jnp.float32),
            jax.ShapeDtypeStruct((tok_rows, 2 * width), jnp.float32),
            jax.ShapeDtypeStruct((meta_rows, tok_rows), jnp.bfloat16),
        ],
        in_specs=[vmem] * 5,
        out_specs=[vmem] * 7,
    )(tokens, norm_gain[None, :], refusal_dir[None, :], expert_ids.T, gate_probs.T)


def route_kernel(exp_dev, meta_ref, picks_ref, weights_ref):
    n_seq, twice_k, tok_rows = meta_ref.shape
    top_k = twice_k // 2
    first = (lax.axis_index("seq") * exp_dev).astype(jnp.float32)
    exp_iota = lax.broadcasted_iota(jnp.int32, (exp_dev, tok_rows), 0).astype(jnp.float32) + first
    earlier = (
        lax.broadcasted_iota(jnp.int32, (tok_rows, tok_rows), 0)
        < lax.broadcasted_iota(jnp.int32, (tok_rows, tok_rows), 1)
    ).astype(jnp.float32).astype(jnp.bfloat16)
    slot_iota = lax.broadcasted_iota(jnp.int32, (exp_dev, SLOTS, tok_rows), 1).astype(jnp.float32)

    def place_pair(pair, carry):
        blocks = (2 * pair, 2 * pair + 1)
        hits, probs = [], []
        for j in blocks:
            meta = meta_ref[j].astype(jnp.float32)
            hit = jnp.zeros((exp_dev, tok_rows), jnp.float32)
            prob = jnp.zeros((exp_dev, tok_rows), jnp.float32)
            for k in range(top_k):
                same = meta[k : k + 1, :] == exp_iota
                hit = jnp.where(same, 1.0, hit)
                prob = jnp.where(same, meta[top_k + k : top_k + k + 1, :], prob)
            hits.append(hit)
            probs.append(prob)
        ranks = contract(jnp.concatenate(hits, axis=0).astype(jnp.bfloat16), earlier, 1, 0)
        for n, j in enumerate(blocks):
            rank = ranks[n * exp_dev : (n + 1) * exp_dev]
            slot = jnp.where(hits[n] > 0.0, rank, -1.0)
            here = slot[:, None, :] == slot_iota
            onehot = jnp.where(here, 1.0, 0.0).reshape(exp_dev * SLOTS, tok_rows)
            weight = jnp.where(here, probs[n][:, None, :], 0.0)
            weight = weight.reshape(exp_dev * SLOTS, tok_rows)
            picks_ref[j] = onehot.astype(jnp.bfloat16)
            weights_ref[j] = weight.T.astype(jnp.bfloat16)
        return carry

    lax.fori_loop(0, n_seq // 2, place_pair, 0)


def route(meta, exp_dev):
    n_seq, _, tok_rows = meta.shape
    vmem = pl.BlockSpec(memory_space=pltpu.VMEM)
    return pl.pallas_call(
        functools.partial(route_kernel, exp_dev),
        out_shape=[
            jax.ShapeDtypeStruct((n_seq, exp_dev * SLOTS, tok_rows), jnp.bfloat16),
            jax.ShapeDtypeStruct((n_seq, tok_rows, exp_dev * SLOTS), jnp.bfloat16),
        ],
        in_specs=[vmem],
        out_specs=[vmem] * 2,
        cost_estimate=pl.CostEstimate(
            flops=4_000_000_000, bytes_accessed=8 * n_seq * exp_dev * SLOTS * tok_rows,
            transcendentals=0,
        ),
    )(meta)


def most_rows(tok_rows):
    return tok_rows // 128 * 112


def moe_kernel(n_pieces, *refs):
    picks_hbm, weights_hbm, unit_ref, own_hbm = refs[:4]
    pieces_in = refs[4 : 4 + n_pieces]
    w_gate_hbm, w_up_hbm, w_down_hbm = refs[4 + n_pieces : 7 + n_pieces]
    out_refs = refs[7 + n_pieces : 13 + n_pieces]
    (picks, weights, w_in, w_down, toks, rows, both, hidden, mixed, along, table_sems, tok_sems,
     in_sems, down_sems) = refs[13 + n_pieces :]
    n_z, _, tok_rows, model_width = toks.shape
    n_seq = 2 * n_z
    exp_dev, hid_dev, _ = w_gate_hbm.shape
    width = model_width // 8
    slots_src = exp_dev * SLOTS
    rep = lax.axis_index("rep")
    split = most_rows(tok_rows)
    def in_copies(e):
        at = lax.rem(e, RING)
        return [
            pltpu.make_async_copy(
                src.at[e], w_in.at[at, pl.ds(i * hid_dev, hid_dev)], in_sems.at[i, at]
            )
            for i, src in enumerate((w_gate_hbm, w_up_hbm))
        ]

    def down_copy(e):
        return pltpu.make_async_copy(w_down_hbm.at[e], w_down.at[e], down_sems.at[e])

    tables = [
        pltpu.make_async_copy(picks_hbm, picks, table_sems.at[0]),
        pltpu.make_async_copy(weights_hbm, weights, table_sems.at[1]),
    ]
    tables[0].start()

    kinds = token_pieces(n_z)
    tok_copies = [pltpu.make_async_copy(own_hbm, toks.at[0, 0], tok_sems.at[0])]
    for i, piece in enumerate(pieces_in):
        blocks, runs = kinds[i % len(kinds)]
        for n, (color, dx) in enumerate(runs):
            cols = pl.ds(group_offset(rep, color, dx, i // len(kinds), width), width)
            for at, dz, count, dy in blocks:
                tok_copies.append(
                    pltpu.make_async_copy(
                        piece.at[pl.ds(at, count), pl.ds(0, tok_rows), pl.ds(n * width, width)],
                        toks.at[pl.ds(dz, count), dy, :, cols],
                        tok_sems.at[len(tok_copies)],
                    )
                )
    for copy in tok_copies:
        copy.start()

    for e in range(min(RING, exp_dev)):
        for copy in in_copies(e):
            copy.start()
    tables[1].start()
    quarters = [slice(2 * q * width, 2 * (q + 1) * width) for q in range(4)]
    tables[0].wait()

    for copy in tok_copies:
        copy.wait()

    def pick(dz, carry):
        for dy in range(2):
            onehot = picks[2 * dz + dy]
            for cols in quarters:
                got = contract(onehot, toks[dz, dy, :, cols], 1, 0).astype(jnp.bfloat16)
                rows[2 * dz + dy, :, :, cols] = got.reshape(exp_dev, SLOTS, 2 * width)
        return carry

    lax.fori_loop(0, n_z, pick, 0)

    def activate(pair):
        for i in range(2):
            gate_val, up_val = both[i, :hid_dev], both[i, hid_dev:]
            act = gate_val / (1.0 + jnp.exp(-gate_val)) * up_val
            hidden[2 * pair + i] = act.T.astype(jnp.bfloat16)

    def widen(pair, carry):
        experts = (2 * pair, 2 * pair + 1)
        for e in experts:
            for copy in in_copies(e):
                copy.wait()
        activate(jnp.maximum(pair - 1, 0))
        for i, e in enumerate(experts):
            both[i] = contract(
                w_in[lax.rem(e, RING)], rows[:, e].reshape(n_seq * SLOTS, model_width), 1, 1
            )
        for e in experts:
            down_copy(e).start()

            @pl.when(e + RING < exp_dev)
            def _():
                for copy in in_copies(e + RING):
                    copy.start()

        return carry

    lax.fori_loop(0, exp_dev // 2, widen, 0)
    activate(exp_dev // 2 - 1)

    def narrow(pair, carry):
        experts = (2 * pair, 2 * pair + 1)
        for e in experts:
            down_copy(e).wait()
        for e in experts:
            for cols in quarters:
                piece = contract(hidden[e], w_down[e, :, cols], 1, 0).astype(jnp.bfloat16)
                rows[:, e, :, cols] = piece.reshape(n_seq, SLOTS, 2 * width)
        return carry

    lax.fori_loop(0, exp_dev // 2, narrow, 0)
    tables[1].wait()

    def project(dz):
        for dy in range(2):
            for dc in range(2):
                far, near, rest = out_refs[3 * dc : 3 * dc + 3]
                for n, (color, dx) in enumerate(((0, 1), (0, 0), (1, 0), (1, 1))):
                    cols = pl.ds(group_offset(rep, color, dx, dc, width), width)
                    value = mixed[dy, :, cols] - along[dy] * unit_ref[:, cols]
                    value = value.astype(jnp.bfloat16)
                    rest[dz, dy, :, n * width : (n + 1) * width] = value[split:]
                    leaves, kind = (dy, 2 + dx) if color else (dx, dy)
                    (far if leaves else near)[kind, dz] = value[:split]

    def combine(dz, carry):
        project(jnp.maximum(dz - 1, 0))
        for dy in range(2):
            j = 2 * dz + dy
            total = jnp.zeros((tok_rows, 1), jnp.float32)
            for cols in quarters:
                got = contract(
                    weights[j], rows[j, :, :, cols].reshape(slots_src, 2 * width), 1, 0
                )
                mixed[dy, :, cols] = got
                total += jnp.sum(got * unit_ref[:, cols], axis=1, keepdims=True)
            along[dy] = total
        return carry

    lax.fori_loop(0, n_z, combine, 0)
    project(n_z - 1)


def moe_partial(picks, weights, unit_dir, own, pieces, w_gate, w_up, w_down):
    n_seq, _, tok_rows = picks.shape
    exp_dev, hid_dev, model_width = w_gate.shape
    width = model_width // 8
    vmem = pl.BlockSpec(memory_space=pltpu.VMEM)
    hbm = pl.BlockSpec(memory_space=pltpu.HBM)
    whole = pl.BlockSpec(memory_space=pl.ANY)
    n_pieces = len(pieces)
    pieces = [pltpu.with_memory_space_constraint(piece, pltpu.VMEM) for piece in pieces]
    picks, weights, own = [
        pltpu.with_memory_space_constraint(value, pltpu.HBM) for value in (picks, weights, own)
    ]
    n_z, split = n_seq // 2, most_rows(tok_rows)
    most = (4, n_z, split, width)
    rest = (n_z, 2, tok_rows - split, 4 * width)
    outs = [
        jax.ShapeDtypeStruct(shape, jnp.bfloat16) for _ in range(2) for shape in (most, most, rest)
    ]
    return pl.pallas_call(
        functools.partial(moe_kernel, n_pieces),
        out_shape=outs,
        in_specs=[hbm, hbm, vmem, hbm] + [whole] * n_pieces + [hbm] * 3,
        out_specs=[vmem] * len(outs),
        scratch_shapes=[
            pltpu.VMEM(picks.shape, jnp.bfloat16),
            pltpu.VMEM(weights.shape, jnp.bfloat16),
            pltpu.VMEM((RING, 2 * hid_dev, model_width), jnp.bfloat16),
            pltpu.VMEM(w_down.shape, jnp.bfloat16),
            pltpu.VMEM((n_z, 2, tok_rows, model_width), jnp.bfloat16),
            pltpu.VMEM((n_seq, exp_dev, SLOTS, model_width), jnp.bfloat16),
            pltpu.VMEM((2, 2 * hid_dev, n_seq * SLOTS), jnp.float32),
            pltpu.VMEM((exp_dev, n_seq * SLOTS, hid_dev), jnp.bfloat16),
            pltpu.VMEM((2, tok_rows, model_width), jnp.float32),
            pltpu.VMEM((2, tok_rows, 1), jnp.float32),
            pltpu.SemaphoreType.DMA((2,)),
            pltpu.SemaphoreType.DMA((len(pieces) + 7,)),
            pltpu.SemaphoreType.DMA((2, RING)),
            pltpu.SemaphoreType.DMA((exp_dev,)),
        ],
        compiler_params=pltpu.CompilerParams(vmem_limit_bytes=42 * 1024 * 1024),
        cost_estimate=pl.CostEstimate(
            flops=6 * n_seq * SLOTS * exp_dev * hid_dev * model_width,
            bytes_accessed=6 * exp_dev * hid_dev * model_width + 4 * n_seq * own.size,
            transcendentals=0,
        ),
    )(picks, weights, unit_dir, own, *pieces, w_gate, w_up, w_down)


def swap(value, axis, distance):
    size = lax.axis_size(axis)
    return lax.ppermute(value, axis, [(i, i ^ distance) for i in range(size)])


def added(*terms):
    return sum(term.astype(jnp.float32) for term in terms).astype(jnp.bfloat16)


def gathered(tokens, norm_gain, refusal_dir, expert_ids, gate_probs, w_gate, w_up, w_down):
    tok_rows, model_width = tokens.shape
    n_z = lax.axis_size("seq") // 2
    others = range(1, n_z)
    exp_dev = w_gate.shape[0]
    width = model_width // 8

    normed, second, first, to_y, unit_dir, base, meta = norm_and_base(
        tokens, norm_gain, refusal_dir, expert_ids, gate_probs
    )
    second = [swap(second, "seq", 2 * d) for d in others]
    from_y = swap(to_y[None], "seq", 1)
    first, second, from_y = lax.optimization_barrier((first, jnp.stack(second), from_y))
    first = jnp.stack([swap(first, "seq", 2 * d) for d in others])
    x_two = swap(second[:, :tok_rows], "rep", 2)
    y_one = swap(second, "seq", 1)
    y_two = swap(first, "seq", 1)
    x_one = swap(jnp.concatenate([from_y[:, :tok_rows, :width], first]), "rep", 2)
    to_y, to_core = lax.optimization_barrier((x_two, second))
    y_three = swap(to_y, "seq", 1)
    below = [meta, from_y[0, tok_rows:, :tok_rows]]
    for d in range(n_z - 1):
        below += [second[d, tok_rows:, :tok_rows], y_one[d, tok_rows:, :tok_rows]]
    picks, weights = route(jnp.stack(below), exp_dev)
    to_core_y, picks, weights = lax.optimization_barrier((from_y, picks, weights))
    early = [swap(piece, "rep", 1) for piece in (to_core, first, to_core_y)]
    x_three = swap(y_two, "rep", 2)
    last = [x_two, y_one, x_one, y_two, y_three, x_three]
    pieces = [second, first, from_y, *last, *early, *[swap(piece, "rep", 1) for piece in last]]

    sums = moe_partial(picks, weights, unit_dir, normed, pieces, w_gate, w_up, w_down)
    return (base + summed_up(sums[:3], sums[3:], width)).astype(jnp.bfloat16)


def summed_up(kept, sent, width):
    n_z = kept[0].shape[1]
    others = range(1, n_z)
    far, near, rest = zip(kept, [swap(piece, "rep", 1) for piece in sent])

    to_x, to_y, rest_kept = lax.optimization_barrier(
        (added(*[term[:2] for term in far]), added(*[term[2:] for term in far]), rest[0])
    )
    by_x, by_y = swap(to_x, "rep", 2), swap(to_y, "seq", 1)
    rest = added(rest_kept, rest[1])
    by_z = [swap(rest[d], "seq", 2 * d) for d in others]
    to_y, to_x, *by_z = lax.optimization_barrier(
        (
            added(*[term[1] for term in near], by_x[1]),
            added(*[term[3] for term in near], by_y[1]),
            *by_z,
        )
    )
    first_far, second_far = swap(to_y, "seq", 1), swap(to_x, "rep", 2)
    first = added(*[term[0] for term in near], by_x[0], first_far)
    second = added(*[term[2] for term in near], by_y[0], second_far)
    blocks = jnp.concatenate([first, second], axis=2)
    most = [swap(blocks[d], "seq", 2 * d) for d in reversed(others)] + [blocks[0]]
    rest = added(rest[0], *by_z)
    rest = added(rest[0], swap(rest[1], "seq", 1))
    far = jnp.concatenate([rest[:, :width], rest[:, 3 * width :]], axis=1)
    rest = [rest[:, width : 3 * width], swap(far, "rep", 2)]
    return jnp.concatenate(
        [sum(term.astype(jnp.float32) for term in terms) for terms in (most, rest)], axis=0
    )


def exchanged(tokens, norm_gain, refusal_dir, expert_ids, gate_probs, w_gate, w_up, w_down):
    tok_rows, model_width = tokens.shape
    top_k = expert_ids.shape[1]
    n_seq = lax.axis_size("seq")
    n_rep = lax.axis_size("rep")
    exp_dev = w_gate.shape[0]
    experts = exp_dev * n_seq
    slot_count = tok_rows * top_k
    part_width = model_width // n_rep
    tokens_f32 = tokens.astype(jnp.float32)
    inv_rms = lax.rsqrt(jnp.mean(tokens_f32 * tokens_f32, axis=1, keepdims=True) + 1e-06)
    normed = (tokens_f32 * inv_rms * norm_gain).astype(jnp.bfloat16)
    flat_ids = expert_ids.reshape(slot_count)
    onehot = (flat_ids[:, None] == jnp.arange(experts, dtype=jnp.int32)[None, :]).astype(jnp.int32)
    slot_rank = jnp.sum(jnp.cumsum(onehot, axis=0) * onehot, axis=1) - 1
    target = flat_ids * CAP + slot_rank
    repeated = jnp.broadcast_to(normed[:, None, :], (tok_rows, top_k, model_width)).reshape(
        slot_count, model_width
    )
    sendbuf = jnp.zeros((experts * CAP, model_width), jnp.bfloat16).at[target].set(repeated)
    sendbuf = sendbuf.reshape(n_seq, exp_dev, CAP, model_width)
    arrived = lax.all_to_all(sendbuf, "seq", split_axis=0, concat_axis=0, tiled=True)
    gate_val = jnp.einsum("secd,efd->secf", arrived, w_gate, preferred_element_type=jnp.float32)
    up_val = jnp.einsum("secd,efd->secf", arrived, w_up, preferred_element_type=jnp.float32)
    hidden = (jax.nn.silu(gate_val) * up_val).astype(jnp.bfloat16)
    pieces = jnp.einsum(
        "secf,efd->secd", hidden, w_down, preferred_element_type=jnp.float32
    ).astype(jnp.bfloat16)
    probs_flat = gate_probs.reshape(slot_count)[:, None]
    returned = lax.all_to_all(pieces, "seq", split_axis=0, concat_axis=0, tiled=True)
    returned = returned.reshape(experts * CAP, model_width)
    weighted = returned[target].astype(jnp.float32) * probs_flat
    moe_part = jnp.sum(weighted.reshape(tok_rows, top_k, model_width), axis=1)
    summed = lax.psum_scatter(
        moe_part.astype(jnp.bfloat16), "rep", scatter_dimension=1, tiled=True
    ).astype(jnp.float32)
    unit_dir = refusal_dir / jnp.sqrt(jnp.sum(refusal_dir * refusal_dir) + 1e-06)
    rep_offset = lax.axis_index("rep") * part_width
    unit_slice = lax.dynamic_slice_in_dim(unit_dir, rep_offset, part_width, 0)
    own_tokens = lax.dynamic_slice_in_dim(tokens_f32, rep_offset, part_width, 1)
    residual = own_tokens + summed
    along_dir = lax.psum(jnp.sum(residual * unit_slice, axis=1), "rep")
    return (residual - along_dir[:, None] * unit_slice).astype(jnp.bfloat16)


def local(tokens, norm_gain, refusal_dir, expert_ids, gate_probs, w_gate, w_up, w_down):
    plan = gathered if w_gate.shape[0] * CAP >= tokens.shape[0] else exchanged
    return plan(tokens, norm_gain, refusal_dir, expert_ids, gate_probs, w_gate, w_up, w_down)


def solution(mesh):
    placed = (
        P("seq", None),
        P(),
        P(),
        P("seq", None),
        P("seq", None),
        P("seq", "rep", None),
        P("seq", "rep", None),
        P("seq", "rep", None),
    )
    return jax.shard_map(
        local, mesh=mesh, in_specs=placed, out_specs=P("seq", "rep"), check_vma=False
    )
```

```python
import functools

import jax
import jax.numpy as jnp
from jax import lax
from jax.experimental import pallas as pl
from jax.experimental.pallas import tpu as pltpu
from jax.sharding import PartitionSpec as P

CAP = 12
SLOTS = 16
RING = 6


def contract(lhs, rhs, lhs_dim, rhs_dim):
    return lax.dot_general(
        lhs, rhs, (((lhs_dim,), (rhs_dim,)), ((), ())), preferred_element_type=jnp.float32
    )


def group_offset(rep, color, dx, dc, width):
    return pl.multiple_of((rep ^ (2 * dx + dc)) * 2 * width + color * width, width)


PIECES = [(0, 1, 0), (0, 0, 0), (0, 1, 1), (1, 1, 0), (0, 0, 1), (1, 0, 0), (1, 1, 1), (1, 0, 1)]
X_ONE = 4
OWN_Y = [(0, 0), (1, 0), (1, 1)]


def norm_kernel(
    tokens_ref, gain_ref, refusal_ref, ids_ref, probs_ref,
    normed_ref, second_ref, first_ref, to_y_ref, unit_ref, base_ref, meta_ref,
):
    tok_rows, model_width = tokens_ref.shape
    width = model_width // 8
    rep = lax.axis_index("rep")
    toks = tokens_ref[...].astype(jnp.float32)
    refusal = refusal_ref[...]
    unit = refusal / jnp.sqrt(jnp.sum(refusal * refusal, axis=1, keepdims=True) + 1e-06)
    unit_ref[...] = unit
    inv_rms = lax.rsqrt(jnp.mean(toks * toks, axis=1, keepdims=True) + 1e-06)
    normed_ref[...] = (toks * inv_rms * gain_ref[...]).astype(jnp.bfloat16)
    own = pl.ds(group_offset(rep, 0, 0, 0, width), 2 * width)
    other = pl.ds(group_offset(rep, 1, 1, 0, width), width)
    first_ref[...] = normed_ref[:, pl.ds(group_offset(rep, 0, 0, 0, width), width)]
    second_ref[:tok_rows] = normed_ref[:, pl.ds(group_offset(rep, 1, 0, 0, width), width)]
    to_y_ref[:tok_rows, : 2 * width] = normed_ref[:, own]
    to_y_ref[:tok_rows, 2 * width :] = normed_ref[:, other]
    meta = jnp.concatenate([ids_ref[...].astype(jnp.float32), probs_ref[...]], axis=0)
    meta = meta.astype(jnp.bfloat16)
    meta_ref[...] = meta
    for ref in (second_ref, to_y_ref):
        ref[tok_rows:] = jnp.zeros((meta.shape[0], ref.shape[1]), jnp.bfloat16)
        ref[tok_rows:, :tok_rows] = meta
    along = jnp.sum(toks * unit, axis=1, keepdims=True)
    base_ref[...] = tokens_ref[:, own].astype(jnp.float32) - along * unit_ref[:, own]


def norm_and_base(tokens, norm_gain, refusal_dir, expert_ids, gate_probs):
    tok_rows, model_width = tokens.shape
    width = model_width // 8
    meta_rows = 2 * expert_ids.shape[1]
    vmem = pl.BlockSpec(memory_space=pltpu.VMEM)
    return pl.pallas_call(
        norm_kernel,
        out_shape=[
            jax.ShapeDtypeStruct((tok_rows, model_width), jnp.bfloat16),
            jax.ShapeDtypeStruct((tok_rows + meta_rows, width), jnp.bfloat16),
            jax.ShapeDtypeStruct((tok_rows, width), jnp.bfloat16),
            jax.ShapeDtypeStruct((tok_rows + meta_rows, 3 * width), jnp.bfloat16),
            jax.ShapeDtypeStruct((1, model_width), jnp.float32),
            jax.ShapeDtypeStruct((tok_rows, 2 * width), jnp.float32),
            jax.ShapeDtypeStruct((meta_rows, tok_rows), jnp.bfloat16),
        ],
        in_specs=[vmem] * 5,
        out_specs=[vmem] * 7,
    )(tokens, norm_gain[None, :], refusal_dir[None, :], expert_ids.T, gate_probs.T)


def route_kernel(exp_dev, meta_ref, picks_ref, weights_ref):
    n_seq, twice_k, tok_rows = meta_ref.shape
    top_k = twice_k // 2
    first = (lax.axis_index("seq") * exp_dev).astype(jnp.float32)
    exp_iota = lax.broadcasted_iota(jnp.int32, (exp_dev, tok_rows), 0).astype(jnp.float32) + first
    earlier = (
        lax.broadcasted_iota(jnp.int32, (tok_rows, tok_rows), 0)
        < lax.broadcasted_iota(jnp.int32, (tok_rows, tok_rows), 1)
    ).astype(jnp.float32).astype(jnp.bfloat16)
    slot_iota = lax.broadcasted_iota(jnp.int32, (exp_dev, SLOTS, tok_rows), 1).astype(jnp.float32)

    def place_pair(pair, carry):
        blocks = (2 * pair, 2 * pair + 1)
        hits, probs = [], []
        for j in blocks:
            meta = meta_ref[j].astype(jnp.float32)
            hit = jnp.zeros((exp_dev, tok_rows), jnp.float32)
            prob = jnp.zeros((exp_dev, tok_rows), jnp.float32)
            for k in range(top_k):
                same = meta[k : k + 1, :] == exp_iota
                hit = jnp.where(same, 1.0, hit)
                prob = jnp.where(same, meta[top_k + k : top_k + k + 1, :], prob)
            hits.append(hit)
            probs.append(prob)
        ranks = contract(jnp.concatenate(hits, axis=0).astype(jnp.bfloat16), earlier, 1, 0)
        for n, j in enumerate(blocks):
            rank = ranks[n * exp_dev : (n + 1) * exp_dev]
            slot = jnp.where(hits[n] > 0.0, rank, -1.0)
            here = slot[:, None, :] == slot_iota
            onehot = jnp.where(here, 1.0, 0.0).reshape(exp_dev * SLOTS, tok_rows)
            weight = jnp.where(here, probs[n][:, None, :], 0.0)
            weight = weight.reshape(exp_dev * SLOTS, tok_rows)
            picks_ref[j] = onehot.astype(jnp.bfloat16)
            weights_ref[j] = weight.T.astype(jnp.bfloat16)
        return carry

    lax.fori_loop(0, n_seq // 2, place_pair, 0)


def route(meta, exp_dev):
    n_seq, _, tok_rows = meta.shape
    vmem = pl.BlockSpec(memory_space=pltpu.VMEM)
    return pl.pallas_call(
        functools.partial(route_kernel, exp_dev),
        out_shape=[
            jax.ShapeDtypeStruct((n_seq, exp_dev * SLOTS, tok_rows), jnp.bfloat16),
            jax.ShapeDtypeStruct((n_seq, tok_rows, exp_dev * SLOTS), jnp.bfloat16),
        ],
        in_specs=[vmem],
        out_specs=[vmem] * 2,
        cost_estimate=pl.CostEstimate(
            flops=4_000_000_000, bytes_accessed=8 * n_seq * exp_dev * SLOTS * tok_rows,
            transcendentals=0,
        ),
    )(meta)


def most_rows(tok_rows):
    return tok_rows // 128 * 112


def moe_kernel(n_pieces, *refs):
    picks_hbm, weights_hbm, unit_ref, own = refs[:4]
    pieces_in = refs[4 : 4 + n_pieces]
    w_gate_hbm, w_up_hbm, w_down_hbm = refs[4 + n_pieces : 7 + n_pieces]
    out_refs = refs[7 + n_pieces : 13 + n_pieces]
    (picks, weights, w_in, w_down, rows, both, hidden, mixed, along, table_sems, in_sems,
     down_sems) = refs[13 + n_pieces :]
    tok_rows, model_width = own.shape
    n_seq = picks.shape[0]
    n_z = n_seq // 2
    exp_dev, hid_dev, _ = w_gate_hbm.shape
    width = model_width // 8
    slots_src = exp_dev * SLOTS
    rep = lax.axis_index("rep")
    split = most_rows(tok_rows)
    def in_copies(e):
        at = lax.rem(e, RING)
        return [
            pltpu.make_async_copy(
                src.at[e], w_in.at[at, pl.ds(i * hid_dev, hid_dev)], in_sems.at[i, at]
            )
            for i, src in enumerate((w_gate_hbm, w_up_hbm))
        ]

    def down_copy(e):
        return pltpu.make_async_copy(w_down_hbm.at[e], w_down.at[e], down_sems.at[e])

    tables = [
        pltpu.make_async_copy(picks_hbm, picks, table_sems.at[0]),
        pltpu.make_async_copy(weights_hbm, weights, table_sems.at[1]),
    ]
    tables[0].start()

    for e in range(min(RING, exp_dev)):
        for copy in in_copies(e):
            copy.start()
    tables[1].start()
    quarters = [slice(2 * q * width, 2 * (q + 1) * width) for q in range(4)]
    tables[0].wait()

    def pick(j, toks, columns):
        got = contract(picks[j], toks, 1, 0).astype(jnp.bfloat16)
        rows[j, :, :, columns] = got.reshape(exp_dev, SLOTS, toks.shape[1])

    def runs(dc, color, dx):
        return pl.ds(group_offset(rep, color, dx, dc, width), width)

    halves = [pieces_in[:9], pieces_in[9:]]
    for cols in quarters:
        pick(0, own[:, cols], cols)
    for dc, (from_y, *arrays) in enumerate(halves):
        for n, (color, dx) in enumerate(OWN_Y):
            pick(1, from_y[0, :tok_rows, n * width : (n + 1) * width], runs(dc, color, dx))
        pick(1, arrays[X_ONE][0], runs(dc, 0, 1))

    def pick_row(at, carry):
        for dc, (_, *arrays) in enumerate(halves):
            for i, (dy, color, dx) in enumerate(PIECES):
                toks = arrays[i][at + (i == X_ONE), :tok_rows]
                pick(2 * (at + 1) + dy, toks, runs(dc, color, dx))
        return carry

    lax.fori_loop(0, n_z - 1, pick_row, 0)

    def activate(pair):
        for i in range(2):
            gate_val, up_val = both[i, :hid_dev], both[i, hid_dev:]
            act = gate_val / (1.0 + jnp.exp(-gate_val)) * up_val
            hidden[2 * pair + i] = act.T.astype(jnp.bfloat16)

    def widen(pair, carry):
        experts = (2 * pair, 2 * pair + 1)
        for e in experts:
            for copy in in_copies(e):
                copy.wait()
        activate(jnp.maximum(pair - 1, 0))
        for i, e in enumerate(experts):
            both[i] = contract(
                w_in[lax.rem(e, RING)], rows[:, e].reshape(n_seq * SLOTS, model_width), 1, 1
            )
        for e in experts:
            down_copy(e).start()

            @pl.when(e + RING < exp_dev)
            def _():
                for copy in in_copies(e + RING):
                    copy.start()

        return carry

    lax.fori_loop(0, exp_dev // 2, widen, 0)
    activate(exp_dev // 2 - 1)

    def narrow(pair, carry):
        experts = (2 * pair, 2 * pair + 1)
        for e in experts:
            down_copy(e).wait()
        for e in experts:
            for cols in quarters:
                piece = contract(hidden[e], w_down[e, :, cols], 1, 0).astype(jnp.bfloat16)
                rows[:, e, :, cols] = piece.reshape(n_seq, SLOTS, 2 * width)
        return carry

    lax.fori_loop(0, exp_dev // 2, narrow, 0)
    tables[1].wait()

    def project(dz):
        for dy in range(2):
            for dc in range(2):
                far, near, rest = out_refs[3 * dc : 3 * dc + 3]
                for n, (color, dx) in enumerate(((0, 1), (0, 0), (1, 0), (1, 1))):
                    cols = pl.ds(group_offset(rep, color, dx, dc, width), width)
                    value = mixed[dy, :, cols] - along[dy] * unit_ref[:, cols]
                    value = value.astype(jnp.bfloat16)
                    rest[dz, dy, :, n * width : (n + 1) * width] = value[split:]
                    leaves, kind = (dy, 2 + dx) if color else (dx, dy)
                    (far if leaves else near)[kind, dz] = value[:split]

    def combine(dz, carry):
        project(jnp.maximum(dz - 1, 0))
        for dy in range(2):
            j = 2 * dz + dy
            total = jnp.zeros((tok_rows, 1), jnp.float32)
            for cols in quarters:
                got = contract(
                    weights[j], rows[j, :, :, cols].reshape(slots_src, 2 * width), 1, 0
                )
                mixed[dy, :, cols] = got
                total += jnp.sum(got * unit_ref[:, cols], axis=1, keepdims=True)
            along[dy] = total
        return carry

    lax.fori_loop(0, n_z, combine, 0)
    project(n_z - 1)


def moe_partial(picks, weights, unit_dir, own, pieces, w_gate, w_up, w_down):
    n_seq, _, tok_rows = picks.shape
    exp_dev, hid_dev, model_width = w_gate.shape
    width = model_width // 8
    vmem = pl.BlockSpec(memory_space=pltpu.VMEM)
    hbm = pl.BlockSpec(memory_space=pltpu.HBM)
    n_pieces = len(pieces)
    own, *pieces = [
        pltpu.with_memory_space_constraint(value, pltpu.VMEM) for value in (own, *pieces)
    ]
    picks, weights = [
        pltpu.with_memory_space_constraint(value, pltpu.HBM) for value in (picks, weights)
    ]
    n_z, split = n_seq // 2, most_rows(tok_rows)
    most = (4, n_z, split, width)
    rest = (n_z, 2, tok_rows - split, 4 * width)
    outs = [
        jax.ShapeDtypeStruct(shape, jnp.bfloat16) for _ in range(2) for shape in (most, most, rest)
    ]
    return pl.pallas_call(
        functools.partial(moe_kernel, n_pieces),
        out_shape=outs,
        in_specs=[hbm, hbm, vmem] + [vmem] * (1 + n_pieces) + [hbm] * 3,
        out_specs=[vmem] * len(outs),
        scratch_shapes=[
            pltpu.VMEM(picks.shape, jnp.bfloat16),
            pltpu.VMEM(weights.shape, jnp.bfloat16),
            pltpu.VMEM((RING, 2 * hid_dev, model_width), jnp.bfloat16),
            pltpu.VMEM(w_down.shape, jnp.bfloat16),
            pltpu.VMEM((n_seq, exp_dev, SLOTS, model_width), jnp.bfloat16),
            pltpu.VMEM((2, 2 * hid_dev, n_seq * SLOTS), jnp.float32),
            pltpu.VMEM((exp_dev, n_seq * SLOTS, hid_dev), jnp.bfloat16),
            pltpu.VMEM((2, tok_rows, model_width), jnp.float32),
            pltpu.VMEM((2, tok_rows, 1), jnp.float32),
            pltpu.SemaphoreType.DMA((2,)),
            pltpu.SemaphoreType.DMA((2, RING)),
            pltpu.SemaphoreType.DMA((exp_dev,)),
        ],
        compiler_params=pltpu.CompilerParams(vmem_limit_bytes=40 * 1024 * 1024),
        cost_estimate=pl.CostEstimate(
            flops=6 * n_seq * SLOTS * exp_dev * hid_dev * model_width,
            bytes_accessed=6 * exp_dev * hid_dev * model_width + 4 * n_seq * own.size,
            transcendentals=0,
        ),
    )(picks, weights, unit_dir, own, *pieces, w_gate, w_up, w_down)


def swap(value, axis, distance):
    size = lax.axis_size(axis)
    return lax.ppermute(value, axis, [(i, i ^ distance) for i in range(size)])


def added(*terms):
    return sum(term.astype(jnp.float32) for term in terms).astype(jnp.bfloat16)


def gathered(tokens, norm_gain, refusal_dir, expert_ids, gate_probs, w_gate, w_up, w_down):
    tok_rows, model_width = tokens.shape
    n_z = lax.axis_size("seq") // 2
    others = range(1, n_z)
    exp_dev = w_gate.shape[0]
    width = model_width // 8

    normed, second, first, to_y, unit_dir, base, meta = norm_and_base(
        tokens, norm_gain, refusal_dir, expert_ids, gate_probs
    )
    second = [swap(second, "seq", 2 * d) for d in others]
    from_y = swap(to_y[None], "seq", 1)
    first, second, from_y = lax.optimization_barrier((first, jnp.stack(second), from_y))
    first = jnp.stack([swap(first, "seq", 2 * d) for d in others])
    x_two = swap(second[:, :tok_rows], "rep", 2)
    y_one = swap(second, "seq", 1)
    y_two = swap(first, "seq", 1)
    x_one = swap(jnp.concatenate([from_y[:, :tok_rows, :width], first]), "rep", 2)
    to_y, to_core = lax.optimization_barrier((x_two, second))
    y_three = swap(to_y, "seq", 1)
    below = [meta, from_y[0, tok_rows:, :tok_rows]]
    for d in range(n_z - 1):
        below += [second[d, tok_rows:, :tok_rows], y_one[d, tok_rows:, :tok_rows]]
    picks, weights = route(jnp.stack(below), exp_dev)
    to_core_y, picks, weights = lax.optimization_barrier((from_y, picks, weights))
    x_three = swap(y_two, "rep", 2)
    pieces = [from_y, second, first, x_two, y_one, x_one, y_two, y_three, x_three]
    to_core = [to_core_y, to_core, *pieces[2:]]
    pieces = pieces + [swap(piece, "rep", 1) for piece in to_core]

    sums = moe_partial(picks, weights, unit_dir, normed, pieces, w_gate, w_up, w_down)
    return (base + summed_up(sums[:3], sums[3:], width)).astype(jnp.bfloat16)


def summed_up(kept, sent, width):
    n_z = kept[0].shape[1]
    others = range(1, n_z)
    far, near, rest = zip(kept, [swap(piece, "rep", 1) for piece in sent])

    to_x, to_y, rest_kept = lax.optimization_barrier(
        (added(*[term[:2] for term in far]), added(*[term[2:] for term in far]), rest[0])
    )
    by_x, by_y = swap(to_x, "rep", 2), swap(to_y, "seq", 1)
    rest = added(rest_kept, rest[1])
    by_z = [swap(rest[d], "seq", 2 * d) for d in others]
    to_y, to_x, *by_z = lax.optimization_barrier(
        (
            added(*[term[1] for term in near], by_x[1]),
            added(*[term[3] for term in near], by_y[1]),
            *by_z,
        )
    )
    first_far, second_far = swap(to_y, "seq", 1), swap(to_x, "rep", 2)
    first = added(*[term[0] for term in near], by_x[0], first_far)
    second = added(*[term[2] for term in near], by_y[0], second_far)
    blocks = jnp.concatenate([first, second], axis=2)
    most = [swap(blocks[d], "seq", 2 * d) for d in reversed(others)] + [blocks[0]]
    rest = added(rest[0], *by_z)
    rest = added(rest[0], swap(rest[1], "seq", 1))
    far = jnp.concatenate([rest[:, :width], rest[:, 3 * width :]], axis=1)
    rest = [rest[:, width : 3 * width], swap(far, "rep", 2)]
    return jnp.concatenate(
        [sum(term.astype(jnp.float32) for term in terms) for terms in (most, rest)], axis=0
    )


def exchanged(tokens, norm_gain, refusal_dir, expert_ids, gate_probs, w_gate, w_up, w_down):
    tok_rows, model_width = tokens.shape
    top_k = expert_ids.shape[1]
    n_seq = lax.axis_size("seq")
    n_rep = lax.axis_size("rep")
    exp_dev = w_gate.shape[0]
    experts = exp_dev * n_seq
    slot_count = tok_rows * top_k
    part_width = model_width // n_rep
    tokens_f32 = tokens.astype(jnp.float32)
    inv_rms = lax.rsqrt(jnp.mean(tokens_f32 * tokens_f32, axis=1, keepdims=True) + 1e-06)
    normed = (tokens_f32 * inv_rms * norm_gain).astype(jnp.bfloat16)
    flat_ids = expert_ids.reshape(slot_count)
    onehot = (flat_ids[:, None] == jnp.arange(experts, dtype=jnp.int32)[None, :]).astype(jnp.int32)
    slot_rank = jnp.sum(jnp.cumsum(onehot, axis=0) * onehot, axis=1) - 1
    target = flat_ids * CAP + slot_rank
    repeated = jnp.broadcast_to(normed[:, None, :], (tok_rows, top_k, model_width)).reshape(
        slot_count, model_width
    )
    sendbuf = jnp.zeros((experts * CAP, model_width), jnp.bfloat16).at[target].set(repeated)
    sendbuf = sendbuf.reshape(n_seq, exp_dev, CAP, model_width)
    arrived = lax.all_to_all(sendbuf, "seq", split_axis=0, concat_axis=0, tiled=True)
    gate_val = jnp.einsum("secd,efd->secf", arrived, w_gate, preferred_element_type=jnp.float32)
    up_val = jnp.einsum("secd,efd->secf", arrived, w_up, preferred_element_type=jnp.float32)
    hidden = (jax.nn.silu(gate_val) * up_val).astype(jnp.bfloat16)
    pieces = jnp.einsum(
        "secf,efd->secd", hidden, w_down, preferred_element_type=jnp.float32
    ).astype(jnp.bfloat16)
    probs_flat = gate_probs.reshape(slot_count)[:, None]
    returned = lax.all_to_all(pieces, "seq", split_axis=0, concat_axis=0, tiled=True)
    returned = returned.reshape(experts * CAP, model_width)
    weighted = returned[target].astype(jnp.float32) * probs_flat
    moe_part = jnp.sum(weighted.reshape(tok_rows, top_k, model_width), axis=1)
    summed = lax.psum_scatter(
        moe_part.astype(jnp.bfloat16), "rep", scatter_dimension=1, tiled=True
    ).astype(jnp.float32)
    unit_dir = refusal_dir / jnp.sqrt(jnp.sum(refusal_dir * refusal_dir) + 1e-06)
    rep_offset = lax.axis_index("rep") * part_width
    unit_slice = lax.dynamic_slice_in_dim(unit_dir, rep_offset, part_width, 0)
    own_tokens = lax.dynamic_slice_in_dim(tokens_f32, rep_offset, part_width, 1)
    residual = own_tokens + summed
    along_dir = lax.psum(jnp.sum(residual * unit_slice, axis=1), "rep")
    return (residual - along_dir[:, None] * unit_slice).astype(jnp.bfloat16)


def local(tokens, norm_gain, refusal_dir, expert_ids, gate_probs, w_gate, w_up, w_down):
    plan = gathered if w_gate.shape[0] * CAP >= tokens.shape[0] else exchanged
    return plan(tokens, norm_gain, refusal_dir, expert_ids, gate_probs, w_gate, w_up, w_down)


def solution(mesh):
    placed = (
        P("seq", None),
        P(),
        P(),
        P("seq", None),
        P("seq", None),
        P("seq", "rep", None),
        P("seq", "rep", None),
        P("seq", "rep", None),
    )
    return jax.shard_map(
        local, mesh=mesh, in_specs=placed, out_specs=P("seq", "rep"), check_vma=False
    )
```

```python
import functools

import jax
import jax.numpy as jnp
from jax import lax
from jax.experimental import pallas as pl
from jax.experimental.pallas import tpu as pltpu
from jax.sharding import PartitionSpec as P

CAP = 12
SLOTS = 16
RING = 6


def contract(lhs, rhs, lhs_dim, rhs_dim):
    return lax.dot_general(
        lhs, rhs, (((lhs_dim,), (rhs_dim,)), ((), ())), preferred_element_type=jnp.float32
    )


def group_offset(rep, color, dx, dc, width):
    return pl.multiple_of((rep ^ (2 * dx + dc)) * 2 * width + color * width, width)


def token_pieces(n_z):
    near, far = (0, 1, n_z - 1, 0), (0, 1, n_z - 1, 1)
    return [
        ([near], [(1, 0)]),
        ([near], [(0, 0)]),
        ([(0, 0, 1, 1)], [(0, 0), (1, 0), (1, 1)]),
        ([near], [(1, 1)]),
        ([far], [(1, 0)]),
        ([(0, 0, 1, 1), (1, 1, n_z - 1, 0)], [(0, 1)]),
        ([far], [(0, 0)]),
        ([far], [(1, 1)]),
        ([far], [(0, 1)]),
    ]


def norm_kernel(
    tokens_ref, gain_ref, refusal_ref, ids_ref, probs_ref,
    normed_ref, second_ref, first_ref, to_y_ref, unit_ref, base_ref, meta_ref,
):
    tok_rows, model_width = tokens_ref.shape
    width = model_width // 8
    rep = lax.axis_index("rep")
    toks = tokens_ref[...].astype(jnp.float32)
    refusal = refusal_ref[...]
    unit = refusal / jnp.sqrt(jnp.sum(refusal * refusal, axis=1, keepdims=True) + 1e-06)
    unit_ref[...] = unit
    inv_rms = lax.rsqrt(jnp.mean(toks * toks, axis=1, keepdims=True) + 1e-06)
    normed_ref[...] = (toks * inv_rms * gain_ref[...]).astype(jnp.bfloat16)
    own = pl.ds(group_offset(rep, 0, 0, 0, width), 2 * width)
    other = pl.ds(group_offset(rep, 1, 1, 0, width), width)
    first_ref[...] = normed_ref[:, pl.ds(group_offset(rep, 0, 0, 0, width), width)]
    second_ref[:tok_rows] = normed_ref[:, pl.ds(group_offset(rep, 1, 0, 0, width), width)]
    to_y_ref[:tok_rows, : 2 * width] = normed_ref[:, own]
    to_y_ref[:tok_rows, 2 * width :] = normed_ref[:, other]
    meta = jnp.concatenate([ids_ref[...].astype(jnp.float32), probs_ref[...]], axis=0)
    meta = meta.astype(jnp.bfloat16)
    meta_ref[...] = meta
    for ref in (second_ref, to_y_ref):
        ref[tok_rows:] = jnp.zeros((meta.shape[0], ref.shape[1]), jnp.bfloat16)
        ref[tok_rows:, :tok_rows] = meta
    along = jnp.sum(toks * unit, axis=1, keepdims=True)
    base_ref[...] = tokens_ref[:, own].astype(jnp.float32) - along * unit_ref[:, own]


def norm_and_base(tokens, norm_gain, refusal_dir, expert_ids, gate_probs):
    tok_rows, model_width = tokens.shape
    width = model_width // 8
    meta_rows = 2 * expert_ids.shape[1]
    vmem = pl.BlockSpec(memory_space=pltpu.VMEM)
    return pl.pallas_call(
        norm_kernel,
        out_shape=[
            jax.ShapeDtypeStruct((tok_rows, model_width), jnp.bfloat16),
            jax.ShapeDtypeStruct((tok_rows + meta_rows, width), jnp.bfloat16),
            jax.ShapeDtypeStruct((tok_rows, width), jnp.bfloat16),
            jax.ShapeDtypeStruct((tok_rows + meta_rows, 3 * width), jnp.bfloat16),
            jax.ShapeDtypeStruct((1, model_width), jnp.float32),
            jax.ShapeDtypeStruct((tok_rows, 2 * width), jnp.float32),
            jax.ShapeDtypeStruct((meta_rows, tok_rows), jnp.bfloat16),
        ],
        in_specs=[vmem] * 5,
        out_specs=[vmem] * 7,
    )(tokens, norm_gain[None, :], refusal_dir[None, :], expert_ids.T, gate_probs.T)


def route_kernel(exp_dev, meta_ref, picks_ref, weights_ref):
    n_seq, twice_k, tok_rows = meta_ref.shape
    top_k = twice_k // 2
    first = (lax.axis_index("seq") * exp_dev).astype(jnp.float32)
    exp_iota = lax.broadcasted_iota(jnp.int32, (exp_dev, tok_rows), 0).astype(jnp.float32) + first
    earlier = (
        lax.broadcasted_iota(jnp.int32, (tok_rows, tok_rows), 0)
        < lax.broadcasted_iota(jnp.int32, (tok_rows, tok_rows), 1)
    ).astype(jnp.float32).astype(jnp.bfloat16)
    slot_iota = lax.broadcasted_iota(jnp.int32, (exp_dev, SLOTS, tok_rows), 1).astype(jnp.float32)

    def place_pair(pair, carry):
        blocks = (2 * pair, 2 * pair + 1)
        hits, probs = [], []
        for j in blocks:
            meta = meta_ref[j].astype(jnp.float32)
            hit = jnp.zeros((exp_dev, tok_rows), jnp.float32)
            prob = jnp.zeros((exp_dev, tok_rows), jnp.float32)
            for k in range(top_k):
                same = meta[k : k + 1, :] == exp_iota
                hit = jnp.where(same, 1.0, hit)
                prob = jnp.where(same, meta[top_k + k : top_k + k + 1, :], prob)
            hits.append(hit)
            probs.append(prob)
        ranks = contract(jnp.concatenate(hits, axis=0).astype(jnp.bfloat16), earlier, 1, 0)
        for n, j in enumerate(blocks):
            rank = ranks[n * exp_dev : (n + 1) * exp_dev]
            slot = jnp.where(hits[n] > 0.0, rank, -1.0)
            here = slot[:, None, :] == slot_iota
            onehot = jnp.where(here, 1.0, 0.0).reshape(exp_dev * SLOTS, tok_rows)
            weight = jnp.where(here, probs[n][:, None, :], 0.0)
            weight = weight.reshape(exp_dev * SLOTS, tok_rows)
            picks_ref[j] = onehot.astype(jnp.bfloat16)
            weights_ref[j] = weight.T.astype(jnp.bfloat16)
        return carry

    lax.fori_loop(0, n_seq // 2, place_pair, 0)


def route(meta, exp_dev):
    n_seq, _, tok_rows = meta.shape
    vmem = pl.BlockSpec(memory_space=pltpu.VMEM)
    return pl.pallas_call(
        functools.partial(route_kernel, exp_dev),
        out_shape=[
            jax.ShapeDtypeStruct((n_seq, exp_dev * SLOTS, tok_rows), jnp.bfloat16),
            jax.ShapeDtypeStruct((n_seq, tok_rows, exp_dev * SLOTS), jnp.bfloat16),
        ],
        in_specs=[vmem],
        out_specs=[vmem] * 2,
        cost_estimate=pl.CostEstimate(
            flops=4_000_000_000, bytes_accessed=8 * n_seq * exp_dev * SLOTS * tok_rows,
            transcendentals=0,
        ),
    )(meta)


def most_rows(tok_rows):
    return tok_rows // 128 * 112


def moe_kernel(n_pieces, *refs):
    picks_hbm, weights_hbm, unit_ref, own_hbm = refs[:4]
    pieces_in = refs[4 : 4 + n_pieces]
    w_gate_hbm, w_up_hbm, w_down_hbm = refs[4 + n_pieces : 7 + n_pieces]
    out_refs = refs[7 + n_pieces : 13 + n_pieces]
    (picks, weights, w_in, w_down, toks, rows, both, hidden, mixed, along, table_sems, tok_sems,
     in_sems, down_sems) = refs[13 + n_pieces :]
    n_z, _, tok_rows, model_width = toks.shape
    n_seq = 2 * n_z
    exp_dev, hid_dev, _ = w_gate_hbm.shape
    width = model_width // 8
    slots_src = exp_dev * SLOTS
    rep = lax.axis_index("rep")
    split = most_rows(tok_rows)
    def in_copies(e):
        at = lax.rem(e, RING)
        return [
            pltpu.make_async_copy(
                src.at[e], w_in.at[at, pl.ds(i * hid_dev, hid_dev)], in_sems.at[i, at]
            )
            for i, src in enumerate((w_gate_hbm, w_up_hbm))
        ]

    def down_copy(e):
        return pltpu.make_async_copy(w_down_hbm.at[e], w_down.at[e], down_sems.at[e])

    tables = [
        pltpu.make_async_copy(picks_hbm, picks, table_sems.at[0]),
        pltpu.make_async_copy(weights_hbm, weights, table_sems.at[1]),
    ]
    tables[0].start()

    kinds = token_pieces(n_z)
    pltpu.make_async_copy(own_hbm, toks.at[0, 0], tok_sems.at[0, 0]).start()
    for i, piece in enumerate(pieces_in):
        blocks, runs = kinds[i % len(kinds)]
        for n, (color, dx) in enumerate(runs):
            cols = pl.ds(group_offset(rep, color, dx, i // len(kinds), width), width)
            for at, dz, count, dy in blocks:
                for k in range(count):
                    pltpu.make_async_copy(
                        piece.at[at + k, pl.ds(0, tok_rows), pl.ds(n * width, width)],
                        toks.at[dz + k, dy, :, cols],
                        tok_sems.at[dz + k, dy],
                    ).start()
    for e in range(min(RING, exp_dev)):
        for copy in in_copies(e):
            copy.start()
    tables[1].start()
    quarters = [slice(2 * q * width, 2 * (q + 1) * width) for q in range(4)]
    tables[0].wait()

    def pick(dz, carry):
        for dy in range(2):
            pltpu.make_async_copy(toks.at[dz, dy], toks.at[dz, dy], tok_sems.at[dz, dy]).wait()
        for dy in range(2):
            onehot = picks[2 * dz + dy]
            for cols in quarters:
                got = contract(onehot, toks[dz, dy, :, cols], 1, 0).astype(jnp.bfloat16)
                rows[2 * dz + dy, :, :, cols] = got.reshape(exp_dev, SLOTS, 2 * width)
        return carry

    lax.fori_loop(0, n_z, pick, 0)

    def activate(pair):
        for i in range(2):
            gate_val, up_val = both[i, :hid_dev], both[i, hid_dev:]
            act = gate_val / (1.0 + jnp.exp(-gate_val)) * up_val
            hidden[2 * pair + i] = act.T.astype(jnp.bfloat16)

    def widen(pair, carry):
        experts = (2 * pair, 2 * pair + 1)
        for e in experts:
            for copy in in_copies(e):
                copy.wait()
        activate(jnp.maximum(pair - 1, 0))
        for i, e in enumerate(experts):
            both[i] = contract(
                w_in[lax.rem(e, RING)], rows[:, e].reshape(n_seq * SLOTS, model_width), 1, 1
            )
        for e in experts:
            down_copy(e).start()

            @pl.when(e + RING < exp_dev)
            def _():
                for copy in in_copies(e + RING):
                    copy.start()

        return carry

    lax.fori_loop(0, exp_dev // 2, widen, 0)
    activate(exp_dev // 2 - 1)

    def narrow(pair, carry):
        experts = (2 * pair, 2 * pair + 1)
        for e in experts:
            down_copy(e).wait()
        for e in experts:
            for cols in quarters:
                piece = contract(hidden[e], w_down[e, :, cols], 1, 0).astype(jnp.bfloat16)
                rows[:, e, :, cols] = piece.reshape(n_seq, SLOTS, 2 * width)
        return carry

    lax.fori_loop(0, exp_dev // 2, narrow, 0)
    tables[1].wait()

    def project(dz):
        for dy in range(2):
            for dc in range(2):
                far, near, rest = out_refs[3 * dc : 3 * dc + 3]
                for n, (color, dx) in enumerate(((0, 1), (0, 0), (1, 0), (1, 1))):
                    cols = pl.ds(group_offset(rep, color, dx, dc, width), width)
                    value = mixed[dy, :, cols] - along[dy] * unit_ref[:, cols]
                    value = value.astype(jnp.bfloat16)
                    rest[dz, dy, :, n * width : (n + 1) * width] = value[split:]
                    leaves, kind = (dy, 2 + dx) if color else (dx, dy)
                    (far if leaves else near)[kind, dz] = value[:split]

    def combine(dz, carry):
        project(jnp.maximum(dz - 1, 0))
        for dy in range(2):
            j = 2 * dz + dy
            total = jnp.zeros((tok_rows, 1), jnp.float32)
            for cols in quarters:
                got = contract(
                    weights[j], rows[j, :, :, cols].reshape(slots_src, 2 * width), 1, 0
                )
                mixed[dy, :, cols] = got
                total += jnp.sum(got * unit_ref[:, cols], axis=1, keepdims=True)
            along[dy] = total
        return carry

    lax.fori_loop(0, n_z, combine, 0)
    project(n_z - 1)


def moe_partial(picks, weights, unit_dir, own, pieces, w_gate, w_up, w_down):
    n_seq, _, tok_rows = picks.shape
    exp_dev, hid_dev, model_width = w_gate.shape
    width = model_width // 8
    vmem = pl.BlockSpec(memory_space=pltpu.VMEM)
    hbm = pl.BlockSpec(memory_space=pltpu.HBM)
    whole = pl.BlockSpec(memory_space=pl.ANY)
    n_pieces = len(pieces)
    pieces = [pltpu.with_memory_space_constraint(piece, pltpu.VMEM) for piece in pieces]
    picks, weights, own = [
        pltpu.with_memory_space_constraint(value, pltpu.HBM) for value in (picks, weights, own)
    ]
    n_z, split = n_seq // 2, most_rows(tok_rows)
    most = (4, n_z, split, width)
    rest = (n_z, 2, tok_rows - split, 4 * width)
    outs = [
        jax.ShapeDtypeStruct(shape, jnp.bfloat16) for _ in range(2) for shape in (most, most, rest)
    ]
    return pl.pallas_call(
        functools.partial(moe_kernel, n_pieces),
        out_shape=outs,
        in_specs=[hbm, hbm, vmem, hbm] + [whole] * n_pieces + [hbm] * 3,
        out_specs=[vmem] * len(outs),
        scratch_shapes=[
            pltpu.VMEM(picks.shape, jnp.bfloat16),
            pltpu.VMEM(weights.shape, jnp.bfloat16),
            pltpu.VMEM((RING, 2 * hid_dev, model_width), jnp.bfloat16),
            pltpu.VMEM(w_down.shape, jnp.bfloat16),
            pltpu.VMEM((n_z, 2, tok_rows, model_width), jnp.bfloat16),
            pltpu.VMEM((n_seq, exp_dev, SLOTS, model_width), jnp.bfloat16),
            pltpu.VMEM((2, 2 * hid_dev, n_seq * SLOTS), jnp.float32),
            pltpu.VMEM((exp_dev, n_seq * SLOTS, hid_dev), jnp.bfloat16),
            pltpu.VMEM((2, tok_rows, model_width), jnp.float32),
            pltpu.VMEM((2, tok_rows, 1), jnp.float32),
            pltpu.SemaphoreType.DMA((2,)),
            pltpu.SemaphoreType.DMA((n_z, 2)),
            pltpu.SemaphoreType.DMA((2, RING)),
            pltpu.SemaphoreType.DMA((exp_dev,)),
        ],
        compiler_params=pltpu.CompilerParams(vmem_limit_bytes=42 * 1024 * 1024),
        cost_estimate=pl.CostEstimate(
            flops=6 * n_seq * SLOTS * exp_dev * hid_dev * model_width,
            bytes_accessed=6 * exp_dev * hid_dev * model_width + 4 * n_seq * own.size,
            transcendentals=0,
        ),
    )(picks, weights, unit_dir, own, *pieces, w_gate, w_up, w_down)


def swap(value, axis, distance):
    size = lax.axis_size(axis)
    return lax.ppermute(value, axis, [(i, i ^ distance) for i in range(size)])


def added(*terms):
    return sum(term.astype(jnp.float32) for term in terms).astype(jnp.bfloat16)


def gathered(tokens, norm_gain, refusal_dir, expert_ids, gate_probs, w_gate, w_up, w_down):
    tok_rows, model_width = tokens.shape
    n_z = lax.axis_size("seq") // 2
    others = range(1, n_z)
    exp_dev = w_gate.shape[0]
    width = model_width // 8

    normed, second, first, to_y, unit_dir, base, meta = norm_and_base(
        tokens, norm_gain, refusal_dir, expert_ids, gate_probs
    )
    second = [swap(second, "seq", 2 * d) for d in others]
    from_y = swap(to_y[None], "seq", 1)
    first, second, from_y = lax.optimization_barrier((first, jnp.stack(second), from_y))
    first = jnp.stack([swap(first, "seq", 2 * d) for d in others])
    x_two = swap(second[:, :tok_rows], "rep", 2)
    y_one = swap(second, "seq", 1)
    y_two = swap(first, "seq", 1)
    x_one = swap(jnp.concatenate([from_y[:, :tok_rows, :width], first]), "rep", 2)
    to_y, to_core = lax.optimization_barrier((x_two, second))
    y_three = swap(to_y, "seq", 1)
    below = [meta, from_y[0, tok_rows:, :tok_rows]]
    for d in range(n_z - 1):
        below += [second[d, tok_rows:, :tok_rows], y_one[d, tok_rows:, :tok_rows]]
    picks, weights = route(jnp.stack(below), exp_dev)
    to_core_y, picks, weights = lax.optimization_barrier((from_y, picks, weights))
    early = [swap(piece, "rep", 1) for piece in (to_core, first, to_core_y)]
    x_three = swap(y_two, "rep", 2)
    last = [x_two, y_one, x_one, y_two, y_three, x_three]
    pieces = [second, first, from_y, *last, *early, *[swap(piece, "rep", 1) for piece in last]]

    sums = moe_partial(picks, weights, unit_dir, normed, pieces, w_gate, w_up, w_down)
    return (base + summed_up(sums[:3], sums[3:], width)).astype(jnp.bfloat16)


def summed_up(kept, sent, width):
    n_z = kept[0].shape[1]
    others = range(1, n_z)
    far, near, rest = zip(kept, [swap(piece, "rep", 1) for piece in sent])

    to_x, to_y, rest_kept = lax.optimization_barrier(
        (added(*[term[:2] for term in far]), added(*[term[2:] for term in far]), rest[0])
    )
    by_x, by_y = swap(to_x, "rep", 2), swap(to_y, "seq", 1)
    rest = added(rest_kept, rest[1])
    by_z = [swap(rest[d], "seq", 2 * d) for d in others]
    to_y, to_x, *by_z = lax.optimization_barrier(
        (
            added(*[term[1] for term in near], by_x[1]),
            added(*[term[3] for term in near], by_y[1]),
            *by_z,
        )
    )
    first_far, second_far = swap(to_y, "seq", 1), swap(to_x, "rep", 2)
    first = added(*[term[0] for term in near], by_x[0], first_far)
    second = added(*[term[2] for term in near], by_y[0], second_far)
    blocks = jnp.concatenate([first, second], axis=2)
    most = [swap(blocks[d], "seq", 2 * d) for d in reversed(others)] + [blocks[0]]
    rest = added(rest[0], *by_z)
    rest = added(rest[0], swap(rest[1], "seq", 1))
    far = jnp.concatenate([rest[:, :width], rest[:, 3 * width :]], axis=1)
    rest = [rest[:, width : 3 * width], swap(far, "rep", 2)]
    return jnp.concatenate(
        [sum(term.astype(jnp.float32) for term in terms) for terms in (most, rest)], axis=0
    )


def exchanged(tokens, norm_gain, refusal_dir, expert_ids, gate_probs, w_gate, w_up, w_down):
    tok_rows, model_width = tokens.shape
    top_k = expert_ids.shape[1]
    n_seq = lax.axis_size("seq")
    n_rep = lax.axis_size("rep")
    exp_dev = w_gate.shape[0]
    experts = exp_dev * n_seq
    slot_count = tok_rows * top_k
    part_width = model_width // n_rep
    tokens_f32 = tokens.astype(jnp.float32)
    inv_rms = lax.rsqrt(jnp.mean(tokens_f32 * tokens_f32, axis=1, keepdims=True) + 1e-06)
    normed = (tokens_f32 * inv_rms * norm_gain).astype(jnp.bfloat16)
    flat_ids = expert_ids.reshape(slot_count)
    onehot = (flat_ids[:, None] == jnp.arange(experts, dtype=jnp.int32)[None, :]).astype(jnp.int32)
    slot_rank = jnp.sum(jnp.cumsum(onehot, axis=0) * onehot, axis=1) - 1
    target = flat_ids * CAP + slot_rank
    repeated = jnp.broadcast_to(normed[:, None, :], (tok_rows, top_k, model_width)).reshape(
        slot_count, model_width
    )
    sendbuf = jnp.zeros((experts * CAP, model_width), jnp.bfloat16).at[target].set(repeated)
    sendbuf = sendbuf.reshape(n_seq, exp_dev, CAP, model_width)
    arrived = lax.all_to_all(sendbuf, "seq", split_axis=0, concat_axis=0, tiled=True)
    gate_val = jnp.einsum("secd,efd->secf", arrived, w_gate, preferred_element_type=jnp.float32)
    up_val = jnp.einsum("secd,efd->secf", arrived, w_up, preferred_element_type=jnp.float32)
    hidden = (jax.nn.silu(gate_val) * up_val).astype(jnp.bfloat16)
    pieces = jnp.einsum(
        "secf,efd->secd", hidden, w_down, preferred_element_type=jnp.float32
    ).astype(jnp.bfloat16)
    probs_flat = gate_probs.reshape(slot_count)[:, None]
    returned = lax.all_to_all(pieces, "seq", split_axis=0, concat_axis=0, tiled=True)
    returned = returned.reshape(experts * CAP, model_width)
    weighted = returned[target].astype(jnp.float32) * probs_flat
    moe_part = jnp.sum(weighted.reshape(tok_rows, top_k, model_width), axis=1)
    summed = lax.psum_scatter(
        moe_part.astype(jnp.bfloat16), "rep", scatter_dimension=1, tiled=True
    ).astype(jnp.float32)
    unit_dir = refusal_dir / jnp.sqrt(jnp.sum(refusal_dir * refusal_dir) + 1e-06)
    rep_offset = lax.axis_index("rep") * part_width
    unit_slice = lax.dynamic_slice_in_dim(unit_dir, rep_offset, part_width, 0)
    own_tokens = lax.dynamic_slice_in_dim(tokens_f32, rep_offset, part_width, 1)
    residual = own_tokens + summed
    along_dir = lax.psum(jnp.sum(residual * unit_slice, axis=1), "rep")
    return (residual - along_dir[:, None] * unit_slice).astype(jnp.bfloat16)


def local(tokens, norm_gain, refusal_dir, expert_ids, gate_probs, w_gate, w_up, w_down):
    plan = gathered if w_gate.shape[0] * CAP >= tokens.shape[0] else exchanged
    return plan(tokens, norm_gain, refusal_dir, expert_ids, gate_probs, w_gate, w_up, w_down)


def solution(mesh):
    placed = (
        P("seq", None),
        P(),
        P(),
        P("seq", None),
        P("seq", None),
        P("seq", "rep", None),
        P("seq", "rep", None),
        P("seq", "rep", None),
    )
    return jax.shard_map(
        local, mesh=mesh, in_specs=placed, out_specs=P("seq", "rep"), check_vma=False
    )
```

```python
import functools

import jax
import jax.numpy as jnp
from jax import lax
from jax.experimental import pallas as pl
from jax.experimental.pallas import tpu as pltpu
from jax.sharding import PartitionSpec as P

CAP = 12
SLOTS = 16
RING = 6


def contract(lhs, rhs, lhs_dim, rhs_dim):
    return lax.dot_general(
        lhs, rhs, (((lhs_dim,), (rhs_dim,)), ((), ())), preferred_element_type=jnp.float32
    )


def group_offset(rep, color, dx, dc, width):
    return pl.multiple_of((rep ^ (2 * dx + dc)) * 2 * width + color * width, width)


def token_pieces(n_z):
    near, far = (0, 1, n_z - 1, 0), (0, 1, n_z - 1, 1)
    return [
        ([near], [(1, 0)]),
        ([near], [(0, 0)]),
        ([(0, 0, 1, 1)], [(0, 0), (1, 0), (1, 1)]),
        ([near], [(1, 1)]),
        ([far], [(1, 0)]),
        ([(0, 0, 1, 1), (1, 1, n_z - 1, 0)], [(0, 1)]),
        ([far], [(0, 0)]),
        ([far], [(1, 1)]),
        ([far], [(0, 1)]),
    ]


def norm_kernel(
    tokens_ref, gain_ref, refusal_ref, ids_ref, probs_ref,
    normed_ref, second_ref, first_ref, to_y_ref, unit_ref, base_ref, meta_ref,
):
    tok_rows, model_width = tokens_ref.shape
    width = model_width // 8
    rep = lax.axis_index("rep")
    toks = tokens_ref[...].astype(jnp.float32)
    refusal = refusal_ref[...]
    unit = refusal / jnp.sqrt(jnp.sum(refusal * refusal, axis=1, keepdims=True) + 1e-06)
    unit_ref[...] = unit
    inv_rms = lax.rsqrt(jnp.mean(toks * toks, axis=1, keepdims=True) + 1e-06)
    normed_ref[...] = (toks * inv_rms * gain_ref[...]).astype(jnp.bfloat16)
    own = pl.ds(group_offset(rep, 0, 0, 0, width), 2 * width)
    other = pl.ds(group_offset(rep, 1, 1, 0, width), width)
    first_ref[...] = normed_ref[:, pl.ds(group_offset(rep, 0, 0, 0, width), width)]
    second_ref[:tok_rows] = normed_ref[:, pl.ds(group_offset(rep, 1, 0, 0, width), width)]
    to_y_ref[:tok_rows, : 2 * width] = normed_ref[:, own]
    to_y_ref[:tok_rows, 2 * width :] = normed_ref[:, other]
    meta = jnp.concatenate([ids_ref[...].astype(jnp.float32), probs_ref[...]], axis=0)
    meta = meta.astype(jnp.bfloat16)
    meta_ref[...] = meta
    for ref in (second_ref, to_y_ref):
        ref[tok_rows:] = jnp.zeros((meta.shape[0], ref.shape[1]), jnp.bfloat16)
        ref[tok_rows:, :tok_rows] = meta
    along = jnp.sum(toks * unit, axis=1, keepdims=True)
    base_ref[...] = tokens_ref[:, own].astype(jnp.float32) - along * unit_ref[:, own]


def norm_and_base(tokens, norm_gain, refusal_dir, expert_ids, gate_probs):
    tok_rows, model_width = tokens.shape
    width = model_width // 8
    meta_rows = 2 * expert_ids.shape[1]
    vmem = pl.BlockSpec(memory_space=pltpu.VMEM)
    return pl.pallas_call(
        norm_kernel,
        out_shape=[
            jax.ShapeDtypeStruct((tok_rows, model_width), jnp.bfloat16),
            jax.ShapeDtypeStruct((tok_rows + meta_rows, width), jnp.bfloat16),
            jax.ShapeDtypeStruct((tok_rows, width), jnp.bfloat16),
            jax.ShapeDtypeStruct((tok_rows + meta_rows, 3 * width), jnp.bfloat16),
            jax.ShapeDtypeStruct((1, model_width), jnp.float32),
            jax.ShapeDtypeStruct((tok_rows, 2 * width), jnp.float32),
            jax.ShapeDtypeStruct((meta_rows, tok_rows), jnp.bfloat16),
        ],
        in_specs=[vmem] * 5,
        out_specs=[vmem] * 7,
    )(tokens, norm_gain[None, :], refusal_dir[None, :], expert_ids.T, gate_probs.T)


def route_kernel(exp_dev, meta_ref, picks_ref, weights_ref):
    n_seq, twice_k, tok_rows = meta_ref.shape
    top_k = twice_k // 2
    first = (lax.axis_index("seq") * exp_dev).astype(jnp.float32)
    exp_iota = lax.broadcasted_iota(jnp.int32, (exp_dev, tok_rows), 0).astype(jnp.float32) + first
    earlier = (
        lax.broadcasted_iota(jnp.int32, (tok_rows, tok_rows), 0)
        < lax.broadcasted_iota(jnp.int32, (tok_rows, tok_rows), 1)
    ).astype(jnp.float32).astype(jnp.bfloat16)
    slot_iota = lax.broadcasted_iota(jnp.int32, (exp_dev, SLOTS, tok_rows), 1).astype(jnp.float32)

    def place_pair(pair, carry):
        blocks = (2 * pair, 2 * pair + 1)
        hits, probs = [], []
        for j in blocks:
            meta = meta_ref[j].astype(jnp.float32)
            hit = jnp.zeros((exp_dev, tok_rows), jnp.float32)
            prob = jnp.zeros((exp_dev, tok_rows), jnp.float32)
            for k in range(top_k):
                same = meta[k : k + 1, :] == exp_iota
                hit = jnp.where(same, 1.0, hit)
                prob = jnp.where(same, meta[top_k + k : top_k + k + 1, :], prob)
            hits.append(hit)
            probs.append(prob)
        ranks = contract(jnp.concatenate(hits, axis=0).astype(jnp.bfloat16), earlier, 1, 0)
        for n, j in enumerate(blocks):
            rank = ranks[n * exp_dev : (n + 1) * exp_dev]
            slot = jnp.where(hits[n] > 0.0, rank, -1.0)
            here = slot[:, None, :] == slot_iota
            onehot = jnp.where(here, 1.0, 0.0).reshape(exp_dev * SLOTS, tok_rows)
            weight = jnp.where(here, probs[n][:, None, :], 0.0)
            weight = weight.reshape(exp_dev * SLOTS, tok_rows)
            picks_ref[j] = onehot.astype(jnp.bfloat16)
            weights_ref[j] = weight.T.astype(jnp.bfloat16)
        return carry

    lax.fori_loop(0, n_seq // 2, place_pair, 0)


def route(meta, exp_dev):
    n_seq, _, tok_rows = meta.shape
    vmem = pl.BlockSpec(memory_space=pltpu.VMEM)
    return pl.pallas_call(
        functools.partial(route_kernel, exp_dev),
        out_shape=[
            jax.ShapeDtypeStruct((n_seq, exp_dev * SLOTS, tok_rows), jnp.bfloat16),
            jax.ShapeDtypeStruct((n_seq, tok_rows, exp_dev * SLOTS), jnp.bfloat16),
        ],
        in_specs=[vmem],
        out_specs=[vmem] * 2,
        cost_estimate=pl.CostEstimate(
            flops=4_000_000_000, bytes_accessed=8 * n_seq * exp_dev * SLOTS * tok_rows,
            transcendentals=0,
        ),
    )(meta)


def most_rows(tok_rows):
    return tok_rows // 128 * 112


def moe_kernel(n_pieces, *refs):
    picks_hbm, weights_hbm, unit_ref, own_hbm = refs[:4]
    pieces_in = refs[4 : 4 + n_pieces]
    w_gate_hbm, w_up_hbm, w_down_hbm = refs[4 + n_pieces : 7 + n_pieces]
    out_refs = refs[7 + n_pieces : 13 + n_pieces]
    (picks, weights, w_in, w_down, toks, rows, hidden, mixed, table_sems, tok_sems, in_sems,
     down_sems) = refs[13 + n_pieces :]
    n_z, _, tok_rows, model_width = toks.shape
    n_seq = 2 * n_z
    exp_dev, hid_dev, _ = w_gate_hbm.shape
    width = model_width // 8
    slots_src = exp_dev * SLOTS
    rep = lax.axis_index("rep")
    split = most_rows(tok_rows)
    def in_copies(e):
        at = lax.rem(e, RING)
        return [
            pltpu.make_async_copy(
                src.at[e], w_in.at[at, pl.ds(i * hid_dev, hid_dev)], in_sems.at[i, at]
            )
            for i, src in enumerate((w_gate_hbm, w_up_hbm))
        ]

    def down_copy(e):
        return pltpu.make_async_copy(w_down_hbm.at[e], w_down.at[e], down_sems.at[e])

    tables = [
        pltpu.make_async_copy(picks_hbm, picks, table_sems.at[0]),
        pltpu.make_async_copy(weights_hbm, weights, table_sems.at[1]),
    ]
    tables[0].start()

    kinds = token_pieces(n_z)
    pltpu.make_async_copy(own_hbm, toks.at[0, 0], tok_sems.at[0, 0]).start()
    for i, piece in enumerate(pieces_in):
        blocks, runs = kinds[i % len(kinds)]
        for n, (color, dx) in enumerate(runs):
            cols = pl.ds(group_offset(rep, color, dx, i // len(kinds), width), width)
            for at, dz, count, dy in blocks:
                for k in range(count):
                    pltpu.make_async_copy(
                        piece.at[at + k, pl.ds(0, tok_rows), pl.ds(n * width, width)],
                        toks.at[dz + k, dy, :, cols],
                        tok_sems.at[dz + k, dy],
                    ).start()
    for e in range(min(RING, exp_dev)):
        for copy in in_copies(e):
            copy.start()
    tables[1].start()
    quarters = [slice(2 * q * width, 2 * (q + 1) * width) for q in range(4)]
    tables[0].wait()

    def pick(dz, carry):
        for dy in range(2):
            pltpu.make_async_copy(toks.at[dz, dy], toks.at[dz, dy], tok_sems.at[dz, dy]).wait()
        for dy in range(2):
            onehot = picks[2 * dz + dy]
            for cols in quarters:
                got = contract(onehot, toks[dz, dy, :, cols], 1, 0).astype(jnp.bfloat16)
                rows[2 * dz + dy, :, :, cols] = got.reshape(exp_dev, SLOTS, 2 * width)
        return carry

    lax.fori_loop(0, n_z, pick, 0)

    def widen(pair, carry):
        experts = (2 * pair, 2 * pair + 1)
        for e in experts:
            for copy in in_copies(e):
                copy.wait()
        taken = [rows[:, e].reshape(n_seq * SLOTS, model_width) for e in experts]
        both = [
            [
                contract(value, w_in[lax.rem(e, RING), i * hid_dev : (i + 1) * hid_dev], 1, 1)
                for i in range(2)
            ]
            for e, value in zip(experts, taken)
        ]
        for e, (gate_val, up_val) in zip(experts, both):
            hidden[e] = (gate_val / (1.0 + jnp.exp(-gate_val)) * up_val).astype(jnp.bfloat16)
        for e in experts:
            down_copy(e).start()

            @pl.when(e + RING < exp_dev)
            def _():
                for copy in in_copies(e + RING):
                    copy.start()

        return carry

    lax.fori_loop(0, exp_dev // 2, widen, 0)

    def narrow(pair, carry):
        experts = (2 * pair, 2 * pair + 1)
        for e in experts:
            down_copy(e).wait()
        for e in experts:
            for cols in quarters:
                piece = contract(hidden[e], w_down[e, :, cols], 1, 0).astype(jnp.bfloat16)
                rows[:, e, :, cols] = piece.reshape(n_seq, SLOTS, 2 * width)
        return carry

    lax.fori_loop(0, exp_dev // 2, narrow, 0)
    tables[1].wait()

    def combine(dz, carry):
        along = [jnp.zeros((tok_rows, 1), jnp.float32)] * 2
        for dy in range(2):
            j = 2 * dz + dy
            weight = weights[j]
            for cols in quarters:
                got = contract(weight, rows[j, :, :, cols].reshape(slots_src, 2 * width), 1, 0)
                mixed[dy, :, cols] = got
                along[dy] += jnp.sum(got * unit_ref[:, cols], axis=1, keepdims=True)
        for dy in range(2):
            for dc in range(2):
                far, near, rest = out_refs[3 * dc : 3 * dc + 3]
                for n, (color, dx) in enumerate(((0, 1), (0, 0), (1, 0), (1, 1))):
                    cols = pl.ds(group_offset(rep, color, dx, dc, width), width)
                    value = mixed[dy, :, cols] - along[dy] * unit_ref[:, cols]
                    value = value.astype(jnp.bfloat16)
                    rest[dz, dy, :, n * width : (n + 1) * width] = value[split:]
                    leaves, kind = (dy, 2 + dx) if color else (dx, dy)
                    (far if leaves else near)[kind, dz] = value[:split]
        return carry

    lax.fori_loop(0, n_z, combine, 0)


def moe_partial(picks, weights, unit_dir, own, pieces, w_gate, w_up, w_down):
    n_seq, _, tok_rows = picks.shape
    exp_dev, hid_dev, model_width = w_gate.shape
    width = model_width // 8
    vmem = pl.BlockSpec(memory_space=pltpu.VMEM)
    hbm = pl.BlockSpec(memory_space=pltpu.HBM)
    whole = pl.BlockSpec(memory_space=pl.ANY)
    n_pieces = len(pieces)
    pieces = [pltpu.with_memory_space_constraint(piece, pltpu.VMEM) for piece in pieces]
    picks, weights, own = [
        pltpu.with_memory_space_constraint(value, pltpu.HBM) for value in (picks, weights, own)
    ]
    n_z, split = n_seq // 2, most_rows(tok_rows)
    most = (4, n_z, split, width)
    rest = (n_z, 2, tok_rows - split, 4 * width)
    outs = [
        jax.ShapeDtypeStruct(shape, jnp.bfloat16) for _ in range(2) for shape in (most, most, rest)
    ]
    return pl.pallas_call(
        functools.partial(moe_kernel, n_pieces),
        out_shape=outs,
        in_specs=[hbm, hbm, vmem, hbm] + [whole] * n_pieces + [hbm] * 3,
        out_specs=[vmem] * len(outs),
        scratch_shapes=[
            pltpu.VMEM(picks.shape, jnp.bfloat16),
            pltpu.VMEM(weights.shape, jnp.bfloat16),
            pltpu.VMEM((RING, 2 * hid_dev, model_width), jnp.bfloat16),
            pltpu.VMEM(w_down.shape, jnp.bfloat16),
            pltpu.VMEM((n_z, 2, tok_rows, model_width), jnp.bfloat16),
            pltpu.VMEM((n_seq, exp_dev, SLOTS, model_width), jnp.bfloat16),
            pltpu.VMEM((exp_dev, n_seq * SLOTS, hid_dev), jnp.bfloat16),
            pltpu.VMEM((2, tok_rows, model_width), jnp.float32),
            pltpu.SemaphoreType.DMA((2,)),
            pltpu.SemaphoreType.DMA((n_z, 2)),
            pltpu.SemaphoreType.DMA((2, RING)),
            pltpu.SemaphoreType.DMA((exp_dev,)),
        ],
        compiler_params=pltpu.CompilerParams(vmem_limit_bytes=42 * 1024 * 1024),
        cost_estimate=pl.CostEstimate(
            flops=6 * n_seq * SLOTS * exp_dev * hid_dev * model_width,
            bytes_accessed=6 * exp_dev * hid_dev * model_width + 4 * n_seq * own.size,
            transcendentals=0,
        ),
    )(picks, weights, unit_dir, own, *pieces, w_gate, w_up, w_down)


def swap(value, axis, distance):
    size = lax.axis_size(axis)
    return lax.ppermute(value, axis, [(i, i ^ distance) for i in range(size)])


def added(*terms):
    return sum(term.astype(jnp.float32) for term in terms).astype(jnp.bfloat16)


def gathered(tokens, norm_gain, refusal_dir, expert_ids, gate_probs, w_gate, w_up, w_down):
    tok_rows, model_width = tokens.shape
    n_z = lax.axis_size("seq") // 2
    others = range(1, n_z)
    exp_dev = w_gate.shape[0]
    width = model_width // 8

    normed, second, first, to_y, unit_dir, base, meta = norm_and_base(
        tokens, norm_gain, refusal_dir, expert_ids, gate_probs
    )
    second = [swap(second, "seq", 2 * d) for d in others]
    from_y = swap(to_y[None], "seq", 1)
    first, second, from_y = lax.optimization_barrier((first, jnp.stack(second), from_y))
    first = jnp.stack([swap(first, "seq", 2 * d) for d in others])
    x_two = swap(second[:, :tok_rows], "rep", 2)
    y_one = swap(second, "seq", 1)
    y_two = swap(first, "seq", 1)
    x_one = swap(jnp.concatenate([from_y[:, :tok_rows, :width], first]), "rep", 2)
    to_y, to_core = lax.optimization_barrier((x_two, second))
    y_three = swap(to_y, "seq", 1)
    below = [meta, from_y[0, tok_rows:, :tok_rows]]
    for d in range(n_z - 1):
        below += [second[d, tok_rows:, :tok_rows], y_one[d, tok_rows:, :tok_rows]]
    picks, weights = route(jnp.stack(below), exp_dev)
    to_core_y, picks, weights = lax.optimization_barrier((from_y, picks, weights))
    early = [swap(piece, "rep", 1) for piece in (to_core, first, to_core_y)]
    x_three = swap(y_two, "rep", 2)
    last = [x_two, y_one, x_one, y_two, y_three, x_three]
    pieces = [second, first, from_y, *last, *early, *[swap(piece, "rep", 1) for piece in last]]

    sums = moe_partial(picks, weights, unit_dir, normed, pieces, w_gate, w_up, w_down)
    return (base + summed_up(sums[:3], sums[3:], width)).astype(jnp.bfloat16)


def summed_up(kept, sent, width):
    n_z = kept[0].shape[1]
    others = range(1, n_z)
    far, near, rest = zip(kept, [swap(piece, "rep", 1) for piece in sent])

    to_x, to_y, rest_kept = lax.optimization_barrier(
        (added(*[term[:2] for term in far]), added(*[term[2:] for term in far]), rest[0])
    )
    by_x, by_y = swap(to_x, "rep", 2), swap(to_y, "seq", 1)
    rest = added(rest_kept, rest[1])
    by_z = [swap(rest[d], "seq", 2 * d) for d in others]
    to_y, to_x, *by_z = lax.optimization_barrier(
        (
            added(*[term[1] for term in near], by_x[1]),
            added(*[term[3] for term in near], by_y[1]),
            *by_z,
        )
    )
    first_far, second_far = swap(to_y, "seq", 1), swap(to_x, "rep", 2)
    first = added(*[term[0] for term in near], by_x[0], first_far)
    second = added(*[term[2] for term in near], by_y[0], second_far)
    blocks = jnp.concatenate([first, second], axis=2)
    most = [swap(blocks[d], "seq", 2 * d) for d in reversed(others)] + [blocks[0]]
    rest = added(rest[0], *by_z)
    rest = added(rest[0], swap(rest[1], "seq", 1))
    far = jnp.concatenate([rest[:, :width], rest[:, 3 * width :]], axis=1)
    rest = [rest[:, width : 3 * width], swap(far, "rep", 2)]
    return jnp.concatenate(
        [sum(term.astype(jnp.float32) for term in terms) for terms in (most, rest)], axis=0
    )


def exchanged(tokens, norm_gain, refusal_dir, expert_ids, gate_probs, w_gate, w_up, w_down):
    tok_rows, model_width = tokens.shape
    top_k = expert_ids.shape[1]
    n_seq = lax.axis_size("seq")
    n_rep = lax.axis_size("rep")
    exp_dev = w_gate.shape[0]
    experts = exp_dev * n_seq
    slot_count = tok_rows * top_k
    part_width = model_width // n_rep
    tokens_f32 = tokens.astype(jnp.float32)
    inv_rms = lax.rsqrt(jnp.mean(tokens_f32 * tokens_f32, axis=1, keepdims=True) + 1e-06)
    normed = (tokens_f32 * inv_rms * norm_gain).astype(jnp.bfloat16)
    flat_ids = expert_ids.reshape(slot_count)
    onehot = (flat_ids[:, None] == jnp.arange(experts, dtype=jnp.int32)[None, :]).astype(jnp.int32)
    slot_rank = jnp.sum(jnp.cumsum(onehot, axis=0) * onehot, axis=1) - 1
    target = flat_ids * CAP + slot_rank
    repeated = jnp.broadcast_to(normed[:, None, :], (tok_rows, top_k, model_width)).reshape(
        slot_count, model_width
    )
    sendbuf = jnp.zeros((experts * CAP, model_width), jnp.bfloat16).at[target].set(repeated)
    sendbuf = sendbuf.reshape(n_seq, exp_dev, CAP, model_width)
    arrived = lax.all_to_all(sendbuf, "seq", split_axis=0, concat_axis=0, tiled=True)
    gate_val = jnp.einsum("secd,efd->secf", arrived, w_gate, preferred_element_type=jnp.float32)
    up_val = jnp.einsum("secd,efd->secf", arrived, w_up, preferred_element_type=jnp.float32)
    hidden = (jax.nn.silu(gate_val) * up_val).astype(jnp.bfloat16)
    pieces = jnp.einsum(
        "secf,efd->secd", hidden, w_down, preferred_element_type=jnp.float32
    ).astype(jnp.bfloat16)
    probs_flat = gate_probs.reshape(slot_count)[:, None]
    returned = lax.all_to_all(pieces, "seq", split_axis=0, concat_axis=0, tiled=True)
    returned = returned.reshape(experts * CAP, model_width)
    weighted = returned[target].astype(jnp.float32) * probs_flat
    moe_part = jnp.sum(weighted.reshape(tok_rows, top_k, model_width), axis=1)
    summed = lax.psum_scatter(
        moe_part.astype(jnp.bfloat16), "rep", scatter_dimension=1, tiled=True
    ).astype(jnp.float32)
    unit_dir = refusal_dir / jnp.sqrt(jnp.sum(refusal_dir * refusal_dir) + 1e-06)
    rep_offset = lax.axis_index("rep") * part_width
    unit_slice = lax.dynamic_slice_in_dim(unit_dir, rep_offset, part_width, 0)
    own_tokens = lax.dynamic_slice_in_dim(tokens_f32, rep_offset, part_width, 1)
    residual = own_tokens + summed
    along_dir = lax.psum(jnp.sum(residual * unit_slice, axis=1), "rep")
    return (residual - along_dir[:, None] * unit_slice).astype(jnp.bfloat16)


def local(tokens, norm_gain, refusal_dir, expert_ids, gate_probs, w_gate, w_up, w_down):
    plan = gathered if w_gate.shape[0] * CAP >= tokens.shape[0] else exchanged
    return plan(tokens, norm_gain, refusal_dir, expert_ids, gate_probs, w_gate, w_up, w_down)


def solution(mesh):
    placed = (
        P("seq", None),
        P(),
        P(),
        P("seq", None),
        P("seq", None),
        P("seq", "rep", None),
        P("seq", "rep", None),
        P("seq", "rep", None),
    )
    return jax.shard_map(
        local, mesh=mesh, in_specs=placed, out_specs=P("seq", "rep"), check_vma=False
    )
```

```python
import functools

import jax
import jax.numpy as jnp
from jax import lax
from jax.experimental import pallas as pl
from jax.experimental.pallas import tpu as pltpu
from jax.sharding import PartitionSpec as P

CAP = 12
SLOTS = 16
RING = 10


def contract(lhs, rhs, lhs_dim, rhs_dim):
    return lax.dot_general(
        lhs, rhs, (((lhs_dim,), (rhs_dim,)), ((), ())), preferred_element_type=jnp.float32
    )


def group_offset(rep, color, dx, dc, width):
    return pl.multiple_of((rep ^ (2 * dx + dc)) * 2 * width + color * width, width)


def token_pieces(n_z):
    near, far = (0, 1, n_z - 1, 0), (0, 1, n_z - 1, 1)
    return [
        ([near], [(1, 0)]),
        ([near], [(0, 0)]),
        ([(0, 0, 1, 1)], [(0, 0), (1, 0), (1, 1)]),
        ([near], [(1, 1)]),
        ([far], [(1, 0)]),
        ([(0, 0, 1, 1), (1, 1, n_z - 1, 0)], [(0, 1)]),
        ([far], [(0, 0)]),
        ([far], [(1, 1)]),
        ([far], [(0, 1)]),
    ]


def norm_kernel(
    tokens_ref, gain_ref, refusal_ref, ids_ref, probs_ref,
    normed_ref, second_ref, first_ref, to_y_ref, unit_ref, base_ref, meta_ref,
):
    tok_rows, model_width = tokens_ref.shape
    width = model_width // 8
    rep = lax.axis_index("rep")
    toks = tokens_ref[...].astype(jnp.float32)
    refusal = refusal_ref[...]
    unit = refusal / jnp.sqrt(jnp.sum(refusal * refusal, axis=1, keepdims=True) + 1e-06)
    unit_ref[...] = unit
    inv_rms = lax.rsqrt(jnp.mean(toks * toks, axis=1, keepdims=True) + 1e-06)
    normed_ref[...] = (toks * inv_rms * gain_ref[...]).astype(jnp.bfloat16)
    own = pl.ds(group_offset(rep, 0, 0, 0, width), 2 * width)
    other = pl.ds(group_offset(rep, 1, 1, 0, width), width)
    first_ref[...] = normed_ref[:, pl.ds(group_offset(rep, 0, 0, 0, width), width)]
    second_ref[:tok_rows] = normed_ref[:, pl.ds(group_offset(rep, 1, 0, 0, width), width)]
    to_y_ref[:tok_rows, : 2 * width] = normed_ref[:, own]
    to_y_ref[:tok_rows, 2 * width :] = normed_ref[:, other]
    meta = jnp.concatenate([ids_ref[...].astype(jnp.float32), probs_ref[...]], axis=0)
    meta = meta.astype(jnp.bfloat16)
    meta_ref[...] = meta
    for ref in (second_ref, to_y_ref):
        ref[tok_rows:] = jnp.zeros((meta.shape[0], ref.shape[1]), jnp.bfloat16)
        ref[tok_rows:, :tok_rows] = meta
    along = jnp.sum(toks * unit, axis=1, keepdims=True)
    base_ref[...] = tokens_ref[:, own].astype(jnp.float32) - along * unit_ref[:, own]


def norm_and_base(tokens, norm_gain, refusal_dir, expert_ids, gate_probs):
    tok_rows, model_width = tokens.shape
    width = model_width // 8
    meta_rows = 2 * expert_ids.shape[1]
    vmem = pl.BlockSpec(memory_space=pltpu.VMEM)
    return pl.pallas_call(
        norm_kernel,
        out_shape=[
            jax.ShapeDtypeStruct((tok_rows, model_width), jnp.bfloat16),
            jax.ShapeDtypeStruct((tok_rows + meta_rows, width), jnp.bfloat16),
            jax.ShapeDtypeStruct((tok_rows, width), jnp.bfloat16),
            jax.ShapeDtypeStruct((tok_rows + meta_rows, 3 * width), jnp.bfloat16),
            jax.ShapeDtypeStruct((1, model_width), jnp.float32),
            jax.ShapeDtypeStruct((tok_rows, 2 * width), jnp.float32),
            jax.ShapeDtypeStruct((meta_rows, tok_rows), jnp.bfloat16),
        ],
        in_specs=[vmem] * 5,
        out_specs=[vmem] * 7,
    )(tokens, norm_gain[None, :], refusal_dir[None, :], expert_ids.T, gate_probs.T)


def route_kernel(exp_dev, meta_ref, picks_ref, weights_ref):
    n_seq, twice_k, tok_rows = meta_ref.shape
    top_k = twice_k // 2
    first = (lax.axis_index("seq") * exp_dev).astype(jnp.float32)
    exp_iota = lax.broadcasted_iota(jnp.int32, (exp_dev, tok_rows), 0).astype(jnp.float32) + first
    earlier = (
        lax.broadcasted_iota(jnp.int32, (tok_rows, tok_rows), 0)
        < lax.broadcasted_iota(jnp.int32, (tok_rows, tok_rows), 1)
    ).astype(jnp.float32).astype(jnp.bfloat16)
    slot_iota = lax.broadcasted_iota(jnp.int32, (exp_dev, SLOTS, tok_rows), 1).astype(jnp.float32)

    def place_pair(pair, carry):
        blocks = (2 * pair, 2 * pair + 1)
        hits, probs = [], []
        for j in blocks:
            meta = meta_ref[j].astype(jnp.float32)
            hit = jnp.zeros((exp_dev, tok_rows), jnp.float32)
            prob = jnp.zeros((exp_dev, tok_rows), jnp.float32)
            for k in range(top_k):
                same = meta[k : k + 1, :] == exp_iota
                hit = jnp.where(same, 1.0, hit)
                prob = jnp.where(same, meta[top_k + k : top_k + k + 1, :], prob)
            hits.append(hit)
            probs.append(prob)
        ranks = contract(jnp.concatenate(hits, axis=0).astype(jnp.bfloat16), earlier, 1, 0)
        for n, j in enumerate(blocks):
            rank = ranks[n * exp_dev : (n + 1) * exp_dev]
            slot = jnp.where(hits[n] > 0.0, rank, -1.0)
            here = slot[:, None, :] == slot_iota
            onehot = jnp.where(here, 1.0, 0.0).reshape(exp_dev * SLOTS, tok_rows)
            weight = jnp.where(here, probs[n][:, None, :], 0.0)
            weight = weight.reshape(exp_dev * SLOTS, tok_rows)
            picks_ref[j] = onehot.astype(jnp.bfloat16)
            weights_ref[j] = weight.T.astype(jnp.bfloat16)
        return carry

    lax.fori_loop(0, n_seq // 2, place_pair, 0)


def route(meta, exp_dev):
    n_seq, _, tok_rows = meta.shape
    vmem = pl.BlockSpec(memory_space=pltpu.VMEM)
    return pl.pallas_call(
        functools.partial(route_kernel, exp_dev),
        out_shape=[
            jax.ShapeDtypeStruct((n_seq, exp_dev * SLOTS, tok_rows), jnp.bfloat16),
            jax.ShapeDtypeStruct((n_seq, tok_rows, exp_dev * SLOTS), jnp.bfloat16),
        ],
        in_specs=[vmem],
        out_specs=[vmem] * 2,
        cost_estimate=pl.CostEstimate(
            flops=4_000_000_000, bytes_accessed=8 * n_seq * exp_dev * SLOTS * tok_rows,
            transcendentals=0,
        ),
    )(meta)


def most_rows(tok_rows):
    return tok_rows // 128 * 112


def moe_kernel(n_pieces, *refs):
    picks_hbm, weights_hbm, unit_ref, own_hbm = refs[:4]
    pieces_in = refs[4 : 4 + n_pieces]
    w_gate_hbm, w_up_hbm, w_down_hbm = refs[4 + n_pieces : 7 + n_pieces]
    out_refs = refs[7 + n_pieces : 13 + n_pieces]
    (picks, weights, w_in, w_down, toks, rows, hidden, mixed, table_sems, tok_sems, in_sems,
     down_sems) = refs[13 + n_pieces :]
    n_z, _, tok_rows, model_width = toks.shape
    n_seq = 2 * n_z
    exp_dev, hid_dev, _ = w_gate_hbm.shape
    width = model_width // 8
    slots_src = exp_dev * SLOTS
    rep = lax.axis_index("rep")
    split = most_rows(tok_rows)
    def in_copies(e):
        at = lax.rem(e, RING)
        return [
            pltpu.make_async_copy(
                src.at[e], w_in.at[at, pl.ds(i * hid_dev, hid_dev)], in_sems.at[i, at]
            )
            for i, src in enumerate((w_gate_hbm, w_up_hbm))
        ]

    def down_copy(e):
        return pltpu.make_async_copy(w_down_hbm.at[e], w_down.at[e], down_sems.at[e])

    def start_down(e, carry):
        down_copy(e).start()
        return carry

    tables = [
        pltpu.make_async_copy(picks_hbm, picks, table_sems.at[0]),
        pltpu.make_async_copy(weights_hbm, weights, table_sems.at[1]),
    ]
    tables[0].start()

    kinds = token_pieces(n_z)
    pltpu.make_async_copy(own_hbm, toks.at[0, 0], tok_sems.at[0, 0]).start()
    for i, piece in enumerate(pieces_in):
        blocks, runs = kinds[i % len(kinds)]
        for n, (color, dx) in enumerate(runs):
            cols = pl.ds(group_offset(rep, color, dx, i // len(kinds), width), width)
            for at, dz, count, dy in blocks:
                for k in range(count):
                    pltpu.make_async_copy(
                        piece.at[at + k, pl.ds(0, tok_rows), pl.ds(n * width, width)],
                        toks.at[dz + k, dy, :, cols],
                        tok_sems.at[dz + k, dy],
                    ).start()
    for e in range(min(RING, exp_dev)):
        for copy in in_copies(e):
            copy.start()
    tables[1].start()
    quarters = [slice(2 * q * width, 2 * (q + 1) * width) for q in range(4)]
    tables[0].wait()

    def pick(dz, carry):
        for dy in range(2):
            pltpu.make_async_copy(toks.at[dz, dy], toks.at[dz, dy], tok_sems.at[dz, dy]).wait()
        for dy in range(2):
            onehot = picks[2 * dz + dy]
            for cols in quarters:
                got = contract(onehot, toks[dz, dy, :, cols], 1, 0).astype(jnp.bfloat16)
                rows[2 * dz + dy, :, :, cols] = got.reshape(exp_dev, SLOTS, 2 * width)
        return carry

    lax.fori_loop(0, n_z, pick, 0)

    def widen(pair, carry):
        experts = (2 * pair, 2 * pair + 1)
        for e in experts:
            for copy in in_copies(e):
                copy.wait()
        taken = [rows[:, e].reshape(n_seq * SLOTS, model_width) for e in experts]
        both = [
            [
                contract(value, w_in[lax.rem(e, RING), i * hid_dev : (i + 1) * hid_dev], 1, 1)
                for i in range(2)
            ]
            for e, value in zip(experts, taken)
        ]
        for e, (gate_val, up_val) in zip(experts, both):
            hidden[e] = (gate_val / (1.0 + jnp.exp(-gate_val)) * up_val).astype(jnp.bfloat16)
        for e in experts:

            @pl.when(e + RING < exp_dev)
            def _():
                for copy in in_copies(e + RING):
                    copy.start()

        @pl.when(pair == max((exp_dev - RING) // 2 - 1, 0))
        def _():
            lax.fori_loop(0, exp_dev, start_down, 0)

        return carry

    lax.fori_loop(0, exp_dev // 2, widen, 0)

    def narrow(pair, carry):
        experts = (2 * pair, 2 * pair + 1)
        for e in experts:
            down_copy(e).wait()
        for e in experts:
            for cols in quarters:
                piece = contract(hidden[e], w_down[e, :, cols], 1, 0).astype(jnp.bfloat16)
                rows[:, e, :, cols] = piece.reshape(n_seq, SLOTS, 2 * width)
        return carry

    lax.fori_loop(0, exp_dev // 2, narrow, 0)
    tables[1].wait()

    def combine(dz, carry):
        along = [jnp.zeros((tok_rows, 1), jnp.float32)] * 2
        for dy in range(2):
            j = 2 * dz + dy
            weight = weights[j]
            for cols in quarters:
                got = contract(weight, rows[j, :, :, cols].reshape(slots_src, 2 * width), 1, 0)
                mixed[dy, :, cols] = got
                along[dy] += jnp.sum(got * unit_ref[:, cols], axis=1, keepdims=True)
        for dy in range(2):
            for dc in range(2):
                far, near, rest = out_refs[3 * dc : 3 * dc + 3]
                for n, (color, dx) in enumerate(((0, 1), (0, 0), (1, 0), (1, 1))):
                    cols = pl.ds(group_offset(rep, color, dx, dc, width), width)
                    value = mixed[dy, :, cols] - along[dy] * unit_ref[:, cols]
                    value = value.astype(jnp.bfloat16)
                    rest[dz, dy, :, n * width : (n + 1) * width] = value[split:]
                    leaves, kind = (dy, 2 + dx) if color else (dx, dy)
                    (far if leaves else near)[kind, dz] = value[:split]
        return carry

    lax.fori_loop(0, n_z, combine, 0)


def moe_partial(picks, weights, unit_dir, own, pieces, w_gate, w_up, w_down):
    n_seq, _, tok_rows = picks.shape
    exp_dev, hid_dev, model_width = w_gate.shape
    width = model_width // 8
    vmem = pl.BlockSpec(memory_space=pltpu.VMEM)
    hbm = pl.BlockSpec(memory_space=pltpu.HBM)
    whole = pl.BlockSpec(memory_space=pl.ANY)
    n_pieces = len(pieces)
    pieces = [pltpu.with_memory_space_constraint(piece, pltpu.VMEM) for piece in pieces]
    picks, weights, own = [
        pltpu.with_memory_space_constraint(value, pltpu.HBM) for value in (picks, weights, own)
    ]
    n_z, split = n_seq // 2, most_rows(tok_rows)
    most = (4, n_z, split, width)
    rest = (n_z, 2, tok_rows - split, 4 * width)
    outs = [
        jax.ShapeDtypeStruct(shape, jnp.bfloat16) for _ in range(2) for shape in (most, most, rest)
    ]
    return pl.pallas_call(
        functools.partial(moe_kernel, n_pieces),
        out_shape=outs,
        in_specs=[hbm, hbm, vmem, hbm] + [whole] * n_pieces + [hbm] * 3,
        out_specs=[vmem] * len(outs),
        scratch_shapes=[
            pltpu.VMEM(picks.shape, jnp.bfloat16),
            pltpu.VMEM(weights.shape, jnp.bfloat16),
            pltpu.VMEM((RING, 2 * hid_dev, model_width), jnp.bfloat16),
            pltpu.VMEM(w_down.shape, jnp.bfloat16),
            pltpu.VMEM((n_z, 2, tok_rows, model_width), jnp.bfloat16),
            pltpu.VMEM((n_seq, exp_dev, SLOTS, model_width), jnp.bfloat16),
            pltpu.VMEM((exp_dev, n_seq * SLOTS, hid_dev), jnp.bfloat16),
            pltpu.VMEM((2, tok_rows, model_width), jnp.float32),
            pltpu.SemaphoreType.DMA((2,)),
            pltpu.SemaphoreType.DMA((n_z, 2)),
            pltpu.SemaphoreType.DMA((2, RING)),
            pltpu.SemaphoreType.DMA((exp_dev,)),
        ],
        compiler_params=pltpu.CompilerParams(vmem_limit_bytes=48 * 1024 * 1024),
        cost_estimate=pl.CostEstimate(
            flops=6 * n_seq * SLOTS * exp_dev * hid_dev * model_width,
            bytes_accessed=6 * exp_dev * hid_dev * model_width + 4 * n_seq * own.size,
            transcendentals=0,
        ),
    )(picks, weights, unit_dir, own, *pieces, w_gate, w_up, w_down)


def swap(value, axis, distance):
    size = lax.axis_size(axis)
    return lax.ppermute(value, axis, [(i, i ^ distance) for i in range(size)])


def added(*terms):
    return sum(term.astype(jnp.float32) for term in terms).astype(jnp.bfloat16)


def gathered(tokens, norm_gain, refusal_dir, expert_ids, gate_probs, w_gate, w_up, w_down):
    tok_rows, model_width = tokens.shape
    n_z = lax.axis_size("seq") // 2
    others = range(1, n_z)
    exp_dev = w_gate.shape[0]
    width = model_width // 8

    normed, second, first, to_y, unit_dir, base, meta = norm_and_base(
        tokens, norm_gain, refusal_dir, expert_ids, gate_probs
    )
    second = [swap(second, "seq", 2 * d) for d in others]
    from_y = swap(to_y[None], "seq", 1)
    first, second, from_y = lax.optimization_barrier((first, jnp.stack(second), from_y))
    first = jnp.stack([swap(first, "seq", 2 * d) for d in others])
    x_two = swap(second[:, :tok_rows], "rep", 2)
    y_one = swap(second, "seq", 1)
    y_two = swap(first, "seq", 1)
    x_one = swap(jnp.concatenate([from_y[:, :tok_rows, :width], first]), "rep", 2)
    to_y, to_core = lax.optimization_barrier((x_two, second))
    y_three = swap(to_y, "seq", 1)
    below = [meta, from_y[0, tok_rows:, :tok_rows]]
    for d in range(n_z - 1):
        below += [second[d, tok_rows:, :tok_rows], y_one[d, tok_rows:, :tok_rows]]
    picks, weights = route(jnp.stack(below), exp_dev)
    to_core_y, picks, weights = lax.optimization_barrier((from_y, picks, weights))
    early = [swap(piece, "rep", 1) for piece in (to_core, first, to_core_y)]
    x_three = swap(y_two, "rep", 2)
    last = [x_two, y_one, x_one, y_two, y_three, x_three]
    pieces = [second, first, from_y, *last, *early, *[swap(piece, "rep", 1) for piece in last]]

    sums = moe_partial(picks, weights, unit_dir, normed, pieces, w_gate, w_up, w_down)
    return (base + summed_up(sums[:3], sums[3:], width)).astype(jnp.bfloat16)


def summed_up(kept, sent, width):
    n_z = kept[0].shape[1]
    others = range(1, n_z)
    far, near, rest = zip(kept, [swap(piece, "rep", 1) for piece in sent])

    to_x, to_y, rest_kept = lax.optimization_barrier(
        (added(*[term[:2] for term in far]), added(*[term[2:] for term in far]), rest[0])
    )
    by_x, by_y = swap(to_x, "rep", 2), swap(to_y, "seq", 1)
    rest = added(rest_kept, rest[1])
    by_z = [swap(rest[d], "seq", 2 * d) for d in others]
    to_y, to_x, *by_z = lax.optimization_barrier(
        (
            added(*[term[1] for term in near], by_x[1]),
            added(*[term[3] for term in near], by_y[1]),
            *by_z,
        )
    )
    first_far, second_far = swap(to_y, "seq", 1), swap(to_x, "rep", 2)
    first = added(*[term[0] for term in near], by_x[0], first_far)
    second = added(*[term[2] for term in near], by_y[0], second_far)
    blocks = jnp.concatenate([first, second], axis=2)
    most = [swap(blocks[d], "seq", 2 * d) for d in reversed(others)] + [blocks[0]]
    rest = added(rest[0], *by_z)
    rest = added(rest[0], swap(rest[1], "seq", 1))
    far = jnp.concatenate([rest[:, :width], rest[:, 3 * width :]], axis=1)
    rest = [rest[:, width : 3 * width], swap(far, "rep", 2)]
    return jnp.concatenate(
        [sum(term.astype(jnp.float32) for term in terms) for terms in (most, rest)], axis=0
    )


def exchanged(tokens, norm_gain, refusal_dir, expert_ids, gate_probs, w_gate, w_up, w_down):
    tok_rows, model_width = tokens.shape
    top_k = expert_ids.shape[1]
    n_seq = lax.axis_size("seq")
    n_rep = lax.axis_size("rep")
    exp_dev = w_gate.shape[0]
    experts = exp_dev * n_seq
    slot_count = tok_rows * top_k
    part_width = model_width // n_rep
    tokens_f32 = tokens.astype(jnp.float32)
    inv_rms = lax.rsqrt(jnp.mean(tokens_f32 * tokens_f32, axis=1, keepdims=True) + 1e-06)
    normed = (tokens_f32 * inv_rms * norm_gain).astype(jnp.bfloat16)
    flat_ids = expert_ids.reshape(slot_count)
    onehot = (flat_ids[:, None] == jnp.arange(experts, dtype=jnp.int32)[None, :]).astype(jnp.int32)
    slot_rank = jnp.sum(jnp.cumsum(onehot, axis=0) * onehot, axis=1) - 1
    target = flat_ids * CAP + slot_rank
    repeated = jnp.broadcast_to(normed[:, None, :], (tok_rows, top_k, model_width)).reshape(
        slot_count, model_width
    )
    sendbuf = jnp.zeros((experts * CAP, model_width), jnp.bfloat16).at[target].set(repeated)
    sendbuf = sendbuf.reshape(n_seq, exp_dev, CAP, model_width)
    arrived = lax.all_to_all(sendbuf, "seq", split_axis=0, concat_axis=0, tiled=True)
    gate_val = jnp.einsum("secd,efd->secf", arrived, w_gate, preferred_element_type=jnp.float32)
    up_val = jnp.einsum("secd,efd->secf", arrived, w_up, preferred_element_type=jnp.float32)
    hidden = (jax.nn.silu(gate_val) * up_val).astype(jnp.bfloat16)
    pieces = jnp.einsum(
        "secf,efd->secd", hidden, w_down, preferred_element_type=jnp.float32
    ).astype(jnp.bfloat16)
    probs_flat = gate_probs.reshape(slot_count)[:, None]
    returned = lax.all_to_all(pieces, "seq", split_axis=0, concat_axis=0, tiled=True)
    returned = returned.reshape(experts * CAP, model_width)
    weighted = returned[target].astype(jnp.float32) * probs_flat
    moe_part = jnp.sum(weighted.reshape(tok_rows, top_k, model_width), axis=1)
    summed = lax.psum_scatter(
        moe_part.astype(jnp.bfloat16), "rep", scatter_dimension=1, tiled=True
    ).astype(jnp.float32)
    unit_dir = refusal_dir / jnp.sqrt(jnp.sum(refusal_dir * refusal_dir) + 1e-06)
    rep_offset = lax.axis_index("rep") * part_width
    unit_slice = lax.dynamic_slice_in_dim(unit_dir, rep_offset, part_width, 0)
    own_tokens = lax.dynamic_slice_in_dim(tokens_f32, rep_offset, part_width, 1)
    residual = own_tokens + summed
    along_dir = lax.psum(jnp.sum(residual * unit_slice, axis=1), "rep")
    return (residual - along_dir[:, None] * unit_slice).astype(jnp.bfloat16)


def local(tokens, norm_gain, refusal_dir, expert_ids, gate_probs, w_gate, w_up, w_down):
    plan = gathered if w_gate.shape[0] * CAP >= tokens.shape[0] else exchanged
    return plan(tokens, norm_gain, refusal_dir, expert_ids, gate_probs, w_gate, w_up, w_down)


def solution(mesh):
    placed = (
        P("seq", None),
        P(),
        P(),
        P("seq", None),
        P("seq", None),
        P("seq", "rep", None),
        P("seq", "rep", None),
        P("seq", "rep", None),
    )
    return jax.shard_map(
        local, mesh=mesh, in_specs=placed, out_specs=P("seq", "rep"), check_vma=False
    )
```

```python
import functools

import jax
import jax.numpy as jnp
from jax import lax
from jax.experimental import pallas as pl
from jax.experimental.pallas import tpu as pltpu
from jax.sharding import PartitionSpec as P

CAP = 12
SLOTS = 16
RING = 8


def contract(lhs, rhs, lhs_dim, rhs_dim):
    return lax.dot_general(
        lhs, rhs, (((lhs_dim,), (rhs_dim,)), ((), ())), preferred_element_type=jnp.float32
    )


def group_offset(rep, color, dx, dc, width):
    return pl.multiple_of((rep ^ (2 * dx + dc)) * 2 * width + color * width, width)


def token_pieces(n_z):
    near, far = (0, 1, n_z - 1, 0), (0, 1, n_z - 1, 1)
    return [
        ([near], [(1, 0)]),
        ([near], [(0, 0)]),
        ([(0, 0, 1, 1)], [(0, 0), (1, 0), (1, 1)]),
        ([near], [(1, 1)]),
        ([far], [(1, 0)]),
        ([(0, 0, 1, 1), (1, 1, n_z - 1, 0)], [(0, 1)]),
        ([far], [(0, 0)]),
        ([far], [(1, 1)]),
        ([far], [(0, 1)]),
    ]


def norm_kernel(
    tokens_ref, gain_ref, refusal_ref, ids_ref, probs_ref,
    normed_ref, second_ref, first_ref, to_y_ref, unit_ref, base_ref, meta_ref,
):
    tok_rows, model_width = tokens_ref.shape
    width = model_width // 8
    rep = lax.axis_index("rep")
    toks = tokens_ref[...].astype(jnp.float32)
    refusal = refusal_ref[...]
    unit = refusal / jnp.sqrt(jnp.sum(refusal * refusal, axis=1, keepdims=True) + 1e-06)
    unit_ref[...] = unit
    inv_rms = lax.rsqrt(jnp.mean(toks * toks, axis=1, keepdims=True) + 1e-06)
    normed_ref[...] = (toks * inv_rms * gain_ref[...]).astype(jnp.bfloat16)
    own = pl.ds(group_offset(rep, 0, 0, 0, width), 2 * width)
    other = pl.ds(group_offset(rep, 1, 1, 0, width), width)
    first_ref[...] = normed_ref[:, pl.ds(group_offset(rep, 0, 0, 0, width), width)]
    second_ref[:tok_rows] = normed_ref[:, pl.ds(group_offset(rep, 1, 0, 0, width), width)]
    to_y_ref[:tok_rows, : 2 * width] = normed_ref[:, own]
    to_y_ref[:tok_rows, 2 * width :] = normed_ref[:, other]
    meta = jnp.concatenate([ids_ref[...].astype(jnp.float32), probs_ref[...]], axis=0)
    meta = meta.astype(jnp.bfloat16)
    meta_ref[...] = meta
    for ref in (second_ref, to_y_ref):
        ref[tok_rows:] = jnp.zeros((meta.shape[0], ref.shape[1]), jnp.bfloat16)
        ref[tok_rows:, :tok_rows] = meta
    along = jnp.sum(toks * unit, axis=1, keepdims=True)
    base_ref[...] = tokens_ref[:, own].astype(jnp.float32) - along * unit_ref[:, own]


def norm_and_base(tokens, norm_gain, refusal_dir, expert_ids, gate_probs):
    tok_rows, model_width = tokens.shape
    width = model_width // 8
    meta_rows = 2 * expert_ids.shape[1]
    vmem = pl.BlockSpec(memory_space=pltpu.VMEM)
    return pl.pallas_call(
        norm_kernel,
        out_shape=[
            jax.ShapeDtypeStruct((tok_rows, model_width), jnp.bfloat16),
            jax.ShapeDtypeStruct((tok_rows + meta_rows, width), jnp.bfloat16),
            jax.ShapeDtypeStruct((tok_rows, width), jnp.bfloat16),
            jax.ShapeDtypeStruct((tok_rows + meta_rows, 3 * width), jnp.bfloat16),
            jax.ShapeDtypeStruct((1, model_width), jnp.float32),
            jax.ShapeDtypeStruct((tok_rows, 2 * width), jnp.float32),
            jax.ShapeDtypeStruct((meta_rows, tok_rows), jnp.bfloat16),
        ],
        in_specs=[vmem] * 5,
        out_specs=[vmem] * 7,
    )(tokens, norm_gain[None, :], refusal_dir[None, :], expert_ids.T, gate_probs.T)


def route_kernel(exp_dev, meta_ref, picks_ref, weights_ref):
    n_seq, twice_k, tok_rows = meta_ref.shape
    top_k = twice_k // 2
    first = (lax.axis_index("seq") * exp_dev).astype(jnp.float32)
    exp_iota = lax.broadcasted_iota(jnp.int32, (exp_dev, tok_rows), 0).astype(jnp.float32) + first
    earlier = (
        lax.broadcasted_iota(jnp.int32, (tok_rows, tok_rows), 0)
        < lax.broadcasted_iota(jnp.int32, (tok_rows, tok_rows), 1)
    ).astype(jnp.float32).astype(jnp.bfloat16)
    slot_iota = lax.broadcasted_iota(jnp.int32, (exp_dev, SLOTS, tok_rows), 1).astype(jnp.float32)

    def place_pair(pair, carry):
        blocks = (2 * pair, 2 * pair + 1)
        hits, probs = [], []
        for j in blocks:
            meta = meta_ref[j].astype(jnp.float32)
            hit = jnp.zeros((exp_dev, tok_rows), jnp.float32)
            prob = jnp.zeros((exp_dev, tok_rows), jnp.float32)
            for k in range(top_k):
                same = meta[k : k + 1, :] == exp_iota
                hit = jnp.where(same, 1.0, hit)
                prob = jnp.where(same, meta[top_k + k : top_k + k + 1, :], prob)
            hits.append(hit)
            probs.append(prob)
        ranks = contract(jnp.concatenate(hits, axis=0).astype(jnp.bfloat16), earlier, 1, 0)
        for n, j in enumerate(blocks):
            rank = ranks[n * exp_dev : (n + 1) * exp_dev]
            slot = jnp.where(hits[n] > 0.0, rank, -1.0)
            here = slot[:, None, :] == slot_iota
            onehot = jnp.where(here, 1.0, 0.0).reshape(exp_dev * SLOTS, tok_rows)
            weight = jnp.where(here, probs[n][:, None, :], 0.0)
            weight = weight.reshape(exp_dev * SLOTS, tok_rows)
            picks_ref[j] = onehot.astype(jnp.bfloat16)
            weights_ref[j] = weight.T.astype(jnp.bfloat16)
        return carry

    lax.fori_loop(0, n_seq // 2, place_pair, 0)


def route(meta, exp_dev):
    n_seq, _, tok_rows = meta.shape
    vmem = pl.BlockSpec(memory_space=pltpu.VMEM)
    return pl.pallas_call(
        functools.partial(route_kernel, exp_dev),
        out_shape=[
            jax.ShapeDtypeStruct((n_seq, exp_dev * SLOTS, tok_rows), jnp.bfloat16),
            jax.ShapeDtypeStruct((n_seq, tok_rows, exp_dev * SLOTS), jnp.bfloat16),
        ],
        in_specs=[vmem],
        out_specs=[vmem] * 2,
        cost_estimate=pl.CostEstimate(
            flops=4_000_000_000, bytes_accessed=8 * n_seq * exp_dev * SLOTS * tok_rows,
            transcendentals=0,
        ),
    )(meta)


def most_rows(tok_rows):
    return tok_rows // 128 * 112


def moe_kernel(n_pieces, *refs):
    picks_hbm, weights_hbm, unit_ref, own_hbm = refs[:4]
    pieces_in = refs[4 : 4 + n_pieces]
    w_gate_hbm, w_up_hbm, w_down_hbm = refs[4 + n_pieces : 7 + n_pieces]
    out_refs = refs[7 + n_pieces : 13 + n_pieces]
    (picks, weights, w_in, w_down, toks, rows, hidden, mixed, table_sems, tok_sems, in_sems,
     down_sems) = refs[13 + n_pieces :]
    n_z, _, tok_rows, model_width = toks.shape
    n_seq = 2 * n_z
    exp_dev, hid_dev, _ = w_gate_hbm.shape
    width = model_width // 8
    slots_src = exp_dev * SLOTS
    rep = lax.axis_index("rep")
    split = most_rows(tok_rows)
    def in_copies(e):
        at = lax.rem(e, RING)
        return [
            pltpu.make_async_copy(
                src.at[e], w_in.at[at, pl.ds(i * hid_dev, hid_dev)], in_sems.at[i, at]
            )
            for i, src in enumerate((w_gate_hbm, w_up_hbm))
        ]

    def down_copy(e):
        return pltpu.make_async_copy(w_down_hbm.at[e], w_down.at[e], down_sems.at[e])

    tables = [
        pltpu.make_async_copy(picks_hbm, picks, table_sems.at[0]),
        pltpu.make_async_copy(weights_hbm, weights, table_sems.at[1]),
    ]
    tables[0].start()

    kinds = token_pieces(n_z)
    pltpu.make_async_copy(own_hbm, toks.at[0, 0], tok_sems.at[0, 0]).start()
    for i, piece in enumerate(pieces_in):
        blocks, runs = kinds[i % len(kinds)]
        for n, (color, dx) in enumerate(runs):
            cols = pl.ds(group_offset(rep, color, dx, i // len(kinds), width), width)
            for at, dz, count, dy in blocks:
                for k in range(count):
                    pltpu.make_async_copy(
                        piece.at[at + k, pl.ds(0, tok_rows), pl.ds(n * width, width)],
                        toks.at[dz + k, dy, :, cols],
                        tok_sems.at[dz + k, dy],
                    ).start()
    for e in range(min(RING, exp_dev)):
        for copy in in_copies(e):
            copy.start()
    for e in range(exp_dev // 2):
        down_copy(e).start()
    tables[1].start()
    quarters = [slice(2 * q * width, 2 * (q + 1) * width) for q in range(4)]
    tables[0].wait()

    def pick(dz, carry):
        for dy in range(2):
            pltpu.make_async_copy(toks.at[dz, dy], toks.at[dz, dy], tok_sems.at[dz, dy]).wait()
        for dy in range(2):
            onehot = picks[2 * dz + dy]
            for cols in quarters:
                got = contract(onehot, toks[dz, dy, :, cols], 1, 0).astype(jnp.bfloat16)
                rows[2 * dz + dy, :, :, cols] = got.reshape(exp_dev, SLOTS, 2 * width)
        return carry

    lax.fori_loop(0, n_z, pick, 0)

    def widen(pair, carry):
        experts = (2 * pair, 2 * pair + 1)
        for e in experts:
            for copy in in_copies(e):
                copy.wait()
        taken = [rows[:, e].reshape(n_seq * SLOTS, model_width) for e in experts]
        both = [
            [
                contract(value, w_in[lax.rem(e, RING), i * hid_dev : (i + 1) * hid_dev], 1, 1)
                for i in range(2)
            ]
            for e, value in zip(experts, taken)
        ]
        for e, (gate_val, up_val) in zip(experts, both):
            hidden[e] = (gate_val / (1.0 + jnp.exp(-gate_val)) * up_val).astype(jnp.bfloat16)
        down_copy(exp_dev // 2 + pair).start()
        for e in experts:

            @pl.when(e + RING < exp_dev)
            def _():
                for copy in in_copies(e + RING):
                    copy.start()

        return carry

    lax.fori_loop(0, exp_dev // 2, widen, 0)

    def narrow(pair, carry):
        experts = (2 * pair, 2 * pair + 1)
        for e in experts:
            down_copy(e).wait()
        for e in experts:
            for cols in quarters:
                piece = contract(hidden[e], w_down[e, :, cols], 1, 0).astype(jnp.bfloat16)
                rows[:, e, :, cols] = piece.reshape(n_seq, SLOTS, 2 * width)
        return carry

    lax.fori_loop(0, exp_dev // 2, narrow, 0)
    tables[1].wait()

    def combine(dz, carry):
        along = [jnp.zeros((tok_rows, 1), jnp.float32)] * 2
        for dy in range(2):
            j = 2 * dz + dy
            weight = weights[j]
            for cols in quarters:
                got = contract(weight, rows[j, :, :, cols].reshape(slots_src, 2 * width), 1, 0)
                mixed[dy, :, cols] = got
                along[dy] += jnp.sum(got * unit_ref[:, cols], axis=1, keepdims=True)
        for dy in range(2):
            for dc in range(2):
                far, near, rest = out_refs[3 * dc : 3 * dc + 3]
                for n, (color, dx) in enumerate(((0, 1), (0, 0), (1, 0), (1, 1))):
                    cols = pl.ds(group_offset(rep, color, dx, dc, width), width)
                    value = mixed[dy, :, cols] - along[dy] * unit_ref[:, cols]
                    value = value.astype(jnp.bfloat16)
                    rest[dz, dy, :, n * width : (n + 1) * width] = value[split:]
                    leaves, kind = (dy, 2 + dx) if color else (dx, dy)
                    (far if leaves else near)[kind, dz] = value[:split]
        return carry

    lax.fori_loop(0, n_z, combine, 0)


def moe_partial(picks, weights, unit_dir, own, pieces, w_gate, w_up, w_down):
    n_seq, _, tok_rows = picks.shape
    exp_dev, hid_dev, model_width = w_gate.shape
    width = model_width // 8
    vmem = pl.BlockSpec(memory_space=pltpu.VMEM)
    hbm = pl.BlockSpec(memory_space=pltpu.HBM)
    whole = pl.BlockSpec(memory_space=pl.ANY)
    n_pieces = len(pieces)
    pieces = [pltpu.with_memory_space_constraint(piece, pltpu.VMEM) for piece in pieces]
    picks, weights, own = [
        pltpu.with_memory_space_constraint(value, pltpu.HBM) for value in (picks, weights, own)
    ]
    n_z, split = n_seq // 2, most_rows(tok_rows)
    most = (4, n_z, split, width)
    rest = (n_z, 2, tok_rows - split, 4 * width)
    outs = [
        jax.ShapeDtypeStruct(shape, jnp.bfloat16) for _ in range(2) for shape in (most, most, rest)
    ]
    return pl.pallas_call(
        functools.partial(moe_kernel, n_pieces),
        out_shape=outs,
        in_specs=[hbm, hbm, vmem, hbm] + [whole] * n_pieces + [hbm] * 3,
        out_specs=[vmem] * len(outs),
        scratch_shapes=[
            pltpu.VMEM(picks.shape, jnp.bfloat16),
            pltpu.VMEM(weights.shape, jnp.bfloat16),
            pltpu.VMEM((RING, 2 * hid_dev, model_width), jnp.bfloat16),
            pltpu.VMEM(w_down.shape, jnp.bfloat16),
            pltpu.VMEM((n_z, 2, tok_rows, model_width), jnp.bfloat16),
            pltpu.VMEM((n_seq, exp_dev, SLOTS, model_width), jnp.bfloat16),
            pltpu.VMEM((exp_dev, n_seq * SLOTS, hid_dev), jnp.bfloat16),
            pltpu.VMEM((2, tok_rows, model_width), jnp.float32),
            pltpu.SemaphoreType.DMA((2,)),
            pltpu.SemaphoreType.DMA((n_z, 2)),
            pltpu.SemaphoreType.DMA((2, RING)),
            pltpu.SemaphoreType.DMA((exp_dev,)),
        ],
        compiler_params=pltpu.CompilerParams(vmem_limit_bytes=45 * 1024 * 1024),
        cost_estimate=pl.CostEstimate(
            flops=6 * n_seq * SLOTS * exp_dev * hid_dev * model_width,
            bytes_accessed=6 * exp_dev * hid_dev * model_width + 4 * n_seq * own.size,
            transcendentals=0,
        ),
    )(picks, weights, unit_dir, own, *pieces, w_gate, w_up, w_down)


def swap(value, axis, distance):
    size = lax.axis_size(axis)
    return lax.ppermute(value, axis, [(i, i ^ distance) for i in range(size)])


def added(*terms):
    return sum(term.astype(jnp.float32) for term in terms).astype(jnp.bfloat16)


def gathered(tokens, norm_gain, refusal_dir, expert_ids, gate_probs, w_gate, w_up, w_down):
    tok_rows, model_width = tokens.shape
    n_z = lax.axis_size("seq") // 2
    others = range(1, n_z)
    exp_dev = w_gate.shape[0]
    width = model_width // 8

    normed, second, first, to_y, unit_dir, base, meta = norm_and_base(
        tokens, norm_gain, refusal_dir, expert_ids, gate_probs
    )
    second = [swap(second, "seq", 2 * d) for d in others]
    from_y = swap(to_y[None], "seq", 1)
    first, second, from_y = lax.optimization_barrier((first, jnp.stack(second), from_y))
    first = jnp.stack([swap(first, "seq", 2 * d) for d in others])
    x_two = swap(second[:, :tok_rows], "rep", 2)
    y_one = swap(second, "seq", 1)
    y_two = swap(first, "seq", 1)
    x_one = swap(jnp.concatenate([from_y[:, :tok_rows, :width], first]), "rep", 2)
    to_y, to_core = lax.optimization_barrier((x_two, second))
    y_three = swap(to_y, "seq", 1)
    below = [meta, from_y[0, tok_rows:, :tok_rows]]
    for d in range(n_z - 1):
        below += [second[d, tok_rows:, :tok_rows], y_one[d, tok_rows:, :tok_rows]]
    picks, weights = route(jnp.stack(below), exp_dev)
    to_core_y, picks, weights = lax.optimization_barrier((from_y, picks, weights))
    early = [swap(piece, "rep", 1) for piece in (to_core, first, to_core_y)]
    x_three = swap(y_two, "rep", 2)
    last = [x_two, y_one, x_one, y_two, y_three, x_three]
    pieces = [second, first, from_y, *last, *early, *[swap(piece, "rep", 1) for piece in last]]

    sums = moe_partial(picks, weights, unit_dir, normed, pieces, w_gate, w_up, w_down)
    return (base + summed_up(sums[:3], sums[3:], width)).astype(jnp.bfloat16)


def summed_up(kept, sent, width):
    n_z = kept[0].shape[1]
    others = range(1, n_z)
    far, near, rest = zip(kept, [swap(piece, "rep", 1) for piece in sent])

    to_x, to_y, rest_kept = lax.optimization_barrier(
        (added(*[term[:2] for term in far]), added(*[term[2:] for term in far]), rest[0])
    )
    by_x, by_y = swap(to_x, "rep", 2), swap(to_y, "seq", 1)
    rest = added(rest_kept, rest[1])
    by_z = [swap(rest[d], "seq", 2 * d) for d in others]
    to_y, to_x, *by_z = lax.optimization_barrier(
        (
            added(*[term[1] for term in near], by_x[1]),
            added(*[term[3] for term in near], by_y[1]),
            *by_z,
        )
    )
    first_far, second_far = swap(to_y, "seq", 1), swap(to_x, "rep", 2)
    first = added(*[term[0] for term in near], by_x[0], first_far)
    second = added(*[term[2] for term in near], by_y[0], second_far)
    blocks = jnp.concatenate([first, second], axis=2)
    most = [swap(blocks[d], "seq", 2 * d) for d in reversed(others)] + [blocks[0]]
    rest = added(rest[0], *by_z)
    rest = added(rest[0], swap(rest[1], "seq", 1))
    far = jnp.concatenate([rest[:, :width], rest[:, 3 * width :]], axis=1)
    rest = [rest[:, width : 3 * width], swap(far, "rep", 2)]
    return jnp.concatenate(
        [sum(term.astype(jnp.float32) for term in terms) for terms in (most, rest)], axis=0
    )


def exchanged(tokens, norm_gain, refusal_dir, expert_ids, gate_probs, w_gate, w_up, w_down):
    tok_rows, model_width = tokens.shape
    top_k = expert_ids.shape[1]
    n_seq = lax.axis_size("seq")
    n_rep = lax.axis_size("rep")
    exp_dev = w_gate.shape[0]
    experts = exp_dev * n_seq
    slot_count = tok_rows * top_k
    part_width = model_width // n_rep
    tokens_f32 = tokens.astype(jnp.float32)
    inv_rms = lax.rsqrt(jnp.mean(tokens_f32 * tokens_f32, axis=1, keepdims=True) + 1e-06)
    normed = (tokens_f32 * inv_rms * norm_gain).astype(jnp.bfloat16)
    flat_ids = expert_ids.reshape(slot_count)
    onehot = (flat_ids[:, None] == jnp.arange(experts, dtype=jnp.int32)[None, :]).astype(jnp.int32)
    slot_rank = jnp.sum(jnp.cumsum(onehot, axis=0) * onehot, axis=1) - 1
    target = flat_ids * CAP + slot_rank
    repeated = jnp.broadcast_to(normed[:, None, :], (tok_rows, top_k, model_width)).reshape(
        slot_count, model_width
    )
    sendbuf = jnp.zeros((experts * CAP, model_width), jnp.bfloat16).at[target].set(repeated)
    sendbuf = sendbuf.reshape(n_seq, exp_dev, CAP, model_width)
    arrived = lax.all_to_all(sendbuf, "seq", split_axis=0, concat_axis=0, tiled=True)
    gate_val = jnp.einsum("secd,efd->secf", arrived, w_gate, preferred_element_type=jnp.float32)
    up_val = jnp.einsum("secd,efd->secf", arrived, w_up, preferred_element_type=jnp.float32)
    hidden = (jax.nn.silu(gate_val) * up_val).astype(jnp.bfloat16)
    pieces = jnp.einsum(
        "secf,efd->secd", hidden, w_down, preferred_element_type=jnp.float32
    ).astype(jnp.bfloat16)
    probs_flat = gate_probs.reshape(slot_count)[:, None]
    returned = lax.all_to_all(pieces, "seq", split_axis=0, concat_axis=0, tiled=True)
    returned = returned.reshape(experts * CAP, model_width)
    weighted = returned[target].astype(jnp.float32) * probs_flat
    moe_part = jnp.sum(weighted.reshape(tok_rows, top_k, model_width), axis=1)
    summed = lax.psum_scatter(
        moe_part.astype(jnp.bfloat16), "rep", scatter_dimension=1, tiled=True
    ).astype(jnp.float32)
    unit_dir = refusal_dir / jnp.sqrt(jnp.sum(refusal_dir * refusal_dir) + 1e-06)
    rep_offset = lax.axis_index("rep") * part_width
    unit_slice = lax.dynamic_slice_in_dim(unit_dir, rep_offset, part_width, 0)
    own_tokens = lax.dynamic_slice_in_dim(tokens_f32, rep_offset, part_width, 1)
    residual = own_tokens + summed
    along_dir = lax.psum(jnp.sum(residual * unit_slice, axis=1), "rep")
    return (residual - along_dir[:, None] * unit_slice).astype(jnp.bfloat16)


def local(tokens, norm_gain, refusal_dir, expert_ids, gate_probs, w_gate, w_up, w_down):
    plan = gathered if w_gate.shape[0] * CAP >= tokens.shape[0] else exchanged
    return plan(tokens, norm_gain, refusal_dir, expert_ids, gate_probs, w_gate, w_up, w_down)


def solution(mesh):
    placed = (
        P("seq", None),
        P(),
        P(),
        P("seq", None),
        P("seq", None),
        P("seq", "rep", None),
        P("seq", "rep", None),
        P("seq", "rep", None),
    )
    return jax.shard_map(
        local, mesh=mesh, in_specs=placed, out_specs=P("seq", "rep"), check_vma=False
    )
```

```python
import functools

import jax
import jax.numpy as jnp
from jax import lax
from jax.experimental import pallas as pl
from jax.experimental.pallas import tpu as pltpu
from jax.sharding import PartitionSpec as P

CAP = 12
SLOTS = 16
RING = 8


def contract(lhs, rhs, lhs_dim, rhs_dim):
    return lax.dot_general(
        lhs, rhs, (((lhs_dim,), (rhs_dim,)), ((), ())), preferred_element_type=jnp.float32
    )


def group_offset(rep, color, dx, dc, width):
    return pl.multiple_of((rep ^ (2 * dx + dc)) * 2 * width + color * width, width)


def token_pieces(n_z):
    near, far = (0, 1, n_z - 1, 0), (0, 1, n_z - 1, 1)
    return [
        ([near], [(1, 0)]),
        ([near], [(0, 0)]),
        ([(0, 0, 1, 1)], [(0, 0), (1, 0), (1, 1)]),
        ([near], [(1, 1)]),
        ([far], [(1, 0)]),
        ([(0, 0, 1, 1), (1, 1, n_z - 1, 0)], [(0, 1)]),
        ([far], [(0, 0)]),
        ([far], [(1, 1)]),
        ([far], [(0, 1)]),
    ]


def norm_kernel(
    tokens_ref, gain_ref, refusal_ref, ids_ref, probs_ref,
    normed_ref, second_ref, first_ref, to_y_ref, unit_ref, base_ref, meta_ref,
):
    tok_rows, model_width = tokens_ref.shape
    width = model_width // 8
    rep = lax.axis_index("rep")
    toks = tokens_ref[...].astype(jnp.float32)
    refusal = refusal_ref[...]
    unit = refusal / jnp.sqrt(jnp.sum(refusal * refusal, axis=1, keepdims=True) + 1e-06)
    unit_ref[...] = unit
    inv_rms = lax.rsqrt(jnp.mean(toks * toks, axis=1, keepdims=True) + 1e-06)
    normed_ref[...] = (toks * inv_rms * gain_ref[...]).astype(jnp.bfloat16)
    own = pl.ds(group_offset(rep, 0, 0, 0, width), 2 * width)
    other = pl.ds(group_offset(rep, 1, 1, 0, width), width)
    first_ref[...] = normed_ref[:, pl.ds(group_offset(rep, 0, 0, 0, width), width)]
    second_ref[:tok_rows] = normed_ref[:, pl.ds(group_offset(rep, 1, 0, 0, width), width)]
    to_y_ref[:tok_rows, : 2 * width] = normed_ref[:, own]
    to_y_ref[:tok_rows, 2 * width :] = normed_ref[:, other]
    meta = jnp.concatenate([ids_ref[...].astype(jnp.float32), probs_ref[...]], axis=0)
    meta = meta.astype(jnp.bfloat16)
    meta_ref[...] = meta
    for ref in (second_ref, to_y_ref):
        ref[tok_rows:] = jnp.zeros((meta.shape[0], ref.shape[1]), jnp.bfloat16)
        ref[tok_rows:, :tok_rows] = meta
    along = jnp.sum(toks * unit, axis=1, keepdims=True)
    base_ref[...] = tokens_ref[:, own].astype(jnp.float32) - along * unit_ref[:, own]


def norm_and_base(tokens, norm_gain, refusal_dir, expert_ids, gate_probs):
    tok_rows, model_width = tokens.shape
    width = model_width // 8
    meta_rows = 2 * expert_ids.shape[1]
    vmem = pl.BlockSpec(memory_space=pltpu.VMEM)
    return pl.pallas_call(
        norm_kernel,
        out_shape=[
            jax.ShapeDtypeStruct((tok_rows, model_width), jnp.bfloat16),
            jax.ShapeDtypeStruct((tok_rows + meta_rows, width), jnp.bfloat16),
            jax.ShapeDtypeStruct((tok_rows, width), jnp.bfloat16),
            jax.ShapeDtypeStruct((tok_rows + meta_rows, 3 * width), jnp.bfloat16),
            jax.ShapeDtypeStruct((1, model_width), jnp.float32),
            jax.ShapeDtypeStruct((tok_rows, 2 * width), jnp.float32),
            jax.ShapeDtypeStruct((meta_rows, tok_rows), jnp.bfloat16),
        ],
        in_specs=[vmem] * 5,
        out_specs=[vmem] * 7,
    )(tokens, norm_gain[None, :], refusal_dir[None, :], expert_ids.T, gate_probs.T)


def route_kernel(exp_dev, meta_ref, picks_ref, weights_ref):
    n_seq, twice_k, tok_rows = meta_ref.shape
    top_k = twice_k // 2
    first = (lax.axis_index("seq") * exp_dev).astype(jnp.float32)
    exp_iota = lax.broadcasted_iota(jnp.int32, (exp_dev, tok_rows), 0).astype(jnp.float32) + first
    earlier = (
        lax.broadcasted_iota(jnp.int32, (tok_rows, tok_rows), 0)
        < lax.broadcasted_iota(jnp.int32, (tok_rows, tok_rows), 1)
    ).astype(jnp.float32).astype(jnp.bfloat16)
    slot_iota = lax.broadcasted_iota(jnp.int32, (exp_dev, SLOTS, tok_rows), 1).astype(jnp.float32)

    def place_pair(pair, carry):
        blocks = (2 * pair, 2 * pair + 1)
        hits, probs = [], []
        for j in blocks:
            meta = meta_ref[j].astype(jnp.float32)
            hit = jnp.zeros((exp_dev, tok_rows), jnp.float32)
            prob = jnp.zeros((exp_dev, tok_rows), jnp.float32)
            for k in range(top_k):
                same = meta[k : k + 1, :] == exp_iota
                hit = jnp.where(same, 1.0, hit)
                prob = jnp.where(same, meta[top_k + k : top_k + k + 1, :], prob)
            hits.append(hit)
            probs.append(prob)
        ranks = contract(jnp.concatenate(hits, axis=0).astype(jnp.bfloat16), earlier, 1, 0)
        for n, j in enumerate(blocks):
            rank = ranks[n * exp_dev : (n + 1) * exp_dev]
            slot = jnp.where(hits[n] > 0.0, rank, -1.0)
            here = slot[:, None, :] == slot_iota
            onehot = jnp.where(here, 1.0, 0.0).reshape(exp_dev * SLOTS, tok_rows)
            weight = jnp.where(here, probs[n][:, None, :], 0.0)
            weight = weight.reshape(exp_dev * SLOTS, tok_rows)
            picks_ref[j] = onehot.astype(jnp.bfloat16)
            weights_ref[j] = weight.T.astype(jnp.bfloat16)
        return carry

    lax.fori_loop(0, n_seq // 2, place_pair, 0)


def route(meta, exp_dev):
    n_seq, _, tok_rows = meta.shape
    vmem = pl.BlockSpec(memory_space=pltpu.VMEM)
    return pl.pallas_call(
        functools.partial(route_kernel, exp_dev),
        out_shape=[
            jax.ShapeDtypeStruct((n_seq, exp_dev * SLOTS, tok_rows), jnp.bfloat16),
            jax.ShapeDtypeStruct((n_seq, tok_rows, exp_dev * SLOTS), jnp.bfloat16),
        ],
        in_specs=[vmem],
        out_specs=[vmem] * 2,
        cost_estimate=pl.CostEstimate(
            flops=4_000_000_000, bytes_accessed=8 * n_seq * exp_dev * SLOTS * tok_rows,
            transcendentals=0,
        ),
    )(meta)


def most_rows(tok_rows):
    return tok_rows // 128 * 112


def moe_kernel(n_pieces, *refs):
    picks_hbm, weights_hbm, unit_ref, own_hbm = refs[:4]
    pieces_in = refs[4 : 4 + n_pieces]
    w_gate_hbm, w_up_hbm, w_down_hbm = refs[4 + n_pieces : 7 + n_pieces]
    out_refs = refs[7 + n_pieces : 15 + n_pieces]
    (picks, weights, w_in, w_down, toks, rows, hidden, mixed, table_sems, tok_sems, in_sems,
     down_sems) = refs[15 + n_pieces :]
    n_z, _, tok_rows, model_width = toks.shape
    n_seq = 2 * n_z
    exp_dev, hid_dev, _ = w_gate_hbm.shape
    width = model_width // 8
    slots_src = exp_dev * SLOTS
    rep = lax.axis_index("rep")
    split = most_rows(tok_rows)
    def in_copies(e):
        at = lax.rem(e, RING)
        return [
            pltpu.make_async_copy(
                src.at[e], w_in.at[at, pl.ds(i * hid_dev, hid_dev)], in_sems.at[i, at]
            )
            for i, src in enumerate((w_gate_hbm, w_up_hbm))
        ]

    def down_copy(e):
        return pltpu.make_async_copy(w_down_hbm.at[e], w_down.at[e], down_sems.at[e])

    tables = [
        pltpu.make_async_copy(picks_hbm, picks, table_sems.at[0]),
        pltpu.make_async_copy(weights_hbm, weights, table_sems.at[1]),
    ]
    tables[0].start()

    kinds = token_pieces(n_z)
    pltpu.make_async_copy(own_hbm, toks.at[0, 0], tok_sems.at[0, 0]).start()
    for i, piece in enumerate(pieces_in):
        blocks, runs = kinds[i % len(kinds)]
        for n, (color, dx) in enumerate(runs):
            cols = pl.ds(group_offset(rep, color, dx, i // len(kinds), width), width)
            for at, dz, count, dy in blocks:
                for k in range(count):
                    pltpu.make_async_copy(
                        piece.at[at + k, pl.ds(0, tok_rows), pl.ds(n * width, width)],
                        toks.at[dz + k, dy, :, cols],
                        tok_sems.at[dz + k, dy],
                    ).start()
    for e in range(min(RING, exp_dev)):
        for copy in in_copies(e):
            copy.start()
    for e in range(exp_dev // 2):
        down_copy(e).start()
    tables[1].start()
    quarters = [slice(2 * q * width, 2 * (q + 1) * width) for q in range(4)]
    tables[0].wait()

    def pick(dz, carry):
        for dy in range(2):
            pltpu.make_async_copy(toks.at[dz, dy], toks.at[dz, dy], tok_sems.at[dz, dy]).wait()
        for dy in range(2):
            onehot = picks[2 * dz + dy]
            for cols in quarters:
                got = contract(onehot, toks[dz, dy, :, cols], 1, 0).astype(jnp.bfloat16)
                rows[2 * dz + dy, :, :, cols] = got.reshape(exp_dev, SLOTS, 2 * width)
        return carry

    lax.fori_loop(0, n_z, pick, 0)

    def widen(pair, carry):
        experts = (2 * pair, 2 * pair + 1)
        for e in experts:
            for copy in in_copies(e):
                copy.wait()
        taken = [rows[:, e].reshape(n_seq * SLOTS, model_width) for e in experts]
        both = [
            [
                contract(value, w_in[lax.rem(e, RING), i * hid_dev : (i + 1) * hid_dev], 1, 1)
                for i in range(2)
            ]
            for e, value in zip(experts, taken)
        ]
        for e, (gate_val, up_val) in zip(experts, both):
            hidden[e] = (gate_val / (1.0 + jnp.exp(-gate_val)) * up_val).astype(jnp.bfloat16)
        down_copy(exp_dev // 2 + pair).start()
        for e in experts:

            @pl.when(e + RING < exp_dev)
            def _():
                for copy in in_copies(e + RING):
                    copy.start()

        return carry

    lax.fori_loop(0, exp_dev // 2, widen, 0)

    def narrow(pair, carry):
        experts = (2 * pair, 2 * pair + 1)
        for e in experts:
            down_copy(e).wait()
        for e in experts:
            for cols in quarters:
                piece = contract(hidden[e], w_down[e, :, cols], 1, 0).astype(jnp.bfloat16)
                rows[:, e, :, cols] = piece.reshape(n_seq, SLOTS, 2 * width)
        return carry

    lax.fori_loop(0, exp_dev // 2, narrow, 0)
    tables[1].wait()

    def combine(dz, carry):
        along = [jnp.zeros((tok_rows, 1), jnp.float32)] * 2
        for dy in range(2):
            j = 2 * dz + dy
            weight = weights[j]
            for cols in quarters:
                got = contract(weight, rows[j, :, :, cols].reshape(slots_src, 2 * width), 1, 0)
                mixed[dy, :, cols] = got
                along[dy] += jnp.sum(got * unit_ref[:, cols], axis=1, keepdims=True)
        for dy in range(2):
            for dc in range(2):
                far_x, far_y, near, rest = out_refs[4 * dc : 4 * dc + 4]
                for n, (color, dx) in enumerate(((0, 1), (0, 0), (1, 0), (1, 1))):
                    cols = pl.ds(group_offset(rep, color, dx, dc, width), width)
                    value = mixed[dy, :, cols] - along[dy] * unit_ref[:, cols]
                    value = value.astype(jnp.bfloat16)
                    rest[dz, dy, :, n * width : (n + 1) * width] = value[split:]
                    if color and dy:
                        far_y[dx, dz] = value[:split]
                    elif not color and dx:
                        far_x[dy, dz] = value[:split]
                    else:
                        near[2 + dx if color else dy, dz] = value[:split]
        return carry

    lax.fori_loop(0, n_z, combine, 0)


def moe_partial(picks, weights, unit_dir, own, pieces, w_gate, w_up, w_down):
    n_seq, _, tok_rows = picks.shape
    exp_dev, hid_dev, model_width = w_gate.shape
    width = model_width // 8
    vmem = pl.BlockSpec(memory_space=pltpu.VMEM)
    hbm = pl.BlockSpec(memory_space=pltpu.HBM)
    whole = pl.BlockSpec(memory_space=pl.ANY)
    n_pieces = len(pieces)
    pieces = [pltpu.with_memory_space_constraint(piece, pltpu.VMEM) for piece in pieces]
    picks, weights, own = [
        pltpu.with_memory_space_constraint(value, pltpu.HBM) for value in (picks, weights, own)
    ]
    n_z, split = n_seq // 2, most_rows(tok_rows)
    far, near = (2, n_z, split, width), (4, n_z, split, width)
    rest = (n_z, 2, tok_rows - split, 4 * width)
    outs = [
        jax.ShapeDtypeStruct(shape, jnp.bfloat16)
        for _ in range(2)
        for shape in (far, far, near, rest)
    ]
    return pl.pallas_call(
        functools.partial(moe_kernel, n_pieces),
        out_shape=outs,
        in_specs=[hbm, hbm, vmem, hbm] + [whole] * n_pieces + [hbm] * 3,
        out_specs=[vmem] * len(outs),
        scratch_shapes=[
            pltpu.VMEM(picks.shape, jnp.bfloat16),
            pltpu.VMEM(weights.shape, jnp.bfloat16),
            pltpu.VMEM((RING, 2 * hid_dev, model_width), jnp.bfloat16),
            pltpu.VMEM(w_down.shape, jnp.bfloat16),
            pltpu.VMEM((n_z, 2, tok_rows, model_width), jnp.bfloat16),
            pltpu.VMEM((n_seq, exp_dev, SLOTS, model_width), jnp.bfloat16),
            pltpu.VMEM((exp_dev, n_seq * SLOTS, hid_dev), jnp.bfloat16),
            pltpu.VMEM((2, tok_rows, model_width), jnp.float32),
            pltpu.SemaphoreType.DMA((2,)),
            pltpu.SemaphoreType.DMA((n_z, 2)),
            pltpu.SemaphoreType.DMA((2, RING)),
            pltpu.SemaphoreType.DMA((exp_dev,)),
        ],
        compiler_params=pltpu.CompilerParams(vmem_limit_bytes=45 * 1024 * 1024),
        cost_estimate=pl.CostEstimate(
            flops=6 * n_seq * SLOTS * exp_dev * hid_dev * model_width,
            bytes_accessed=6 * exp_dev * hid_dev * model_width + 4 * n_seq * own.size,
            transcendentals=0,
        ),
    )(picks, weights, unit_dir, own, *pieces, w_gate, w_up, w_down)


def swap(value, axis, distance):
    size = lax.axis_size(axis)
    return lax.ppermute(value, axis, [(i, i ^ distance) for i in range(size)])


def added(*terms):
    return sum(term.astype(jnp.float32) for term in terms).astype(jnp.bfloat16)


def gathered(tokens, norm_gain, refusal_dir, expert_ids, gate_probs, w_gate, w_up, w_down):
    tok_rows, model_width = tokens.shape
    n_z = lax.axis_size("seq") // 2
    others = range(1, n_z)
    exp_dev = w_gate.shape[0]
    width = model_width // 8

    normed, second, first, to_y, unit_dir, base, meta = norm_and_base(
        tokens, norm_gain, refusal_dir, expert_ids, gate_probs
    )
    second = [swap(second, "seq", 2 * d) for d in others]
    from_y = swap(to_y[None], "seq", 1)
    first, second, from_y = lax.optimization_barrier((first, jnp.stack(second), from_y))
    first = jnp.stack([swap(first, "seq", 2 * d) for d in others])
    x_two = swap(second[:, :tok_rows], "rep", 2)
    y_one = swap(second, "seq", 1)
    y_two = swap(first, "seq", 1)
    x_one = swap(jnp.concatenate([from_y[:, :tok_rows, :width], first]), "rep", 2)
    to_y, to_core = lax.optimization_barrier((x_two, second))
    y_three = swap(to_y, "seq", 1)
    below = [meta, from_y[0, tok_rows:, :tok_rows]]
    for d in range(n_z - 1):
        below += [second[d, tok_rows:, :tok_rows], y_one[d, tok_rows:, :tok_rows]]
    picks, weights = route(jnp.stack(below), exp_dev)
    to_core_y, picks, weights = lax.optimization_barrier((from_y, picks, weights))
    early = [swap(piece, "rep", 1) for piece in (to_core, first, to_core_y)]
    x_three = swap(y_two, "rep", 2)
    last = [x_two, y_one, x_one, y_two, y_three, x_three]
    pieces = [second, first, from_y, *last, *early, *[swap(piece, "rep", 1) for piece in last]]

    sums = moe_partial(picks, weights, unit_dir, normed, pieces, w_gate, w_up, w_down)
    return (base + summed_up(sums[:4], sums[4:], width)).astype(jnp.bfloat16)


def summed_up(kept, sent, width):
    n_z = kept[0].shape[1]
    others = range(1, n_z)
    far_x, far_y, near, rest = zip(kept, [swap(piece, "rep", 1) for piece in sent])

    to_x = added(*far_x)
    to_y, rest_kept, arrived = lax.optimization_barrier((added(*far_y), rest[0], near[1]))
    near = (near[0], arrived)
    by_x, by_y = swap(to_x, "rep", 2), swap(to_y, "seq", 1)
    rest = added(rest_kept, rest[1])
    by_z = [swap(rest[d], "seq", 2 * d) for d in others]
    to_y, to_x, *by_z = lax.optimization_barrier(
        (
            added(*[term[1] for term in near], by_x[1]),
            added(*[term[3] for term in near], by_y[1]),
            *by_z,
        )
    )
    first_far, second_far = swap(to_y, "seq", 1), swap(to_x, "rep", 2)
    first = added(*[term[0] for term in near], by_x[0], first_far)
    second = added(*[term[2] for term in near], by_y[0], second_far)
    blocks = jnp.concatenate([first, second], axis=2)
    most = [swap(blocks[d], "seq", 2 * d) for d in reversed(others)] + [blocks[0]]
    rest = added(rest[0], *by_z)
    rest = added(rest[0], swap(rest[1], "seq", 1))
    far = jnp.concatenate([rest[:, :width], rest[:, 3 * width :]], axis=1)
    rest = [rest[:, width : 3 * width], swap(far, "rep", 2)]
    return jnp.concatenate(
        [sum(term.astype(jnp.float32) for term in terms) for terms in (most, rest)], axis=0
    )


def exchanged(tokens, norm_gain, refusal_dir, expert_ids, gate_probs, w_gate, w_up, w_down):
    tok_rows, model_width = tokens.shape
    top_k = expert_ids.shape[1]
    n_seq = lax.axis_size("seq")
    n_rep = lax.axis_size("rep")
    exp_dev = w_gate.shape[0]
    experts = exp_dev * n_seq
    slot_count = tok_rows * top_k
    part_width = model_width // n_rep
    tokens_f32 = tokens.astype(jnp.float32)
    inv_rms = lax.rsqrt(jnp.mean(tokens_f32 * tokens_f32, axis=1, keepdims=True) + 1e-06)
    normed = (tokens_f32 * inv_rms * norm_gain).astype(jnp.bfloat16)
    flat_ids = expert_ids.reshape(slot_count)
    onehot = (flat_ids[:, None] == jnp.arange(experts, dtype=jnp.int32)[None, :]).astype(jnp.int32)
    slot_rank = jnp.sum(jnp.cumsum(onehot, axis=0) * onehot, axis=1) - 1
    target = flat_ids * CAP + slot_rank
    repeated = jnp.broadcast_to(normed[:, None, :], (tok_rows, top_k, model_width)).reshape(
        slot_count, model_width
    )
    sendbuf = jnp.zeros((experts * CAP, model_width), jnp.bfloat16).at[target].set(repeated)
    sendbuf = sendbuf.reshape(n_seq, exp_dev, CAP, model_width)
    arrived = lax.all_to_all(sendbuf, "seq", split_axis=0, concat_axis=0, tiled=True)
    gate_val = jnp.einsum("secd,efd->secf", arrived, w_gate, preferred_element_type=jnp.float32)
    up_val = jnp.einsum("secd,efd->secf", arrived, w_up, preferred_element_type=jnp.float32)
    hidden = (jax.nn.silu(gate_val) * up_val).astype(jnp.bfloat16)
    pieces = jnp.einsum(
        "secf,efd->secd", hidden, w_down, preferred_element_type=jnp.float32
    ).astype(jnp.bfloat16)
    probs_flat = gate_probs.reshape(slot_count)[:, None]
    returned = lax.all_to_all(pieces, "seq", split_axis=0, concat_axis=0, tiled=True)
    returned = returned.reshape(experts * CAP, model_width)
    weighted = returned[target].astype(jnp.float32) * probs_flat
    moe_part = jnp.sum(weighted.reshape(tok_rows, top_k, model_width), axis=1)
    summed = lax.psum_scatter(
        moe_part.astype(jnp.bfloat16), "rep", scatter_dimension=1, tiled=True
    ).astype(jnp.float32)
    unit_dir = refusal_dir / jnp.sqrt(jnp.sum(refusal_dir * refusal_dir) + 1e-06)
    rep_offset = lax.axis_index("rep") * part_width
    unit_slice = lax.dynamic_slice_in_dim(unit_dir, rep_offset, part_width, 0)
    own_tokens = lax.dynamic_slice_in_dim(tokens_f32, rep_offset, part_width, 1)
    residual = own_tokens + summed
    along_dir = lax.psum(jnp.sum(residual * unit_slice, axis=1), "rep")
    return (residual - along_dir[:, None] * unit_slice).astype(jnp.bfloat16)


def local(tokens, norm_gain, refusal_dir, expert_ids, gate_probs, w_gate, w_up, w_down):
    plan = gathered if w_gate.shape[0] * CAP >= tokens.shape[0] else exchanged
    return plan(tokens, norm_gain, refusal_dir, expert_ids, gate_probs, w_gate, w_up, w_down)


def solution(mesh):
    placed = (
        P("seq", None),
        P(),
        P(),
        P("seq", None),
        P("seq", None),
        P("seq", "rep", None),
        P("seq", "rep", None),
        P("seq", "rep", None),
    )
    return jax.shard_map(
        local, mesh=mesh, in_specs=placed, out_specs=P("seq", "rep"), check_vma=False
    )
```

```python
import functools

import jax
import jax.numpy as jnp
from jax import lax
from jax.experimental import pallas as pl
from jax.experimental.pallas import tpu as pltpu
from jax.sharding import PartitionSpec as P

CAP = 12
SLOTS = 16
RING = 8


def contract(lhs, rhs, lhs_dim, rhs_dim):
    return lax.dot_general(
        lhs, rhs, (((lhs_dim,), (rhs_dim,)), ((), ())), preferred_element_type=jnp.float32
    )


def group_offset(rep, color, dx, dc, width):
    return pl.multiple_of((rep ^ (2 * dx + dc)) * 2 * width + color * width, width)


def token_pieces(n_z):
    near, far = (0, 1, n_z - 1, 0), (0, 1, n_z - 1, 1)
    return [
        ([near], [(1, 0)]),
        ([near], [(0, 0)]),
        ([(0, 0, 1, 1)], [(0, 0), (1, 0), (1, 1)]),
        ([near], [(1, 1)]),
        ([far], [(1, 0)]),
        ([(0, 0, 1, 1), (1, 1, n_z - 1, 0)], [(0, 1)]),
        ([far], [(0, 0)]),
        ([far], [(1, 1)]),
        ([far], [(0, 1)]),
    ]


def norm_kernel(
    tokens_ref, gain_ref, refusal_ref, ids_ref, probs_ref,
    normed_ref, second_ref, first_ref, to_y_ref, unit_ref, base_ref, meta_ref,
):
    tok_rows, model_width = tokens_ref.shape
    width = model_width // 8
    rep = lax.axis_index("rep")
    toks = tokens_ref[...].astype(jnp.float32)
    refusal = refusal_ref[...]
    unit = refusal / jnp.sqrt(jnp.sum(refusal * refusal, axis=1, keepdims=True) + 1e-06)
    unit_ref[...] = unit
    inv_rms = lax.rsqrt(jnp.mean(toks * toks, axis=1, keepdims=True) + 1e-06)
    normed_ref[...] = (toks * inv_rms * gain_ref[...]).astype(jnp.bfloat16)
    own = pl.ds(group_offset(rep, 0, 0, 0, width), 2 * width)
    other = pl.ds(group_offset(rep, 1, 1, 0, width), width)
    first_ref[...] = normed_ref[:, pl.ds(group_offset(rep, 0, 0, 0, width), width)]
    second_ref[:tok_rows] = normed_ref[:, pl.ds(group_offset(rep, 1, 0, 0, width), width)]
    to_y_ref[:tok_rows, : 2 * width] = normed_ref[:, own]
    to_y_ref[:tok_rows, 2 * width :] = normed_ref[:, other]
    meta = jnp.concatenate([ids_ref[...].astype(jnp.float32), probs_ref[...]], axis=0)
    meta = meta.astype(jnp.bfloat16)
    meta_ref[...] = meta
    for ref in (second_ref, to_y_ref):
        ref[tok_rows:] = jnp.zeros((meta.shape[0], ref.shape[1]), jnp.bfloat16)
        ref[tok_rows:, :tok_rows] = meta
    along = jnp.sum(toks * unit, axis=1, keepdims=True)
    base_ref[...] = tokens_ref[:, own].astype(jnp.float32) - along * unit_ref[:, own]


def norm_and_base(tokens, norm_gain, refusal_dir, expert_ids, gate_probs):
    tok_rows, model_width = tokens.shape
    width = model_width // 8
    meta_rows = 2 * expert_ids.shape[1]
    vmem = pl.BlockSpec(memory_space=pltpu.VMEM)
    return pl.pallas_call(
        norm_kernel,
        out_shape=[
            jax.ShapeDtypeStruct((tok_rows, model_width), jnp.bfloat16),
            jax.ShapeDtypeStruct((tok_rows + meta_rows, width), jnp.bfloat16),
            jax.ShapeDtypeStruct((tok_rows, width), jnp.bfloat16),
            jax.ShapeDtypeStruct((tok_rows + meta_rows, 3 * width), jnp.bfloat16),
            jax.ShapeDtypeStruct((1, model_width), jnp.float32),
            jax.ShapeDtypeStruct((tok_rows, 2 * width), jnp.float32),
            jax.ShapeDtypeStruct((meta_rows, tok_rows), jnp.bfloat16),
        ],
        in_specs=[vmem] * 5,
        out_specs=[vmem] * 7,
    )(tokens, norm_gain[None, :], refusal_dir[None, :], expert_ids.T, gate_probs.T)


def route_kernel(exp_dev, meta_ref, picks_ref, weights_ref):
    n_seq, twice_k, tok_rows = meta_ref.shape
    top_k = twice_k // 2
    first = (lax.axis_index("seq") * exp_dev).astype(jnp.float32)
    exp_iota = lax.broadcasted_iota(jnp.int32, (exp_dev, tok_rows), 0).astype(jnp.float32) + first
    earlier = (
        lax.broadcasted_iota(jnp.int32, (tok_rows, tok_rows), 0)
        < lax.broadcasted_iota(jnp.int32, (tok_rows, tok_rows), 1)
    ).astype(jnp.float32).astype(jnp.bfloat16)
    slot_iota = lax.broadcasted_iota(jnp.int32, (exp_dev, SLOTS, tok_rows), 1).astype(jnp.float32)

    def place_pair(pair, carry):
        blocks = (2 * pair, 2 * pair + 1)
        hits, probs = [], []
        for j in blocks:
            meta = meta_ref[j].astype(jnp.float32)
            hit = jnp.zeros((exp_dev, tok_rows), jnp.float32)
            prob = jnp.zeros((exp_dev, tok_rows), jnp.float32)
            for k in range(top_k):
                same = meta[k : k + 1, :] == exp_iota
                hit = jnp.where(same, 1.0, hit)
                prob = jnp.where(same, meta[top_k + k : top_k + k + 1, :], prob)
            hits.append(hit)
            probs.append(prob)
        ranks = contract(jnp.concatenate(hits, axis=0).astype(jnp.bfloat16), earlier, 1, 0)
        for n, j in enumerate(blocks):
            rank = ranks[n * exp_dev : (n + 1) * exp_dev]
            slot = jnp.where(hits[n] > 0.0, rank, -1.0)
            here = slot[:, None, :] == slot_iota
            onehot = jnp.where(here, 1.0, 0.0).reshape(exp_dev * SLOTS, tok_rows)
            weight = jnp.where(here, probs[n][:, None, :], 0.0)
            weight = weight.reshape(exp_dev * SLOTS, tok_rows)
            picks_ref[j] = onehot.astype(jnp.bfloat16)
            weights_ref[j] = weight.T.astype(jnp.bfloat16)
        return carry

    lax.fori_loop(0, n_seq // 2, place_pair, 0)


def route(meta, exp_dev):
    n_seq, _, tok_rows = meta.shape
    vmem = pl.BlockSpec(memory_space=pltpu.VMEM)
    return pl.pallas_call(
        functools.partial(route_kernel, exp_dev),
        out_shape=[
            jax.ShapeDtypeStruct((n_seq, exp_dev * SLOTS, tok_rows), jnp.bfloat16),
            jax.ShapeDtypeStruct((n_seq, tok_rows, exp_dev * SLOTS), jnp.bfloat16),
        ],
        in_specs=[vmem],
        out_specs=[vmem] * 2,
        cost_estimate=pl.CostEstimate(
            flops=4_000_000_000, bytes_accessed=8 * n_seq * exp_dev * SLOTS * tok_rows,
            transcendentals=0,
        ),
    )(meta)


def most_rows(tok_rows):
    return tok_rows // 4 * 3


def moe_kernel(n_pieces, *refs):
    picks_hbm, weights_hbm, unit_ref, own_hbm = refs[:4]
    pieces_in = refs[4 : 4 + n_pieces]
    w_gate_hbm, w_up_hbm, w_down_hbm = refs[4 + n_pieces : 7 + n_pieces]
    out_refs = refs[7 + n_pieces : 13 + n_pieces]
    (picks, weights, w_in, w_down, toks, rows, hidden, mixed, table_sems, tok_sems, in_sems,
     down_sems) = refs[13 + n_pieces :]
    n_z, _, tok_rows, model_width = toks.shape
    n_seq = 2 * n_z
    exp_dev, hid_dev, _ = w_gate_hbm.shape
    width = model_width // 8
    slots_src = exp_dev * SLOTS
    rep = lax.axis_index("rep")
    split = most_rows(tok_rows)
    def in_copies(e):
        at = lax.rem(e, RING)
        return [
            pltpu.make_async_copy(
                src.at[e], w_in.at[at, pl.ds(i * hid_dev, hid_dev)], in_sems.at[i, at]
            )
            for i, src in enumerate((w_gate_hbm, w_up_hbm))
        ]

    def down_copy(e):
        return pltpu.make_async_copy(w_down_hbm.at[e], w_down.at[e], down_sems.at[e])

    tables = [
        pltpu.make_async_copy(picks_hbm, picks, table_sems.at[0]),
        pltpu.make_async_copy(weights_hbm, weights, table_sems.at[1]),
    ]
    tables[0].start()

    kinds = token_pieces(n_z)
    pltpu.make_async_copy(own_hbm, toks.at[0, 0], tok_sems.at[0, 0]).start()
    for i, piece in enumerate(pieces_in):
        blocks, runs = kinds[i % len(kinds)]
        for n, (color, dx) in enumerate(runs):
            cols = pl.ds(group_offset(rep, color, dx, i // len(kinds), width), width)
            for at, dz, count, dy in blocks:
                for k in range(count):
                    pltpu.make_async_copy(
                        piece.at[at + k, pl.ds(0, tok_rows), pl.ds(n * width, width)],
                        toks.at[dz + k, dy, :, cols],
                        tok_sems.at[dz + k, dy],
                    ).start()
    for e in range(min(RING, exp_dev)):
        for copy in in_copies(e):
            copy.start()
    for e in range(exp_dev // 2):
        down_copy(e).start()
    tables[1].start()
    quarters = [slice(2 * q * width, 2 * (q + 1) * width) for q in range(4)]
    tables[0].wait()

    def pick(dz, carry):
        for dy in range(2):
            pltpu.make_async_copy(toks.at[dz, dy], toks.at[dz, dy], tok_sems.at[dz, dy]).wait()
        for dy in range(2):
            onehot = picks[2 * dz + dy]
            for cols in quarters:
                got = contract(onehot, toks[dz, dy, :, cols], 1, 0).astype(jnp.bfloat16)
                rows[2 * dz + dy, :, :, cols] = got.reshape(exp_dev, SLOTS, 2 * width)
        return carry

    lax.fori_loop(0, n_z, pick, 0)

    def widen(pair, carry):
        experts = (2 * pair, 2 * pair + 1)
        for e in experts:
            for copy in in_copies(e):
                copy.wait()
        taken = [rows[:, e].reshape(n_seq * SLOTS, model_width) for e in experts]
        both = [
            [
                contract(value, w_in[lax.rem(e, RING), i * hid_dev : (i + 1) * hid_dev], 1, 1)
                for i in range(2)
            ]
            for e, value in zip(experts, taken)
        ]
        for e, (gate_val, up_val) in zip(experts, both):
            hidden[e] = (gate_val / (1.0 + jnp.exp(-gate_val)) * up_val).astype(jnp.bfloat16)
        down_copy(exp_dev // 2 + pair).start()
        for e in experts:

            @pl.when(e + RING < exp_dev)
            def _():
                for copy in in_copies(e + RING):
                    copy.start()

        return carry

    lax.fori_loop(0, exp_dev // 2, widen, 0)

    def narrow(pair, carry):
        experts = (2 * pair, 2 * pair + 1)
        for e in experts:
            down_copy(e).wait()
        for e in experts:
            for cols in quarters:
                piece = contract(hidden[e], w_down[e, :, cols], 1, 0).astype(jnp.bfloat16)
                rows[:, e, :, cols] = piece.reshape(n_seq, SLOTS, 2 * width)
        return carry

    lax.fori_loop(0, exp_dev // 2, narrow, 0)
    tables[1].wait()

    def combine(dz, carry):
        along = [jnp.zeros((tok_rows, 1), jnp.float32)] * 2
        for dy in range(2):
            j = 2 * dz + dy
            weight = weights[j]
            for cols in quarters:
                got = contract(weight, rows[j, :, :, cols].reshape(slots_src, 2 * width), 1, 0)
                mixed[dy, :, cols] = got
                along[dy] += jnp.sum(got * unit_ref[:, cols], axis=1, keepdims=True)
        for dy in range(2):
            for dc in range(2):
                far, near, rest = out_refs[3 * dc : 3 * dc + 3]
                for n, (color, dx) in enumerate(((0, 1), (0, 0), (1, 0), (1, 1))):
                    cols = pl.ds(group_offset(rep, color, dx, dc, width), width)
                    value = mixed[dy, :, cols] - along[dy] * unit_ref[:, cols]
                    value = value.astype(jnp.bfloat16)
                    rest[dz, dy, :, n * width : (n + 1) * width] = value[split:]
                    leaves, kind = (dy, 2 + dx) if color else (dx, dy)
                    (far if leaves else near)[kind, dz] = value[:split]
        return carry

    lax.fori_loop(0, n_z, combine, 0)


def moe_partial(picks, weights, unit_dir, own, pieces, w_gate, w_up, w_down):
    n_seq, _, tok_rows = picks.shape
    exp_dev, hid_dev, model_width = w_gate.shape
    width = model_width // 8
    vmem = pl.BlockSpec(memory_space=pltpu.VMEM)
    hbm = pl.BlockSpec(memory_space=pltpu.HBM)
    whole = pl.BlockSpec(memory_space=pl.ANY)
    n_pieces = len(pieces)
    pieces = [pltpu.with_memory_space_constraint(piece, pltpu.VMEM) for piece in pieces]
    picks, weights, own = [
        pltpu.with_memory_space_constraint(value, pltpu.HBM) for value in (picks, weights, own)
    ]
    n_z, split = n_seq // 2, most_rows(tok_rows)
    most = (4, n_z, split, width)
    rest = (n_z, 2, tok_rows - split, 4 * width)
    outs = [
        jax.ShapeDtypeStruct(shape, jnp.bfloat16) for _ in range(2) for shape in (most, most, rest)
    ]
    return pl.pallas_call(
        functools.partial(moe_kernel, n_pieces),
        out_shape=outs,
        in_specs=[hbm, hbm, vmem, hbm] + [whole] * n_pieces + [hbm] * 3,
        out_specs=[vmem] * len(outs),
        scratch_shapes=[
            pltpu.VMEM(picks.shape, jnp.bfloat16),
            pltpu.VMEM(weights.shape, jnp.bfloat16),
            pltpu.VMEM((RING, 2 * hid_dev, model_width), jnp.bfloat16),
            pltpu.VMEM(w_down.shape, jnp.bfloat16),
            pltpu.VMEM((n_z, 2, tok_rows, model_width), jnp.bfloat16),
            pltpu.VMEM((n_seq, exp_dev, SLOTS, model_width), jnp.bfloat16),
            pltpu.VMEM((exp_dev, n_seq * SLOTS, hid_dev), jnp.bfloat16),
            pltpu.VMEM((2, tok_rows, model_width), jnp.float32),
            pltpu.SemaphoreType.DMA((2,)),
            pltpu.SemaphoreType.DMA((n_z, 2)),
            pltpu.SemaphoreType.DMA((2, RING)),
            pltpu.SemaphoreType.DMA((exp_dev,)),
        ],
        compiler_params=pltpu.CompilerParams(vmem_limit_bytes=45 * 1024 * 1024),
        cost_estimate=pl.CostEstimate(
            flops=6 * n_seq * SLOTS * exp_dev * hid_dev * model_width,
            bytes_accessed=6 * exp_dev * hid_dev * model_width + 4 * n_seq * own.size,
            transcendentals=0,
        ),
    )(picks, weights, unit_dir, own, *pieces, w_gate, w_up, w_down)


def swap(value, axis, distance):
    size = lax.axis_size(axis)
    return lax.ppermute(value, axis, [(i, i ^ distance) for i in range(size)])


def added(*terms):
    return sum(term.astype(jnp.float32) for term in terms).astype(jnp.bfloat16)


def gathered(tokens, norm_gain, refusal_dir, expert_ids, gate_probs, w_gate, w_up, w_down):
    tok_rows, model_width = tokens.shape
    n_z = lax.axis_size("seq") // 2
    others = range(1, n_z)
    exp_dev = w_gate.shape[0]
    width = model_width // 8

    normed, second, first, to_y, unit_dir, base, meta = norm_and_base(
        tokens, norm_gain, refusal_dir, expert_ids, gate_probs
    )
    second = [swap(second, "seq", 2 * d) for d in others]
    from_y = swap(to_y[None], "seq", 1)
    first, second, from_y = lax.optimization_barrier((first, jnp.stack(second), from_y))
    first = jnp.stack([swap(first, "seq", 2 * d) for d in others])
    x_two = swap(second[:, :tok_rows], "rep", 2)
    y_one = swap(second, "seq", 1)
    y_two = swap(first, "seq", 1)
    x_one = swap(jnp.concatenate([from_y[:, :tok_rows, :width], first]), "rep", 2)
    to_y, to_core = lax.optimization_barrier((x_two, second))
    y_three = swap(to_y, "seq", 1)
    below = [meta, from_y[0, tok_rows:, :tok_rows]]
    for d in range(n_z - 1):
        below += [second[d, tok_rows:, :tok_rows], y_one[d, tok_rows:, :tok_rows]]
    picks, weights = route(jnp.stack(below), exp_dev)
    to_core_y, picks, weights = lax.optimization_barrier((from_y, picks, weights))
    early = [swap(piece, "rep", 1) for piece in (to_core, first, to_core_y)]
    x_three = swap(y_two, "rep", 2)
    last = [x_two, y_one, x_one, y_two, y_three, x_three]
    pieces = [second, first, from_y, *last, *early, *[swap(piece, "rep", 1) for piece in last]]

    sums = moe_partial(picks, weights, unit_dir, normed, pieces, w_gate, w_up, w_down)
    return (base + summed_up(sums[:3], sums[3:], width)).astype(jnp.bfloat16)


def summed_up(kept, sent, width):
    n_z = kept[0].shape[1]
    others = range(1, n_z)
    far, near, rest = zip(kept, [swap(piece, "rep", 1) for piece in sent])

    to_x, to_y, rest_kept = lax.optimization_barrier(
        (added(*[term[:2] for term in far]), added(*[term[2:] for term in far]), rest[0])
    )
    by_x, by_y = swap(to_x, "rep", 2), swap(to_y, "seq", 1)
    rest = added(rest_kept, rest[1])
    by_z = [swap(rest[d], "seq", 2 * d) for d in others]
    to_y, to_x, *by_z[1:] = lax.optimization_barrier(
        (
            added(*[term[1] for term in near], by_x[1]),
            added(*[term[3] for term in near], by_y[1]),
            *by_z[1:],
        )
    )
    first_far, second_far, rest = lax.optimization_barrier(
        (swap(to_y, "seq", 1), swap(to_x, "rep", 2), rest[0])
    )
    first = added(*[term[0] for term in near], by_x[0], first_far)
    second = added(*[term[2] for term in near], by_y[0], second_far)
    blocks = jnp.concatenate([first, second], axis=2)
    most = [swap(blocks[d], "seq", 2 * d) for d in reversed(others)] + [blocks[0]]
    rest = added(rest, *by_z)
    rest = added(rest[0], swap(rest[1], "seq", 1))
    most[0], rest = lax.optimization_barrier((most[0], rest))
    far = jnp.concatenate([rest[:, :width], rest[:, 3 * width :]], axis=1)
    rest = [rest[:, width : 3 * width], swap(far, "rep", 2)]
    return jnp.concatenate(
        [sum(term.astype(jnp.float32) for term in terms) for terms in (most, rest)], axis=0
    )


def exchanged(tokens, norm_gain, refusal_dir, expert_ids, gate_probs, w_gate, w_up, w_down):
    tok_rows, model_width = tokens.shape
    top_k = expert_ids.shape[1]
    n_seq = lax.axis_size("seq")
    n_rep = lax.axis_size("rep")
    exp_dev = w_gate.shape[0]
    experts = exp_dev * n_seq
    slot_count = tok_rows * top_k
    part_width = model_width // n_rep
    tokens_f32 = tokens.astype(jnp.float32)
    inv_rms = lax.rsqrt(jnp.mean(tokens_f32 * tokens_f32, axis=1, keepdims=True) + 1e-06)
    normed = (tokens_f32 * inv_rms * norm_gain).astype(jnp.bfloat16)
    flat_ids = expert_ids.reshape(slot_count)
    onehot = (flat_ids[:, None] == jnp.arange(experts, dtype=jnp.int32)[None, :]).astype(jnp.int32)
    slot_rank = jnp.sum(jnp.cumsum(onehot, axis=0) * onehot, axis=1) - 1
    target = flat_ids * CAP + slot_rank
    repeated = jnp.broadcast_to(normed[:, None, :], (tok_rows, top_k, model_width)).reshape(
        slot_count, model_width
    )
    sendbuf = jnp.zeros((experts * CAP, model_width), jnp.bfloat16).at[target].set(repeated)
    sendbuf = sendbuf.reshape(n_seq, exp_dev, CAP, model_width)
    arrived = lax.all_to_all(sendbuf, "seq", split_axis=0, concat_axis=0, tiled=True)
    gate_val = jnp.einsum("secd,efd->secf", arrived, w_gate, preferred_element_type=jnp.float32)
    up_val = jnp.einsum("secd,efd->secf", arrived, w_up, preferred_element_type=jnp.float32)
    hidden = (jax.nn.silu(gate_val) * up_val).astype(jnp.bfloat16)
    pieces = jnp.einsum(
        "secf,efd->secd", hidden, w_down, preferred_element_type=jnp.float32
    ).astype(jnp.bfloat16)
    probs_flat = gate_probs.reshape(slot_count)[:, None]
    returned = lax.all_to_all(pieces, "seq", split_axis=0, concat_axis=0, tiled=True)
    returned = returned.reshape(experts * CAP, model_width)
    weighted = returned[target].astype(jnp.float32) * probs_flat
    moe_part = jnp.sum(weighted.reshape(tok_rows, top_k, model_width), axis=1)
    summed = lax.psum_scatter(
        moe_part.astype(jnp.bfloat16), "rep", scatter_dimension=1, tiled=True
    ).astype(jnp.float32)
    unit_dir = refusal_dir / jnp.sqrt(jnp.sum(refusal_dir * refusal_dir) + 1e-06)
    rep_offset = lax.axis_index("rep") * part_width
    unit_slice = lax.dynamic_slice_in_dim(unit_dir, rep_offset, part_width, 0)
    own_tokens = lax.dynamic_slice_in_dim(tokens_f32, rep_offset, part_width, 1)
    residual = own_tokens + summed
    along_dir = lax.psum(jnp.sum(residual * unit_slice, axis=1), "rep")
    return (residual - along_dir[:, None] * unit_slice).astype(jnp.bfloat16)


def local(tokens, norm_gain, refusal_dir, expert_ids, gate_probs, w_gate, w_up, w_down):
    plan = gathered if w_gate.shape[0] * CAP >= tokens.shape[0] else exchanged
    return plan(tokens, norm_gain, refusal_dir, expert_ids, gate_probs, w_gate, w_up, w_down)


def solution(mesh):
    placed = (
        P("seq", None),
        P(),
        P(),
        P("seq", None),
        P("seq", None),
        P("seq", "rep", None),
        P("seq", "rep", None),
        P("seq", "rep", None),
    )
    return jax.shard_map(
        local, mesh=mesh, in_specs=placed, out_specs=P("seq", "rep"), check_vma=False
    )
```

```python
import functools

import jax
import jax.numpy as jnp
from jax import lax
from jax.experimental import pallas as pl
from jax.experimental.pallas import tpu as pltpu
from jax.sharding import PartitionSpec as P

CAP = 12
SLOTS = 16
RING = 8


def contract(lhs, rhs, lhs_dim, rhs_dim):
    return lax.dot_general(
        lhs, rhs, (((lhs_dim,), (rhs_dim,)), ((), ())), preferred_element_type=jnp.float32
    )


def group_offset(rep, color, dx, dc, width):
    return pl.multiple_of((rep ^ (2 * dx + dc)) * 2 * width + color * width, width)


def token_pieces(n_z):
    near, far = (0, 1, n_z - 1, 0), (0, 1, n_z - 1, 1)
    return [
        ([near], [(1, 0)]),
        ([near], [(0, 0)]),
        ([(0, 0, 1, 1)], [(0, 0), (1, 0), (1, 1)]),
        ([near], [(1, 1)]),
        ([far], [(1, 0)]),
        ([(0, 0, 1, 1), (1, 1, n_z - 1, 0)], [(0, 1)]),
        ([far], [(0, 0)]),
        ([far], [(1, 1)]),
        ([far], [(0, 1)]),
    ]


def norm_kernel(
    tokens_ref, gain_ref, refusal_ref, ids_ref, probs_ref,
    normed_ref, second_ref, first_ref, to_y_ref, unit_ref, base_ref, meta_ref,
):
    tok_rows, model_width = tokens_ref.shape
    width = model_width // 8
    rep = lax.axis_index("rep")
    toks = tokens_ref[...].astype(jnp.float32)
    refusal = refusal_ref[...]
    unit = refusal / jnp.sqrt(jnp.sum(refusal * refusal, axis=1, keepdims=True) + 1e-06)
    unit_ref[...] = unit
    inv_rms = lax.rsqrt(jnp.mean(toks * toks, axis=1, keepdims=True) + 1e-06)
    normed_ref[...] = (toks * inv_rms * gain_ref[...]).astype(jnp.bfloat16)
    own = pl.ds(group_offset(rep, 0, 0, 0, width), 2 * width)
    other = pl.ds(group_offset(rep, 1, 1, 0, width), width)
    first_ref[...] = normed_ref[:, pl.ds(group_offset(rep, 0, 0, 0, width), width)]
    second_ref[:tok_rows] = normed_ref[:, pl.ds(group_offset(rep, 1, 0, 0, width), width)]
    to_y_ref[:tok_rows, : 2 * width] = normed_ref[:, own]
    to_y_ref[:tok_rows, 2 * width :] = normed_ref[:, other]
    meta = jnp.concatenate([ids_ref[...].astype(jnp.float32), probs_ref[...]], axis=0)
    meta = meta.astype(jnp.bfloat16)
    meta_ref[...] = meta
    for ref in (second_ref, to_y_ref):
        ref[tok_rows:] = jnp.zeros((meta.shape[0], ref.shape[1]), jnp.bfloat16)
        ref[tok_rows:, :tok_rows] = meta
    along = jnp.sum(toks * unit, axis=1, keepdims=True)
    base_ref[...] = tokens_ref[:, own].astype(jnp.float32) - along * unit_ref[:, own]


def norm_and_base(tokens, norm_gain, refusal_dir, expert_ids, gate_probs):
    tok_rows, model_width = tokens.shape
    width = model_width // 8
    meta_rows = 2 * expert_ids.shape[1]
    vmem = pl.BlockSpec(memory_space=pltpu.VMEM)
    return pl.pallas_call(
        norm_kernel,
        out_shape=[
            jax.ShapeDtypeStruct((tok_rows, model_width), jnp.bfloat16),
            jax.ShapeDtypeStruct((tok_rows + meta_rows, width), jnp.bfloat16),
            jax.ShapeDtypeStruct((tok_rows, width), jnp.bfloat16),
            jax.ShapeDtypeStruct((tok_rows + meta_rows, 3 * width), jnp.bfloat16),
            jax.ShapeDtypeStruct((1, model_width), jnp.float32),
            jax.ShapeDtypeStruct((tok_rows, 2 * width), jnp.float32),
            jax.ShapeDtypeStruct((meta_rows, tok_rows), jnp.bfloat16),
        ],
        in_specs=[vmem] * 5,
        out_specs=[vmem] * 7,
    )(tokens, norm_gain[None, :], refusal_dir[None, :], expert_ids.T, gate_probs.T)


def route_kernel(exp_dev, meta_ref, picks_ref, weights_ref):
    n_seq, twice_k, tok_rows = meta_ref.shape
    top_k = twice_k // 2
    first = (lax.axis_index("seq") * exp_dev).astype(jnp.float32)
    exp_iota = lax.broadcasted_iota(jnp.int32, (exp_dev, tok_rows), 0).astype(jnp.float32) + first
    earlier = (
        lax.broadcasted_iota(jnp.int32, (tok_rows, tok_rows), 0)
        < lax.broadcasted_iota(jnp.int32, (tok_rows, tok_rows), 1)
    ).astype(jnp.float32).astype(jnp.bfloat16)
    slot_iota = lax.broadcasted_iota(jnp.int32, (exp_dev, SLOTS, tok_rows), 1).astype(jnp.float32)

    def place_pair(pair, carry):
        blocks = (2 * pair, 2 * pair + 1)
        hits, probs = [], []
        for j in blocks:
            meta = meta_ref[j].astype(jnp.float32)
            hit = jnp.zeros((exp_dev, tok_rows), jnp.float32)
            prob = jnp.zeros((exp_dev, tok_rows), jnp.float32)
            for k in range(top_k):
                same = meta[k : k + 1, :] == exp_iota
                hit = jnp.where(same, 1.0, hit)
                prob = jnp.where(same, meta[top_k + k : top_k + k + 1, :], prob)
            hits.append(hit)
            probs.append(prob)
        ranks = contract(jnp.concatenate(hits, axis=0).astype(jnp.bfloat16), earlier, 1, 0)
        for n, j in enumerate(blocks):
            rank = ranks[n * exp_dev : (n + 1) * exp_dev]
            slot = jnp.where(hits[n] > 0.0, rank, -1.0)
            here = slot[:, None, :] == slot_iota
            onehot = jnp.where(here, 1.0, 0.0).reshape(exp_dev * SLOTS, tok_rows)
            weight = jnp.where(here, probs[n][:, None, :], 0.0)
            weight = weight.reshape(exp_dev * SLOTS, tok_rows)
            picks_ref[j] = onehot.astype(jnp.bfloat16)
            weights_ref[j] = weight.T.astype(jnp.bfloat16)
        return carry

    lax.fori_loop(0, n_seq // 2, place_pair, 0)


def route(meta, exp_dev):
    n_seq, _, tok_rows = meta.shape
    vmem = pl.BlockSpec(memory_space=pltpu.VMEM)
    return pl.pallas_call(
        functools.partial(route_kernel, exp_dev),
        out_shape=[
            jax.ShapeDtypeStruct((n_seq, exp_dev * SLOTS, tok_rows), jnp.bfloat16),
            jax.ShapeDtypeStruct((n_seq, tok_rows, exp_dev * SLOTS), jnp.bfloat16),
        ],
        in_specs=[vmem],
        out_specs=[vmem] * 2,
        cost_estimate=pl.CostEstimate(
            flops=4_000_000_000, bytes_accessed=8 * n_seq * exp_dev * SLOTS * tok_rows,
            transcendentals=0,
        ),
    )(meta)


def most_rows(tok_rows):
    return tok_rows // 128 * 112


def moe_kernel(n_pieces, *refs):
    picks_hbm, weights_hbm, unit_ref, own_hbm = refs[:4]
    pieces_in = refs[4 : 4 + n_pieces]
    w_gate_hbm, w_up_hbm, w_down_hbm = refs[4 + n_pieces : 7 + n_pieces]
    out_refs = refs[7 + n_pieces : 13 + n_pieces]
    (picks, weights, w_in, w_down, toks, rows, hidden, mixed, table_sems, tok_sems, in_sems,
     down_sems) = refs[13 + n_pieces :]
    n_z, _, tok_rows, model_width = toks.shape
    n_seq = 2 * n_z
    exp_dev, hid_dev, _ = w_gate_hbm.shape
    width = model_width // 8
    slots_src = exp_dev * SLOTS
    rep = lax.axis_index("rep")
    split = most_rows(tok_rows)
    def in_copies(e):
        at = lax.rem(e, RING)
        return [
            pltpu.make_async_copy(
                src.at[e], w_in.at[at, pl.ds(i * hid_dev, hid_dev)], in_sems.at[i, at]
            )
            for i, src in enumerate((w_gate_hbm, w_up_hbm))
        ]

    def down_copy(e):
        return pltpu.make_async_copy(w_down_hbm.at[e], w_down.at[e], down_sems.at[e])

    tables = [
        pltpu.make_async_copy(picks_hbm, picks, table_sems.at[0]),
        pltpu.make_async_copy(weights_hbm, weights, table_sems.at[1]),
    ]
    tables[0].start()

    kinds = token_pieces(n_z)
    pltpu.make_async_copy(own_hbm, toks.at[0, 0], tok_sems.at[0, 0]).start()
    for i, piece in enumerate(pieces_in):
        blocks, runs = kinds[i % len(kinds)]
        for n, (color, dx) in enumerate(runs):
            cols = pl.ds(group_offset(rep, color, dx, i // len(kinds), width), width)
            for at, dz, count, dy in blocks:
                for k in range(count):
                    pltpu.make_async_copy(
                        piece.at[at + k, pl.ds(0, tok_rows), pl.ds(n * width, width)],
                        toks.at[dz + k, dy, :, cols],
                        tok_sems.at[dz + k, dy],
                    ).start()
    for e in range(min(RING, exp_dev)):
        for copy in in_copies(e):
            copy.start()
    for e in range(exp_dev // 2):
        down_copy(e).start()
    tables[1].start()
    quarters = [slice(2 * q * width, 2 * (q + 1) * width) for q in range(4)]
    tables[0].wait()

    def pick(dz, carry):
        for dy in range(2):
            pltpu.make_async_copy(toks.at[dz, dy], toks.at[dz, dy], tok_sems.at[dz, dy]).wait()
        for dy in range(2):
            onehot = picks[2 * dz + dy]
            for cols in quarters:
                got = contract(onehot, toks[dz, dy, :, cols], 1, 0).astype(jnp.bfloat16)
                rows[2 * dz + dy, :, :, cols] = got.reshape(exp_dev, SLOTS, 2 * width)
        return carry

    lax.fori_loop(0, n_z, pick, 0)

    def widen(pair, carry):
        experts = (2 * pair, 2 * pair + 1)
        for e in experts:
            for copy in in_copies(e):
                copy.wait()
        taken = [rows[:, e].reshape(n_seq * SLOTS, model_width) for e in experts]
        both = [
            [
                contract(value, w_in[lax.rem(e, RING), i * hid_dev : (i + 1) * hid_dev], 1, 1)
                for i in range(2)
            ]
            for e, value in zip(experts, taken)
        ]
        for e, (gate_val, up_val) in zip(experts, both):
            hidden[e] = (gate_val / (1.0 + jnp.exp(-gate_val)) * up_val).astype(jnp.bfloat16)
        down_copy(exp_dev // 2 + pair).start()
        for e in experts:

            @pl.when(e + RING < exp_dev)
            def _():
                for copy in in_copies(e + RING):
                    copy.start()

        return carry

    lax.fori_loop(0, exp_dev // 2, widen, 0)

    def narrow(pair, carry):
        experts = (2 * pair, 2 * pair + 1)
        for e in experts:
            down_copy(e).wait()
        for e in experts:
            for cols in quarters:
                piece = contract(hidden[e], w_down[e, :, cols], 1, 0).astype(jnp.bfloat16)
                rows[:, e, :, cols] = piece.reshape(n_seq, SLOTS, 2 * width)
        return carry

    lax.fori_loop(0, exp_dev // 2, narrow, 0)
    tables[1].wait()

    def combine(dz, carry):
        along = [jnp.zeros((tok_rows, 1), jnp.float32)] * 2
        for dy in range(2):
            j = 2 * dz + dy
            weight = weights[j]
            for cols in quarters:
                got = contract(weight, rows[j, :, :, cols].reshape(slots_src, 2 * width), 1, 0)
                mixed[dy, :, cols] = got
                along[dy] += jnp.sum(got * unit_ref[:, cols], axis=1, keepdims=True)
        for dy in range(2):
            for dc in range(2):
                far, near, rest = out_refs[3 * dc : 3 * dc + 3]
                for n, (color, dx) in enumerate(((0, 1), (0, 0), (1, 0), (1, 1))):
                    cols = pl.ds(group_offset(rep, color, dx, dc, width), width)
                    value = mixed[dy, :, cols] - along[dy] * unit_ref[:, cols]
                    value = value.astype(jnp.bfloat16)
                    rest[dz, dy, :, n * width : (n + 1) * width] = value[split:]
                    leaves, kind = (dy, 2 + dx) if color else (dx, dy)
                    (far if leaves else near)[kind, dz] = value[:split]
        return carry

    lax.fori_loop(0, n_z, combine, 0)


def moe_partial(picks, weights, unit_dir, own, pieces, w_gate, w_up, w_down):
    n_seq, _, tok_rows = picks.shape
    exp_dev, hid_dev, model_width = w_gate.shape
    width = model_width // 8
    vmem = pl.BlockSpec(memory_space=pltpu.VMEM)
    hbm = pl.BlockSpec(memory_space=pltpu.HBM)
    whole = pl.BlockSpec(memory_space=pl.ANY)
    n_pieces = len(pieces)
    pieces = [pltpu.with_memory_space_constraint(piece, pltpu.VMEM) for piece in pieces]
    picks, weights, own = [
        pltpu.with_memory_space_constraint(value, pltpu.HBM) for value in (picks, weights, own)
    ]
    n_z, split = n_seq // 2, most_rows(tok_rows)
    most = (4, n_z, split, width)
    rest = (n_z, 2, tok_rows - split, 4 * width)
    outs = [
        jax.ShapeDtypeStruct(shape, jnp.bfloat16) for _ in range(2) for shape in (most, most, rest)
    ]
    return pl.pallas_call(
        functools.partial(moe_kernel, n_pieces),
        out_shape=outs,
        in_specs=[hbm, hbm, vmem, hbm] + [whole] * n_pieces + [hbm] * 3,
        out_specs=[vmem] * len(outs),
        scratch_shapes=[
            pltpu.VMEM(picks.shape, jnp.bfloat16),
            pltpu.VMEM(weights.shape, jnp.bfloat16),
            pltpu.VMEM((RING, 2 * hid_dev, model_width), jnp.bfloat16),
            pltpu.VMEM(w_down.shape, jnp.bfloat16),
            pltpu.VMEM((n_z, 2, tok_rows, model_width), jnp.bfloat16),
            pltpu.VMEM((n_seq, exp_dev, SLOTS, model_width), jnp.bfloat16),
            pltpu.VMEM((exp_dev, n_seq * SLOTS, hid_dev), jnp.bfloat16),
            pltpu.VMEM((2, tok_rows, model_width), jnp.float32),
            pltpu.SemaphoreType.DMA((2,)),
            pltpu.SemaphoreType.DMA((n_z, 2)),
            pltpu.SemaphoreType.DMA((2, RING)),
            pltpu.SemaphoreType.DMA((exp_dev,)),
        ],
        compiler_params=pltpu.CompilerParams(vmem_limit_bytes=45 * 1024 * 1024),
        cost_estimate=pl.CostEstimate(
            flops=6 * n_seq * SLOTS * exp_dev * hid_dev * model_width,
            bytes_accessed=6 * exp_dev * hid_dev * model_width + 4 * n_seq * own.size,
            transcendentals=0,
        ),
    )(picks, weights, unit_dir, own, *pieces, w_gate, w_up, w_down)


def swap(value, axis, distance):
    size = lax.axis_size(axis)
    return lax.ppermute(value, axis, [(i, i ^ distance) for i in range(size)])


def added(*terms):
    return sum(term.astype(jnp.float32) for term in terms).astype(jnp.bfloat16)


def gathered(tokens, norm_gain, refusal_dir, expert_ids, gate_probs, w_gate, w_up, w_down):
    tok_rows, model_width = tokens.shape
    n_z = lax.axis_size("seq") // 2
    others = range(1, n_z)
    exp_dev = w_gate.shape[0]
    width = model_width // 8

    normed, second, first, to_y, unit_dir, base, meta = norm_and_base(
        tokens, norm_gain, refusal_dir, expert_ids, gate_probs
    )
    second = [swap(second, "seq", 2 * d) for d in others]
    from_y = swap(to_y[None], "seq", 1)
    first, second, from_y = lax.optimization_barrier((first, jnp.stack(second), from_y))
    first = jnp.stack([swap(first, "seq", 2 * d) for d in others])
    x_two = swap(second[:, :tok_rows], "rep", 2)
    y_one = swap(second, "seq", 1)
    y_two = swap(first, "seq", 1)
    x_one = swap(jnp.concatenate([from_y[:, :tok_rows, :width], first]), "rep", 2)
    to_y, to_core = lax.optimization_barrier((x_two, second))
    y_three = swap(to_y, "seq", 1)
    below = [meta, from_y[0, tok_rows:, :tok_rows]]
    for d in range(n_z - 1):
        below += [second[d, tok_rows:, :tok_rows], y_one[d, tok_rows:, :tok_rows]]
    picks, weights = route(jnp.stack(below), exp_dev)
    to_core_y, picks, weights = lax.optimization_barrier((from_y, picks, weights))
    early = [swap(piece, "rep", 1) for piece in (to_core, first, to_core_y)]
    x_three = swap(y_two, "rep", 2)
    last = [x_two, y_one, x_one, y_two, y_three, x_three]
    to_core = list(last)
    to_core[1:4] = lax.optimization_barrier((y_one, x_one, y_two))
    pieces = [second, first, from_y, *last, *early, *[swap(piece, "rep", 1) for piece in to_core]]

    sums = moe_partial(picks, weights, unit_dir, normed, pieces, w_gate, w_up, w_down)
    return (base + summed_up(sums[:3], sums[3:], width)).astype(jnp.bfloat16)


def summed_up(kept, sent, width):
    n_z = kept[0].shape[1]
    others = range(1, n_z)
    far, near, rest = zip(kept, [swap(piece, "rep", 1) for piece in sent])

    to_x, to_y, rest_kept = lax.optimization_barrier(
        (added(*[term[:2] for term in far]), added(*[term[2:] for term in far]), rest[0])
    )
    by_x, by_y = swap(to_x, "rep", 2), swap(to_y, "seq", 1)
    rest = added(rest_kept, rest[1])
    by_z = [swap(rest[d], "seq", 2 * d) for d in others]
    to_y, to_x, *by_z = lax.optimization_barrier(
        (
            added(*[term[1] for term in near], by_x[1]),
            added(*[term[3] for term in near], by_y[1]),
            *by_z,
        )
    )
    first_far, second_far = swap(to_y, "seq", 1), swap(to_x, "rep", 2)
    first = added(*[term[0] for term in near], by_x[0], first_far)
    second = added(*[term[2] for term in near], by_y[0], second_far)
    blocks = jnp.concatenate([first, second], axis=2)
    most = [swap(blocks[d], "seq", 2 * d) for d in reversed(others)] + [blocks[0]]
    rest = added(rest[0], *by_z)
    rest = added(rest[0], swap(rest[1], "seq", 1))
    far = jnp.concatenate([rest[:, :width], rest[:, 3 * width :]], axis=1)
    rest = [rest[:, width : 3 * width], swap(far, "rep", 2)]
    return jnp.concatenate(
        [sum(term.astype(jnp.float32) for term in terms) for terms in (most, rest)], axis=0
    )


def exchanged(tokens, norm_gain, refusal_dir, expert_ids, gate_probs, w_gate, w_up, w_down):
    tok_rows, model_width = tokens.shape
    top_k = expert_ids.shape[1]
    n_seq = lax.axis_size("seq")
    n_rep = lax.axis_size("rep")
    exp_dev = w_gate.shape[0]
    experts = exp_dev * n_seq
    slot_count = tok_rows * top_k
    part_width = model_width // n_rep
    tokens_f32 = tokens.astype(jnp.float32)
    inv_rms = lax.rsqrt(jnp.mean(tokens_f32 * tokens_f32, axis=1, keepdims=True) + 1e-06)
    normed = (tokens_f32 * inv_rms * norm_gain).astype(jnp.bfloat16)
    flat_ids = expert_ids.reshape(slot_count)
    onehot = (flat_ids[:, None] == jnp.arange(experts, dtype=jnp.int32)[None, :]).astype(jnp.int32)
    slot_rank = jnp.sum(jnp.cumsum(onehot, axis=0) * onehot, axis=1) - 1
    target = flat_ids * CAP + slot_rank
    repeated = jnp.broadcast_to(normed[:, None, :], (tok_rows, top_k, model_width)).reshape(
        slot_count, model_width
    )
    sendbuf = jnp.zeros((experts * CAP, model_width), jnp.bfloat16).at[target].set(repeated)
    sendbuf = sendbuf.reshape(n_seq, exp_dev, CAP, model_width)
    arrived = lax.all_to_all(sendbuf, "seq", split_axis=0, concat_axis=0, tiled=True)
    gate_val = jnp.einsum("secd,efd->secf", arrived, w_gate, preferred_element_type=jnp.float32)
    up_val = jnp.einsum("secd,efd->secf", arrived, w_up, preferred_element_type=jnp.float32)
    hidden = (jax.nn.silu(gate_val) * up_val).astype(jnp.bfloat16)
    pieces = jnp.einsum(
        "secf,efd->secd", hidden, w_down, preferred_element_type=jnp.float32
    ).astype(jnp.bfloat16)
    probs_flat = gate_probs.reshape(slot_count)[:, None]
    returned = lax.all_to_all(pieces, "seq", split_axis=0, concat_axis=0, tiled=True)
    returned = returned.reshape(experts * CAP, model_width)
    weighted = returned[target].astype(jnp.float32) * probs_flat
    moe_part = jnp.sum(weighted.reshape(tok_rows, top_k, model_width), axis=1)
    summed = lax.psum_scatter(
        moe_part.astype(jnp.bfloat16), "rep", scatter_dimension=1, tiled=True
    ).astype(jnp.float32)
    unit_dir = refusal_dir / jnp.sqrt(jnp.sum(refusal_dir * refusal_dir) + 1e-06)
    rep_offset = lax.axis_index("rep") * part_width
    unit_slice = lax.dynamic_slice_in_dim(unit_dir, rep_offset, part_width, 0)
    own_tokens = lax.dynamic_slice_in_dim(tokens_f32, rep_offset, part_width, 1)
    residual = own_tokens + summed
    along_dir = lax.psum(jnp.sum(residual * unit_slice, axis=1), "rep")
    return (residual - along_dir[:, None] * unit_slice).astype(jnp.bfloat16)


def local(tokens, norm_gain, refusal_dir, expert_ids, gate_probs, w_gate, w_up, w_down):
    plan = gathered if w_gate.shape[0] * CAP >= tokens.shape[0] else exchanged
    return plan(tokens, norm_gain, refusal_dir, expert_ids, gate_probs, w_gate, w_up, w_down)


def solution(mesh):
    placed = (
        P("seq", None),
        P(),
        P(),
        P("seq", None),
        P("seq", None),
        P("seq", "rep", None),
        P("seq", "rep", None),
        P("seq", "rep", None),
    )
    return jax.shard_map(
        local, mesh=mesh, in_specs=placed, out_specs=P("seq", "rep"), check_vma=False
    )
```

```python
import functools

import jax
import jax.numpy as jnp
from jax import lax
from jax.experimental import pallas as pl
from jax.experimental.pallas import tpu as pltpu
from jax.sharding import PartitionSpec as P

CAP = 12
SLOTS = 16
RING = 8


def contract(lhs, rhs, lhs_dim, rhs_dim):
    return lax.dot_general(
        lhs, rhs, (((lhs_dim,), (rhs_dim,)), ((), ())), preferred_element_type=jnp.float32
    )


def group_offset(rep, color, dx, dc, width):
    return pl.multiple_of((rep ^ (2 * dx + dc)) * 2 * width + color * width, width)


def token_pieces(n_z):
    near, far = (0, 1, n_z - 1, 0), (0, 1, n_z - 1, 1)
    return [
        ([near], [(1, 0)]),
        ([near], [(0, 0)]),
        ([(0, 0, 1, 1)], [(0, 0), (1, 0), (1, 1)]),
        ([near], [(1, 1)]),
        ([far], [(1, 0)]),
        ([(0, 0, 1, 1), (1, 1, n_z - 1, 0)], [(0, 1)]),
        ([far], [(0, 0)]),
        ([far], [(1, 1)]),
        ([far], [(0, 1)]),
    ]


def norm_kernel(
    tokens_ref, gain_ref, refusal_ref, ids_ref, probs_ref,
    normed_ref, second_ref, first_ref, to_y_ref, unit_ref, base_ref, meta_ref,
):
    tok_rows, model_width = tokens_ref.shape
    width = model_width // 8
    rep = lax.axis_index("rep")
    toks = tokens_ref[...].astype(jnp.float32)
    refusal = refusal_ref[...]
    unit = refusal / jnp.sqrt(jnp.sum(refusal * refusal, axis=1, keepdims=True) + 1e-06)
    unit_ref[...] = unit
    inv_rms = lax.rsqrt(jnp.mean(toks * toks, axis=1, keepdims=True) + 1e-06)
    normed_ref[...] = (toks * inv_rms * gain_ref[...]).astype(jnp.bfloat16)
    own = pl.ds(group_offset(rep, 0, 0, 0, width), 2 * width)
    other = pl.ds(group_offset(rep, 1, 1, 0, width), width)
    first_ref[...] = normed_ref[:, pl.ds(group_offset(rep, 0, 0, 0, width), width)]
    second_ref[:tok_rows] = normed_ref[:, pl.ds(group_offset(rep, 1, 0, 0, width), width)]
    to_y_ref[:tok_rows, : 2 * width] = normed_ref[:, own]
    to_y_ref[:tok_rows, 2 * width :] = normed_ref[:, other]
    meta = jnp.concatenate([ids_ref[...].astype(jnp.float32), probs_ref[...]], axis=0)
    meta = meta.astype(jnp.bfloat16)
    meta_ref[...] = meta
    for ref in (second_ref, to_y_ref):
        ref[tok_rows:] = jnp.zeros((meta.shape[0], ref.shape[1]), jnp.bfloat16)
        ref[tok_rows:, :tok_rows] = meta
    along = jnp.sum(toks * unit, axis=1, keepdims=True)
    base_ref[...] = tokens_ref[:, own].astype(jnp.float32) - along * unit_ref[:, own]


def norm_and_base(tokens, norm_gain, refusal_dir, expert_ids, gate_probs):
    tok_rows, model_width = tokens.shape
    width = model_width // 8
    meta_rows = 2 * expert_ids.shape[1]
    vmem = pl.BlockSpec(memory_space=pltpu.VMEM)
    return pl.pallas_call(
        norm_kernel,
        out_shape=[
            jax.ShapeDtypeStruct((tok_rows, model_width), jnp.bfloat16),
            jax.ShapeDtypeStruct((tok_rows + meta_rows, width), jnp.bfloat16),
            jax.ShapeDtypeStruct((tok_rows, width), jnp.bfloat16),
            jax.ShapeDtypeStruct((tok_rows + meta_rows, 3 * width), jnp.bfloat16),
            jax.ShapeDtypeStruct((1, model_width), jnp.float32),
            jax.ShapeDtypeStruct((tok_rows, 2 * width), jnp.float32),
            jax.ShapeDtypeStruct((meta_rows, tok_rows), jnp.bfloat16),
        ],
        in_specs=[vmem] * 5,
        out_specs=[vmem] * 7,
    )(tokens, norm_gain[None, :], refusal_dir[None, :], expert_ids.T, gate_probs.T)


def route_kernel(exp_dev, meta_ref, picks_ref, weights_ref):
    n_seq, twice_k, tok_rows = meta_ref.shape
    top_k = twice_k // 2
    first = (lax.axis_index("seq") * exp_dev).astype(jnp.float32)
    exp_iota = lax.broadcasted_iota(jnp.int32, (exp_dev, tok_rows), 0).astype(jnp.float32) + first
    earlier = (
        lax.broadcasted_iota(jnp.int32, (tok_rows, tok_rows), 0)
        < lax.broadcasted_iota(jnp.int32, (tok_rows, tok_rows), 1)
    ).astype(jnp.float32).astype(jnp.bfloat16)
    slot_iota = lax.broadcasted_iota(jnp.int32, (exp_dev, SLOTS, tok_rows), 1).astype(jnp.float32)

    def place_pair(pair, carry):
        blocks = (2 * pair, 2 * pair + 1)
        hits, probs = [], []
        for j in blocks:
            meta = meta_ref[j].astype(jnp.float32)
            hit = jnp.zeros((exp_dev, tok_rows), jnp.float32)
            prob = jnp.zeros((exp_dev, tok_rows), jnp.float32)
            for k in range(top_k):
                same = meta[k : k + 1, :] == exp_iota
                hit = jnp.where(same, 1.0, hit)
                prob = jnp.where(same, meta[top_k + k : top_k + k + 1, :], prob)
            hits.append(hit)
            probs.append(prob)
        ranks = contract(jnp.concatenate(hits, axis=0).astype(jnp.bfloat16), earlier, 1, 0)
        for n, j in enumerate(blocks):
            rank = ranks[n * exp_dev : (n + 1) * exp_dev]
            slot = jnp.where(hits[n] > 0.0, rank, -1.0)
            here = slot[:, None, :] == slot_iota
            onehot = jnp.where(here, 1.0, 0.0).reshape(exp_dev * SLOTS, tok_rows)
            weight = jnp.where(here, probs[n][:, None, :], 0.0)
            weight = weight.reshape(exp_dev * SLOTS, tok_rows)
            picks_ref[j] = onehot.astype(jnp.bfloat16)
            weights_ref[j] = weight.T.astype(jnp.bfloat16)
        return carry

    lax.fori_loop(0, n_seq // 2, place_pair, 0)


def route(meta, exp_dev):
    n_seq, _, tok_rows = meta.shape
    vmem = pl.BlockSpec(memory_space=pltpu.VMEM)
    return pl.pallas_call(
        functools.partial(route_kernel, exp_dev),
        out_shape=[
            jax.ShapeDtypeStruct((n_seq, exp_dev * SLOTS, tok_rows), jnp.bfloat16),
            jax.ShapeDtypeStruct((n_seq, tok_rows, exp_dev * SLOTS), jnp.bfloat16),
        ],
        in_specs=[vmem],
        out_specs=[vmem] * 2,
        cost_estimate=pl.CostEstimate(
            flops=4_000_000_000, bytes_accessed=8 * n_seq * exp_dev * SLOTS * tok_rows,
            transcendentals=0,
        ),
    )(meta)


def most_rows(tok_rows):
    return tok_rows // 128 * 112


def moe_kernel(n_pieces, *refs):
    picks_hbm, weights_hbm, unit_ref, own_hbm = refs[:4]
    pieces_in = refs[4 : 4 + n_pieces]
    w_gate_hbm, w_up_hbm, w_down_hbm = refs[4 + n_pieces : 7 + n_pieces]
    out_refs = refs[7 + n_pieces : 13 + n_pieces]
    (picks, weights, w_in, w_down, toks, rows, hidden, mixed, table_sems, tok_sems, in_sems,
     down_sems) = refs[13 + n_pieces :]
    n_z, _, tok_rows, model_width = toks.shape
    n_seq = 2 * n_z
    exp_dev, hid_dev, _ = w_gate_hbm.shape
    width = model_width // 8
    slots_src = exp_dev * SLOTS
    rep = lax.axis_index("rep")
    split = most_rows(tok_rows)
    def in_copies(e):
        at = lax.rem(e, RING)
        return [
            pltpu.make_async_copy(
                src.at[e], w_in.at[at, pl.ds(i * hid_dev, hid_dev)], in_sems.at[i, at]
            )
            for i, src in enumerate((w_gate_hbm, w_up_hbm))
        ]

    def down_copy(e):
        return pltpu.make_async_copy(w_down_hbm.at[e], w_down.at[e], down_sems.at[e])

    tables = [
        pltpu.make_async_copy(picks_hbm, picks, table_sems.at[0]),
        pltpu.make_async_copy(weights_hbm, weights, table_sems.at[1]),
    ]
    tables[0].start()

    kinds = token_pieces(n_z)
    pltpu.make_async_copy(own_hbm, toks.at[0, 0], tok_sems.at[0, 0]).start()
    for i, piece in enumerate(pieces_in):
        blocks, runs = kinds[i % len(kinds)]
        for n, (color, dx) in enumerate(runs):
            cols = pl.ds(group_offset(rep, color, dx, i // len(kinds), width), width)
            for at, dz, count, dy in blocks:
                for k in range(count):
                    pltpu.make_async_copy(
                        piece.at[at + k, pl.ds(0, tok_rows), pl.ds(n * width, width)],
                        toks.at[dz + k, dy, :, cols],
                        tok_sems.at[dz + k, dy],
                    ).start()
    for e in range(min(RING, exp_dev)):
        for copy in in_copies(e):
            copy.start()
    for e in range(exp_dev):
        down_copy(e).start()
    tables[1].start()
    quarters = [slice(2 * q * width, 2 * (q + 1) * width) for q in range(4)]
    tables[0].wait()

    def pick(dz, carry):
        for dy in range(2):
            pltpu.make_async_copy(toks.at[dz, dy], toks.at[dz, dy], tok_sems.at[dz, dy]).wait()
        for dy in range(2):
            onehot = picks[2 * dz + dy]
            for cols in quarters:
                got = contract(onehot, toks[dz, dy, :, cols], 1, 0).astype(jnp.bfloat16)
                rows[2 * dz + dy, :, :, cols] = got.reshape(exp_dev, SLOTS, 2 * width)
        return carry

    lax.fori_loop(0, n_z, pick, 0)

    def widen(pair, carry):
        experts = (2 * pair, 2 * pair + 1)
        for e in experts:
            for copy in in_copies(e):
                copy.wait()
        taken = [rows[:, e].reshape(n_seq * SLOTS, model_width) for e in experts]
        both = [
            [
                contract(value, w_in[lax.rem(e, RING), i * hid_dev : (i + 1) * hid_dev], 1, 1)
                for i in range(2)
            ]
            for e, value in zip(experts, taken)
        ]
        for e, (gate_val, up_val) in zip(experts, both):
            hidden[e] = (gate_val / (1.0 + jnp.exp(-gate_val)) * up_val).astype(jnp.bfloat16)
        for e in experts:

            @pl.when(e + RING < exp_dev)
            def _():
                for copy in in_copies(e + RING):
                    copy.start()

        return carry

    lax.fori_loop(0, exp_dev // 2, widen, 0)

    def narrow(pair, carry):
        experts = (2 * pair, 2 * pair + 1)
        for e in experts:
            down_copy(e).wait()
        for e in experts:
            for cols in quarters:
                piece = contract(hidden[e], w_down[e, :, cols], 1, 0).astype(jnp.bfloat16)
                rows[:, e, :, cols] = piece.reshape(n_seq, SLOTS, 2 * width)
        return carry

    lax.fori_loop(0, exp_dev // 2, narrow, 0)
    tables[1].wait()

    def combine(dz, carry):
        along = [jnp.zeros((tok_rows, 1), jnp.float32)] * 2
        for dy in range(2):
            j = 2 * dz + dy
            weight = weights[j]
            for cols in quarters:
                got = contract(weight, rows[j, :, :, cols].reshape(slots_src, 2 * width), 1, 0)
                mixed[dy, :, cols] = got
                along[dy] += jnp.sum(got * unit_ref[:, cols], axis=1, keepdims=True)
        for dy in range(2):
            for dc in range(2):
                far, near, rest = out_refs[3 * dc : 3 * dc + 3]
                for n, (color, dx) in enumerate(((0, 1), (0, 0), (1, 0), (1, 1))):
                    cols = pl.ds(group_offset(rep, color, dx, dc, width), width)
                    value = mixed[dy, :, cols] - along[dy] * unit_ref[:, cols]
                    value = value.astype(jnp.bfloat16)
                    rest[dz, dy, :, n * width : (n + 1) * width] = value[split:]
                    leaves, kind = (dy, 2 + dx) if color else (dx, dy)
                    (far if leaves else near)[kind, dz] = value[:split]
        return carry

    lax.fori_loop(0, n_z, combine, 0)


def moe_partial(picks, weights, unit_dir, own, pieces, w_gate, w_up, w_down):
    n_seq, _, tok_rows = picks.shape
    exp_dev, hid_dev, model_width = w_gate.shape
    width = model_width // 8
    vmem = pl.BlockSpec(memory_space=pltpu.VMEM)
    hbm = pl.BlockSpec(memory_space=pltpu.HBM)
    whole = pl.BlockSpec(memory_space=pl.ANY)
    n_pieces = len(pieces)
    pieces = [pltpu.with_memory_space_constraint(piece, pltpu.VMEM) for piece in pieces]
    picks, weights, own = [
        pltpu.with_memory_space_constraint(value, pltpu.HBM) for value in (picks, weights, own)
    ]
    n_z, split = n_seq // 2, most_rows(tok_rows)
    most = (4, n_z, split, width)
    rest = (n_z, 2, tok_rows - split, 4 * width)
    outs = [
        jax.ShapeDtypeStruct(shape, jnp.bfloat16) for _ in range(2) for shape in (most, most, rest)
    ]
    return pl.pallas_call(
        functools.partial(moe_kernel, n_pieces),
        out_shape=outs,
        in_specs=[hbm, hbm, vmem, hbm] + [whole] * n_pieces + [hbm] * 3,
        out_specs=[vmem] * len(outs),
        scratch_shapes=[
            pltpu.VMEM(picks.shape, jnp.bfloat16),
            pltpu.VMEM(weights.shape, jnp.bfloat16),
            pltpu.VMEM((RING, 2 * hid_dev, model_width), jnp.bfloat16),
            pltpu.VMEM(w_down.shape, jnp.bfloat16),
            pltpu.VMEM((n_z, 2, tok_rows, model_width), jnp.bfloat16),
            pltpu.VMEM((n_seq, exp_dev, SLOTS, model_width), jnp.bfloat16),
            pltpu.VMEM((exp_dev, n_seq * SLOTS, hid_dev), jnp.bfloat16),
            pltpu.VMEM((2, tok_rows, model_width), jnp.float32),
            pltpu.SemaphoreType.DMA((2,)),
            pltpu.SemaphoreType.DMA((n_z, 2)),
            pltpu.SemaphoreType.DMA((2, RING)),
            pltpu.SemaphoreType.DMA((exp_dev,)),
        ],
        compiler_params=pltpu.CompilerParams(vmem_limit_bytes=45 * 1024 * 1024),
        cost_estimate=pl.CostEstimate(
            flops=6 * n_seq * SLOTS * exp_dev * hid_dev * model_width,
            bytes_accessed=6 * exp_dev * hid_dev * model_width + 4 * n_seq * own.size,
            transcendentals=0,
        ),
    )(picks, weights, unit_dir, own, *pieces, w_gate, w_up, w_down)


def swap(value, axis, distance):
    size = lax.axis_size(axis)
    return lax.ppermute(value, axis, [(i, i ^ distance) for i in range(size)])


def added(*terms):
    return sum(term.astype(jnp.float32) for term in terms).astype(jnp.bfloat16)


def gathered(tokens, norm_gain, refusal_dir, expert_ids, gate_probs, w_gate, w_up, w_down):
    tok_rows, model_width = tokens.shape
    n_z = lax.axis_size("seq") // 2
    others = range(1, n_z)
    exp_dev = w_gate.shape[0]
    width = model_width // 8

    normed, second, first, to_y, unit_dir, base, meta = norm_and_base(
        tokens, norm_gain, refusal_dir, expert_ids, gate_probs
    )
    second = [swap(second, "seq", 2 * d) for d in others]
    from_y = swap(to_y[None], "seq", 1)
    first, second, from_y = lax.optimization_barrier((first, jnp.stack(second), from_y))
    first = jnp.stack([swap(first, "seq", 2 * d) for d in others])
    x_two = swap(second[:, :tok_rows], "rep", 2)
    y_one = swap(second, "seq", 1)
    y_two = swap(first, "seq", 1)
    x_one = swap(jnp.concatenate([from_y[:, :tok_rows, :width], first]), "rep", 2)
    to_y, to_core = lax.optimization_barrier((x_two, second))
    y_three = swap(to_y, "seq", 1)
    below = [meta, from_y[0, tok_rows:, :tok_rows]]
    for d in range(n_z - 1):
        below += [second[d, tok_rows:, :tok_rows], y_one[d, tok_rows:, :tok_rows]]
    picks, weights = route(jnp.stack(below), exp_dev)
    to_core_y, picks, weights = lax.optimization_barrier((from_y, picks, weights))
    early = [swap(piece, "rep", 1) for piece in (to_core, first, to_core_y)]
    x_three = swap(y_two, "rep", 2)
    last = [x_two, y_one, x_one, y_two, y_three, x_three]
    to_core = list(last)
    to_core[1:4] = lax.optimization_barrier((y_one, x_one, y_two))
    pieces = [second, first, from_y, *last, *early, *[swap(piece, "rep", 1) for piece in to_core]]

    sums = moe_partial(picks, weights, unit_dir, normed, pieces, w_gate, w_up, w_down)
    return (base + summed_up(sums[:3], sums[3:], width)).astype(jnp.bfloat16)


def summed_up(kept, sent, width):
    n_z = kept[0].shape[1]
    others = range(1, n_z)
    far, near, rest = zip(kept, [swap(piece, "rep", 1) for piece in sent])

    to_x, to_y, rest_kept = lax.optimization_barrier(
        (added(*[term[:2] for term in far]), added(*[term[2:] for term in far]), rest[0])
    )
    by_x, by_y = swap(to_x, "rep", 2), swap(to_y, "seq", 1)
    rest = added(rest_kept, rest[1])
    by_z = [swap(rest[d], "seq", 2 * d) for d in others]
    to_y, to_x, *by_z = lax.optimization_barrier(
        (
            added(*[term[1] for term in near], by_x[1]),
            added(*[term[3] for term in near], by_y[1]),
            *by_z,
        )
    )
    first_far, second_far = swap(to_y, "seq", 1), swap(to_x, "rep", 2)
    first = added(*[term[0] for term in near], by_x[0], first_far)
    second = added(*[term[2] for term in near], by_y[0], second_far)
    blocks = jnp.concatenate([first, second], axis=2)
    most = [swap(blocks[d], "seq", 2 * d) for d in reversed(others)] + [blocks[0]]
    rest = added(rest[0], *by_z)
    rest = added(rest[0], swap(rest[1], "seq", 1))
    far = jnp.concatenate([rest[:, :width], rest[:, 3 * width :]], axis=1)
    rest = [rest[:, width : 3 * width], swap(far, "rep", 2)]
    return jnp.concatenate(
        [sum(term.astype(jnp.float32) for term in terms) for terms in (most, rest)], axis=0
    )


def exchanged(tokens, norm_gain, refusal_dir, expert_ids, gate_probs, w_gate, w_up, w_down):
    tok_rows, model_width = tokens.shape
    top_k = expert_ids.shape[1]
    n_seq = lax.axis_size("seq")
    n_rep = lax.axis_size("rep")
    exp_dev = w_gate.shape[0]
    experts = exp_dev * n_seq
    slot_count = tok_rows * top_k
    part_width = model_width // n_rep
    tokens_f32 = tokens.astype(jnp.float32)
    inv_rms = lax.rsqrt(jnp.mean(tokens_f32 * tokens_f32, axis=1, keepdims=True) + 1e-06)
    normed = (tokens_f32 * inv_rms * norm_gain).astype(jnp.bfloat16)
    flat_ids = expert_ids.reshape(slot_count)
    onehot = (flat_ids[:, None] == jnp.arange(experts, dtype=jnp.int32)[None, :]).astype(jnp.int32)
    slot_rank = jnp.sum(jnp.cumsum(onehot, axis=0) * onehot, axis=1) - 1
    target = flat_ids * CAP + slot_rank
    repeated = jnp.broadcast_to(normed[:, None, :], (tok_rows, top_k, model_width)).reshape(
        slot_count, model_width
    )
    sendbuf = jnp.zeros((experts * CAP, model_width), jnp.bfloat16).at[target].set(repeated)
    sendbuf = sendbuf.reshape(n_seq, exp_dev, CAP, model_width)
    arrived = lax.all_to_all(sendbuf, "seq", split_axis=0, concat_axis=0, tiled=True)
    gate_val = jnp.einsum("secd,efd->secf", arrived, w_gate, preferred_element_type=jnp.float32)
    up_val = jnp.einsum("secd,efd->secf", arrived, w_up, preferred_element_type=jnp.float32)
    hidden = (jax.nn.silu(gate_val) * up_val).astype(jnp.bfloat16)
    pieces = jnp.einsum(
        "secf,efd->secd", hidden, w_down, preferred_element_type=jnp.float32
    ).astype(jnp.bfloat16)
    probs_flat = gate_probs.reshape(slot_count)[:, None]
    returned = lax.all_to_all(pieces, "seq", split_axis=0, concat_axis=0, tiled=True)
    returned = returned.reshape(experts * CAP, model_width)
    weighted = returned[target].astype(jnp.float32) * probs_flat
    moe_part = jnp.sum(weighted.reshape(tok_rows, top_k, model_width), axis=1)
    summed = lax.psum_scatter(
        moe_part.astype(jnp.bfloat16), "rep", scatter_dimension=1, tiled=True
    ).astype(jnp.float32)
    unit_dir = refusal_dir / jnp.sqrt(jnp.sum(refusal_dir * refusal_dir) + 1e-06)
    rep_offset = lax.axis_index("rep") * part_width
    unit_slice = lax.dynamic_slice_in_dim(unit_dir, rep_offset, part_width, 0)
    own_tokens = lax.dynamic_slice_in_dim(tokens_f32, rep_offset, part_width, 1)
    residual = own_tokens + summed
    along_dir = lax.psum(jnp.sum(residual * unit_slice, axis=1), "rep")
    return (residual - along_dir[:, None] * unit_slice).astype(jnp.bfloat16)


def local(tokens, norm_gain, refusal_dir, expert_ids, gate_probs, w_gate, w_up, w_down):
    plan = gathered if w_gate.shape[0] * CAP >= tokens.shape[0] else exchanged
    return plan(tokens, norm_gain, refusal_dir, expert_ids, gate_probs, w_gate, w_up, w_down)


def solution(mesh):
    placed = (
        P("seq", None),
        P(),
        P(),
        P("seq", None),
        P("seq", None),
        P("seq", "rep", None),
        P("seq", "rep", None),
        P("seq", "rep", None),
    )
    return jax.shard_map(
        local, mesh=mesh, in_specs=placed, out_specs=P("seq", "rep"), check_vma=False
    )
```
